32 devices in a mesh: batch: 8 (over z, core), seq: 4 (over y, x).
Axes of the slice: x: 2, y: 2, z: 4, core: 2. Of those that a mesh axis runs over, the one named last changes fastest.
Arguments:
- image_tokens: bfloat16 [16, 1024, 1536], P('batch', 'seq'), may hold values from -6 to 6
- text_tokens: bfloat16 [16, 160, 1536], P('batch', 'seq'), may hold values from -6 to 6
- conditioning: bfloat16 [16, 1536], P('batch'), may hold values from -6 to 6
- key_mask: int32 [16, 1184], P('batch'), may hold values from 0 to 1, as said below
- mod_weight: bfloat16 [2, 1536, 9216], P(None, None, ('batch', 'seq')), may hold values from -0.21875 to 0.21875
- mod_bias: bfloat16 [2, 9216], P(None, ('batch', 'seq')), may hold values from -3 to 3
- qkv_weight: bfloat16 [2, 1536, 4608], P(None, None, ('batch', 'seq')), may hold values from -0.15625 to 0.15625
- qv_bias: bfloat16 [2, 3072], P(None, ('batch', 'seq')), may hold values from -3 to 3
- out_weight: bfloat16 [2, 1536, 1536], P(None, None, ('batch', 'seq')), may hold values from -2.5 to 2.5
- out_bias: bfloat16 [2, 1536], P(None, ('batch', 'seq')), may hold values from -3 to 3
- up_weight: bfloat16 [2, 1536, 6144], P(None, None, ('batch', 'seq')), may hold values from -0.15625 to 0.15625
- up_bias: bfloat16 [2, 6144], P(None, ('batch', 'seq')), may hold values from -3 to 3
- down_weight: bfloat16 [2, 1536, 6144], P(None, None, ('batch', 'seq')), may hold values from -0.078125 to 0.078125
- down_bias: bfloat16 [2, 1536], P(None, ('batch', 'seq')), may hold values from -3 to 3
- image_cotangent: bfloat16 [16, 1024, 1536], P('batch', 'seq'), may hold values from -6 to 6
- text_cotangent: bfloat16 [16, 160, 1536], P('batch', 'seq'), may hold values from -6 to 6
Outputs:
- image_out: bfloat16 [16, 1024, 1536], P('batch', 'seq')
- text_out: bfloat16 [16, 160, 1536], P('batch', 'seq')
- image_grad: float32 [16, 1024, 1536], P('batch', 'seq')
- text_grad: float32 [16, 160, 1536], P('batch', 'seq')
- cond_grad: float32 [16, 1536], P('batch')
- mod_weight_grad: float32 [2, 1536, 9216], P(None, None, ('batch', 'seq'))
- mod_bias_grad: float32 [2, 9216], P(None, ('batch', 'seq'))
- qkv_weight_grad: float32 [2, 1536, 4608], P(None, None, ('batch', 'seq'))
- qv_bias_grad: float32 [2, 3072], P(None, ('batch', 'seq'))
- out_weight_grad: float32 [2, 1536, 1536], P(None, None, ('batch', 'seq'))
- out_bias_grad: float32 [2, 1536], P(None, ('batch', 'seq'))
- up_weight_grad: float32 [2, 1536, 6144], P(None, None, ('batch', 'seq'))
- up_bias_grad: float32 [2, 6144], P(None, ('batch', 'seq'))
- down_weight_grad: float32 [2, 1536, 6144], P(None, None, ('batch', 'seq'))
- down_bias_grad: float32 [2, 1536], P(None, ('batch', 'seq'))
The draws below stay inside these ranges and needn't reach their ends.
Inputs may be any that keep to these rules, and one draw needn't show every extreme that they name: `key_mask`: in each sequence all 1024 image keys are live, and of its 160 text slots the first n are live and the rest masked, n drawn for each sequence between 40 and (24640) // 160; at least one sequence that is not masked has n = 154. Exactly one of the 16 sequences, drawn from the seed, has every key masked.
All inputs are finite; a program needn't handle non-finite values.
Results may differ from the reference program's by a relative error of at most 0.015.
The reference program's roundings to bfloat16 on the way count: a program that leaves them out, or rounds other values in their place, can miss the bound.
Values may be sent and summed in bfloat16 or wider, within the bound.
No kernel may reach another device: no remote copies, remote signals or barrier semaphores. Data moves between devices by JAX's collectives and lax.ppermute only.
A program may use at most 704 MiB of HBM per device.

```python
import math
import jax
import jax.numpy as jnp
from jax import lax

D = 1536
HEADS = 24
FF = 6144
IMG = 1024
TXT = 160
SEQS = 2
SEQUENCES = 16
N_BATCH = 8


def draw_key_mask(key, part):
    key = jax.random.fold_in(key, 7)
    masked_key = jax.random.fold_in(key, 1)
    longest_key = jax.random.fold_in(key, 2)
    count_key = jax.random.fold_in(key, 3)
    masked_seq = jax.random.randint(masked_key, (), 0, SEQUENCES)
    longest_seq = (masked_seq + 1 + jax.random.randint(longest_key, (), 0, SEQUENCES - 1)) % SEQUENCES
    most_text = 154 * TXT // 160
    least_text = max(TXT // 4, 1)
    text_live = jax.random.randint(count_key, (SEQUENCES,), least_text, most_text + 1)
    sequence_ids = jnp.arange(SEQUENCES)
    text_live = jnp.where(sequence_ids == longest_seq, most_text, text_live)
    positions = jnp.arange(IMG + TXT)[None, :]
    live_keys = (positions < IMG + text_live[:, None]) & (sequence_ids[:, None] != masked_seq)
    return live_keys.astype(jnp.int32)


def level_of(stream_key, dims, split, smallest, high):
    gain = 1.0
    for axis_at, parts in split:
        steps = jax.random.uniform(jax.random.fold_in(jax.random.fold_in(stream_key, 6), axis_at), (parts,), jnp.float32, smallest / len(split), high / len(split))
        gain = gain * jnp.repeat(jnp.exp(steps), dims[axis_at] // parts).reshape((-1,) + (1,) * (len(dims) - 1 - axis_at))
    return gain


def bell_draw(rng, shape, spread, reach, cuts=(), dtype=jnp.bfloat16):
    gain = level_of(rng, shape, cuts, -0.22, 0.18) if cuts else 1.0
    values = jax.random.normal(rng, shape, jnp.float32) * spread * gain
    return jnp.minimum(jnp.maximum(values, -reach), reach).astype(dtype)


def setup_inputs(seed: int = 0) -> dict:
    key_list = jax.random.split(jax.random.key(seed), 17)
    image_tokens = bell_draw(key_list[0], (SEQUENCES, IMG, D), 1.0, 6.0, ((0, 8), (1, 4)))
    text_tokens = bell_draw(key_list[1], (SEQUENCES, TXT, D), 1.0, 6.0, ((0, 8), (1, 4)))
    conditioning = bell_draw(key_list[2], (SEQUENCES, D), 1.0, 6.0, ((0, 8),))
    key_mask = draw_key_mask(jax.random.fold_in(key_list[16], 71), 0)
    mod_weight = bell_draw(key_list[4], (2, D, 6 * D), (D // 2) ** -0.5, 0.21875, ((2, 32),))
    mod_bias = bell_draw(key_list[5], (2, 6 * D), 0.5, 3.0, ((1, 32),))
    qkv_weight = bell_draw(key_list[6], (2, D, 3 * D), D ** -0.5, 0.15625, ((2, 32),))
    qv_bias = bell_draw(key_list[7], (2, 2 * D), 0.5, 3.0, ((1, 32),))
    out_weight = bell_draw(key_list[8], (2, D, D), (max(D // 256, 1)) ** -0.5, 2.5, ((2, 32),))
    out_bias = bell_draw(key_list[9], (2, D), 0.5, 3.0, ((1, 32),))
    up_weight = bell_draw(key_list[10], (2, D, FF), D ** -0.5, 0.15625, ((2, 32),))
    up_bias = bell_draw(key_list[11], (2, FF), 0.5, 3.0, ((1, 32),))
    down_weight = bell_draw(key_list[12], (2, D, FF), FF ** -0.5, 0.078125, ((2, 32),))
    down_bias = bell_draw(key_list[13], (2, D), 0.5, 3.0, ((1, 32),))
    image_cotangent = bell_draw(key_list[14], (SEQUENCES, IMG, D), 1.0, 6.0, ((0, 8), (1, 4)))
    text_cotangent = bell_draw(key_list[15], (SEQUENCES, TXT, D), 1.0, 6.0, ((0, 8), (1, 4)))
    return dict(image_tokens=image_tokens, text_tokens=text_tokens, conditioning=conditioning, key_mask=key_mask, mod_weight=mod_weight, mod_bias=mod_bias, qkv_weight=qkv_weight, qv_bias=qv_bias, out_weight=out_weight, out_bias=out_bias, up_weight=up_weight, up_bias=up_bias, down_weight=down_weight, down_bias=down_bias, image_cotangent=image_cotangent, text_cotangent=text_cotangent)


NORM_EPSILON = 1e-06
FLOOR_SCORE = -10000.0
PRECISE = lax.Precision.HIGHEST

@jax.custom_vjp
def low(v):
    return lax.optimization_barrier(v.astype(jnp.bfloat16)).astype(jnp.float32)

@jax.custom_vjp
def low_back(v):
    return v

def low_keep(v):
    return (low(v), None)

def low_pass(kept, grad):
    return (grad,)

def back_keep(v):
    return (v, None)

def back_low(kept, grad):
    return (low(grad),)
low.defvjp(low_keep, low_pass)
low_back.defvjp(back_keep, back_low)

def modulate(tokens, shift_vec, scale_vec):
    row_mean = lax.optimization_barrier(jnp.mean(tokens, axis=-1, keepdims=True))
    centered = tokens - row_mean
    row_var = lax.optimization_barrier(jnp.mean(centered * centered, axis=-1, keepdims=True))
    return centered * lax.rsqrt(row_var + NORM_EPSILON) * (1.0 + scale_vec[:, None, :]) + shift_vec[:, None, :]

def group_layer(params, image_group, text_group, cond_group, mask_group):
    mod_weight, mod_bias, qkv_weight, qv_bias, out_weight, out_bias, up_weight, up_bias, down_weight, down_bias = params
    local_seqs, image_count, model_width = image_group.shape
    head_size = model_width // HEADS
    factor = 1.0 / math.sqrt(head_size)
    inputs = (image_group, text_group)
    smooth = low(jax.nn.silu(cond_group))
    modulations, queries, keys_list, values_list = ([], [], [], [])
    for modality in range(2):
        pieces = low_back(jnp.einsum('sd,df->sf', smooth, mod_weight[modality], precision=PRECISE) + mod_bias[modality])
        pieces = pieces.reshape(local_seqs, 6, model_width)
        normed = low(modulate(inputs[modality], pieces[:, 0], pieces[:, 1]))
        projected = jnp.einsum('srd,df->srf', normed, qkv_weight[modality], precision=PRECISE)
        queries.append(low(low_back(projected[..., :model_width] + qv_bias[modality, :model_width])))
        keys_list.append(low(low_back(projected[..., model_width:2 * model_width])))
        values_list.append(low(low_back(projected[..., 2 * model_width:] + qv_bias[modality, model_width:])))
        modulations.append(pieces)
    query_heads = jnp.concatenate(queries, axis=1).reshape(local_seqs, -1, HEADS, head_size)
    key_heads = jnp.concatenate(keys_list, axis=1).reshape(local_seqs, -1, HEADS, head_size)
    value_heads = jnp.concatenate(values_list, axis=1).reshape(local_seqs, -1, HEADS, head_size)
    key_live = (mask_group > 0)[:, None, None, :]
    scores = low_back(jnp.einsum('sqhe,skhe->shqk', query_heads, key_heads, precision=PRECISE) * factor)
    row_max = lax.optimization_barrier(jnp.max(jnp.where(key_live, scores, FLOOR_SCORE), axis=-1, keepdims=True))
    exp_terms = jnp.exp(jnp.where(key_live, scores - row_max, FLOOR_SCORE))
    probs = low(exp_terms / jnp.maximum(lax.optimization_barrier(jnp.sum(exp_terms, axis=-1, keepdims=True)), 1.0))
    attended = jnp.einsum('shqk,skhe->sqhe', probs, value_heads, precision=PRECISE).reshape(local_seqs, -1, model_width)
    attended = low(low_back(attended))
    results = []
    for modality in range(2):
        if modality == 0:
            branch_rows = attended[:, :image_count]
        else:
            branch_rows = attended[:, image_count:]
        pieces = modulations[modality]
        projection = low_back(jnp.einsum('srd,df->srf', branch_rows, out_weight[modality], precision=PRECISE) + out_bias[modality])
        middle = inputs[modality] + pieces[:, 2][:, None, :] * projection
        second = low(modulate(middle, pieces[:, 3], pieces[:, 4]))
        hidden_pre = low_back(jnp.einsum('srd,df->srf', second, up_weight[modality], precision=PRECISE) + up_bias[modality])
        hidden_act = low(jax.nn.gelu(hidden_pre, approximate=True))
        mlp_out = low_back(jnp.einsum('srf,df->srd', hidden_act, down_weight[modality], precision=PRECISE) + down_bias[modality])
        results.append(middle + pieces[:, 5][:, None, :] * mlp_out)
    return (results[0], results[1])

def reference(image_tokens, text_tokens, conditioning, key_mask, mod_weight, mod_bias, qkv_weight, qv_bias, out_weight, out_bias, up_weight, up_bias, down_weight, down_bias, image_cotangent, text_cotangent):
    params = tuple((array_in.astype(jnp.float32) for array_in in (mod_weight, mod_bias, qkv_weight, qv_bias, out_weight, out_bias, up_weight, up_bias, down_weight, down_bias)))
    image_all = image_tokens.astype(jnp.float32).reshape(N_BATCH, SEQS, IMG, D)
    text_all = text_tokens.astype(jnp.float32).reshape(N_BATCH, SEQS, TXT, D)
    cond_all = conditioning.astype(jnp.float32).reshape(N_BATCH, SEQS, D)
    mask_all = key_mask.reshape(N_BATCH, SEQS, IMG + TXT)

    def forward(image_in, text_in, cond_in, weights_in):

        def one_group(group):
            return group_layer(weights_in, group[0], group[1], group[2], group[3])
        return lax.map(jax.checkpoint(one_group), (image_in, text_in, cond_in, mask_all))
    outputs, pullback = jax.vjp(forward, image_all, text_all, cond_all, params)
    image_cot = image_cotangent.astype(jnp.float32).reshape(N_BATCH, SEQS, IMG, D)
    text_cot = text_cotangent.astype(jnp.float32).reshape(N_BATCH, SEQS, TXT, D)
    image_grad, text_grad, cond_grad, weight_grads = pullback((image_cot, text_cot))
    return (outputs[0].reshape(SEQUENCES, IMG, D).astype(jnp.bfloat16), outputs[1].reshape(SEQUENCES, TXT, D).astype(jnp.bfloat16), image_grad.reshape(SEQUENCES, IMG, D), text_grad.reshape(SEQUENCES, TXT, D), cond_grad.reshape(SEQUENCES, D), weight_grads[0], weight_grads[1], weight_grads[2], weight_grads[3], weight_grads[4], weight_grads[5], weight_grads[6], weight_grads[7], weight_grads[8], weight_grads[9])
```

```python
import functools
import math

import jax
import jax.numpy as jnp
import numpy as np
from jax import lax
from jax.experimental import pallas as pl
from jax.experimental.pallas import tpu as pltpu
from jax.sharding import PartitionSpec as P

HEADS = 24


NORM_EPSILON = 1e-06
FLOOR_SCORE = -10000.0


def modulate(tokens, shift_vec, scale_vec):
    row_mean = jnp.mean(tokens, axis=-1, keepdims=True)
    centered = tokens - row_mean
    row_var = jnp.mean(centered * centered, axis=-1, keepdims=True)
    return (
        centered * lax.rsqrt(row_var + NORM_EPSILON) * (1.0 + scale_vec[:, None, :])
        + shift_vec[:, None, :]
    )


def gelu_tanh(values):
    return jax.nn.gelu(values, approximate=True)


def unmix_columns(values, seq_devices, batch_devices):
    array_shape = values.shape
    piece_width = array_shape[-1] // (seq_devices * batch_devices)
    grid_view = values.reshape(array_shape[:-1] + (seq_devices, batch_devices, piece_width))
    return jnp.swapaxes(grid_view, -3, -2).reshape(array_shape)


def remix_columns(values, seq_devices, batch_devices):
    array_shape = values.shape
    piece_width = array_shape[-1] // (seq_devices * batch_devices)
    grid_view = values.reshape(array_shape[:-1] + (batch_devices, seq_devices, piece_width))
    return jnp.swapaxes(grid_view, -3, -2).reshape(array_shape)


def fetch_columns(
    up_weight,
    down_weight,
    mod_weight,
    qkv_weight,
    out_weight,
    up_bias,
    mod_bias,
    qv_bias,
    out_bias,
    down_bias,
):
    return (
        lax.all_gather(up_weight, "batch", axis=2, tiled=True),
        lax.all_gather(down_weight, "batch", axis=2, tiled=True),
        lax.all_gather(mod_weight, "batch", axis=2, tiled=True),
        lax.all_gather(qkv_weight, "batch", axis=2, tiled=True),
        lax.all_gather(out_weight, "batch", axis=2, tiled=True),
        lax.all_gather(up_bias, "batch", axis=1, tiled=True),
        lax.all_gather(mod_bias, "batch", axis=1, tiled=True),
        lax.all_gather(qv_bias, "batch", axis=1, tiled=True),
        lax.all_gather(out_bias, "batch", axis=1, tiled=True),
        lax.all_gather(down_bias, "batch", axis=1, tiled=True),
    )


def fetch_modulation(mod_part, mod_bias_part):
    return (
        lax.all_gather(mod_part, "seq", axis=2, tiled=True),
        lax.all_gather(mod_bias_part, "seq", axis=1, tiled=True),
    )


def gather_rows(first, second):
    return (
        lax.all_gather(first, "seq", axis=1, tiled=True),
        lax.all_gather(second, "seq", axis=1, tiled=True),
    )


def sum_rows(first, second, seq_devices):
    local_seqs, first_rows, width = first.shape
    first_local = first_rows // seq_devices
    second_local = second.shape[1] // seq_devices
    joined = jnp.concatenate(
        [
            first.reshape(local_seqs, seq_devices, first_local, width),
            second.reshape(local_seqs, seq_devices, second_local, width),
        ],
        axis=2,
    )
    joined = joined.reshape(local_seqs, seq_devices * (first_local + second_local), width)
    total = lax.psum_scatter(joined, "seq", scatter_dimension=1, tiled=True)
    return (total[:, :first_local], total[:, first_local:])


def to_rows(first, second):
    return (
        lax.all_to_all(first, "seq", split_axis=1, concat_axis=2, tiled=True),
        lax.all_to_all(second, "seq", split_axis=1, concat_axis=2, tiled=True),
    )


def to_columns(first, second):
    return (
        lax.all_to_all(first, "seq", split_axis=2, concat_axis=1, tiled=True),
        lax.all_to_all(second, "seq", split_axis=2, concat_axis=1, tiled=True),
    )


def own_block(values, seq_index, seq_devices):
    width = values.shape[1] // seq_devices
    return lax.dynamic_slice_in_dim(values, seq_index * width, width, 1)


def general_layer(
    image_tokens,
    text_tokens,
    conditioning,
    key_mask,
    mod_weight,
    mod_bias,
    qkv_weight,
    qv_bias,
    out_weight,
    out_bias,
    up_weight,
    up_bias,
    down_weight,
    down_bias,
    image_cotangent,
    text_cotangent,
):
    seq_devices = lax.axis_size("seq")
    batch_devices = lax.axis_size("batch")
    seq_index = lax.axis_index("seq")
    local_seqs, image_count, model_width = image_tokens.shape
    text_count = text_tokens.shape[1]
    block_rows = image_count + text_count
    key_count = block_rows * seq_devices
    head_size = model_width // HEADS
    factor = 1.0 / math.sqrt(head_size)
    inputs = (image_tokens.astype(jnp.float32), text_tokens.astype(jnp.float32))
    cotangents = (image_cotangent.astype(jnp.float32), text_cotangent.astype(jnp.float32))
    row_spans = ((0, image_count), (image_count, block_rows))
    image_keys = key_mask[:, : image_count * seq_devices].reshape(
        local_seqs, seq_devices, image_count
    )
    text_keys = key_mask[:, image_count * seq_devices :].reshape(
        local_seqs, seq_devices, text_count
    )
    key_live = (
        jnp.concatenate([image_keys, text_keys], axis=2).reshape(local_seqs, key_count) > 0
    )[:, None, None, :]
    cond_float = conditioning.astype(jnp.float32)
    smooth = jax.nn.silu(cond_float).astype(jnp.bfloat16)
    fetched = fetch_columns(
        up_weight,
        down_weight,
        mod_weight,
        qkv_weight,
        out_weight,
        up_bias,
        mod_bias,
        qv_bias,
        out_bias,
        down_bias,
    )
    (
        up_part,
        down_part,
        mod_part,
        qkv_part,
        out_part,
        up_bias_part,
        mod_bias_part,
        qv_part,
        out_bias_part,
        down_bias_part,
    ) = fetched
    mod_full, mod_bias_full = fetch_modulation(mod_part, mod_bias_part)
    mixed_mod = (
        jnp.einsum("sd,tdf->tsf", smooth, mod_full, preferred_element_type=jnp.float32)
        + mod_bias_full.astype(jnp.float32)[:, None, :]
    )
    modulation = unmix_columns(mixed_mod, seq_devices, batch_devices).reshape(
        2, local_seqs, 6, model_width
    )
    first_norms = []
    for modality in range(2):
        pieces = modulation[modality]
        first_norms.append(
            modulate(inputs[modality], pieces[:, 0], pieces[:, 1]).astype(jnp.bfloat16)
        )
    norm_image_all, norm_text_all, qv_seq, out_bias_seq, down_bias_seq = (
        lax.all_gather(first_norms[0], "seq", axis=1, tiled=True),
        lax.all_gather(first_norms[1], "seq", axis=1, tiled=True),
        lax.all_gather(qv_part, "seq", axis=1, tiled=True),
        lax.all_gather(out_bias_part, "seq", axis=1, tiled=True),
        lax.all_gather(down_bias_part, "seq", axis=1, tiled=True),
    )
    first_all = (norm_image_all, norm_text_all)
    qv_full = unmix_columns(qv_seq, seq_devices, batch_devices).astype(jnp.float32)
    out_bias_full = unmix_columns(out_bias_seq, seq_devices, batch_devices).astype(jnp.float32)
    down_bias_full = unmix_columns(down_bias_seq, seq_devices, batch_devices).astype(jnp.float32)
    qkv_cols = [
        jnp.einsum(
            "srd,df->srf",
            first_all[modality],
            qkv_part[modality],
            preferred_element_type=jnp.float32,
        )
        for modality in range(2)
    ]
    qkv_rows = to_rows(qkv_cols[0], qkv_cols[1])
    queries, keyvals = ([], [])
    for modality in range(2):
        projected = unmix_columns(qkv_rows[modality], seq_devices, batch_devices)
        qv_vector = qv_full[modality]
        queries.append(
            (projected[..., :model_width] + qv_vector[:model_width]).astype(jnp.bfloat16)
        )
        value_shift = jnp.concatenate(
            [jnp.zeros((model_width,), jnp.float32), qv_vector[model_width:]]
        )
        keyvals.append((projected[..., model_width:] + value_shift).astype(jnp.bfloat16))
    joined_query = jnp.concatenate(queries, axis=1)
    joined_keyval = jnp.concatenate(keyvals, axis=1)
    all_keyval = lax.all_gather(joined_keyval, "seq", axis=1, tiled=True)
    query_heads = joined_query.reshape(local_seqs, block_rows, HEADS, head_size)
    key_heads = all_keyval[..., :model_width].reshape(local_seqs, key_count, HEADS, head_size)
    value_heads = all_keyval[..., model_width:].reshape(local_seqs, key_count, HEADS, head_size)
    scores = (
        jnp.einsum("sqhe,skhe->shqk", query_heads, key_heads, preferred_element_type=jnp.float32)
        * factor
    )
    row_max = jnp.max(jnp.where(key_live, scores, FLOOR_SCORE), axis=-1, keepdims=True)
    exp_terms = jnp.exp(jnp.where(key_live, scores - row_max, FLOOR_SCORE))
    denominator = jnp.maximum(jnp.sum(exp_terms, axis=-1, keepdims=True), 1.0)
    prob_low = (exp_terms / denominator).astype(jnp.bfloat16)
    logsum = row_max + jnp.log(denominator)
    attended = jnp.einsum(
        "shqk,skhe->sqhe", prob_low, value_heads, preferred_element_type=jnp.float32
    )
    attended = attended.reshape(local_seqs, block_rows, model_width).astype(jnp.bfloat16)
    attended_all = gather_rows(attended[:, :image_count], attended[:, image_count:])
    out_cols = [
        jnp.einsum(
            "srd,df->srf",
            attended_all[modality],
            out_part[modality],
            preferred_element_type=jnp.float32,
        )
        for modality in range(2)
    ]
    out_rows = to_rows(out_cols[0], out_cols[1])
    projections, middles, second_norms = ([], [], [])
    for modality in range(2):
        pieces = modulation[modality]
        projection = (
            unmix_columns(out_rows[modality], seq_devices, batch_devices) + out_bias_full[modality]
        )
        middle = inputs[modality] + pieces[:, 2][:, None, :] * projection
        second_norms.append(modulate(middle, pieces[:, 3], pieces[:, 4]).astype(jnp.bfloat16))
        projections.append(projection)
        middles.append(middle)
    group_rows = gather_rows(second_norms[0], second_norms[1])
    hidden_pre, hidden_act, partials = ([], [], [])
    for modality in range(2):
        pre_values = jnp.einsum(
            "srd,df->srf",
            group_rows[modality],
            up_part[modality],
            preferred_element_type=jnp.float32,
        ) + up_bias_part[modality].astype(jnp.float32)
        act_values = gelu_tanh(pre_values).astype(jnp.bfloat16)
        partials.append(
            jnp.einsum(
                "srf,df->srd", act_values, down_part[modality], preferred_element_type=jnp.float32
            )
        )
        hidden_pre.append(pre_values)
        hidden_act.append(act_values)
    mlp_rows = sum_rows(partials[0], partials[1], seq_devices)
    mlp_outs, results = ([], [])
    for modality in range(2):
        pieces = modulation[modality]
        mlp_value = mlp_rows[modality] + down_bias_full[modality]
        results.append(
            (middles[modality] + pieces[:, 5][:, None, :] * mlp_value).astype(jnp.bfloat16)
        )
        mlp_outs.append(mlp_value)
    fetched_back = fetch_columns(
        up_weight,
        down_weight,
        mod_weight,
        qkv_weight,
        out_weight,
        up_bias,
        mod_bias,
        qv_bias,
        out_bias,
        down_bias,
    )
    up_back, down_back, mod_back, qkv_back, out_back = (
        fetched_back[0],
        fetched_back[1],
        fetched_back[2],
        fetched_back[3],
        fetched_back[4],
    )
    mod_bias_back = fetched_back[6]
    mlp_grads, gate_twos, down_bias_grads = ([], [], [])
    for modality in range(2):
        pieces = modulation[modality]
        mlp_grad = (pieces[:, 5][:, None, :] * cotangents[modality]).astype(jnp.bfloat16)
        gate_twos.append(jnp.sum(cotangents[modality] * mlp_outs[modality], axis=1))
        down_bias_grads.append(jnp.sum(mlp_grad.astype(jnp.float32), axis=(0, 1)))
        mlp_grads.append(mlp_grad)
    group_grads = gather_rows(mlp_grads[0], mlp_grads[1])
    down_grads, up_grads, up_bias_grads, norm_partials = ([], [], [], [])
    for modality in range(2):
        down_grads.append(
            jnp.einsum(
                "srd,srf->df",
                group_grads[modality],
                hidden_act[modality],
                preferred_element_type=jnp.float32,
            )
        )
        act_grad = jnp.einsum(
            "srd,df->srf",
            group_grads[modality],
            down_back[modality],
            preferred_element_type=jnp.float32,
        )
        pullback = jax.vjp(gelu_tanh, hidden_pre[modality])[1]
        pre_grad = pullback(act_grad)[0].astype(jnp.bfloat16)
        up_grads.append(
            jnp.einsum(
                "srd,srf->df", group_rows[modality], pre_grad, preferred_element_type=jnp.float32
            )
        )
        up_bias_grads.append(jnp.sum(pre_grad.astype(jnp.float32), axis=(0, 1)))
        norm_partials.append(
            jnp.einsum(
                "srf,df->srd", pre_grad, up_back[modality], preferred_element_type=jnp.float32
            )
        )
    norm_grads = sum_rows(norm_partials[0], norm_partials[1], seq_devices)
    middle_grads, shift_twos, scale_twos, gate_ones, out_bias_grads, proj_grads = (
        [],
        [],
        [],
        [],
        [],
        [],
    )
    for modality in range(2):
        pieces = modulation[modality]
        pullback = jax.vjp(modulate, middles[modality], pieces[:, 3], pieces[:, 4])[1]
        middle_part, shift_two, scale_two = pullback(norm_grads[modality])
        middle_grad = cotangents[modality] + middle_part
        proj_grad = (pieces[:, 2][:, None, :] * middle_grad).astype(jnp.bfloat16)
        gate_ones.append(jnp.sum(middle_grad * projections[modality], axis=1))
        out_bias_grads.append(jnp.sum(proj_grad.astype(jnp.float32), axis=(0, 1)))
        proj_grads.append(remix_columns(proj_grad, seq_devices, batch_devices))
        middle_grads.append(middle_grad)
        shift_twos.append(shift_two)
        scale_twos.append(scale_two)
    proj_cols = to_columns(proj_grads[0], proj_grads[1])
    out_grads, attended_partials = ([], [])
    for modality in range(2):
        out_grads.append(
            jnp.einsum(
                "srd,srf->df",
                attended_all[modality],
                proj_cols[modality],
                preferred_element_type=jnp.float32,
            )
        )
        attended_partials.append(
            jnp.einsum(
                "srf,df->srd",
                proj_cols[modality],
                out_back[modality],
                preferred_element_type=jnp.float32,
            )
        )
    attended_sums = sum_rows(attended_partials[0], attended_partials[1], seq_devices)
    attended_grad = jnp.concatenate([attended_sums[0], attended_sums[1]], axis=1).astype(
        jnp.bfloat16
    )
    grad_heads = attended_grad.reshape(local_seqs, block_rows, HEADS, head_size)
    scores_again = (
        jnp.einsum("sqhe,skhe->shqk", query_heads, key_heads, preferred_element_type=jnp.float32)
        * factor
    )
    probs_again = jnp.exp(jnp.where(key_live, scores_again - logsum, FLOOR_SCORE))
    probs_again_low = probs_again.astype(jnp.bfloat16)
    prob_grad = jnp.einsum(
        "sqhe,skhe->shqk", grad_heads, value_heads, preferred_element_type=jnp.float32
    )
    inner_sum = jnp.sum(probs_again * prob_grad, axis=-1, keepdims=True)
    score_grad = (probs_again * (prob_grad - inner_sum)).astype(jnp.bfloat16)
    query_grad = (
        jnp.einsum("shqk,skhe->sqhe", score_grad, key_heads, preferred_element_type=jnp.float32)
        * factor
    )
    query_grad = query_grad.reshape(local_seqs, block_rows, model_width).astype(jnp.bfloat16)
    key_grad = (
        jnp.einsum("shqk,sqhe->skhe", score_grad, query_heads, preferred_element_type=jnp.float32)
        * factor
    )
    value_grad = jnp.einsum(
        "shqk,sqhe->skhe", probs_again_low, grad_heads, preferred_element_type=jnp.float32
    )
    key_rows, value_rows = (
        lax.psum_scatter(
            key_grad.reshape(local_seqs, key_count, model_width),
            "seq",
            scatter_dimension=1,
            tiled=True,
        ),
        lax.psum_scatter(
            value_grad.reshape(local_seqs, key_count, model_width),
            "seq",
            scatter_dimension=1,
            tiled=True,
        ),
    )
    key_rows = key_rows.astype(jnp.bfloat16)
    value_rows = value_rows.astype(jnp.bfloat16)
    qv_bias_grads, joined_grads = ([], [])
    for modality in range(2):
        row_start, row_stop = row_spans[modality]
        query_part = query_grad[:, row_start:row_stop]
        value_part = value_rows[:, row_start:row_stop]
        joined_grad = jnp.concatenate(
            [query_part, key_rows[:, row_start:row_stop], value_part], axis=-1
        )
        qv_bias_grads.append(
            jnp.concatenate(
                [
                    jnp.sum(query_part.astype(jnp.float32), axis=(0, 1)),
                    jnp.sum(value_part.astype(jnp.float32), axis=(0, 1)),
                ]
            )
        )
        joined_grads.append(remix_columns(joined_grad, seq_devices, batch_devices))
    qkv_grad_cols = to_columns(joined_grads[0], joined_grads[1])
    qkv_grads, first_partials = ([], [])
    for modality in range(2):
        qkv_grads.append(
            jnp.einsum(
                "srd,srf->df",
                first_all[modality],
                qkv_grad_cols[modality],
                preferred_element_type=jnp.float32,
            )
        )
        first_partials.append(
            jnp.einsum(
                "srf,df->srd",
                qkv_grad_cols[modality],
                qkv_back[modality],
                preferred_element_type=jnp.float32,
            )
        )
    first_grads = sum_rows(first_partials[0], first_partials[1], seq_devices)
    input_grads, mod_partials = ([], [])
    for modality in range(2):
        pieces = modulation[modality]
        pullback = jax.vjp(modulate, inputs[modality], pieces[:, 0], pieces[:, 1])[1]
        input_part, shift_one, scale_one = pullback(first_grads[modality])
        input_grads.append(middle_grads[modality] + input_part)
        stacked = jnp.stack(
            [
                shift_one,
                scale_one,
                gate_ones[modality],
                shift_twos[modality],
                scale_twos[modality],
                gate_twos[modality],
            ],
            axis=1,
        )
        mod_partials.append(stacked.reshape(local_seqs, 6 * model_width))
    qv_mixed = remix_columns(jnp.stack(qv_bias_grads), seq_devices, batch_devices)
    out_bias_mixed = remix_columns(jnp.stack(out_bias_grads), seq_devices, batch_devices)
    down_bias_mixed = remix_columns(jnp.stack(down_bias_grads), seq_devices, batch_devices)
    mod_sum, qv_summed, out_bias_summed, down_bias_summed = lax.psum(
        (jnp.stack(mod_partials), qv_mixed, out_bias_mixed, down_bias_mixed), "seq"
    )
    mod_low = mod_sum.astype(jnp.bfloat16)
    mod_mixed = remix_columns(mod_low, seq_devices, batch_devices)
    columns = mod_part.shape[2]
    own_columns = lax.dynamic_slice_in_dim(mod_mixed, seq_index * columns, columns, 2)
    mod_grad = jnp.einsum("sd,tsf->tdf", smooth, own_columns, preferred_element_type=jnp.float32)
    mod_bias_grad = jnp.sum(own_columns.astype(jnp.float32), axis=1)
    mod_again = fetch_modulation(mod_back, mod_bias_back)[0]
    smooth_grad = jnp.einsum(
        "tsf,tdf->sd", mod_mixed, mod_again, preferred_element_type=jnp.float32
    )
    cond_pullback = jax.vjp(jax.nn.silu, cond_float)[1]
    cond_grad = cond_pullback(smooth_grad)[0]
    qv_own = own_block(qv_summed, seq_index, seq_devices)
    out_bias_own = own_block(out_bias_summed, seq_index, seq_devices)
    down_bias_own = own_block(down_bias_summed, seq_index, seq_devices)
    column_grads = (
        lax.psum_scatter(jnp.stack(up_grads), "batch", scatter_dimension=2, tiled=True),
        lax.psum_scatter(jnp.stack(down_grads), "batch", scatter_dimension=2, tiled=True),
        lax.psum_scatter(mod_grad, "batch", scatter_dimension=2, tiled=True),
        lax.psum_scatter(jnp.stack(qkv_grads), "batch", scatter_dimension=2, tiled=True),
        lax.psum_scatter(jnp.stack(out_grads), "batch", scatter_dimension=2, tiled=True),
        lax.psum_scatter(jnp.stack(up_bias_grads), "batch", scatter_dimension=1, tiled=True),
        lax.psum_scatter(mod_bias_grad, "batch", scatter_dimension=1, tiled=True),
        lax.psum_scatter(qv_own, "batch", scatter_dimension=1, tiled=True),
        lax.psum_scatter(out_bias_own, "batch", scatter_dimension=1, tiled=True),
        lax.psum_scatter(down_bias_own, "batch", scatter_dimension=1, tiled=True),
    )
    return (
        results[0],
        results[1],
        input_grads[0],
        input_grads[1],
        cond_grad,
        column_grads[2],
        column_grads[6],
        column_grads[3],
        column_grads[7],
        column_grads[4],
        column_grads[8],
        column_grads[0],
        column_grads[5],
        column_grads[1],
        column_grads[9],
    )


LOG2E = 1.4426950408889634
DEAD = -1e30
BF16 = jnp.bfloat16
F32 = jnp.float32


def dot_nt(a, b):
    return lax.dot_general(a, b, (((1,), (1,)), ((), ())), preferred_element_type=F32)


def dot_nn(a, b):
    return lax.dot_general(a, b, (((1,), (0,)), ((), ())), preferred_element_type=F32)


def dot_tn(a, b):
    return lax.dot_general(a, b, (((0,), (0,)), ((), ())), preferred_element_type=F32)


def attention_kernel(
    query_rows, scale, head, bias_ref, floor_ref, qi, qt, ki, kt, vi, vt, oi, ot, keys, values
):
    image_rows = qi.shape[0]
    keys[:image_rows] = ki[...]
    keys[image_rows:] = kt[...]
    values[:image_rows] = vi[...]
    values[image_rows:] = vt[...]
    bias = bias_ref[...]
    floor = floor_ref[0, 0]
    spans = [(qi, oi, start, query_rows) for start in range(0, image_rows, query_rows)]
    spans.append((qt, ot, 0, qt.shape[0]))
    for source, target, start, size in spans:
        sides = []
        for side in range(2):
            lanes = slice(side * head, (side + 1) * head)
            scores = dot_nt(source[start : start + size, lanes], keys[:, lanes]) * scale + bias
            row_max = jnp.maximum(jnp.max(scores, axis=1, keepdims=True), floor)
            exps = jnp.exp2(scores - row_max)
            total = jnp.maximum(jnp.sum(exps, axis=1, keepdims=True), 1.0)
            probs = (exps * (1.0 / total)).astype(BF16)
            sides.append(dot_nn(probs, values[:, lanes]))
        target[start : start + size, :] = jnp.concatenate(sides, axis=1).astype(BF16)


def pair_block(rows, lanes, pairs, part):
    return pl.BlockSpec((rows, lanes), lambda pair: (0, part * pairs + pair))


def attention(qkv_image, qkv_text, key_bias, floor, head):
    image_rows, width = qkv_image.shape
    text_rows = qkv_text.shape[0]
    rows = image_rows + text_rows
    lanes = 2 * head
    pairs = width // (3 * lanes)
    columns = [
        pair_block(count, lanes, pairs, part)
        for part in range(3)
        for count in (image_rows, text_rows)
    ]
    return pl.pallas_call(
        functools.partial(attention_kernel, 256, LOG2E / math.sqrt(head), head),
        grid=(pairs,),
        in_specs=[
            pl.BlockSpec((1, rows), lambda pair: (0, 0)),
            pl.BlockSpec(memory_space=pltpu.SMEM),
            *columns,
        ],
        out_specs=[columns[0], columns[1]],
        out_shape=[
            jax.ShapeDtypeStruct((image_rows, width // 3), BF16),
            jax.ShapeDtypeStruct((text_rows, width // 3), BF16),
        ],
        scratch_shapes=[pltpu.VMEM((rows, lanes), BF16), pltpu.VMEM((rows, lanes), BF16)],
        compiler_params=pltpu.CompilerParams(vmem_limit_bytes=48 << 20),
        cost_estimate=pl.CostEstimate(
            flops=16 * rows * rows * width // 3,
            bytes_accessed=8 * rows * width // 3,
            transcendentals=rows * rows * width // (3 * head),
        ),
        name="attention",
    )(key_bias[None, :], floor, qkv_image, qkv_text, qkv_image, qkv_text, qkv_image, qkv_text)


def attention_back_kernel(
    query_rows, scale, factor, head, pairs,
    bias_ref, floor_ref, qi, qt, ki, kt, vi, vt, gi, gt, oi, ot, keys, values, key_sum, value_sum,
):
    pair = pl.program_id(0)
    image_rows = qi.shape[0]
    width = 2 * head
    keys[:image_rows] = ki[...]
    keys[image_rows:] = kt[...]
    values[:image_rows] = vi[...]
    values[image_rows:] = vt[...]
    key_sum[...] = jnp.zeros_like(key_sum)
    value_sum[...] = jnp.zeros_like(value_sum)
    bias = bias_ref[...]
    floor = floor_ref[0, 0]
    spans = [(qi, gi, oi, start, query_rows) for start in range(0, image_rows, query_rows)]
    spans.append((qt, gt, ot, 0, qt.shape[0]))
    query_lanes = pl.ds(pl.multiple_of(pair * width, width), width)
    key_lanes = pl.ds(pl.multiple_of((pairs + pair) * width, width), width)
    value_lanes = pl.ds(pl.multiple_of((2 * pairs + pair) * width, width), width)
    for source, grads, target, start, size in spans:
        wide_bias = jnp.concatenate([bias] * -(-size // 128), axis=1)[:, :size]
        dq, dk, dv = ([], [], [])
        for side in range(2):
            lanes = slice(side * head, (side + 1) * head)
            query = source[start : start + size, lanes]
            grad = grads[start : start + size, lanes]
            scores = dot_nt(keys[:, lanes], query) * scale + wide_bias
            top = jnp.maximum(jnp.max(scores, axis=0, keepdims=True), floor)
            exps = jnp.exp2(scores - top)
            total = jnp.maximum(jnp.sum(exps, axis=0, keepdims=True), 1.0)
            probs = exps * (1.0 / total)
            prob_grad = dot_nt(values[:, lanes], grad)
            weighted = probs * prob_grad
            inner = jnp.sum(weighted, axis=0, keepdims=True)
            score_grad = (weighted - probs * inner).astype(BF16)
            dv.append(dot_nn(probs.astype(BF16), grad))
            dk.append(dot_nn(score_grad, query))
            dq.append(dot_tn(score_grad, keys[:, lanes]))
        key_sum[...] += jnp.concatenate(dk, axis=1)
        value_sum[...] += jnp.concatenate(dv, axis=1)
        target[start : start + size, query_lanes] = (
            jnp.concatenate(dq, axis=1) * factor
        ).astype(BF16)
    oi[:, key_lanes] = (key_sum[:image_rows] * factor).astype(BF16)
    ot[:, key_lanes] = (key_sum[image_rows:] * factor).astype(BF16)
    oi[:, value_lanes] = value_sum[:image_rows].astype(BF16)
    ot[:, value_lanes] = value_sum[image_rows:].astype(BF16)


def attention_back(qkv_image, qkv_text, grad_image, grad_text, key_bias, floor, head):
    image_rows, width = qkv_image.shape
    text_rows = qkv_text.shape[0]
    rows = image_rows + text_rows
    lanes = 2 * head
    pairs = width // (3 * lanes)
    columns = [
        pair_block(count, lanes, pairs, part)
        for part in range(3)
        for count in (image_rows, text_rows)
    ]
    return pl.pallas_call(
        functools.partial(
            attention_back_kernel, 256, LOG2E / math.sqrt(head), 1.0 / math.sqrt(head), head, pairs
        ),
        grid=(pairs,),
        in_specs=[
            pl.BlockSpec((rows, 128), lambda pair: (0, 0)),
            pl.BlockSpec(memory_space=pltpu.SMEM),
            *columns,
            columns[0],
            columns[1],
        ],
        out_specs=[
            pl.BlockSpec((image_rows, width), lambda pair: (0, 0)),
            pl.BlockSpec((text_rows, width), lambda pair: (0, 0)),
        ],
        out_shape=[
            jax.ShapeDtypeStruct((image_rows, width), BF16),
            jax.ShapeDtypeStruct((text_rows, width), BF16),
        ],
        scratch_shapes=[
            pltpu.VMEM((rows, lanes), BF16),
            pltpu.VMEM((rows, lanes), BF16),
            pltpu.VMEM((rows, lanes), F32),
            pltpu.VMEM((rows, lanes), F32),
        ],
        compiler_params=pltpu.CompilerParams(vmem_limit_bytes=48 << 20),
        cost_estimate=pl.CostEstimate(
            flops=40 * rows * rows * width // 3,
            bytes_accessed=16 * rows * width // 3,
            transcendentals=rows * rows * width // (3 * head),
        ),
        name="attention_back",
    )(
        jnp.broadcast_to(key_bias[:, None], (rows, 128)),
        floor,
        qkv_image, qkv_text, qkv_image, qkv_text, qkv_image, qkv_text,
        grad_image, grad_text,
    )


def flip(values, bit):
    return lax.ppermute(values, "seq", [(i, i ^ bit) for i in range(4)])


def gather_blocks(own):
    half = own.shape[1] // 2
    near_x = flip(own, 1)
    near_y = flip(own, 2)
    far_a = flip(near_x[:, :half], 2)
    far_b = flip(near_y[:, half:], 1)
    return (own, near_x, near_y, jnp.concatenate([far_a, far_b], axis=1))


def add_low(a, b):
    return (a.astype(F32) + b.astype(F32)).astype(BF16)


def scatter_blocks(blocks):
    own, near_x, near_y, far = blocks
    half = own.shape[1] // 2
    for_y = flip(far[:, :half], 1)
    for_x = flip(far[:, half:], 2)
    from_x_a = flip(near_x[:, :half], 1)
    from_y_b = flip(near_y[:, half:], 2)
    from_x_b = flip(add_low(near_x[:, half:], for_x), 1)
    from_y_a = flip(add_low(near_y[:, :half], for_y), 2)
    return (
        own.astype(F32)
        + jnp.concatenate([from_x_a, from_x_b], axis=1).astype(F32)
        + jnp.concatenate([from_y_a, from_y_b], axis=1).astype(F32)
    )


def join_rows(blocks, image_count):
    return (
        jnp.concatenate([block[:image_count] for block in blocks], axis=0),
        jnp.concatenate([block[image_count:] for block in blocks], axis=0),
    )


def split_rows(image, text, image_count, text_count):
    return [
        jnp.concatenate(
            [
                image[r * image_count : (r + 1) * image_count],
                text[r * text_count : (r + 1) * text_count],
            ],
            axis=0,
        )
        for r in range(4)
    ]


def match_units(batch_devices, seq_devices, per_device, group_units):
    devices = batch_devices * seq_devices
    total = devices * per_device
    part_units = total // 3
    sources, targets = ([], [])
    for seq_at in range(seq_devices):
        listed = [
            part * part_units + seq_at * group_units + k
            for part in range(3)
            for k in range(group_units)
        ]
        for place, unit in enumerate(listed):
            sources.append((unit // per_device, unit % per_device))
            targets.append(
                ((place // per_device) * seq_devices + seq_at, place % per_device)
            )
    edges = list(zip(sources, targets))
    rounds = []
    left = list(range(total))
    for _ in range(per_device):
        by_source = {}
        for e in left:
            by_source.setdefault(edges[e][0][0], []).append(e)
        taken = {}

        def place_edge(device, seen):
            for e in by_source[device]:
                target = edges[e][1][0]
                if target in seen:
                    continue
                seen.add(target)
                if target not in taken or place_edge(edges[taken[target]][0][0], seen):
                    taken[target] = e
                    return True
            return False

        for device in range(devices):
            place_edge(device, set())
        chosen = sorted(taken.values())
        rounds.append(chosen)
        left = [e for e in left if e not in chosen]
    send = np.zeros((per_device, devices), np.int32)
    land = np.zeros((per_device, devices), np.int32)
    perms = []
    for k, chosen in enumerate(rounds):
        pairs = []
        for e in chosen:
            (source, source_slot), (target, target_slot) = edges[e]
            pairs.append((source, target))
            send[k, source] = source_slot
            land[k, target] = target_slot
        perms.append(sorted(pairs))
    return perms, send, land


def move_units(units, perms, take, put, place):
    arrived = jnp.zeros_like(units)
    for k, pairs in enumerate(perms):
        slot = jnp.asarray(take[k])[place]
        moved = lax.ppermute(
            lax.dynamic_index_in_dim(units, slot, 0, keepdims=True), ("batch", "seq"), pairs
        )
        arrived = lax.dynamic_update_slice_in_dim(arrived, moved, jnp.asarray(put[k])[place], 0)
    return arrived


def gather_batch(values):
    return lax.all_gather(values, "batch", axis=0)


def scatter_batch(values):
    return lax.psum_scatter(values, "batch", scatter_dimension=0)


def swap(values, axis):
    return lax.all_to_all(values, axis, 0, 0, tiled=True)


def norm_stats(values):
    mean = jnp.mean(values, axis=-1, keepdims=True)
    centered = values - mean
    variance = jnp.mean(centered * centered, axis=-1, keepdims=True)
    return mean, lax.rsqrt(variance + NORM_EPSILON)


def norm_back(norm, inverse, grad, scale):
    scaled = grad * (1.0 + scale)
    return inverse * (
        scaled
        - jnp.mean(scaled, axis=-1, keepdims=True)
        - norm * jnp.mean(scaled * norm, axis=-1, keepdims=True)
    )


def swift_layer(
    image_tokens,
    text_tokens,
    conditioning,
    key_mask,
    mod_weight,
    mod_bias,
    qkv_weight,
    qv_bias,
    out_weight,
    out_bias,
    up_weight,
    up_bias,
    down_weight,
    down_bias,
    image_cotangent,
    text_cotangent,
):
    S = lax.axis_size("seq")
    B = lax.axis_size("batch")
    seq_index = lax.axis_index("seq")
    place = lax.axis_index(("batch", "seq"))
    L, image_count, D = image_tokens.shape
    text_count = text_tokens.shape[1]
    head = D // HEADS
    own_width = D // S
    spans = (slice(0, image_count), slice(image_count, image_count + text_count))

    bias_widths = [array.shape[1] for array in (qv_bias, out_bias, up_bias, down_bias)]
    bias_ends = np.cumsum(bias_widths)
    own_biases = jnp.concatenate([qv_bias, out_bias, up_bias, down_bias], axis=1)
    near = gather_batch(jnp.concatenate([conditioning, own_biases], axis=1))
    cond_all = near[:, :, :D].reshape(B * L, D)
    column_biases = near[:, :, D:].astype(F32)
    smooth_all = jax.nn.silu(cond_all.astype(F32)).astype(BF16)
    mod_own = (
        jnp.einsum("sd,tdf->tsf", smooth_all, mod_weight, preferred_element_type=F32)
        + mod_bias.astype(F32)[:, None, :]
    )
    mod_width = mod_own.shape[2]
    mod_sent = mod_own.reshape(2, B, L, mod_width).transpose(1, 0, 2, 3)
    mod_came = swap(mod_sent, "batch")
    small = jnp.concatenate(
        [mod_came.reshape(B, 2 * L * mod_width), column_biases.reshape(B, -1)], axis=1
    )
    small_all = lax.all_gather(small, "seq")
    modulation = (
        small_all[:, :, : 2 * L * mod_width]
        .reshape(S, B, 2, L, mod_width)
        .transpose(2, 3, 1, 0, 4)
        .reshape(2, L, 6, D)
    )
    bias_all = (
        small_all[:, :, 2 * L * mod_width :].reshape(S, B, 2, -1).transpose(2, 1, 0, 3)
    )
    qv_full = bias_all[..., : bias_ends[0]].reshape(2, 2 * D)
    out_bias_full = bias_all[..., bias_ends[0] : bias_ends[1]].reshape(2, D)
    down_bias_full = bias_all[..., bias_ends[2] :].reshape(2, D)
    up_bias_part = (
        column_biases[:, :, bias_ends[1] : bias_ends[2]].transpose(1, 0, 2).reshape(2, -1)
    )
    first_feature = seq_index * own_width
    qkv_bias = jnp.concatenate(
        [
            lax.dynamic_slice_in_dim(qv_full, first_feature, own_width, 1),
            jnp.zeros((2, own_width), F32),
            lax.dynamic_slice_in_dim(qv_full, D + first_feature, own_width, 1),
        ],
        axis=1,
    )

    unit = math.gcd(qkv_weight.shape[2], own_width)
    per_device = qkv_weight.shape[2] // unit
    perms, send, land = match_units(B, S, per_device, own_width // unit)
    back_perms = [[(target, source) for source, target in pairs] for pairs in perms]
    qkv_units = jnp.swapaxes(qkv_weight, 1, 2).reshape(2, per_device, unit, D).swapaxes(0, 1)
    qkv_mine = move_units(qkv_units, perms, send, land, place)
    out_units = jnp.swapaxes(out_weight, 1, 2).reshape(2, -1, S, own_width).transpose(2, 0, 1, 3)
    out_mine = swap(out_units, "seq")
    out_columns = out_mine.shape[2]
    heads_all = gather_batch(
        jnp.concatenate([qkv_mine.reshape(-1, D), out_mine.reshape(-1, D)], axis=0)
    )
    qkv_rows = 2 * per_device * unit
    qkv_all = heads_all[:, :qkv_rows].reshape(B, per_device, 2, unit, D)
    out_all = heads_all[:, qkv_rows:].reshape(B, S, 2, out_columns, own_width)
    hidden_all = gather_batch(
        jnp.stack([jnp.swapaxes(up_weight, 1, 2), jnp.swapaxes(down_weight, 1, 2)])
    )
    qkv_part = [qkv_all[:, :, t].reshape(-1, D) for t in range(2)]
    out_part = [out_all[:, :, t].reshape(D, own_width) for t in range(2)]
    up_part = [hidden_all[:, 0, t].reshape(-1, D) for t in range(2)]
    down_part = [hidden_all[:, 1, t].reshape(-1, D) for t in range(2)]
    hidden_columns = up_weight.shape[2]

    order = jnp.bitwise_xor(seq_index, jnp.arange(S))
    image_keys = jnp.take(
        key_mask[:, : S * image_count].reshape(L, S, image_count), order, axis=1
    ).reshape(L, -1)
    text_keys = jnp.take(
        key_mask[:, S * image_count :].reshape(L, S, text_count), order, axis=1
    ).reshape(L, -1)
    live = jnp.concatenate([image_keys, text_keys], axis=1) > 0
    key_bias = jnp.where(live, 0.0, DEAD).astype(F32)
    floors = jnp.where(jnp.all(live, axis=1), -3e38, FLOOR_SCORE * LOG2E).astype(F32)
    floors = floors.reshape(L, 1, 1)

    token_blocks, grad_blocks = ([], [])
    for s in range(L):
        token_blocks.append(
            gather_blocks(jnp.concatenate([image_tokens[s], text_tokens[s]], axis=0))
        )
    for s in range(L):
        grad_blocks.append(
            gather_blocks(jnp.concatenate([image_cotangent[s], text_cotangent[s]], axis=0))
        )
    tokens_all = [join_rows(blocks, image_count) for blocks in token_blocks]
    grads_all = [join_rows(blocks, image_count) for blocks in grad_blocks]
    own_tokens = [[image_tokens[s].astype(F32), text_tokens[s].astype(F32)] for s in range(L)]
    own_grads = [
        [image_cotangent[s].astype(F32), text_cotangent[s].astype(F32)] for s in range(L)
    ]

    first_norms, first_stats, qkvs, attended, projections, middles, middle_stats = (
        [], [], [], [], [], [], [],
    )
    second_all = []
    for s in range(L):
        norms, stats, rows = ([], [], [])
        for t in range(2):
            pieces = modulation[t, s]
            values = tokens_all[s][t].astype(F32)
            mean, inverse = norm_stats(values)
            norm = (
                (values - mean) * inverse * (1.0 + pieces[1][None, :]) + pieces[0][None, :]
            ).astype(BF16)
            rows.append((dot_nt(norm, qkv_part[t]) + qkv_bias[t][None, :]).astype(BF16))
            norms.append(norm)
            stats.append((mean, inverse))
        first_norms.append(norms)
        first_stats.append(stats)
        qkvs.append(rows)
        attended.append(attention(rows[0], rows[1], key_bias[s], floors[s], head))
    for s in range(L):
        partial = [dot_nt(attended[s][t], out_part[t]).astype(BF16) for t in range(2)]
        summed = scatter_blocks(split_rows(partial[0], partial[1], image_count, text_count))
        seconds = []
        kept_projection, kept_middle, kept_stats = ([], [], [])
        for t in range(2):
            pieces = modulation[t, s]
            projection = summed[spans[t]] + out_bias_full[t][None, :]
            middle = own_tokens[s][t] + pieces[2][None, :] * projection
            mean, inverse = norm_stats(middle)
            second = (middle - mean) * inverse * (1.0 + pieces[4][None, :]) + pieces[3][None, :]
            seconds.append(second.astype(BF16))
            kept_projection.append(projection)
            kept_middle.append(middle)
            kept_stats.append((mean, inverse))
        projections.append(kept_projection)
        middles.append(kept_middle)
        middle_stats.append(kept_stats)
        blocks = gather_blocks(jnp.concatenate(seconds, axis=0))
        second_all.append(join_rows(blocks, image_count))
    hidden_acts, hidden_pres, mlp_grads, pre_grads = ([], [], [], [])
    norm2_sums, mlp_sums = ([], [])
    for s in range(L):
        acts, pres, partial, grads, pre_low, back = ([], [], [], [], [], [])
        for t in range(2):
            pre = dot_nt(second_all[s][t], up_part[t]) + up_bias_part[t][None, :]
            act = gelu_tanh(pre).astype(BF16)
            acts.append(act)
            pres.append(pre)
            grad = (modulation[t, s][5][None, :] * grads_all[s][t].astype(F32)).astype(BF16)
            act_grad = dot_nt(grad, down_part[t])
            pre_grad = jax.vjp(gelu_tanh, pre)[1](act_grad)[0].astype(BF16)
            grads.append(grad)
            pre_low.append(pre_grad)
            back.append(dot_nn(pre_grad, up_part[t]).astype(BF16))
            partial.append(dot_nn(act, down_part[t]).astype(BF16))
        hidden_acts.append(acts)
        hidden_pres.append(pres)
        mlp_grads.append(grads)
        pre_grads.append(pre_low)
        norm2_sums.append(
            scatter_blocks(split_rows(back[0], back[1], image_count, text_count))
        )
        mlp_sums.append(
            scatter_blocks(split_rows(partial[0], partial[1], image_count, text_count))
        )

    def both(left, right, t):
        total = dot_tn(left[0][t], right[0][t])
        for s in range(1, L):
            total = total + dot_tn(left[s][t], right[s][t])
        return total.astype(BF16)

    up_sum = [both(pre_grads, second_all, t) for t in range(2)]
    down_sum = [both(hidden_acts, mlp_grads, t) for t in range(2)]
    hidden_grads = scatter_batch(
        jnp.stack(
            [
                jnp.stack([value.reshape(B, hidden_columns, D) for value in values], axis=1)
                for values in (up_sum, down_sum)
            ],
            axis=1,
        )
    )
    up_bias_sum = jnp.stack(
        [
            sum(jnp.sum(pre_grads[s][t].astype(F32), axis=0) for s in range(L))
            for t in range(2)
        ]
    )

    results = [[], []]
    mod_grads = [[[None] * 6 for _ in range(L)] for _ in range(2)]
    middle_grads, proj_all = ([], [])
    out_bias_sum = [0.0, 0.0]
    down_bias_sum = [0.0, 0.0]
    for s in range(L):
        kept, lows = ([], [])
        for t in range(2):
            pieces = modulation[t, s]
            grad = own_grads[s][t]
            mlp_value = mlp_sums[s][spans[t]] + down_bias_full[t][None, :]
            results[t].append(
                (middles[s][t] + pieces[5][None, :] * mlp_value).astype(BF16)
            )
            mod_grads[t][s][5] = jnp.sum(grad * mlp_value, axis=0)
            own_low = (pieces[5][None, :] * grad).astype(BF16)
            down_bias_sum[t] = down_bias_sum[t] + jnp.sum(own_low.astype(F32), axis=0)
            norm_grad = norm2_sums[s][spans[t]]
            mean, inverse = middle_stats[s][t]
            norm = (middles[s][t] - mean) * inverse
            mod_grads[t][s][3] = jnp.sum(norm_grad, axis=0)
            mod_grads[t][s][4] = jnp.sum(norm_grad * norm, axis=0)
            middle_grad = grad + norm_back(norm, inverse, norm_grad, pieces[4][None, :])
            mod_grads[t][s][2] = jnp.sum(middle_grad * projections[s][t], axis=0)
            low = (pieces[2][None, :] * middle_grad).astype(BF16)
            out_bias_sum[t] = out_bias_sum[t] + jnp.sum(low.astype(F32), axis=0)
            kept.append(middle_grad)
            lows.append(low)
        middle_grads.append(kept)
        proj_all.append(join_rows(gather_blocks(jnp.concatenate(lows, axis=0)), image_count))

    qkv_grads, norm1_sums = ([], [])
    for s in range(L):
        attended_grad = [dot_nn(proj_all[s][t], out_part[t]).astype(BF16) for t in range(2)]
        grads = attention_back(
            qkvs[s][0], qkvs[s][1], attended_grad[0], attended_grad[1], key_bias[s], floors[s], head
        )
        qkv_grads.append(grads)
        back = [dot_nn(grads[t], qkv_part[t]).astype(BF16) for t in range(2)]
        for t in range(2):
            wide = back[t].astype(F32)
            mean, inverse = first_stats[s][t]
            norm = (tokens_all[s][t].astype(F32) - mean) * inverse
            mod_grads[t][s][0] = jnp.sum(wide, axis=0)
            mod_grads[t][s][1] = jnp.sum(wide * norm, axis=0)
        norm1_sums.append(
            scatter_blocks(split_rows(back[0], back[1], image_count, text_count))
        )
    out_sum = [both(proj_all, attended, t) for t in range(2)]
    qkv_sum = [both(qkv_grads, first_norms, t) for t in range(2)]
    qkv_sent = jnp.stack(
        [value.reshape(B, per_device, unit, D) for value in qkv_sum], axis=2
    ).reshape(B, qkv_rows, D)
    out_sent = jnp.stack(
        [value.reshape(B, S, out_columns, own_width) for value in out_sum], axis=2
    ).reshape(B, -1, D)
    head_grads = scatter_batch(jnp.concatenate([qkv_sent, out_sent], axis=1))
    qkv_home = move_units(
        head_grads[:qkv_rows].reshape(per_device, 2, unit, D), back_perms, land, send, place
    )
    out_home = swap(head_grads[qkv_rows:].reshape(S, 2, out_columns, own_width), "seq")
    qkv_weight_grad = qkv_home.swapaxes(0, 1).reshape(2, -1, D).swapaxes(1, 2).astype(F32)
    out_weight_grad = (
        out_home.transpose(1, 2, 0, 3).reshape(2, out_columns, D).swapaxes(1, 2).astype(F32)
    )
    up_weight_grad = hidden_grads[0].swapaxes(1, 2).astype(F32)
    down_weight_grad = hidden_grads[1].swapaxes(1, 2).astype(F32)

    input_grads = [[], []]
    for s in range(L):
        for t in range(2):
            mean, inverse = norm_stats(own_tokens[s][t])
            norm = (own_tokens[s][t] - mean) * inverse
            input_grads[t].append(
                middle_grads[s][t]
                + norm_back(
                    norm, inverse, norm1_sums[s][spans[t]], modulation[t, s][1][None, :]
                )
            )

    mod_rows = jnp.stack(
        [jnp.stack([jnp.concatenate(mod_grads[t][s]) for s in range(L)]) for t in range(2)]
    )
    mod_rows = mod_rows.reshape(2, L, B, S, mod_width).transpose(3, 2, 0, 1, 4)
    qv_bias_sum = jnp.zeros((2, 2 * D), F32)
    for part, column in ((0, 0), (1, 2 * own_width)):
        sums = jnp.stack(
            [
                sum(
                    jnp.sum(
                        qkv_grads[s][t][:, column : column + own_width].astype(F32), axis=0
                    )
                    for s in range(L)
                )
                for t in range(2)
            ]
        )
        qv_bias_sum = lax.dynamic_update_slice_in_dim(
            qv_bias_sum, sums, part * D + first_feature, 1
        )
    up_bias_rows = lax.dynamic_update_slice_in_dim(
        jnp.zeros((2, B, S, hidden_columns), F32),
        up_bias_sum.reshape(2, B, 1, hidden_columns),
        seq_index,
        2,
    )
    bias_rows = jnp.concatenate(
        [
            qv_bias_sum.reshape(2, B, S, -1),
            jnp.stack(out_bias_sum).reshape(2, B, S, -1),
            up_bias_rows,
            jnp.stack(down_bias_sum).reshape(2, B, S, -1),
        ],
        axis=3,
    ).transpose(2, 1, 0, 3)
    packed = jnp.concatenate(
        [mod_rows.reshape(S, B, -1), bias_rows.reshape(S, B, -1)], axis=2
    )
    packed = jnp.sum(swap(packed, "seq"), axis=0)
    packed = swap(packed, "batch")
    mod_mine = (
        packed[:, : 2 * L * mod_width]
        .reshape(B, 2, L, mod_width)
        .transpose(1, 0, 2, 3)
        .reshape(2, B * L, mod_width)
        .astype(BF16)
    )
    bias_mine = jnp.sum(packed[:, 2 * L * mod_width :], axis=0).reshape(2, -1)
    qv_bias_grad, out_bias_grad, up_bias_grad, down_bias_grad = jnp.split(
        bias_mine, bias_ends[:3], axis=1
    )
    mod_weight_grad = jnp.einsum(
        "sd,tsf->tdf", smooth_all, mod_mine, preferred_element_type=F32
    )
    mod_bias_grad = jnp.sum(mod_mine.astype(F32), axis=1)
    smooth_part = jnp.einsum("tsf,tdf->sd", mod_mine, mod_weight, preferred_element_type=F32)
    smooth_grad = jnp.sum(swap(smooth_part.reshape(B, L, D), "batch"), axis=0)
    smooth_grad = smooth_grad + flip(smooth_grad, 1)
    smooth_grad = smooth_grad + flip(smooth_grad, 2)
    cond_grad = jax.vjp(jax.nn.silu, conditioning.astype(F32))[1](smooth_grad)[0]
    return (
        jnp.stack(results[0]),
        jnp.stack(results[1]),
        jnp.stack(input_grads[0]),
        jnp.stack(input_grads[1]),
        cond_grad,
        mod_weight_grad,
        mod_bias_grad,
        qkv_weight_grad,
        qv_bias_grad,
        out_weight_grad,
        out_bias_grad,
        up_weight_grad,
        up_bias_grad,
        down_weight_grad,
        down_bias_grad,
    )


def choose_layer(mesh):
    if mesh.shape["seq"] == 4 and HEADS % 8 == 0:
        return swift_layer
    return general_layer


def solution(mesh):
    layer = choose_layer(mesh)
    return jax.shard_map(
        layer,
        mesh=mesh,
        in_specs=(
            P("batch", "seq", None),
            P("batch", "seq", None),
            P("batch", None),
            P("batch", None),
            P(None, None, ("batch", "seq")),
            P(None, ("batch", "seq")),
            P(None, None, ("batch", "seq")),
            P(None, ("batch", "seq")),
            P(None, None, ("batch", "seq")),
            P(None, ("batch", "seq")),
            P(None, None, ("batch", "seq")),
            P(None, ("batch", "seq")),
            P(None, None, ("batch", "seq")),
            P(None, ("batch", "seq")),
            P("batch", "seq", None),
            P("batch", "seq", None),
        ),
        out_specs=(
            P("batch", "seq", None),
            P("batch", "seq", None),
            P("batch", "seq", None),
            P("batch", "seq", None),
            P("batch", None),
            P(None, None, ("batch", "seq")),
            P(None, ("batch", "seq")),
            P(None, None, ("batch", "seq")),
            P(None, ("batch", "seq")),
            P(None, None, ("batch", "seq")),
            P(None, ("batch", "seq")),
            P(None, None, ("batch", "seq")),
            P(None, ("batch", "seq")),
            P(None, None, ("batch", "seq")),
            P(None, ("batch", "seq")),
        ),
        check_vma=False,
    )
```

```python
import functools
import math

import jax
import jax.numpy as jnp
import numpy as np
from jax import lax
from jax.experimental import pallas as pl
from jax.experimental.pallas import tpu as pltpu
from jax.sharding import PartitionSpec as P

HEADS = 24


NORM_EPSILON = 1e-06
FLOOR_SCORE = -10000.0


def modulate(tokens, shift_vec, scale_vec):
    row_mean = jnp.mean(tokens, axis=-1, keepdims=True)
    centered = tokens - row_mean
    row_var = jnp.mean(centered * centered, axis=-1, keepdims=True)
    return (
        centered * lax.rsqrt(row_var + NORM_EPSILON) * (1.0 + scale_vec[:, None, :])
        + shift_vec[:, None, :]
    )


def gelu_tanh(values):
    return jax.nn.gelu(values, approximate=True)


def unmix_columns(values, seq_devices, batch_devices):
    array_shape = values.shape
    piece_width = array_shape[-1] // (seq_devices * batch_devices)
    grid_view = values.reshape(array_shape[:-1] + (seq_devices, batch_devices, piece_width))
    return jnp.swapaxes(grid_view, -3, -2).reshape(array_shape)


def remix_columns(values, seq_devices, batch_devices):
    array_shape = values.shape
    piece_width = array_shape[-1] // (seq_devices * batch_devices)
    grid_view = values.reshape(array_shape[:-1] + (batch_devices, seq_devices, piece_width))
    return jnp.swapaxes(grid_view, -3, -2).reshape(array_shape)


def fetch_columns(
    up_weight,
    down_weight,
    mod_weight,
    qkv_weight,
    out_weight,
    up_bias,
    mod_bias,
    qv_bias,
    out_bias,
    down_bias,
):
    return (
        lax.all_gather(up_weight, "batch", axis=2, tiled=True),
        lax.all_gather(down_weight, "batch", axis=2, tiled=True),
        lax.all_gather(mod_weight, "batch", axis=2, tiled=True),
        lax.all_gather(qkv_weight, "batch", axis=2, tiled=True),
        lax.all_gather(out_weight, "batch", axis=2, tiled=True),
        lax.all_gather(up_bias, "batch", axis=1, tiled=True),
        lax.all_gather(mod_bias, "batch", axis=1, tiled=True),
        lax.all_gather(qv_bias, "batch", axis=1, tiled=True),
        lax.all_gather(out_bias, "batch", axis=1, tiled=True),
        lax.all_gather(down_bias, "batch", axis=1, tiled=True),
    )


def fetch_modulation(mod_part, mod_bias_part):
    return (
        lax.all_gather(mod_part, "seq", axis=2, tiled=True),
        lax.all_gather(mod_bias_part, "seq", axis=1, tiled=True),
    )


def gather_rows(first, second):
    return (
        lax.all_gather(first, "seq", axis=1, tiled=True),
        lax.all_gather(second, "seq", axis=1, tiled=True),
    )


def sum_rows(first, second, seq_devices):
    local_seqs, first_rows, width = first.shape
    first_local = first_rows // seq_devices
    second_local = second.shape[1] // seq_devices
    joined = jnp.concatenate(
        [
            first.reshape(local_seqs, seq_devices, first_local, width),
            second.reshape(local_seqs, seq_devices, second_local, width),
        ],
        axis=2,
    )
    joined = joined.reshape(local_seqs, seq_devices * (first_local + second_local), width)
    total = lax.psum_scatter(joined, "seq", scatter_dimension=1, tiled=True)
    return (total[:, :first_local], total[:, first_local:])


def to_rows(first, second):
    return (
        lax.all_to_all(first, "seq", split_axis=1, concat_axis=2, tiled=True),
        lax.all_to_all(second, "seq", split_axis=1, concat_axis=2, tiled=True),
    )


def to_columns(first, second):
    return (
        lax.all_to_all(first, "seq", split_axis=2, concat_axis=1, tiled=True),
        lax.all_to_all(second, "seq", split_axis=2, concat_axis=1, tiled=True),
    )


def own_block(values, seq_index, seq_devices):
    width = values.shape[1] // seq_devices
    return lax.dynamic_slice_in_dim(values, seq_index * width, width, 1)


def general_layer(
    image_tokens,
    text_tokens,
    conditioning,
    key_mask,
    mod_weight,
    mod_bias,
    qkv_weight,
    qv_bias,
    out_weight,
    out_bias,
    up_weight,
    up_bias,
    down_weight,
    down_bias,
    image_cotangent,
    text_cotangent,
):
    seq_devices = lax.axis_size("seq")
    batch_devices = lax.axis_size("batch")
    seq_index = lax.axis_index("seq")
    local_seqs, image_count, model_width = image_tokens.shape
    text_count = text_tokens.shape[1]
    block_rows = image_count + text_count
    key_count = block_rows * seq_devices
    head_size = model_width // HEADS
    factor = 1.0 / math.sqrt(head_size)
    inputs = (image_tokens.astype(jnp.float32), text_tokens.astype(jnp.float32))
    cotangents = (image_cotangent.astype(jnp.float32), text_cotangent.astype(jnp.float32))
    row_spans = ((0, image_count), (image_count, block_rows))
    image_keys = key_mask[:, : image_count * seq_devices].reshape(
        local_seqs, seq_devices, image_count
    )
    text_keys = key_mask[:, image_count * seq_devices :].reshape(
        local_seqs, seq_devices, text_count
    )
    key_live = (
        jnp.concatenate([image_keys, text_keys], axis=2).reshape(local_seqs, key_count) > 0
    )[:, None, None, :]
    cond_float = conditioning.astype(jnp.float32)
    smooth = jax.nn.silu(cond_float).astype(jnp.bfloat16)
    fetched = fetch_columns(
        up_weight,
        down_weight,
        mod_weight,
        qkv_weight,
        out_weight,
        up_bias,
        mod_bias,
        qv_bias,
        out_bias,
        down_bias,
    )
    (
        up_part,
        down_part,
        mod_part,
        qkv_part,
        out_part,
        up_bias_part,
        mod_bias_part,
        qv_part,
        out_bias_part,
        down_bias_part,
    ) = fetched
    mod_full, mod_bias_full = fetch_modulation(mod_part, mod_bias_part)
    mixed_mod = (
        jnp.einsum("sd,tdf->tsf", smooth, mod_full, preferred_element_type=jnp.float32)
        + mod_bias_full.astype(jnp.float32)[:, None, :]
    )
    modulation = unmix_columns(mixed_mod, seq_devices, batch_devices).reshape(
        2, local_seqs, 6, model_width
    )
    first_norms = []
    for modality in range(2):
        pieces = modulation[modality]
        first_norms.append(
            modulate(inputs[modality], pieces[:, 0], pieces[:, 1]).astype(jnp.bfloat16)
        )
    norm_image_all, norm_text_all, qv_seq, out_bias_seq, down_bias_seq = (
        lax.all_gather(first_norms[0], "seq", axis=1, tiled=True),
        lax.all_gather(first_norms[1], "seq", axis=1, tiled=True),
        lax.all_gather(qv_part, "seq", axis=1, tiled=True),
        lax.all_gather(out_bias_part, "seq", axis=1, tiled=True),
        lax.all_gather(down_bias_part, "seq", axis=1, tiled=True),
    )
    first_all = (norm_image_all, norm_text_all)
    qv_full = unmix_columns(qv_seq, seq_devices, batch_devices).astype(jnp.float32)
    out_bias_full = unmix_columns(out_bias_seq, seq_devices, batch_devices).astype(jnp.float32)
    down_bias_full = unmix_columns(down_bias_seq, seq_devices, batch_devices).astype(jnp.float32)
    qkv_cols = [
        jnp.einsum(
            "srd,df->srf",
            first_all[modality],
            qkv_part[modality],
            preferred_element_type=jnp.float32,
        )
        for modality in range(2)
    ]
    qkv_rows = to_rows(qkv_cols[0], qkv_cols[1])
    queries, keyvals = ([], [])
    for modality in range(2):
        projected = unmix_columns(qkv_rows[modality], seq_devices, batch_devices)
        qv_vector = qv_full[modality]
        queries.append(
            (projected[..., :model_width] + qv_vector[:model_width]).astype(jnp.bfloat16)
        )
        value_shift = jnp.concatenate(
            [jnp.zeros((model_width,), jnp.float32), qv_vector[model_width:]]
        )
        keyvals.append((projected[..., model_width:] + value_shift).astype(jnp.bfloat16))
    joined_query = jnp.concatenate(queries, axis=1)
    joined_keyval = jnp.concatenate(keyvals, axis=1)
    all_keyval = lax.all_gather(joined_keyval, "seq", axis=1, tiled=True)
    query_heads = joined_query.reshape(local_seqs, block_rows, HEADS, head_size)
    key_heads = all_keyval[..., :model_width].reshape(local_seqs, key_count, HEADS, head_size)
    value_heads = all_keyval[..., model_width:].reshape(local_seqs, key_count, HEADS, head_size)
    scores = (
        jnp.einsum("sqhe,skhe->shqk", query_heads, key_heads, preferred_element_type=jnp.float32)
        * factor
    )
    row_max = jnp.max(jnp.where(key_live, scores, FLOOR_SCORE), axis=-1, keepdims=True)
    exp_terms = jnp.exp(jnp.where(key_live, scores - row_max, FLOOR_SCORE))
    denominator = jnp.maximum(jnp.sum(exp_terms, axis=-1, keepdims=True), 1.0)
    prob_low = (exp_terms / denominator).astype(jnp.bfloat16)
    logsum = row_max + jnp.log(denominator)
    attended = jnp.einsum(
        "shqk,skhe->sqhe", prob_low, value_heads, preferred_element_type=jnp.float32
    )
    attended = attended.reshape(local_seqs, block_rows, model_width).astype(jnp.bfloat16)
    attended_all = gather_rows(attended[:, :image_count], attended[:, image_count:])
    out_cols = [
        jnp.einsum(
            "srd,df->srf",
            attended_all[modality],
            out_part[modality],
            preferred_element_type=jnp.float32,
        )
        for modality in range(2)
    ]
    out_rows = to_rows(out_cols[0], out_cols[1])
    projections, middles, second_norms = ([], [], [])
    for modality in range(2):
        pieces = modulation[modality]
        projection = (
            unmix_columns(out_rows[modality], seq_devices, batch_devices) + out_bias_full[modality]
        )
        middle = inputs[modality] + pieces[:, 2][:, None, :] * projection
        second_norms.append(modulate(middle, pieces[:, 3], pieces[:, 4]).astype(jnp.bfloat16))
        projections.append(projection)
        middles.append(middle)
    group_rows = gather_rows(second_norms[0], second_norms[1])
    hidden_pre, hidden_act, partials = ([], [], [])
    for modality in range(2):
        pre_values = jnp.einsum(
            "srd,df->srf",
            group_rows[modality],
            up_part[modality],
            preferred_element_type=jnp.float32,
        ) + up_bias_part[modality].astype(jnp.float32)
        act_values = gelu_tanh(pre_values).astype(jnp.bfloat16)
        partials.append(
            jnp.einsum(
                "srf,df->srd", act_values, down_part[modality], preferred_element_type=jnp.float32
            )
        )
        hidden_pre.append(pre_values)
        hidden_act.append(act_values)
    mlp_rows = sum_rows(partials[0], partials[1], seq_devices)
    mlp_outs, results = ([], [])
    for modality in range(2):
        pieces = modulation[modality]
        mlp_value = mlp_rows[modality] + down_bias_full[modality]
        results.append(
            (middles[modality] + pieces[:, 5][:, None, :] * mlp_value).astype(jnp.bfloat16)
        )
        mlp_outs.append(mlp_value)
    fetched_back = fetch_columns(
        up_weight,
        down_weight,
        mod_weight,
        qkv_weight,
        out_weight,
        up_bias,
        mod_bias,
        qv_bias,
        out_bias,
        down_bias,
    )
    up_back, down_back, mod_back, qkv_back, out_back = (
        fetched_back[0],
        fetched_back[1],
        fetched_back[2],
        fetched_back[3],
        fetched_back[4],
    )
    mod_bias_back = fetched_back[6]
    mlp_grads, gate_twos, down_bias_grads = ([], [], [])
    for modality in range(2):
        pieces = modulation[modality]
        mlp_grad = (pieces[:, 5][:, None, :] * cotangents[modality]).astype(jnp.bfloat16)
        gate_twos.append(jnp.sum(cotangents[modality] * mlp_outs[modality], axis=1))
        down_bias_grads.append(jnp.sum(mlp_grad.astype(jnp.float32), axis=(0, 1)))
        mlp_grads.append(mlp_grad)
    group_grads = gather_rows(mlp_grads[0], mlp_grads[1])
    down_grads, up_grads, up_bias_grads, norm_partials = ([], [], [], [])
    for modality in range(2):
        down_grads.append(
            jnp.einsum(
                "srd,srf->df",
                group_grads[modality],
                hidden_act[modality],
                preferred_element_type=jnp.float32,
            )
        )
        act_grad = jnp.einsum(
            "srd,df->srf",
            group_grads[modality],
            down_back[modality],
            preferred_element_type=jnp.float32,
        )
        pullback = jax.vjp(gelu_tanh, hidden_pre[modality])[1]
        pre_grad = pullback(act_grad)[0].astype(jnp.bfloat16)
        up_grads.append(
            jnp.einsum(
                "srd,srf->df", group_rows[modality], pre_grad, preferred_element_type=jnp.float32
            )
        )
        up_bias_grads.append(jnp.sum(pre_grad.astype(jnp.float32), axis=(0, 1)))
        norm_partials.append(
            jnp.einsum(
                "srf,df->srd", pre_grad, up_back[modality], preferred_element_type=jnp.float32
            )
        )
    norm_grads = sum_rows(norm_partials[0], norm_partials[1], seq_devices)
    middle_grads, shift_twos, scale_twos, gate_ones, out_bias_grads, proj_grads = (
        [],
        [],
        [],
        [],
        [],
        [],
    )
    for modality in range(2):
        pieces = modulation[modality]
        pullback = jax.vjp(modulate, middles[modality], pieces[:, 3], pieces[:, 4])[1]
        middle_part, shift_two, scale_two = pullback(norm_grads[modality])
        middle_grad = cotangents[modality] + middle_part
        proj_grad = (pieces[:, 2][:, None, :] * middle_grad).astype(jnp.bfloat16)
        gate_ones.append(jnp.sum(middle_grad * projections[modality], axis=1))
        out_bias_grads.append(jnp.sum(proj_grad.astype(jnp.float32), axis=(0, 1)))
        proj_grads.append(remix_columns(proj_grad, seq_devices, batch_devices))
        middle_grads.append(middle_grad)
        shift_twos.append(shift_two)
        scale_twos.append(scale_two)
    proj_cols = to_columns(proj_grads[0], proj_grads[1])
    out_grads, attended_partials = ([], [])
    for modality in range(2):
        out_grads.append(
            jnp.einsum(
                "srd,srf->df",
                attended_all[modality],
                proj_cols[modality],
                preferred_element_type=jnp.float32,
            )
        )
        attended_partials.append(
            jnp.einsum(
                "srf,df->srd",
                proj_cols[modality],
                out_back[modality],
                preferred_element_type=jnp.float32,
            )
        )
    attended_sums = sum_rows(attended_partials[0], attended_partials[1], seq_devices)
    attended_grad = jnp.concatenate([attended_sums[0], attended_sums[1]], axis=1).astype(
        jnp.bfloat16
    )
    grad_heads = attended_grad.reshape(local_seqs, block_rows, HEADS, head_size)
    scores_again = (
        jnp.einsum("sqhe,skhe->shqk", query_heads, key_heads, preferred_element_type=jnp.float32)
        * factor
    )
    probs_again = jnp.exp(jnp.where(key_live, scores_again - logsum, FLOOR_SCORE))
    probs_again_low = probs_again.astype(jnp.bfloat16)
    prob_grad = jnp.einsum(
        "sqhe,skhe->shqk", grad_heads, value_heads, preferred_element_type=jnp.float32
    )
    inner_sum = jnp.sum(probs_again * prob_grad, axis=-1, keepdims=True)
    score_grad = (probs_again * (prob_grad - inner_sum)).astype(jnp.bfloat16)
    query_grad = (
        jnp.einsum("shqk,skhe->sqhe", score_grad, key_heads, preferred_element_type=jnp.float32)
        * factor
    )
    query_grad = query_grad.reshape(local_seqs, block_rows, model_width).astype(jnp.bfloat16)
    key_grad = (
        jnp.einsum("shqk,sqhe->skhe", score_grad, query_heads, preferred_element_type=jnp.float32)
        * factor
    )
    value_grad = jnp.einsum(
        "shqk,sqhe->skhe", probs_again_low, grad_heads, preferred_element_type=jnp.float32
    )
    key_rows, value_rows = (
        lax.psum_scatter(
            key_grad.reshape(local_seqs, key_count, model_width),
            "seq",
            scatter_dimension=1,
            tiled=True,
        ),
        lax.psum_scatter(
            value_grad.reshape(local_seqs, key_count, model_width),
            "seq",
            scatter_dimension=1,
            tiled=True,
        ),
    )
    key_rows = key_rows.astype(jnp.bfloat16)
    value_rows = value_rows.astype(jnp.bfloat16)
    qv_bias_grads, joined_grads = ([], [])
    for modality in range(2):
        row_start, row_stop = row_spans[modality]
        query_part = query_grad[:, row_start:row_stop]
        value_part = value_rows[:, row_start:row_stop]
        joined_grad = jnp.concatenate(
            [query_part, key_rows[:, row_start:row_stop], value_part], axis=-1
        )
        qv_bias_grads.append(
            jnp.concatenate(
                [
                    jnp.sum(query_part.astype(jnp.float32), axis=(0, 1)),
                    jnp.sum(value_part.astype(jnp.float32), axis=(0, 1)),
                ]
            )
        )
        joined_grads.append(remix_columns(joined_grad, seq_devices, batch_devices))
    qkv_grad_cols = to_columns(joined_grads[0], joined_grads[1])
    qkv_grads, first_partials = ([], [])
    for modality in range(2):
        qkv_grads.append(
            jnp.einsum(
                "srd,srf->df",
                first_all[modality],
                qkv_grad_cols[modality],
                preferred_element_type=jnp.float32,
            )
        )
        first_partials.append(
            jnp.einsum(
                "srf,df->srd",
                qkv_grad_cols[modality],
                qkv_back[modality],
                preferred_element_type=jnp.float32,
            )
        )
    first_grads = sum_rows(first_partials[0], first_partials[1], seq_devices)
    input_grads, mod_partials = ([], [])
    for modality in range(2):
        pieces = modulation[modality]
        pullback = jax.vjp(modulate, inputs[modality], pieces[:, 0], pieces[:, 1])[1]
        input_part, shift_one, scale_one = pullback(first_grads[modality])
        input_grads.append(middle_grads[modality] + input_part)
        stacked = jnp.stack(
            [
                shift_one,
                scale_one,
                gate_ones[modality],
                shift_twos[modality],
                scale_twos[modality],
                gate_twos[modality],
            ],
            axis=1,
        )
        mod_partials.append(stacked.reshape(local_seqs, 6 * model_width))
    qv_mixed = remix_columns(jnp.stack(qv_bias_grads), seq_devices, batch_devices)
    out_bias_mixed = remix_columns(jnp.stack(out_bias_grads), seq_devices, batch_devices)
    down_bias_mixed = remix_columns(jnp.stack(down_bias_grads), seq_devices, batch_devices)
    mod_sum, qv_summed, out_bias_summed, down_bias_summed = lax.psum(
        (jnp.stack(mod_partials), qv_mixed, out_bias_mixed, down_bias_mixed), "seq"
    )
    mod_low = mod_sum.astype(jnp.bfloat16)
    mod_mixed = remix_columns(mod_low, seq_devices, batch_devices)
    columns = mod_part.shape[2]
    own_columns = lax.dynamic_slice_in_dim(mod_mixed, seq_index * columns, columns, 2)
    mod_grad = jnp.einsum("sd,tsf->tdf", smooth, own_columns, preferred_element_type=jnp.float32)
    mod_bias_grad = jnp.sum(own_columns.astype(jnp.float32), axis=1)
    mod_again = fetch_modulation(mod_back, mod_bias_back)[0]
    smooth_grad = jnp.einsum(
        "tsf,tdf->sd", mod_mixed, mod_again, preferred_element_type=jnp.float32
    )
    cond_pullback = jax.vjp(jax.nn.silu, cond_float)[1]
    cond_grad = cond_pullback(smooth_grad)[0]
    qv_own = own_block(qv_summed, seq_index, seq_devices)
    out_bias_own = own_block(out_bias_summed, seq_index, seq_devices)
    down_bias_own = own_block(down_bias_summed, seq_index, seq_devices)
    column_grads = (
        lax.psum_scatter(jnp.stack(up_grads), "batch", scatter_dimension=2, tiled=True),
        lax.psum_scatter(jnp.stack(down_grads), "batch", scatter_dimension=2, tiled=True),
        lax.psum_scatter(mod_grad, "batch", scatter_dimension=2, tiled=True),
        lax.psum_scatter(jnp.stack(qkv_grads), "batch", scatter_dimension=2, tiled=True),
        lax.psum_scatter(jnp.stack(out_grads), "batch", scatter_dimension=2, tiled=True),
        lax.psum_scatter(jnp.stack(up_bias_grads), "batch", scatter_dimension=1, tiled=True),
        lax.psum_scatter(mod_bias_grad, "batch", scatter_dimension=1, tiled=True),
        lax.psum_scatter(qv_own, "batch", scatter_dimension=1, tiled=True),
        lax.psum_scatter(out_bias_own, "batch", scatter_dimension=1, tiled=True),
        lax.psum_scatter(down_bias_own, "batch", scatter_dimension=1, tiled=True),
    )
    return (
        results[0],
        results[1],
        input_grads[0],
        input_grads[1],
        cond_grad,
        column_grads[2],
        column_grads[6],
        column_grads[3],
        column_grads[7],
        column_grads[4],
        column_grads[8],
        column_grads[0],
        column_grads[5],
        column_grads[1],
        column_grads[9],
    )


LOG2E = 1.4426950408889634
DEAD = -1e30
BF16 = jnp.bfloat16
F32 = jnp.float32


def dot_nt(a, b):
    return lax.dot_general(a, b, (((1,), (1,)), ((), ())), preferred_element_type=F32)


def dot_nn(a, b):
    return lax.dot_general(a, b, (((1,), (0,)), ((), ())), preferred_element_type=F32)


def dot_tn(a, b):
    return lax.dot_general(a, b, (((0,), (0,)), ((), ())), preferred_element_type=F32)


def attention_kernel(
    query_rows, scale, head, bias_ref, floor_ref, qi, qt, ki, kt, vi, vt, oi, ot, keys, values
):
    image_rows = qi.shape[0]
    keys[:image_rows] = ki[...]
    keys[image_rows:] = kt[...]
    values[:image_rows] = vi[...]
    values[image_rows:] = vt[...]
    bias = bias_ref[...]
    floor = floor_ref[0, 0]
    spans = [(qi, oi, start, query_rows) for start in range(0, image_rows, query_rows)]
    spans.append((qt, ot, 0, qt.shape[0]))
    for source, target, start, size in spans:
        sides = []
        for side in range(2):
            lanes = slice(side * head, (side + 1) * head)
            scores = dot_nt(source[start : start + size, lanes], keys[:, lanes]) * scale + bias
            row_max = jnp.maximum(jnp.max(scores, axis=1, keepdims=True), floor)
            exps = jnp.exp2(scores - row_max)
            total = jnp.maximum(jnp.sum(exps, axis=1, keepdims=True), 1.0)
            probs = (exps * (1.0 / total)).astype(BF16)
            sides.append(dot_nn(probs, values[:, lanes]))
        target[start : start + size, :] = jnp.concatenate(sides, axis=1).astype(BF16)


def pair_block(rows, lanes, pairs, part):
    return pl.BlockSpec((rows, lanes), lambda pair: (0, part * pairs + pair))


def attention(qkv_image, qkv_text, key_bias, floor, head):
    image_rows, width = qkv_image.shape
    text_rows = qkv_text.shape[0]
    rows = image_rows + text_rows
    lanes = 2 * head
    pairs = width // (3 * lanes)
    columns = [
        pair_block(count, lanes, pairs, part)
        for part in range(3)
        for count in (image_rows, text_rows)
    ]
    return pl.pallas_call(
        functools.partial(attention_kernel, 256, LOG2E / math.sqrt(head), head),
        grid=(pairs,),
        in_specs=[
            pl.BlockSpec((1, rows), lambda pair: (0, 0)),
            pl.BlockSpec(memory_space=pltpu.SMEM),
            *columns,
        ],
        out_specs=[columns[0], columns[1]],
        out_shape=[
            jax.ShapeDtypeStruct((image_rows, width // 3), BF16),
            jax.ShapeDtypeStruct((text_rows, width // 3), BF16),
        ],
        scratch_shapes=[pltpu.VMEM((rows, lanes), BF16), pltpu.VMEM((rows, lanes), BF16)],
        compiler_params=pltpu.CompilerParams(vmem_limit_bytes=48 << 20),
        cost_estimate=pl.CostEstimate(
            flops=16 * rows * rows * width // 3,
            bytes_accessed=8 * rows * width // 3,
            transcendentals=rows * rows * width // (3 * head),
        ),
        name="attention",
    )(key_bias[None, :], floor, qkv_image, qkv_text, qkv_image, qkv_text, qkv_image, qkv_text)


def attention_back_kernel(
    query_rows, scale, factor, head, pairs,
    bias_ref, floor_ref, qi, qt, ki, kt, vi, vt, gi, gt, oi, ot, keys, values, key_sum, value_sum,
):
    pair = pl.program_id(0)
    image_rows = qi.shape[0]
    width = 2 * head
    keys[:image_rows] = ki[...]
    keys[image_rows:] = kt[...]
    values[:image_rows] = vi[...]
    values[image_rows:] = vt[...]
    key_sum[...] = jnp.zeros_like(key_sum)
    value_sum[...] = jnp.zeros_like(value_sum)
    bias = bias_ref[...]
    floor = floor_ref[0, 0]
    spans = [(qi, gi, oi, start, query_rows) for start in range(0, image_rows, query_rows)]
    spans.append((qt, gt, ot, 0, qt.shape[0]))
    query_lanes = pl.ds(pl.multiple_of(pair * width, width), width)
    key_lanes = pl.ds(pl.multiple_of((pairs + pair) * width, width), width)
    value_lanes = pl.ds(pl.multiple_of((2 * pairs + pair) * width, width), width)
    for source, grads, target, start, size in spans:
        wide_bias = jnp.concatenate([bias] * -(-size // 128), axis=1)[:, :size]
        dq, dk, dv = ([], [], [])
        for side in range(2):
            lanes = slice(side * head, (side + 1) * head)
            query = source[start : start + size, lanes]
            grad = grads[start : start + size, lanes]
            scores = dot_nt(keys[:, lanes], query) * scale + wide_bias
            top = jnp.maximum(jnp.max(scores, axis=0, keepdims=True), floor)
            exps = jnp.exp2(scores - top)
            total = jnp.maximum(jnp.sum(exps, axis=0, keepdims=True), 1.0)
            probs = exps * (1.0 / total)
            prob_grad = dot_nt(values[:, lanes], grad)
            weighted = probs * prob_grad
            inner = jnp.sum(weighted, axis=0, keepdims=True)
            score_grad = (weighted - probs * inner).astype(BF16)
            dv.append(dot_nn(probs.astype(BF16), grad))
            dk.append(dot_nn(score_grad, query))
            dq.append(dot_tn(score_grad, keys[:, lanes]))
        key_sum[...] += jnp.concatenate(dk, axis=1)
        value_sum[...] += jnp.concatenate(dv, axis=1)
        target[start : start + size, query_lanes] = (
            jnp.concatenate(dq, axis=1) * factor
        ).astype(BF16)
    oi[:, key_lanes] = (key_sum[:image_rows] * factor).astype(BF16)
    ot[:, key_lanes] = (key_sum[image_rows:] * factor).astype(BF16)
    oi[:, value_lanes] = value_sum[:image_rows].astype(BF16)
    ot[:, value_lanes] = value_sum[image_rows:].astype(BF16)


def attention_back(qkv_image, qkv_text, grad_image, grad_text, key_bias, floor, head):
    image_rows, width = qkv_image.shape
    text_rows = qkv_text.shape[0]
    rows = image_rows + text_rows
    lanes = 2 * head
    pairs = width // (3 * lanes)
    columns = [
        pair_block(count, lanes, pairs, part)
        for part in range(3)
        for count in (image_rows, text_rows)
    ]
    return pl.pallas_call(
        functools.partial(
            attention_back_kernel, 256, LOG2E / math.sqrt(head), 1.0 / math.sqrt(head), head, pairs
        ),
        grid=(pairs,),
        in_specs=[
            pl.BlockSpec((rows, 128), lambda pair: (0, 0)),
            pl.BlockSpec(memory_space=pltpu.SMEM),
            *columns,
            columns[0],
            columns[1],
        ],
        out_specs=[
            pl.BlockSpec((image_rows, width), lambda pair: (0, 0)),
            pl.BlockSpec((text_rows, width), lambda pair: (0, 0)),
        ],
        out_shape=[
            jax.ShapeDtypeStruct((image_rows, width), BF16),
            jax.ShapeDtypeStruct((text_rows, width), BF16),
        ],
        scratch_shapes=[
            pltpu.VMEM((rows, lanes), BF16),
            pltpu.VMEM((rows, lanes), BF16),
            pltpu.VMEM((rows, lanes), F32),
            pltpu.VMEM((rows, lanes), F32),
        ],
        compiler_params=pltpu.CompilerParams(vmem_limit_bytes=48 << 20),
        cost_estimate=pl.CostEstimate(
            flops=40 * rows * rows * width // 3,
            bytes_accessed=16 * rows * width // 3,
            transcendentals=rows * rows * width // (3 * head),
        ),
        name="attention_back",
    )(
        jnp.broadcast_to(key_bias[:, None], (rows, 128)),
        floor,
        qkv_image, qkv_text, qkv_image, qkv_text, qkv_image, qkv_text,
        grad_image, grad_text,
    )


def flip(values, bit):
    return lax.ppermute(values, "seq", [(i, i ^ bit) for i in range(4)])


def gather_blocks(own):
    half = own.shape[-1] // 2
    near_x = flip(own, 1)
    near_y = flip(own, 2)
    far_a = flip(near_x[..., :half], 2)
    far_b = flip(near_y[..., half:], 1)
    return (own, near_x, near_y, jnp.concatenate([far_a, far_b], axis=-1))


def add_low(a, b):
    return (a.astype(F32) + b.astype(F32)).astype(BF16)


def scatter_blocks(blocks):
    own, near_x, near_y, far = blocks
    half = own.shape[-1] // 2
    for_y = flip(far[..., :half], 1)
    for_x = flip(far[..., half:], 2)
    from_x = flip(
        jnp.concatenate([near_x[..., :half], add_low(near_x[..., half:], for_x)], axis=-1), 1
    )
    from_y = flip(
        jnp.concatenate([add_low(near_y[..., :half], for_y), near_y[..., half:]], axis=-1), 2
    )
    return own.astype(F32) + from_x.astype(F32) + from_y.astype(F32)


def join_rows(blocks, image_count):
    return (
        jnp.concatenate([block[:image_count] for block in blocks], axis=0),
        jnp.concatenate([block[image_count:] for block in blocks], axis=0),
    )


def split_rows(image, text, image_count, text_count):
    return [
        jnp.concatenate(
            [
                image[r * image_count : (r + 1) * image_count],
                text[r * text_count : (r + 1) * text_count],
            ],
            axis=0,
        )
        for r in range(4)
    ]


def match_units(batch_devices, seq_devices, per_device, group_units):
    devices = batch_devices * seq_devices
    total = devices * per_device
    part_units = total // 3
    sources, targets = ([], [])
    for seq_at in range(seq_devices):
        listed = [
            part * part_units + seq_at * group_units + k
            for part in range(3)
            for k in range(group_units)
        ]
        for place, unit in enumerate(listed):
            sources.append((unit // per_device, unit % per_device))
            targets.append(
                ((place // per_device) * seq_devices + seq_at, place % per_device)
            )
    edges = list(zip(sources, targets))
    rounds = []
    left = list(range(total))
    for _ in range(per_device):
        by_source = {}
        for e in left:
            by_source.setdefault(edges[e][0][0], []).append(e)
        taken = {}

        def place_edge(device, seen):
            for e in by_source[device]:
                target = edges[e][1][0]
                if target in seen:
                    continue
                seen.add(target)
                if target not in taken or place_edge(edges[taken[target]][0][0], seen):
                    taken[target] = e
                    return True
            return False

        for device in range(devices):
            place_edge(device, set())
        chosen = sorted(taken.values())
        rounds.append(chosen)
        left = [e for e in left if e not in chosen]
    send = np.zeros((per_device, devices), np.int32)
    land = np.zeros((per_device, devices), np.int32)
    perms = []
    for k, chosen in enumerate(rounds):
        pairs = []
        for e in chosen:
            (source, source_slot), (target, target_slot) = edges[e]
            pairs.append((source, target))
            send[k, source] = source_slot
            land[k, target] = target_slot
        perms.append(sorted(pairs))
    return perms, send, land


def move_units(units, perms, take, put, place):
    arrived = jnp.zeros_like(units)
    for k, pairs in enumerate(perms):
        slot = jnp.asarray(take[k])[place]
        moved = lax.ppermute(
            lax.dynamic_index_in_dim(units, slot, 0, keepdims=True), ("batch", "seq"), pairs
        )
        arrived = lax.dynamic_update_slice_in_dim(arrived, moved, jnp.asarray(put[k])[place], 0)
    return arrived


def gather_batch(values):
    return lax.all_gather(values, "batch", axis=0)


def scatter_batch(values):
    return lax.psum_scatter(values, "batch", scatter_dimension=0)


def swap(values, axis):
    return lax.all_to_all(values, axis, 0, 0, tiled=True)


def norm_stats(values):
    mean = jnp.mean(values, axis=-1, keepdims=True)
    centered = values - mean
    variance = jnp.mean(centered * centered, axis=-1, keepdims=True)
    return mean, lax.rsqrt(variance + NORM_EPSILON)


def norm_back(norm, inverse, grad, scale):
    scaled = grad * (1.0 + scale)
    return inverse * (
        scaled
        - jnp.mean(scaled, axis=-1, keepdims=True)
        - norm * jnp.mean(scaled * norm, axis=-1, keepdims=True)
    )


def swift_layer(
    image_tokens,
    text_tokens,
    conditioning,
    key_mask,
    mod_weight,
    mod_bias,
    qkv_weight,
    qv_bias,
    out_weight,
    out_bias,
    up_weight,
    up_bias,
    down_weight,
    down_bias,
    image_cotangent,
    text_cotangent,
):
    S = lax.axis_size("seq")
    B = lax.axis_size("batch")
    seq_index = lax.axis_index("seq")
    place = lax.axis_index(("batch", "seq"))
    L, image_count, D = image_tokens.shape
    live_text = text_tokens.shape[1]
    text_count = -(-live_text // 16) * 16
    pad = ((0, 0), (0, text_count - live_text), (0, 0))
    head = D // HEADS
    own_width = D // S
    is_image = (jnp.arange(image_count + text_count) < image_count)[:, None]

    bias_widths = [array.shape[1] for array in (qv_bias, out_bias, up_bias, down_bias)]
    bias_ends = np.cumsum(bias_widths)
    own_biases = jnp.concatenate([qv_bias, out_bias, up_bias, down_bias], axis=1)
    near = gather_batch(jnp.concatenate([conditioning, own_biases], axis=1))
    cond_all = near[:, :, :D].reshape(B * L, D)
    column_biases = near[:, :, D:].astype(F32)
    smooth_all = jax.nn.silu(cond_all.astype(F32)).astype(BF16)
    mod_own = (
        jnp.einsum("sd,tdf->tsf", smooth_all, mod_weight, preferred_element_type=F32)
        + mod_bias.astype(F32)[:, None, :]
    )
    mod_width = mod_own.shape[2]
    mod_sent = mod_own.reshape(2, B, L, mod_width).transpose(1, 0, 2, 3)
    mod_came = swap(mod_sent, "batch")
    small = jnp.concatenate(
        [mod_came.reshape(B, 2 * L * mod_width), column_biases.reshape(B, -1)], axis=1
    )
    small_all = lax.all_gather(small, "seq")
    modulation = (
        small_all[:, :, : 2 * L * mod_width]
        .reshape(S, B, 2, L, mod_width)
        .transpose(2, 3, 1, 0, 4)
        .reshape(2, L, 6, D)
    )
    bias_all = (
        small_all[:, :, 2 * L * mod_width :].reshape(S, B, 2, -1).transpose(2, 1, 0, 3)
    )
    qv_full = bias_all[..., : bias_ends[0]].reshape(2, 2 * D)
    out_bias_full = bias_all[..., bias_ends[0] : bias_ends[1]].reshape(2, D)
    down_bias_full = bias_all[..., bias_ends[2] :].reshape(2, D)
    up_bias_part = (
        column_biases[:, :, bias_ends[1] : bias_ends[2]].transpose(1, 0, 2).reshape(2, -1)
    )
    first_feature = seq_index * own_width
    qkv_bias = jnp.concatenate(
        [
            lax.dynamic_slice_in_dim(qv_full, first_feature, own_width, 1),
            jnp.zeros((2, own_width), F32),
            lax.dynamic_slice_in_dim(qv_full, D + first_feature, own_width, 1),
        ],
        axis=1,
    )

    unit = math.gcd(qkv_weight.shape[2], own_width)
    per_device = qkv_weight.shape[2] // unit
    perms, send, land = match_units(B, S, per_device, own_width // unit)
    back_perms = [[(target, source) for source, target in pairs] for pairs in perms]
    qkv_units = jnp.swapaxes(qkv_weight, 1, 2).reshape(2, per_device, unit, D).swapaxes(0, 1)
    qkv_mine = move_units(qkv_units, perms, send, land, place).swapaxes(0, 1)
    out_units = jnp.swapaxes(out_weight, 1, 2).reshape(2, -1, S, own_width).transpose(2, 0, 1, 3)
    out_mine = swap(out_units, "seq")
    out_columns = out_mine.shape[2]
    heads_all = gather_batch(
        jnp.concatenate([qkv_mine.reshape(-1, D), out_mine.reshape(-1, D)], axis=0)
    )
    up_all = gather_batch(jnp.swapaxes(up_weight, 1, 2))
    down_all = gather_batch(jnp.swapaxes(down_weight, 1, 2))
    qkv_width = per_device * unit
    qkv_rows = 2 * qkv_width
    out_all = heads_all[:, qkv_rows:].reshape(B, S, 2, out_columns, own_width)
    qkv_part = [
        heads_all[:, t * qkv_width : (t + 1) * qkv_width].reshape(-1, D) for t in range(2)
    ]
    out_part = [out_all[:, :, t].reshape(D, own_width) for t in range(2)]
    up_part = [up_all[:, t].reshape(-1, D) for t in range(2)]
    down_part = [down_all[:, t].reshape(-1, D) for t in range(2)]
    hidden_columns = up_weight.shape[2]

    order = jnp.bitwise_xor(seq_index, jnp.arange(S))
    image_keys = jnp.take(
        key_mask[:, : S * image_count].reshape(L, S, image_count), order, axis=1
    )
    text_keys = jnp.take(
        key_mask[:, S * image_count :].reshape(L, S, live_text), order, axis=1
    )
    text_keys = jnp.pad(text_keys, ((0, 0), (0, 0), (0, text_count - live_text)))
    live = jnp.concatenate([image_keys.reshape(L, -1), text_keys.reshape(L, -1)], axis=1) > 0
    key_bias = jnp.where(live, 0.0, DEAD).astype(F32)
    floors = jnp.where(jnp.all(key_mask > 0, axis=1), -3e38, FLOOR_SCORE * LOG2E).astype(F32)
    floors = floors.reshape(L, 1, 1)

    own_tokens = jnp.concatenate([image_tokens, jnp.pad(text_tokens, pad)], axis=1)
    own_grads = jnp.concatenate([image_cotangent, jnp.pad(text_cotangent, pad)], axis=1)
    token_blocks = gather_blocks(own_tokens)
    grad_blocks = gather_blocks(own_grads)
    tokens_all = [join_rows([block[s] for block in token_blocks], image_count) for s in range(L)]

    def by_row(vectors):
        return jnp.where(is_image, vectors[0][None, :], vectors[1][None, :])

    first_norms, first_stats, qkvs, attended = ([], [], [], [])
    for s in range(L):
        norms, stats, rows = ([], [], [])
        for t in range(2):
            pieces = modulation[t, s]
            values = tokens_all[s][t].astype(F32)
            mean, inverse = norm_stats(values)
            norm = (
                (values - mean) * inverse * (1.0 + pieces[1][None, :]) + pieces[0][None, :]
            ).astype(BF16)
            rows.append((dot_nt(norm, qkv_part[t]) + qkv_bias[t][None, :]).astype(BF16))
            norms.append(norm)
            stats.append((mean, inverse))
        if s == L - 1:
            rows, grad_blocks = lax.optimization_barrier((rows, grad_blocks))
        first_norms.append(norms)
        first_stats.append(stats)
        qkvs.append(rows)
        attended.append(attention(rows[0], rows[1], key_bias[s], floors[s], head))
    grads_all = [join_rows([block[s] for block in grad_blocks], image_count) for s in range(L)]
    projections, middles, middle_stats, second_all = ([], [], [], [])
    for s in range(L):
        partial = [dot_nt(attended[s][t], out_part[t]).astype(BF16) for t in range(2)]
        summed = scatter_blocks(split_rows(partial[0], partial[1], image_count, text_count))
        pieces = [by_row(modulation[:, s, k]) for k in range(6)]
        projection = summed + by_row(out_bias_full)
        middle = own_tokens[s].astype(F32) + pieces[2] * projection
        mean, inverse = norm_stats(middle)
        second = (middle - mean) * inverse * (1.0 + pieces[4]) + pieces[3]
        projections.append(projection)
        middles.append(middle)
        middle_stats.append((mean, inverse))
        second_all.append(join_rows(gather_blocks(second.astype(BF16)), image_count))

    def both(left, right, t):
        total = dot_tn(left[0][t], right[0][t])
        for s in range(1, L):
            total = total + dot_tn(left[s][t], right[s][t])
        return total.astype(BF16)

    def stack_columns(values, width):
        return jnp.stack([value.reshape(B, width, D) for value in values], axis=1)

    hidden_acts, hidden_pres, mlp_grads = ([], [], [])
    for s in range(L):
        acts, pres, grads = ([], [], [])
        for t in range(2):
            pre = dot_nt(second_all[s][t], up_part[t]) + up_bias_part[t][None, :]
            acts.append(gelu_tanh(pre).astype(BF16))
            pres.append(pre)
            grads.append(
                (modulation[t, s][5][None, :] * grads_all[s][t].astype(F32)).astype(BF16)
            )
        hidden_acts.append(acts)
        hidden_pres.append(pres)
        mlp_grads.append(grads)
    down_sent = stack_columns([both(hidden_acts, mlp_grads, t) for t in range(2)], hidden_columns)
    down_came = scatter_batch(down_sent)
    late_pres, down_sent = lax.optimization_barrier((hidden_pres[-1], down_sent))
    hidden_pres[-1] = late_pres
    pre_grads, norm2_sums = ([], [])
    for s in range(L):
        pre_low, back = ([], [])
        for t in range(2):
            act_grad = dot_nt(mlp_grads[s][t], down_part[t])
            pre_grad = jax.vjp(gelu_tanh, hidden_pres[s][t])[1](act_grad)[0].astype(BF16)
            pre_low.append(pre_grad)
            back.append(dot_nn(pre_grad, up_part[t]).astype(BF16))
        pre_grads.append(pre_low)
        norm2_sums.append(
            scatter_blocks(split_rows(back[0], back[1], image_count, text_count))
        )
    up_sent = stack_columns([both(pre_grads, second_all, t) for t in range(2)], hidden_columns)
    up_came = scatter_batch(up_sent)
    up_bias_sum = jnp.stack(
        [
            sum(jnp.sum(pre_grads[s][t].astype(F32), axis=0) for s in range(L))
            for t in range(2)
        ]
    )
    mlp_parts = [
        split_rows(
            dot_nn(hidden_acts[s][0], down_part[0]).astype(BF16),
            dot_nn(hidden_acts[s][1], down_part[1]).astype(BF16),
            image_count,
            text_count,
        )
        for s in range(L)
    ]
    mlp_sums = scatter_blocks([jnp.stack([mlp_parts[s][r] for s in range(L)]) for r in range(4)])

    def row_sums(values):
        return jnp.stack(
            [jnp.sum(values[:image_count], axis=0), jnp.sum(values[image_count:], axis=0)]
        )

    mod_grads = [[None] * 6 for _ in range(L)]
    middle_grads, proj_all = ([], [])
    out_bias_sum = 0.0
    for s in range(L):
        pieces = [by_row(modulation[:, s, k]) for k in range(6)]
        norm_grad = norm2_sums[s]
        mean, inverse = middle_stats[s]
        norm = (middles[s] - mean) * inverse
        middle_grad = own_grads[s].astype(F32) + norm_back(norm, inverse, norm_grad, pieces[4])
        low = (pieces[2] * middle_grad).astype(BF16)
        proj_all.append(join_rows(gather_blocks(low), image_count))
        mod_grads[s][3] = row_sums(norm_grad)
        mod_grads[s][4] = row_sums(norm_grad * norm)
        mod_grads[s][2] = row_sums(middle_grad * projections[s])
        out_bias_sum = out_bias_sum + row_sums(low.astype(F32))
        middle_grads.append(middle_grad)

    qkv_grads, norm1_sums = ([], [])
    for s in range(L):
        attended_grad = [dot_nn(proj_all[s][t], out_part[t]).astype(BF16) for t in range(2)]
        if s == 0:
            attended_grad, up_sent = lax.optimization_barrier((attended_grad, up_sent))
        if s == L - 1:
            attended_grad, mlp_sums = lax.optimization_barrier((attended_grad, mlp_sums))
        grads = attention_back(
            qkvs[s][0], qkvs[s][1], attended_grad[0], attended_grad[1], key_bias[s], floors[s], head
        )
        qkv_grads.append(grads)
        back = [dot_nn(grads[t], qkv_part[t]).astype(BF16) for t in range(2)]
        for k in range(2):
            sums = []
            for t in range(2):
                wide = back[t].astype(F32)
                if k == 1:
                    mean, inverse = first_stats[s][t]
                    wide = wide * ((tokens_all[s][t].astype(F32) - mean) * inverse)
                sums.append(jnp.sum(wide, axis=0))
            mod_grads[s][k] = jnp.stack(sums)
        norm1_sums.append(
            scatter_blocks(split_rows(back[0], back[1], image_count, text_count))
        )
    out_sum = [both(proj_all, attended, t) for t in range(2)]
    qkv_sum = [both(qkv_grads, first_norms, t) for t in range(2)]
    qkv_sent = stack_columns(qkv_sum, qkv_width).reshape(B, qkv_rows, D)
    out_sent = jnp.stack(
        [value.reshape(B, S, out_columns, own_width) for value in out_sum], axis=2
    ).reshape(B, -1, D)
    head_grads = scatter_batch(jnp.concatenate([qkv_sent, out_sent], axis=1))
    qkv_home = move_units(
        head_grads[:qkv_rows].reshape(2, per_device, unit, D).swapaxes(0, 1),
        back_perms,
        land,
        send,
        place,
    )
    out_home = swap(head_grads[qkv_rows:].reshape(S, 2, out_columns, own_width), "seq")
    qkv_weight_grad = qkv_home.swapaxes(0, 1).reshape(2, -1, D).swapaxes(1, 2).astype(F32)
    out_weight_grad = (
        out_home.transpose(1, 2, 0, 3).reshape(2, out_columns, D).swapaxes(1, 2).astype(F32)
    )
    up_weight_grad = up_came.swapaxes(1, 2).astype(F32)
    down_weight_grad = down_came.swapaxes(1, 2).astype(F32)

    results, input_grads = ([], [])
    down_bias_sum = 0.0
    for s in range(L):
        pieces = [by_row(modulation[:, s, k]) for k in range(6)]
        grad = own_grads[s].astype(F32)
        mlp_value = mlp_sums[s] + by_row(down_bias_full)
        results.append((middles[s] + pieces[5] * mlp_value).astype(BF16))
        mod_grads[s][5] = row_sums(grad * mlp_value)
        own_low = (pieces[5] * grad).astype(BF16)
        down_bias_sum = down_bias_sum + row_sums(own_low.astype(F32))
        values = own_tokens[s].astype(F32)
        mean, inverse = norm_stats(values)
        norm = (values - mean) * inverse
        input_grads.append(
            middle_grads[s] + norm_back(norm, inverse, norm1_sums[s], pieces[1])
        )
    text_rows = slice(image_count, image_count + live_text)

    mod_rows = jnp.stack([jnp.concatenate(mod_grads[s], axis=1) for s in range(L)], axis=1)
    mod_rows = mod_rows.reshape(2, L, B, S, mod_width).transpose(3, 2, 0, 1, 4)
    qv_bias_sum = jnp.zeros((2, 2 * D), F32)
    for part, column in ((0, 0), (1, 2 * own_width)):
        sums = jnp.stack(
            [
                sum(
                    jnp.sum(
                        qkv_grads[s][t][:, column : column + own_width].astype(F32), axis=0
                    )
                    for s in range(L)
                )
                for t in range(2)
            ]
        )
        qv_bias_sum = lax.dynamic_update_slice_in_dim(
            qv_bias_sum, sums, part * D + first_feature, 1
        )
    up_bias_rows = lax.dynamic_update_slice_in_dim(
        jnp.zeros((2, B, S, hidden_columns), F32),
        up_bias_sum.reshape(2, B, 1, hidden_columns),
        seq_index,
        2,
    )
    bias_rows = jnp.concatenate(
        [
            qv_bias_sum.reshape(2, B, S, -1),
            out_bias_sum.reshape(2, B, S, -1),
            up_bias_rows,
            down_bias_sum.reshape(2, B, S, -1),
        ],
        axis=3,
    ).transpose(2, 1, 0, 3)
    packed = jnp.concatenate(
        [mod_rows.reshape(S, B, -1), bias_rows.reshape(S, B, -1)], axis=2
    )
    packed = jnp.sum(swap(packed, "seq"), axis=0)
    packed = swap(packed, "batch")
    mod_mine = (
        packed[:, : 2 * L * mod_width]
        .reshape(B, 2, L, mod_width)
        .transpose(1, 0, 2, 3)
        .reshape(2, B * L, mod_width)
        .astype(BF16)
    )
    bias_mine = jnp.sum(packed[:, 2 * L * mod_width :], axis=0).reshape(2, -1)
    qv_bias_grad, out_bias_grad, up_bias_grad, down_bias_grad = jnp.split(
        bias_mine, bias_ends[:3], axis=1
    )
    mod_weight_grad = jnp.einsum(
        "sd,tsf->tdf", smooth_all, mod_mine, preferred_element_type=F32
    )
    mod_bias_grad = jnp.sum(mod_mine.astype(F32), axis=1)
    smooth_part = jnp.einsum("tsf,tdf->sd", mod_mine, mod_weight, preferred_element_type=F32)
    smooth_grad = jnp.sum(swap(smooth_part.reshape(B, L, D), "batch"), axis=0)
    smooth_grad = smooth_grad + flip(smooth_grad, 1)
    smooth_grad = smooth_grad + flip(smooth_grad, 2)
    cond_grad = jax.vjp(jax.nn.silu, conditioning.astype(F32))[1](smooth_grad)[0]
    return (
        jnp.stack([values[:image_count] for values in results]),
        jnp.stack([values[text_rows] for values in results]),
        jnp.stack([values[:image_count] for values in input_grads]),
        jnp.stack([values[text_rows] for values in input_grads]),
        cond_grad,
        mod_weight_grad,
        mod_bias_grad,
        qkv_weight_grad,
        qv_bias_grad,
        out_weight_grad,
        out_bias_grad,
        up_weight_grad,
        up_bias_grad,
        down_weight_grad,
        down_bias_grad,
    )


def choose_layer(mesh):
    if mesh.shape["seq"] == 4 and HEADS % 8 == 0:
        return swift_layer
    return general_layer


def solution(mesh):
    layer = choose_layer(mesh)
    return jax.shard_map(
        layer,
        mesh=mesh,
        in_specs=(
            P("batch", "seq", None),
            P("batch", "seq", None),
            P("batch", None),
            P("batch", None),
            P(None, None, ("batch", "seq")),
            P(None, ("batch", "seq")),
            P(None, None, ("batch", "seq")),
            P(None, ("batch", "seq")),
            P(None, None, ("batch", "seq")),
            P(None, ("batch", "seq")),
            P(None, None, ("batch", "seq")),
            P(None, ("batch", "seq")),
            P(None, None, ("batch", "seq")),
            P(None, ("batch", "seq")),
            P("batch", "seq", None),
            P("batch", "seq", None),
        ),
        out_specs=(
            P("batch", "seq", None),
            P("batch", "seq", None),
            P("batch", "seq", None),
            P("batch", "seq", None),
            P("batch", None),
            P(None, None, ("batch", "seq")),
            P(None, ("batch", "seq")),
            P(None, None, ("batch", "seq")),
            P(None, ("batch", "seq")),
            P(None, None, ("batch", "seq")),
            P(None, ("batch", "seq")),
            P(None, None, ("batch", "seq")),
            P(None, ("batch", "seq")),
            P(None, None, ("batch", "seq")),
            P(None, ("batch", "seq")),
        ),
        check_vma=False,
    )
```

```python
import functools
import math

import jax
import jax.numpy as jnp
import numpy as np
from jax import lax
from jax.experimental import pallas as pl
from jax.experimental.pallas import tpu as pltpu
from jax.sharding import PartitionSpec as P

HEADS = 24


NORM_EPSILON = 1e-06
FLOOR_SCORE = -10000.0


def modulate(tokens, shift_vec, scale_vec):
    row_mean = jnp.mean(tokens, axis=-1, keepdims=True)
    centered = tokens - row_mean
    row_var = jnp.mean(centered * centered, axis=-1, keepdims=True)
    return (
        centered * lax.rsqrt(row_var + NORM_EPSILON) * (1.0 + scale_vec[:, None, :])
        + shift_vec[:, None, :]
    )


def gelu_tanh(values):
    return jax.nn.gelu(values, approximate=True)


def unmix_columns(values, seq_devices, batch_devices):
    array_shape = values.shape
    piece_width = array_shape[-1] // (seq_devices * batch_devices)
    grid_view = values.reshape(array_shape[:-1] + (seq_devices, batch_devices, piece_width))
    return jnp.swapaxes(grid_view, -3, -2).reshape(array_shape)


def remix_columns(values, seq_devices, batch_devices):
    array_shape = values.shape
    piece_width = array_shape[-1] // (seq_devices * batch_devices)
    grid_view = values.reshape(array_shape[:-1] + (batch_devices, seq_devices, piece_width))
    return jnp.swapaxes(grid_view, -3, -2).reshape(array_shape)


def fetch_columns(
    up_weight,
    down_weight,
    mod_weight,
    qkv_weight,
    out_weight,
    up_bias,
    mod_bias,
    qv_bias,
    out_bias,
    down_bias,
):
    return (
        lax.all_gather(up_weight, "batch", axis=2, tiled=True),
        lax.all_gather(down_weight, "batch", axis=2, tiled=True),
        lax.all_gather(mod_weight, "batch", axis=2, tiled=True),
        lax.all_gather(qkv_weight, "batch", axis=2, tiled=True),
        lax.all_gather(out_weight, "batch", axis=2, tiled=True),
        lax.all_gather(up_bias, "batch", axis=1, tiled=True),
        lax.all_gather(mod_bias, "batch", axis=1, tiled=True),
        lax.all_gather(qv_bias, "batch", axis=1, tiled=True),
        lax.all_gather(out_bias, "batch", axis=1, tiled=True),
        lax.all_gather(down_bias, "batch", axis=1, tiled=True),
    )


def fetch_modulation(mod_part, mod_bias_part):
    return (
        lax.all_gather(mod_part, "seq", axis=2, tiled=True),
        lax.all_gather(mod_bias_part, "seq", axis=1, tiled=True),
    )


def gather_rows(first, second):
    return (
        lax.all_gather(first, "seq", axis=1, tiled=True),
        lax.all_gather(second, "seq", axis=1, tiled=True),
    )


def sum_rows(first, second, seq_devices):
    local_seqs, first_rows, width = first.shape
    first_local = first_rows // seq_devices
    second_local = second.shape[1] // seq_devices
    joined = jnp.concatenate(
        [
            first.reshape(local_seqs, seq_devices, first_local, width),
            second.reshape(local_seqs, seq_devices, second_local, width),
        ],
        axis=2,
    )
    joined = joined.reshape(local_seqs, seq_devices * (first_local + second_local), width)
    total = lax.psum_scatter(joined, "seq", scatter_dimension=1, tiled=True)
    return (total[:, :first_local], total[:, first_local:])


def to_rows(first, second):
    return (
        lax.all_to_all(first, "seq", split_axis=1, concat_axis=2, tiled=True),
        lax.all_to_all(second, "seq", split_axis=1, concat_axis=2, tiled=True),
    )


def to_columns(first, second):
    return (
        lax.all_to_all(first, "seq", split_axis=2, concat_axis=1, tiled=True),
        lax.all_to_all(second, "seq", split_axis=2, concat_axis=1, tiled=True),
    )


def own_block(values, seq_index, seq_devices):
    width = values.shape[1] // seq_devices
    return lax.dynamic_slice_in_dim(values, seq_index * width, width, 1)


def general_layer(
    image_tokens,
    text_tokens,
    conditioning,
    key_mask,
    mod_weight,
    mod_bias,
    qkv_weight,
    qv_bias,
    out_weight,
    out_bias,
    up_weight,
    up_bias,
    down_weight,
    down_bias,
    image_cotangent,
    text_cotangent,
):
    seq_devices = lax.axis_size("seq")
    batch_devices = lax.axis_size("batch")
    seq_index = lax.axis_index("seq")
    local_seqs, image_count, model_width = image_tokens.shape
    text_count = text_tokens.shape[1]
    block_rows = image_count + text_count
    key_count = block_rows * seq_devices
    head_size = model_width // HEADS
    factor = 1.0 / math.sqrt(head_size)
    inputs = (image_tokens.astype(jnp.float32), text_tokens.astype(jnp.float32))
    cotangents = (image_cotangent.astype(jnp.float32), text_cotangent.astype(jnp.float32))
    row_spans = ((0, image_count), (image_count, block_rows))
    image_keys = key_mask[:, : image_count * seq_devices].reshape(
        local_seqs, seq_devices, image_count
    )
    text_keys = key_mask[:, image_count * seq_devices :].reshape(
        local_seqs, seq_devices, text_count
    )
    key_live = (
        jnp.concatenate([image_keys, text_keys], axis=2).reshape(local_seqs, key_count) > 0
    )[:, None, None, :]
    cond_float = conditioning.astype(jnp.float32)
    smooth = jax.nn.silu(cond_float).astype(jnp.bfloat16)
    fetched = fetch_columns(
        up_weight,
        down_weight,
        mod_weight,
        qkv_weight,
        out_weight,
        up_bias,
        mod_bias,
        qv_bias,
        out_bias,
        down_bias,
    )
    (
        up_part,
        down_part,
        mod_part,
        qkv_part,
        out_part,
        up_bias_part,
        mod_bias_part,
        qv_part,
        out_bias_part,
        down_bias_part,
    ) = fetched
    mod_full, mod_bias_full = fetch_modulation(mod_part, mod_bias_part)
    mixed_mod = (
        jnp.einsum("sd,tdf->tsf", smooth, mod_full, preferred_element_type=jnp.float32)
        + mod_bias_full.astype(jnp.float32)[:, None, :]
    )
    modulation = unmix_columns(mixed_mod, seq_devices, batch_devices).reshape(
        2, local_seqs, 6, model_width
    )
    first_norms = []
    for modality in range(2):
        pieces = modulation[modality]
        first_norms.append(
            modulate(inputs[modality], pieces[:, 0], pieces[:, 1]).astype(jnp.bfloat16)
        )
    norm_image_all, norm_text_all, qv_seq, out_bias_seq, down_bias_seq = (
        lax.all_gather(first_norms[0], "seq", axis=1, tiled=True),
        lax.all_gather(first_norms[1], "seq", axis=1, tiled=True),
        lax.all_gather(qv_part, "seq", axis=1, tiled=True),
        lax.all_gather(out_bias_part, "seq", axis=1, tiled=True),
        lax.all_gather(down_bias_part, "seq", axis=1, tiled=True),
    )
    first_all = (norm_image_all, norm_text_all)
    qv_full = unmix_columns(qv_seq, seq_devices, batch_devices).astype(jnp.float32)
    out_bias_full = unmix_columns(out_bias_seq, seq_devices, batch_devices).astype(jnp.float32)
    down_bias_full = unmix_columns(down_bias_seq, seq_devices, batch_devices).astype(jnp.float32)
    qkv_cols = [
        jnp.einsum(
            "srd,df->srf",
            first_all[modality],
            qkv_part[modality],
            preferred_element_type=jnp.float32,
        )
        for modality in range(2)
    ]
    qkv_rows = to_rows(qkv_cols[0], qkv_cols[1])
    queries, keyvals = ([], [])
    for modality in range(2):
        projected = unmix_columns(qkv_rows[modality], seq_devices, batch_devices)
        qv_vector = qv_full[modality]
        queries.append(
            (projected[..., :model_width] + qv_vector[:model_width]).astype(jnp.bfloat16)
        )
        value_shift = jnp.concatenate(
            [jnp.zeros((model_width,), jnp.float32), qv_vector[model_width:]]
        )
        keyvals.append((projected[..., model_width:] + value_shift).astype(jnp.bfloat16))
    joined_query = jnp.concatenate(queries, axis=1)
    joined_keyval = jnp.concatenate(keyvals, axis=1)
    all_keyval = lax.all_gather(joined_keyval, "seq", axis=1, tiled=True)
    query_heads = joined_query.reshape(local_seqs, block_rows, HEADS, head_size)
    key_heads = all_keyval[..., :model_width].reshape(local_seqs, key_count, HEADS, head_size)
    value_heads = all_keyval[..., model_width:].reshape(local_seqs, key_count, HEADS, head_size)
    scores = (
        jnp.einsum("sqhe,skhe->shqk", query_heads, key_heads, preferred_element_type=jnp.float32)
        * factor
    )
    row_max = jnp.max(jnp.where(key_live, scores, FLOOR_SCORE), axis=-1, keepdims=True)
    exp_terms = jnp.exp(jnp.where(key_live, scores - row_max, FLOOR_SCORE))
    denominator = jnp.maximum(jnp.sum(exp_terms, axis=-1, keepdims=True), 1.0)
    prob_low = (exp_terms / denominator).astype(jnp.bfloat16)
    logsum = row_max + jnp.log(denominator)
    attended = jnp.einsum(
        "shqk,skhe->sqhe", prob_low, value_heads, preferred_element_type=jnp.float32
    )
    attended = attended.reshape(local_seqs, block_rows, model_width).astype(jnp.bfloat16)
    attended_all = gather_rows(attended[:, :image_count], attended[:, image_count:])
    out_cols = [
        jnp.einsum(
            "srd,df->srf",
            attended_all[modality],
            out_part[modality],
            preferred_element_type=jnp.float32,
        )
        for modality in range(2)
    ]
    out_rows = to_rows(out_cols[0], out_cols[1])
    projections, middles, second_norms = ([], [], [])
    for modality in range(2):
        pieces = modulation[modality]
        projection = (
            unmix_columns(out_rows[modality], seq_devices, batch_devices) + out_bias_full[modality]
        )
        middle = inputs[modality] + pieces[:, 2][:, None, :] * projection
        second_norms.append(modulate(middle, pieces[:, 3], pieces[:, 4]).astype(jnp.bfloat16))
        projections.append(projection)
        middles.append(middle)
    group_rows = gather_rows(second_norms[0], second_norms[1])
    hidden_pre, hidden_act, partials = ([], [], [])
    for modality in range(2):
        pre_values = jnp.einsum(
            "srd,df->srf",
            group_rows[modality],
            up_part[modality],
            preferred_element_type=jnp.float32,
        ) + up_bias_part[modality].astype(jnp.float32)
        act_values = gelu_tanh(pre_values).astype(jnp.bfloat16)
        partials.append(
            jnp.einsum(
                "srf,df->srd", act_values, down_part[modality], preferred_element_type=jnp.float32
            )
        )
        hidden_pre.append(pre_values)
        hidden_act.append(act_values)
    mlp_rows = sum_rows(partials[0], partials[1], seq_devices)
    mlp_outs, results = ([], [])
    for modality in range(2):
        pieces = modulation[modality]
        mlp_value = mlp_rows[modality] + down_bias_full[modality]
        results.append(
            (middles[modality] + pieces[:, 5][:, None, :] * mlp_value).astype(jnp.bfloat16)
        )
        mlp_outs.append(mlp_value)
    fetched_back = fetch_columns(
        up_weight,
        down_weight,
        mod_weight,
        qkv_weight,
        out_weight,
        up_bias,
        mod_bias,
        qv_bias,
        out_bias,
        down_bias,
    )
    up_back, down_back, mod_back, qkv_back, out_back = (
        fetched_back[0],
        fetched_back[1],
        fetched_back[2],
        fetched_back[3],
        fetched_back[4],
    )
    mod_bias_back = fetched_back[6]
    mlp_grads, gate_twos, down_bias_grads = ([], [], [])
    for modality in range(2):
        pieces = modulation[modality]
        mlp_grad = (pieces[:, 5][:, None, :] * cotangents[modality]).astype(jnp.bfloat16)
        gate_twos.append(jnp.sum(cotangents[modality] * mlp_outs[modality], axis=1))
        down_bias_grads.append(jnp.sum(mlp_grad.astype(jnp.float32), axis=(0, 1)))
        mlp_grads.append(mlp_grad)
    group_grads = gather_rows(mlp_grads[0], mlp_grads[1])
    down_grads, up_grads, up_bias_grads, norm_partials = ([], [], [], [])
    for modality in range(2):
        down_grads.append(
            jnp.einsum(
                "srd,srf->df",
                group_grads[modality],
                hidden_act[modality],
                preferred_element_type=jnp.float32,
            )
        )
        act_grad = jnp.einsum(
            "srd,df->srf",
            group_grads[modality],
            down_back[modality],
            preferred_element_type=jnp.float32,
        )
        pullback = jax.vjp(gelu_tanh, hidden_pre[modality])[1]
        pre_grad = pullback(act_grad)[0].astype(jnp.bfloat16)
        up_grads.append(
            jnp.einsum(
                "srd,srf->df", group_rows[modality], pre_grad, preferred_element_type=jnp.float32
            )
        )
        up_bias_grads.append(jnp.sum(pre_grad.astype(jnp.float32), axis=(0, 1)))
        norm_partials.append(
            jnp.einsum(
                "srf,df->srd", pre_grad, up_back[modality], preferred_element_type=jnp.float32
            )
        )
    norm_grads = sum_rows(norm_partials[0], norm_partials[1], seq_devices)
    middle_grads, shift_twos, scale_twos, gate_ones, out_bias_grads, proj_grads = (
        [],
        [],
        [],
        [],
        [],
        [],
    )
    for modality in range(2):
        pieces = modulation[modality]
        pullback = jax.vjp(modulate, middles[modality], pieces[:, 3], pieces[:, 4])[1]
        middle_part, shift_two, scale_two = pullback(norm_grads[modality])
        middle_grad = cotangents[modality] + middle_part
        proj_grad = (pieces[:, 2][:, None, :] * middle_grad).astype(jnp.bfloat16)
        gate_ones.append(jnp.sum(middle_grad * projections[modality], axis=1))
        out_bias_grads.append(jnp.sum(proj_grad.astype(jnp.float32), axis=(0, 1)))
        proj_grads.append(remix_columns(proj_grad, seq_devices, batch_devices))
        middle_grads.append(middle_grad)
        shift_twos.append(shift_two)
        scale_twos.append(scale_two)
    proj_cols = to_columns(proj_grads[0], proj_grads[1])
    out_grads, attended_partials = ([], [])
    for modality in range(2):
        out_grads.append(
            jnp.einsum(
                "srd,srf->df",
                attended_all[modality],
                proj_cols[modality],
                preferred_element_type=jnp.float32,
            )
        )
        attended_partials.append(
            jnp.einsum(
                "srf,df->srd",
                proj_cols[modality],
                out_back[modality],
                preferred_element_type=jnp.float32,
            )
        )
    attended_sums = sum_rows(attended_partials[0], attended_partials[1], seq_devices)
    attended_grad = jnp.concatenate([attended_sums[0], attended_sums[1]], axis=1).astype(
        jnp.bfloat16
    )
    grad_heads = attended_grad.reshape(local_seqs, block_rows, HEADS, head_size)
    scores_again = (
        jnp.einsum("sqhe,skhe->shqk", query_heads, key_heads, preferred_element_type=jnp.float32)
        * factor
    )
    probs_again = jnp.exp(jnp.where(key_live, scores_again - logsum, FLOOR_SCORE))
    probs_again_low = probs_again.astype(jnp.bfloat16)
    prob_grad = jnp.einsum(
        "sqhe,skhe->shqk", grad_heads, value_heads, preferred_element_type=jnp.float32
    )
    inner_sum = jnp.sum(probs_again * prob_grad, axis=-1, keepdims=True)
    score_grad = (probs_again * (prob_grad - inner_sum)).astype(jnp.bfloat16)
    query_grad = (
        jnp.einsum("shqk,skhe->sqhe", score_grad, key_heads, preferred_element_type=jnp.float32)
        * factor
    )
    query_grad = query_grad.reshape(local_seqs, block_rows, model_width).astype(jnp.bfloat16)
    key_grad = (
        jnp.einsum("shqk,sqhe->skhe", score_grad, query_heads, preferred_element_type=jnp.float32)
        * factor
    )
    value_grad = jnp.einsum(
        "shqk,sqhe->skhe", probs_again_low, grad_heads, preferred_element_type=jnp.float32
    )
    key_rows, value_rows = (
        lax.psum_scatter(
            key_grad.reshape(local_seqs, key_count, model_width),
            "seq",
            scatter_dimension=1,
            tiled=True,
        ),
        lax.psum_scatter(
            value_grad.reshape(local_seqs, key_count, model_width),
            "seq",
            scatter_dimension=1,
            tiled=True,
        ),
    )
    key_rows = key_rows.astype(jnp.bfloat16)
    value_rows = value_rows.astype(jnp.bfloat16)
    qv_bias_grads, joined_grads = ([], [])
    for modality in range(2):
        row_start, row_stop = row_spans[modality]
        query_part = query_grad[:, row_start:row_stop]
        value_part = value_rows[:, row_start:row_stop]
        joined_grad = jnp.concatenate(
            [query_part, key_rows[:, row_start:row_stop], value_part], axis=-1
        )
        qv_bias_grads.append(
            jnp.concatenate(
                [
                    jnp.sum(query_part.astype(jnp.float32), axis=(0, 1)),
                    jnp.sum(value_part.astype(jnp.float32), axis=(0, 1)),
                ]
            )
        )
        joined_grads.append(remix_columns(joined_grad, seq_devices, batch_devices))
    qkv_grad_cols = to_columns(joined_grads[0], joined_grads[1])
    qkv_grads, first_partials = ([], [])
    for modality in range(2):
        qkv_grads.append(
            jnp.einsum(
                "srd,srf->df",
                first_all[modality],
                qkv_grad_cols[modality],
                preferred_element_type=jnp.float32,
            )
        )
        first_partials.append(
            jnp.einsum(
                "srf,df->srd",
                qkv_grad_cols[modality],
                qkv_back[modality],
                preferred_element_type=jnp.float32,
            )
        )
    first_grads = sum_rows(first_partials[0], first_partials[1], seq_devices)
    input_grads, mod_partials = ([], [])
    for modality in range(2):
        pieces = modulation[modality]
        pullback = jax.vjp(modulate, inputs[modality], pieces[:, 0], pieces[:, 1])[1]
        input_part, shift_one, scale_one = pullback(first_grads[modality])
        input_grads.append(middle_grads[modality] + input_part)
        stacked = jnp.stack(
            [
                shift_one,
                scale_one,
                gate_ones[modality],
                shift_twos[modality],
                scale_twos[modality],
                gate_twos[modality],
            ],
            axis=1,
        )
        mod_partials.append(stacked.reshape(local_seqs, 6 * model_width))
    qv_mixed = remix_columns(jnp.stack(qv_bias_grads), seq_devices, batch_devices)
    out_bias_mixed = remix_columns(jnp.stack(out_bias_grads), seq_devices, batch_devices)
    down_bias_mixed = remix_columns(jnp.stack(down_bias_grads), seq_devices, batch_devices)
    mod_sum, qv_summed, out_bias_summed, down_bias_summed = lax.psum(
        (jnp.stack(mod_partials), qv_mixed, out_bias_mixed, down_bias_mixed), "seq"
    )
    mod_low = mod_sum.astype(jnp.bfloat16)
    mod_mixed = remix_columns(mod_low, seq_devices, batch_devices)
    columns = mod_part.shape[2]
    own_columns = lax.dynamic_slice_in_dim(mod_mixed, seq_index * columns, columns, 2)
    mod_grad = jnp.einsum("sd,tsf->tdf", smooth, own_columns, preferred_element_type=jnp.float32)
    mod_bias_grad = jnp.sum(own_columns.astype(jnp.float32), axis=1)
    mod_again = fetch_modulation(mod_back, mod_bias_back)[0]
    smooth_grad = jnp.einsum(
        "tsf,tdf->sd", mod_mixed, mod_again, preferred_element_type=jnp.float32
    )
    cond_pullback = jax.vjp(jax.nn.silu, cond_float)[1]
    cond_grad = cond_pullback(smooth_grad)[0]
    qv_own = own_block(qv_summed, seq_index, seq_devices)
    out_bias_own = own_block(out_bias_summed, seq_index, seq_devices)
    down_bias_own = own_block(down_bias_summed, seq_index, seq_devices)
    column_grads = (
        lax.psum_scatter(jnp.stack(up_grads), "batch", scatter_dimension=2, tiled=True),
        lax.psum_scatter(jnp.stack(down_grads), "batch", scatter_dimension=2, tiled=True),
        lax.psum_scatter(mod_grad, "batch", scatter_dimension=2, tiled=True),
        lax.psum_scatter(jnp.stack(qkv_grads), "batch", scatter_dimension=2, tiled=True),
        lax.psum_scatter(jnp.stack(out_grads), "batch", scatter_dimension=2, tiled=True),
        lax.psum_scatter(jnp.stack(up_bias_grads), "batch", scatter_dimension=1, tiled=True),
        lax.psum_scatter(mod_bias_grad, "batch", scatter_dimension=1, tiled=True),
        lax.psum_scatter(qv_own, "batch", scatter_dimension=1, tiled=True),
        lax.psum_scatter(out_bias_own, "batch", scatter_dimension=1, tiled=True),
        lax.psum_scatter(down_bias_own, "batch", scatter_dimension=1, tiled=True),
    )
    return (
        results[0],
        results[1],
        input_grads[0],
        input_grads[1],
        cond_grad,
        column_grads[2],
        column_grads[6],
        column_grads[3],
        column_grads[7],
        column_grads[4],
        column_grads[8],
        column_grads[0],
        column_grads[5],
        column_grads[1],
        column_grads[9],
    )


LOG2E = 1.4426950408889634
DEAD = -1e30
BF16 = jnp.bfloat16
F32 = jnp.float32


def dot_nt(a, b):
    return lax.dot_general(a, b, (((1,), (1,)), ((), ())), preferred_element_type=F32)


def dot_nn(a, b):
    return lax.dot_general(a, b, (((1,), (0,)), ((), ())), preferred_element_type=F32)


def dot_tn(a, b):
    return lax.dot_general(a, b, (((0,), (0,)), ((), ())), preferred_element_type=F32)


def attention_kernel(
    query_rows, scale, head, bias_ref, floor_ref, qi, qt, ki, kt, vi, vt, oi, ot, keys, values
):
    image_rows = qi.shape[0]
    keys[:image_rows] = ki[...]
    keys[image_rows:] = kt[...]
    values[:image_rows] = vi[...]
    values[image_rows:] = vt[...]
    bias = bias_ref[...]
    floor = floor_ref[0, 0]
    spans = [(qi, oi, start, query_rows) for start in range(0, image_rows, query_rows)]
    spans.append((qt, ot, 0, qt.shape[0]))
    for source, target, start, size in spans:
        sides = []
        for side in range(2):
            lanes = slice(side * head, (side + 1) * head)
            scores = dot_nt(source[start : start + size, lanes], keys[:, lanes]) * scale + bias
            row_max = jnp.maximum(jnp.max(scores, axis=1, keepdims=True), floor)
            exps = jnp.exp2(scores - row_max)
            total = jnp.maximum(jnp.sum(exps, axis=1, keepdims=True), 1.0)
            probs = (exps * (1.0 / total)).astype(BF16)
            sides.append(dot_nn(probs, values[:, lanes]))
        target[start : start + size, :] = jnp.concatenate(sides, axis=1).astype(BF16)


def pair_block(rows, lanes, pairs, part):
    return pl.BlockSpec((rows, lanes), lambda pair: (0, part * pairs + pair))


def attention(qkv_image, qkv_text, key_bias, floor, head):
    image_rows, width = qkv_image.shape
    text_rows = qkv_text.shape[0]
    rows = image_rows + text_rows
    lanes = 2 * head
    pairs = width // (3 * lanes)
    columns = [
        pair_block(count, lanes, pairs, part)
        for part in range(3)
        for count in (image_rows, text_rows)
    ]
    return pl.pallas_call(
        functools.partial(attention_kernel, 256, LOG2E / math.sqrt(head), head),
        grid=(pairs,),
        in_specs=[
            pl.BlockSpec((1, rows), lambda pair: (0, 0)),
            pl.BlockSpec(memory_space=pltpu.SMEM),
            *columns,
        ],
        out_specs=[columns[0], columns[1]],
        out_shape=[
            jax.ShapeDtypeStruct((image_rows, width // 3), BF16),
            jax.ShapeDtypeStruct((text_rows, width // 3), BF16),
        ],
        scratch_shapes=[pltpu.VMEM((rows, lanes), BF16), pltpu.VMEM((rows, lanes), BF16)],
        compiler_params=pltpu.CompilerParams(vmem_limit_bytes=48 << 20),
        cost_estimate=pl.CostEstimate(
            flops=16 * rows * rows * width // 3,
            bytes_accessed=8 * rows * width // 3,
            transcendentals=rows * rows * width // (3 * head),
        ),
        name="attention",
    )(key_bias[None, :], floor, qkv_image, qkv_text, qkv_image, qkv_text, qkv_image, qkv_text)


def attention_back_kernel(
    query_rows, scale, factor, head, pairs,
    bias_ref, floor_ref, qi, qt, ki, kt, vi, vt, gi, gt, oi, ot, keys, values, key_sum, value_sum,
):
    pair = pl.program_id(0)
    image_rows = qi.shape[0]
    width = 2 * head
    keys[:image_rows] = ki[...]
    keys[image_rows:] = kt[...]
    values[:image_rows] = vi[...]
    values[image_rows:] = vt[...]
    key_sum[...] = jnp.zeros_like(key_sum)
    value_sum[...] = jnp.zeros_like(value_sum)
    bias = bias_ref[...]
    floor = floor_ref[0, 0]
    spans = [(qi, gi, oi, start, query_rows) for start in range(0, image_rows, query_rows)]
    spans.append((qt, gt, ot, 0, qt.shape[0]))
    query_lanes = pl.ds(pl.multiple_of(pair * width, width), width)
    key_lanes = pl.ds(pl.multiple_of((pairs + pair) * width, width), width)
    value_lanes = pl.ds(pl.multiple_of((2 * pairs + pair) * width, width), width)
    for source, grads, target, start, size in spans:
        wide_bias = jnp.concatenate([bias] * -(-size // 128), axis=1)[:, :size]
        dq, dk, dv = ([], [], [])
        for side in range(2):
            lanes = slice(side * head, (side + 1) * head)
            query = source[start : start + size, lanes]
            grad = grads[start : start + size, lanes]
            scores = dot_nt(keys[:, lanes], query) * scale + wide_bias
            top = jnp.maximum(jnp.max(scores, axis=0, keepdims=True), floor)
            exps = jnp.exp2(scores - top)
            total = jnp.maximum(jnp.sum(exps, axis=0, keepdims=True), 1.0)
            probs = exps * (1.0 / total)
            prob_grad = dot_nt(values[:, lanes], grad)
            weighted = probs * prob_grad
            inner = jnp.sum(weighted, axis=0, keepdims=True)
            score_grad = (weighted - probs * inner).astype(BF16)
            dv.append(dot_nn(probs.astype(BF16), grad))
            dk.append(dot_nn(score_grad, query))
            dq.append(dot_tn(score_grad, keys[:, lanes]))
        key_sum[...] += jnp.concatenate(dk, axis=1)
        value_sum[...] += jnp.concatenate(dv, axis=1)
        target[start : start + size, query_lanes] = (
            jnp.concatenate(dq, axis=1) * factor
        ).astype(BF16)
    oi[:, key_lanes] = (key_sum[:image_rows] * factor).astype(BF16)
    ot[:, key_lanes] = (key_sum[image_rows:] * factor).astype(BF16)
    oi[:, value_lanes] = value_sum[:image_rows].astype(BF16)
    ot[:, value_lanes] = value_sum[image_rows:].astype(BF16)


def attention_back(qkv_image, qkv_text, grad_image, grad_text, key_bias, floor, head):
    image_rows, width = qkv_image.shape
    text_rows = qkv_text.shape[0]
    rows = image_rows + text_rows
    lanes = 2 * head
    pairs = width // (3 * lanes)
    columns = [
        pair_block(count, lanes, pairs, part)
        for part in range(3)
        for count in (image_rows, text_rows)
    ]
    return pl.pallas_call(
        functools.partial(
            attention_back_kernel, 256, LOG2E / math.sqrt(head), 1.0 / math.sqrt(head), head, pairs
        ),
        grid=(pairs,),
        in_specs=[
            pl.BlockSpec((rows, 128), lambda pair: (0, 0)),
            pl.BlockSpec(memory_space=pltpu.SMEM),
            *columns,
            columns[0],
            columns[1],
        ],
        out_specs=[
            pl.BlockSpec((image_rows, width), lambda pair: (0, 0)),
            pl.BlockSpec((text_rows, width), lambda pair: (0, 0)),
        ],
        out_shape=[
            jax.ShapeDtypeStruct((image_rows, width), BF16),
            jax.ShapeDtypeStruct((text_rows, width), BF16),
        ],
        scratch_shapes=[
            pltpu.VMEM((rows, lanes), BF16),
            pltpu.VMEM((rows, lanes), BF16),
            pltpu.VMEM((rows, lanes), F32),
            pltpu.VMEM((rows, lanes), F32),
        ],
        compiler_params=pltpu.CompilerParams(vmem_limit_bytes=48 << 20),
        cost_estimate=pl.CostEstimate(
            flops=40 * rows * rows * width // 3,
            bytes_accessed=16 * rows * width // 3,
            transcendentals=rows * rows * width // (3 * head),
        ),
        name="attention_back",
    )(
        jnp.broadcast_to(key_bias[:, None], (rows, 128)),
        floor,
        qkv_image, qkv_text, qkv_image, qkv_text, qkv_image, qkv_text,
        grad_image, grad_text,
    )


def flip(values, bit):
    return lax.ppermute(values, "seq", [(i, i ^ bit) for i in range(4)])


def gather_blocks(own):
    half = own.shape[-1] // 2
    near_x = flip(own, 1)
    near_y = flip(own, 2)
    far_a = flip(near_x[..., :half], 2)
    far_b = flip(near_y[..., half:], 1)
    return (own, near_x, near_y, jnp.concatenate([far_a, far_b], axis=-1))


def add_low(a, b):
    return (a.astype(F32) + b.astype(F32)).astype(BF16)


def scatter_blocks(blocks):
    own, near_x, near_y, far = blocks
    half = own.shape[-1] // 2
    for_y = flip(far[..., :half], 1)
    for_x = flip(far[..., half:], 2)
    from_x = flip(
        jnp.concatenate([near_x[..., :half], add_low(near_x[..., half:], for_x)], axis=-1), 1
    )
    from_y = flip(
        jnp.concatenate([add_low(near_y[..., :half], for_y), near_y[..., half:]], axis=-1), 2
    )
    return own.astype(F32) + from_x.astype(F32) + from_y.astype(F32)


def join_rows(blocks, image_count):
    return (
        jnp.concatenate([block[:image_count] for block in blocks], axis=0),
        jnp.concatenate([block[image_count:] for block in blocks], axis=0),
    )


def split_rows(image, text, image_count, text_count):
    return [
        jnp.concatenate(
            [
                image[r * image_count : (r + 1) * image_count],
                text[r * text_count : (r + 1) * text_count],
            ],
            axis=0,
        )
        for r in range(4)
    ]


def match_units(batch_devices, seq_devices, per_device, group_units):
    devices = batch_devices * seq_devices
    total = devices * per_device
    part_units = total // 3
    sources, targets = ([], [])
    for seq_at in range(seq_devices):
        listed = [
            part * part_units + seq_at * group_units + k
            for part in range(3)
            for k in range(group_units)
        ]
        for place, unit in enumerate(listed):
            sources.append((unit // per_device, unit % per_device))
            targets.append(
                ((place // per_device) * seq_devices + seq_at, place % per_device)
            )
    edges = list(zip(sources, targets))
    rounds = []
    left = list(range(total))
    for _ in range(per_device):
        by_source = {}
        for e in left:
            by_source.setdefault(edges[e][0][0], []).append(e)
        taken = {}

        def place_edge(device, seen):
            for e in by_source[device]:
                target = edges[e][1][0]
                if target in seen:
                    continue
                seen.add(target)
                if target not in taken or place_edge(edges[taken[target]][0][0], seen):
                    taken[target] = e
                    return True
            return False

        for device in range(devices):
            place_edge(device, set())
        chosen = sorted(taken.values())
        rounds.append(chosen)
        left = [e for e in left if e not in chosen]
    send = np.zeros((per_device, devices), np.int32)
    land = np.zeros((per_device, devices), np.int32)
    perms = []
    for k, chosen in enumerate(rounds):
        pairs = []
        for e in chosen:
            (source, source_slot), (target, target_slot) = edges[e]
            pairs.append((source, target))
            send[k, source] = source_slot
            land[k, target] = target_slot
        perms.append(sorted(pairs))
    return perms, send, land


def move_units(units, perms, take, put, place):
    arrived = jnp.zeros_like(units)
    for k, pairs in enumerate(perms):
        slot = jnp.asarray(take[k])[place]
        moved = lax.ppermute(
            lax.dynamic_index_in_dim(units, slot, 0, keepdims=True), ("batch", "seq"), pairs
        )
        arrived = lax.dynamic_update_slice_in_dim(arrived, moved, jnp.asarray(put[k])[place], 0)
    return arrived


def gather_rows_over_batch(values):
    return lax.all_gather(values, "batch", axis=1, tiled=True)


def gather_small(values, axis):
    count = lax.axis_size(axis)
    held = values[None]
    bit = 1
    while bit < count:
        pairs = [(i, i ^ bit) for i in range(count)]
        held = jnp.concatenate([held, lax.ppermute(held, axis, pairs)])
        bit *= 2
    return jnp.take(held, jnp.bitwise_xor(lax.axis_index(axis), jnp.arange(count)), axis=0)


def after(values, *others):
    return lax.optimization_barrier((values, others))[0]


def scatter_rows_over_batch(values):
    return lax.psum_scatter(values, "batch", scatter_dimension=1, tiled=True)


def swap(values, axis):
    return lax.all_to_all(values, axis, 0, 0, tiled=True)


def norm_stats(values):
    mean = jnp.mean(values, axis=-1, keepdims=True)
    centered = values - mean
    variance = jnp.mean(centered * centered, axis=-1, keepdims=True)
    return mean, lax.rsqrt(variance + NORM_EPSILON)


def norm_back(norm, inverse, grad, scale):
    scaled = grad * (1.0 + scale)
    return inverse * (
        scaled
        - jnp.mean(scaled, axis=-1, keepdims=True)
        - norm * jnp.mean(scaled * norm, axis=-1, keepdims=True)
    )


def swift_layer(
    image_tokens,
    text_tokens,
    conditioning,
    key_mask,
    mod_weight,
    mod_bias,
    qkv_weight,
    qv_bias,
    out_weight,
    out_bias,
    up_weight,
    up_bias,
    down_weight,
    down_bias,
    image_cotangent,
    text_cotangent,
):
    S = lax.axis_size("seq")
    B = lax.axis_size("batch")
    seq_index = lax.axis_index("seq")
    place = lax.axis_index(("batch", "seq"))
    L, image_count, D = image_tokens.shape
    live_text = text_tokens.shape[1]
    text_count = -(-live_text // 16) * 16
    pad = ((0, 0), (0, text_count - live_text), (0, 0))
    head = D // HEADS
    own_width = D // S
    is_image = (jnp.arange(image_count + text_count) < image_count)[:, None]

    bias_widths = [array.shape[1] for array in (qv_bias, out_bias, up_bias, down_bias)]
    bias_ends = np.cumsum(bias_widths)
    own_biases = jnp.concatenate([qv_bias, out_bias, up_bias, down_bias], axis=1)
    near = gather_small(jnp.concatenate([conditioning, own_biases], axis=1), "batch")
    cond_all = near[:, :, :D].reshape(B * L, D)
    column_biases = near[:, :, D:].astype(F32)
    smooth_all = jax.nn.silu(cond_all.astype(F32)).astype(BF16)
    mod_own = (
        jnp.einsum("sd,tdf->tsf", smooth_all, mod_weight, preferred_element_type=F32)
        + mod_bias.astype(F32)[:, None, :]
    )
    mod_width = mod_own.shape[2]
    mod_sent = mod_own.reshape(2, B, L, mod_width).transpose(1, 0, 2, 3)
    mod_came = swap(mod_sent, "batch")
    small = jnp.concatenate(
        [mod_came.reshape(B, 2 * L * mod_width), column_biases.reshape(B, -1)], axis=1
    )
    small_all = gather_small(small, "seq")
    modulation = (
        small_all[:, :, : 2 * L * mod_width]
        .reshape(S, B, 2, L, mod_width)
        .transpose(2, 3, 1, 0, 4)
        .reshape(2, L, 6, D)
    )
    bias_all = (
        small_all[:, :, 2 * L * mod_width :].reshape(S, B, 2, -1).transpose(2, 1, 0, 3)
    )
    qv_full = bias_all[..., : bias_ends[0]].reshape(2, 2 * D)
    out_bias_full = bias_all[..., bias_ends[0] : bias_ends[1]].reshape(2, D)
    down_bias_full = bias_all[..., bias_ends[2] :].reshape(2, D)
    up_bias_part = (
        column_biases[:, :, bias_ends[1] : bias_ends[2]].transpose(1, 0, 2).reshape(2, -1)
    )
    first_feature = seq_index * own_width
    qkv_bias = jnp.concatenate(
        [
            lax.dynamic_slice_in_dim(qv_full, first_feature, own_width, 1),
            jnp.zeros((2, own_width), F32),
            lax.dynamic_slice_in_dim(qv_full, D + first_feature, own_width, 1),
        ],
        axis=1,
    )

    unit = math.gcd(qkv_weight.shape[2], own_width)
    per_device = qkv_weight.shape[2] // unit
    perms, send, land = match_units(B, S, per_device, own_width // unit)
    back_perms = [[(target, source) for source, target in pairs] for pairs in perms]
    qkv_units = jnp.swapaxes(qkv_weight, 1, 2).reshape(2, per_device, unit, D).swapaxes(0, 1)
    qkv_mine = move_units(qkv_units, perms, send, land, place).swapaxes(0, 1)
    out_units = jnp.swapaxes(out_weight, 1, 2).reshape(2, -1, S, own_width).transpose(2, 0, 1, 3)
    out_mine = swap(after(out_units, qkv_mine), "seq")
    out_columns = out_mine.shape[2]
    qkv_width = per_device * unit
    qkv_part = gather_rows_over_batch(qkv_mine.reshape(2, qkv_width, D))
    out_rows = out_mine.transpose(1, 0, 2, 3).reshape(2, S * out_columns, own_width)
    out_part = gather_rows_over_batch(after(out_rows, qkv_part))
    up_part = gather_rows_over_batch(after(jnp.swapaxes(up_weight, 1, 2), out_part))
    down_part = gather_rows_over_batch(after(jnp.swapaxes(down_weight, 1, 2), up_part))
    hidden_columns = up_weight.shape[2]

    order = jnp.bitwise_xor(seq_index, jnp.arange(S))
    image_keys = jnp.take(
        key_mask[:, : S * image_count].reshape(L, S, image_count), order, axis=1
    )
    text_keys = jnp.take(
        key_mask[:, S * image_count :].reshape(L, S, live_text), order, axis=1
    )
    text_keys = jnp.pad(text_keys, ((0, 0), (0, 0), (0, text_count - live_text)))
    live = jnp.concatenate([image_keys.reshape(L, -1), text_keys.reshape(L, -1)], axis=1) > 0
    key_bias = jnp.where(live, 0.0, DEAD).astype(F32)
    floors = jnp.where(jnp.all(key_mask > 0, axis=1), -3e38, FLOOR_SCORE * LOG2E).astype(F32)
    floors = floors.reshape(L, 1, 1)

    own_tokens = jnp.concatenate([image_tokens, jnp.pad(text_tokens, pad)], axis=1)
    own_grads = jnp.concatenate([image_cotangent, jnp.pad(text_cotangent, pad)], axis=1)
    token_blocks = gather_blocks(after(own_tokens, qkv_mine))
    grad_blocks = gather_blocks(after(own_grads, token_blocks))
    tokens_all = [join_rows([block[s] for block in token_blocks], image_count) for s in range(L)]

    def by_row(vectors):
        return jnp.where(is_image, vectors[0][None, :], vectors[1][None, :])

    first_norms, first_stats, qkvs, attended, partials = ([], [], [], [], [])
    for s in range(L):
        norms, stats, rows = ([], [], [])
        for t in range(2):
            pieces = modulation[t, s]
            values = tokens_all[s][t].astype(F32)
            mean, inverse = norm_stats(values)
            norm = (
                (values - mean) * inverse * (1.0 + pieces[1][None, :]) + pieces[0][None, :]
            ).astype(BF16)
            rows.append((dot_nt(norm, qkv_part[t]) + qkv_bias[t][None, :]).astype(BF16))
            norms.append(norm)
            stats.append((mean, inverse))
        if s == L - 1:
            rows, grad_blocks, partials = lax.optimization_barrier((rows, grad_blocks, partials))
        first_norms.append(norms)
        first_stats.append(stats)
        qkvs.append(rows)
        attended.append(attention(rows[0], rows[1], key_bias[s], floors[s], head))
        partials.append([dot_nt(attended[s][t], out_part[t]).astype(BF16) for t in range(2)])
    grads_all = [join_rows([block[s] for block in grad_blocks], image_count) for s in range(L)]
    projections, middles, middle_stats, second_all = ([], [], [], [])
    for s in range(L):
        summed = scatter_blocks(split_rows(*partials[s], image_count, text_count))
        pieces = [by_row(modulation[:, s, k]) for k in range(6)]
        projection = summed + by_row(out_bias_full)
        middle = own_tokens[s].astype(F32) + pieces[2] * projection
        mean, inverse = norm_stats(middle)
        second = (middle - mean) * inverse * (1.0 + pieces[4]) + pieces[3]
        projections.append(projection)
        middles.append(middle)
        middle_stats.append((mean, inverse))
        second_all.append(join_rows(gather_blocks(second.astype(BF16)), image_count))

    def both(left, right, t):
        total = dot_tn(left[0][t], right[0][t])
        for s in range(1, L):
            total = total + dot_tn(left[s][t], right[s][t])
        return total.astype(BF16)

    hidden_acts, hidden_pres, mlp_grads = ([], [], [])
    for s in range(L):
        acts, pres, grads = ([], [], [])
        for t in range(2):
            pre = dot_nt(second_all[s][t], up_part[t]) + up_bias_part[t][None, :]
            acts.append(gelu_tanh(pre).astype(BF16))
            pres.append(pre)
            grads.append(
                (modulation[t, s][5][None, :] * grads_all[s][t].astype(F32)).astype(BF16)
            )
        hidden_acts.append(acts)
        hidden_pres.append(pres)
        mlp_grads.append(grads)
    down_sent = jnp.stack([both(hidden_acts, mlp_grads, t) for t in range(2)])
    down_came = scatter_rows_over_batch(down_sent)
    late_pres, down_sent = lax.optimization_barrier((hidden_pres[-1], down_sent))
    hidden_pres[-1] = late_pres
    pre_grads, norm2_sums = ([], [])
    for s in range(L):
        pre_low, back = ([], [])
        for t in range(2):
            act_grad = dot_nt(mlp_grads[s][t], down_part[t])
            pre_grad = jax.vjp(gelu_tanh, hidden_pres[s][t])[1](act_grad)[0].astype(BF16)
            pre_low.append(pre_grad)
            back.append(dot_nn(pre_grad, up_part[t]).astype(BF16))
        pre_grads.append(pre_low)
        norm2_sums.append(
            scatter_blocks(split_rows(back[0], back[1], image_count, text_count))
        )
    up_sent = jnp.stack([both(pre_grads, second_all, t) for t in range(2)])
    up_came = scatter_rows_over_batch(up_sent)
    up_bias_sum = jnp.stack(
        [
            sum(jnp.sum(pre_grads[s][t].astype(F32), axis=0) for s in range(L))
            for t in range(2)
        ]
    )
    mlp_parts = [
        [dot_nn(hidden_acts[s][t], down_part[t]).astype(BF16) for t in range(2)]
        for s in range(L)
    ]

    def row_sums(values):
        return jnp.stack(
            [jnp.sum(values[:image_count], axis=0), jnp.sum(values[image_count:], axis=0)]
        )

    mod_grads = [[None] * 6 for _ in range(L)]
    middle_grads, proj_all = ([], [])
    out_bias_sum = 0.0
    for s in range(L):
        pieces = [by_row(modulation[:, s, k]) for k in range(6)]
        norm_grad = norm2_sums[s]
        mean, inverse = middle_stats[s]
        norm = (middles[s] - mean) * inverse
        middle_grad = own_grads[s].astype(F32) + norm_back(norm, inverse, norm_grad, pieces[4])
        low = (pieces[2] * middle_grad).astype(BF16)
        proj_all.append(join_rows(gather_blocks(low), image_count))
        mod_grads[s][3] = row_sums(norm_grad)
        mod_grads[s][4] = row_sums(norm_grad * norm)
        mod_grads[s][2] = row_sums(middle_grad * projections[s])
        out_bias_sum = out_bias_sum + row_sums(low.astype(F32))
        middle_grads.append(middle_grad)

    mlp_parts = after(mlp_parts, proj_all)
    mlp_parts = [split_rows(*parts, image_count, text_count) for parts in mlp_parts]
    mlp_sums = scatter_blocks([jnp.stack([mlp_parts[s][r] for s in range(L)]) for r in range(4)])

    qkv_grads, norm1_parts = ([], [])
    for s in range(L):
        attended_grad = [dot_nn(proj_all[s][t], out_part[t]).astype(BF16) for t in range(2)]
        if s == 0:
            attended_grad = after(attended_grad, up_sent)
        if s == L - 1:
            attended_grad = after(attended_grad, mlp_sums, norm1_parts)
        grads = attention_back(
            qkvs[s][0], qkvs[s][1], attended_grad[0], attended_grad[1], key_bias[s], floors[s], head
        )
        qkv_grads.append(grads)
        back = [dot_nn(grads[t], qkv_part[t]).astype(BF16) for t in range(2)]
        for k in range(2):
            sums = []
            for t in range(2):
                wide = back[t].astype(F32)
                if k == 1:
                    mean, inverse = first_stats[s][t]
                    wide = wide * ((tokens_all[s][t].astype(F32) - mean) * inverse)
                sums.append(jnp.sum(wide, axis=0))
            mod_grads[s][k] = jnp.stack(sums)
        norm1_parts.append(split_rows(back[0], back[1], image_count, text_count))
    norm1_sums = [scatter_blocks(parts) for parts in norm1_parts]
    out_sum = [both(proj_all, attended, t) for t in range(2)]
    qkv_sum = [both(qkv_grads, first_norms, t) for t in range(2)]
    out_came = scatter_rows_over_batch(after(jnp.stack(out_sum), up_came))
    qkv_came = scatter_rows_over_batch(after(jnp.stack(qkv_sum), out_came))
    qkv_home = move_units(
        qkv_came.reshape(2, per_device, unit, D).swapaxes(0, 1), back_perms, land, send, place
    )
    out_home = swap(out_came.reshape(2, S, out_columns, own_width).swapaxes(0, 1), "seq")
    qkv_weight_grad = qkv_home.swapaxes(0, 1).reshape(2, -1, D).swapaxes(1, 2).astype(F32)
    out_weight_grad = (
        out_home.transpose(1, 2, 0, 3).reshape(2, out_columns, D).swapaxes(1, 2).astype(F32)
    )
    up_weight_grad = up_came.swapaxes(1, 2).astype(F32)
    down_weight_grad = down_came.swapaxes(1, 2).astype(F32)

    results, input_grads = ([], [])
    down_bias_sum = 0.0
    for s in range(L):
        pieces = [by_row(modulation[:, s, k]) for k in range(6)]
        grad = own_grads[s].astype(F32)
        mlp_value = mlp_sums[s] + by_row(down_bias_full)
        results.append((middles[s] + pieces[5] * mlp_value).astype(BF16))
        mod_grads[s][5] = row_sums(grad * mlp_value)
        own_low = (pieces[5] * grad).astype(BF16)
        down_bias_sum = down_bias_sum + row_sums(own_low.astype(F32))
        values = own_tokens[s].astype(F32)
        mean, inverse = norm_stats(values)
        norm = (values - mean) * inverse
        input_grads.append(
            middle_grads[s] + norm_back(norm, inverse, norm1_sums[s], pieces[1])
        )
    text_rows = slice(image_count, image_count + live_text)

    mod_rows = jnp.stack([jnp.concatenate(mod_grads[s], axis=1) for s in range(L)], axis=1)
    mod_rows = mod_rows.reshape(2, L, B, S, mod_width).transpose(3, 2, 0, 1, 4)
    qv_bias_sum = jnp.zeros((2, 2 * D), F32)
    for part, column in ((0, 0), (1, 2 * own_width)):
        sums = jnp.stack(
            [
                sum(
                    jnp.sum(
                        qkv_grads[s][t][:, column : column + own_width].astype(F32), axis=0
                    )
                    for s in range(L)
                )
                for t in range(2)
            ]
        )
        qv_bias_sum = lax.dynamic_update_slice_in_dim(
            qv_bias_sum, sums, part * D + first_feature, 1
        )
    up_bias_rows = lax.dynamic_update_slice_in_dim(
        jnp.zeros((2, B, S, hidden_columns), F32),
        up_bias_sum.reshape(2, B, 1, hidden_columns),
        seq_index,
        2,
    )
    bias_rows = jnp.concatenate(
        [
            qv_bias_sum.reshape(2, B, S, -1),
            out_bias_sum.reshape(2, B, S, -1),
            up_bias_rows,
            down_bias_sum.reshape(2, B, S, -1),
        ],
        axis=3,
    ).transpose(2, 1, 0, 3)
    packed = jnp.concatenate(
        [mod_rows.reshape(S, B, -1), bias_rows.reshape(S, B, -1)], axis=2
    )
    packed = jnp.sum(swap(packed, "seq"), axis=0)
    packed = swap(packed, "batch")
    mod_mine = (
        packed[:, : 2 * L * mod_width]
        .reshape(B, 2, L, mod_width)
        .transpose(1, 0, 2, 3)
        .reshape(2, B * L, mod_width)
        .astype(BF16)
    )
    bias_mine = jnp.sum(packed[:, 2 * L * mod_width :], axis=0).reshape(2, -1)
    qv_bias_grad, out_bias_grad, up_bias_grad, down_bias_grad = jnp.split(
        bias_mine, bias_ends[:3], axis=1
    )
    mod_weight_grad = jnp.einsum(
        "sd,tsf->tdf", smooth_all, mod_mine, preferred_element_type=F32
    )
    mod_bias_grad = jnp.sum(mod_mine.astype(F32), axis=1)
    smooth_part = jnp.einsum("tsf,tdf->sd", mod_mine, mod_weight, preferred_element_type=F32)
    smooth_grad = jnp.sum(swap(smooth_part.reshape(B, L, D), "batch"), axis=0)
    smooth_grad = smooth_grad + flip(smooth_grad, 1)
    smooth_grad = smooth_grad + flip(smooth_grad, 2)
    cond_grad = jax.vjp(jax.nn.silu, conditioning.astype(F32))[1](smooth_grad)[0]
    return (
        jnp.stack([values[:image_count] for values in results]),
        jnp.stack([values[text_rows] for values in results]),
        jnp.stack([values[:image_count] for values in input_grads]),
        jnp.stack([values[text_rows] for values in input_grads]),
        cond_grad,
        mod_weight_grad,
        mod_bias_grad,
        qkv_weight_grad,
        qv_bias_grad,
        out_weight_grad,
        out_bias_grad,
        up_weight_grad,
        up_bias_grad,
        down_weight_grad,
        down_bias_grad,
    )


def choose_layer(mesh):
    if mesh.shape["seq"] == 4 and HEADS % 8 == 0:
        return swift_layer
    return general_layer


def solution(mesh):
    layer = choose_layer(mesh)
    return jax.shard_map(
        layer,
        mesh=mesh,
        in_specs=(
            P("batch", "seq", None),
            P("batch", "seq", None),
            P("batch", None),
            P("batch", None),
            P(None, None, ("batch", "seq")),
            P(None, ("batch", "seq")),
            P(None, None, ("batch", "seq")),
            P(None, ("batch", "seq")),
            P(None, None, ("batch", "seq")),
            P(None, ("batch", "seq")),
            P(None, None, ("batch", "seq")),
            P(None, ("batch", "seq")),
            P(None, None, ("batch", "seq")),
            P(None, ("batch", "seq")),
            P("batch", "seq", None),
            P("batch", "seq", None),
        ),
        out_specs=(
            P("batch", "seq", None),
            P("batch", "seq", None),
            P("batch", "seq", None),
            P("batch", "seq", None),
            P("batch", None),
            P(None, None, ("batch", "seq")),
            P(None, ("batch", "seq")),
            P(None, None, ("batch", "seq")),
            P(None, ("batch", "seq")),
            P(None, None, ("batch", "seq")),
            P(None, ("batch", "seq")),
            P(None, None, ("batch", "seq")),
            P(None, ("batch", "seq")),
            P(None, None, ("batch", "seq")),
            P(None, ("batch", "seq")),
        ),
        check_vma=False,
    )
```

```python
import functools
import math

import jax
import jax.numpy as jnp
import numpy as np
from jax import lax
from jax.experimental import pallas as pl
from jax.experimental.pallas import tpu as pltpu
from jax.sharding import PartitionSpec as P

HEADS = 24


NORM_EPSILON = 1e-06
FLOOR_SCORE = -10000.0


def modulate(tokens, shift_vec, scale_vec):
    row_mean = jnp.mean(tokens, axis=-1, keepdims=True)
    centered = tokens - row_mean
    row_var = jnp.mean(centered * centered, axis=-1, keepdims=True)
    return (
        centered * lax.rsqrt(row_var + NORM_EPSILON) * (1.0 + scale_vec[:, None, :])
        + shift_vec[:, None, :]
    )


def gelu_tanh(values):
    return jax.nn.gelu(values, approximate=True)


def unmix_columns(values, seq_devices, batch_devices):
    array_shape = values.shape
    piece_width = array_shape[-1] // (seq_devices * batch_devices)
    grid_view = values.reshape(array_shape[:-1] + (seq_devices, batch_devices, piece_width))
    return jnp.swapaxes(grid_view, -3, -2).reshape(array_shape)


def remix_columns(values, seq_devices, batch_devices):
    array_shape = values.shape
    piece_width = array_shape[-1] // (seq_devices * batch_devices)
    grid_view = values.reshape(array_shape[:-1] + (batch_devices, seq_devices, piece_width))
    return jnp.swapaxes(grid_view, -3, -2).reshape(array_shape)


def fetch_columns(
    up_weight,
    down_weight,
    mod_weight,
    qkv_weight,
    out_weight,
    up_bias,
    mod_bias,
    qv_bias,
    out_bias,
    down_bias,
):
    return (
        lax.all_gather(up_weight, "batch", axis=2, tiled=True),
        lax.all_gather(down_weight, "batch", axis=2, tiled=True),
        lax.all_gather(mod_weight, "batch", axis=2, tiled=True),
        lax.all_gather(qkv_weight, "batch", axis=2, tiled=True),
        lax.all_gather(out_weight, "batch", axis=2, tiled=True),
        lax.all_gather(up_bias, "batch", axis=1, tiled=True),
        lax.all_gather(mod_bias, "batch", axis=1, tiled=True),
        lax.all_gather(qv_bias, "batch", axis=1, tiled=True),
        lax.all_gather(out_bias, "batch", axis=1, tiled=True),
        lax.all_gather(down_bias, "batch", axis=1, tiled=True),
    )


def fetch_modulation(mod_part, mod_bias_part):
    return (
        lax.all_gather(mod_part, "seq", axis=2, tiled=True),
        lax.all_gather(mod_bias_part, "seq", axis=1, tiled=True),
    )


def gather_rows(first, second):
    return (
        lax.all_gather(first, "seq", axis=1, tiled=True),
        lax.all_gather(second, "seq", axis=1, tiled=True),
    )


def sum_rows(first, second, seq_devices):
    local_seqs, first_rows, width = first.shape
    first_local = first_rows // seq_devices
    second_local = second.shape[1] // seq_devices
    joined = jnp.concatenate(
        [
            first.reshape(local_seqs, seq_devices, first_local, width),
            second.reshape(local_seqs, seq_devices, second_local, width),
        ],
        axis=2,
    )
    joined = joined.reshape(local_seqs, seq_devices * (first_local + second_local), width)
    total = lax.psum_scatter(joined, "seq", scatter_dimension=1, tiled=True)
    return (total[:, :first_local], total[:, first_local:])


def to_rows(first, second):
    return (
        lax.all_to_all(first, "seq", split_axis=1, concat_axis=2, tiled=True),
        lax.all_to_all(second, "seq", split_axis=1, concat_axis=2, tiled=True),
    )


def to_columns(first, second):
    return (
        lax.all_to_all(first, "seq", split_axis=2, concat_axis=1, tiled=True),
        lax.all_to_all(second, "seq", split_axis=2, concat_axis=1, tiled=True),
    )


def own_block(values, seq_index, seq_devices):
    width = values.shape[1] // seq_devices
    return lax.dynamic_slice_in_dim(values, seq_index * width, width, 1)


def general_layer(
    image_tokens,
    text_tokens,
    conditioning,
    key_mask,
    mod_weight,
    mod_bias,
    qkv_weight,
    qv_bias,
    out_weight,
    out_bias,
    up_weight,
    up_bias,
    down_weight,
    down_bias,
    image_cotangent,
    text_cotangent,
):
    seq_devices = lax.axis_size("seq")
    batch_devices = lax.axis_size("batch")
    seq_index = lax.axis_index("seq")
    local_seqs, image_count, model_width = image_tokens.shape
    text_count = text_tokens.shape[1]
    block_rows = image_count + text_count
    key_count = block_rows * seq_devices
    head_size = model_width // HEADS
    factor = 1.0 / math.sqrt(head_size)
    inputs = (image_tokens.astype(jnp.float32), text_tokens.astype(jnp.float32))
    cotangents = (image_cotangent.astype(jnp.float32), text_cotangent.astype(jnp.float32))
    row_spans = ((0, image_count), (image_count, block_rows))
    image_keys = key_mask[:, : image_count * seq_devices].reshape(
        local_seqs, seq_devices, image_count
    )
    text_keys = key_mask[:, image_count * seq_devices :].reshape(
        local_seqs, seq_devices, text_count
    )
    key_live = (
        jnp.concatenate([image_keys, text_keys], axis=2).reshape(local_seqs, key_count) > 0
    )[:, None, None, :]
    cond_float = conditioning.astype(jnp.float32)
    smooth = jax.nn.silu(cond_float).astype(jnp.bfloat16)
    fetched = fetch_columns(
        up_weight,
        down_weight,
        mod_weight,
        qkv_weight,
        out_weight,
        up_bias,
        mod_bias,
        qv_bias,
        out_bias,
        down_bias,
    )
    (
        up_part,
        down_part,
        mod_part,
        qkv_part,
        out_part,
        up_bias_part,
        mod_bias_part,
        qv_part,
        out_bias_part,
        down_bias_part,
    ) = fetched
    mod_full, mod_bias_full = fetch_modulation(mod_part, mod_bias_part)
    mixed_mod = (
        jnp.einsum("sd,tdf->tsf", smooth, mod_full, preferred_element_type=jnp.float32)
        + mod_bias_full.astype(jnp.float32)[:, None, :]
    )
    modulation = unmix_columns(mixed_mod, seq_devices, batch_devices).reshape(
        2, local_seqs, 6, model_width
    )
    first_norms = []
    for modality in range(2):
        pieces = modulation[modality]
        first_norms.append(
            modulate(inputs[modality], pieces[:, 0], pieces[:, 1]).astype(jnp.bfloat16)
        )
    norm_image_all, norm_text_all, qv_seq, out_bias_seq, down_bias_seq = (
        lax.all_gather(first_norms[0], "seq", axis=1, tiled=True),
        lax.all_gather(first_norms[1], "seq", axis=1, tiled=True),
        lax.all_gather(qv_part, "seq", axis=1, tiled=True),
        lax.all_gather(out_bias_part, "seq", axis=1, tiled=True),
        lax.all_gather(down_bias_part, "seq", axis=1, tiled=True),
    )
    first_all = (norm_image_all, norm_text_all)
    qv_full = unmix_columns(qv_seq, seq_devices, batch_devices).astype(jnp.float32)
    out_bias_full = unmix_columns(out_bias_seq, seq_devices, batch_devices).astype(jnp.float32)
    down_bias_full = unmix_columns(down_bias_seq, seq_devices, batch_devices).astype(jnp.float32)
    qkv_cols = [
        jnp.einsum(
            "srd,df->srf",
            first_all[modality],
            qkv_part[modality],
            preferred_element_type=jnp.float32,
        )
        for modality in range(2)
    ]
    qkv_rows = to_rows(qkv_cols[0], qkv_cols[1])
    queries, keyvals = ([], [])
    for modality in range(2):
        projected = unmix_columns(qkv_rows[modality], seq_devices, batch_devices)
        qv_vector = qv_full[modality]
        queries.append(
            (projected[..., :model_width] + qv_vector[:model_width]).astype(jnp.bfloat16)
        )
        value_shift = jnp.concatenate(
            [jnp.zeros((model_width,), jnp.float32), qv_vector[model_width:]]
        )
        keyvals.append((projected[..., model_width:] + value_shift).astype(jnp.bfloat16))
    joined_query = jnp.concatenate(queries, axis=1)
    joined_keyval = jnp.concatenate(keyvals, axis=1)
    all_keyval = lax.all_gather(joined_keyval, "seq", axis=1, tiled=True)
    query_heads = joined_query.reshape(local_seqs, block_rows, HEADS, head_size)
    key_heads = all_keyval[..., :model_width].reshape(local_seqs, key_count, HEADS, head_size)
    value_heads = all_keyval[..., model_width:].reshape(local_seqs, key_count, HEADS, head_size)
    scores = (
        jnp.einsum("sqhe,skhe->shqk", query_heads, key_heads, preferred_element_type=jnp.float32)
        * factor
    )
    row_max = jnp.max(jnp.where(key_live, scores, FLOOR_SCORE), axis=-1, keepdims=True)
    exp_terms = jnp.exp(jnp.where(key_live, scores - row_max, FLOOR_SCORE))
    denominator = jnp.maximum(jnp.sum(exp_terms, axis=-1, keepdims=True), 1.0)
    prob_low = (exp_terms / denominator).astype(jnp.bfloat16)
    logsum = row_max + jnp.log(denominator)
    attended = jnp.einsum(
        "shqk,skhe->sqhe", prob_low, value_heads, preferred_element_type=jnp.float32
    )
    attended = attended.reshape(local_seqs, block_rows, model_width).astype(jnp.bfloat16)
    attended_all = gather_rows(attended[:, :image_count], attended[:, image_count:])
    out_cols = [
        jnp.einsum(
            "srd,df->srf",
            attended_all[modality],
            out_part[modality],
            preferred_element_type=jnp.float32,
        )
        for modality in range(2)
    ]
    out_rows = to_rows(out_cols[0], out_cols[1])
    projections, middles, second_norms = ([], [], [])
    for modality in range(2):
        pieces = modulation[modality]
        projection = (
            unmix_columns(out_rows[modality], seq_devices, batch_devices) + out_bias_full[modality]
        )
        middle = inputs[modality] + pieces[:, 2][:, None, :] * projection
        second_norms.append(modulate(middle, pieces[:, 3], pieces[:, 4]).astype(jnp.bfloat16))
        projections.append(projection)
        middles.append(middle)
    group_rows = gather_rows(second_norms[0], second_norms[1])
    hidden_pre, hidden_act, partials = ([], [], [])
    for modality in range(2):
        pre_values = jnp.einsum(
            "srd,df->srf",
            group_rows[modality],
            up_part[modality],
            preferred_element_type=jnp.float32,
        ) + up_bias_part[modality].astype(jnp.float32)
        act_values = gelu_tanh(pre_values).astype(jnp.bfloat16)
        partials.append(
            jnp.einsum(
                "srf,df->srd", act_values, down_part[modality], preferred_element_type=jnp.float32
            )
        )
        hidden_pre.append(pre_values)
        hidden_act.append(act_values)
    mlp_rows = sum_rows(partials[0], partials[1], seq_devices)
    mlp_outs, results = ([], [])
    for modality in range(2):
        pieces = modulation[modality]
        mlp_value = mlp_rows[modality] + down_bias_full[modality]
        results.append(
            (middles[modality] + pieces[:, 5][:, None, :] * mlp_value).astype(jnp.bfloat16)
        )
        mlp_outs.append(mlp_value)
    fetched_back = fetch_columns(
        up_weight,
        down_weight,
        mod_weight,
        qkv_weight,
        out_weight,
        up_bias,
        mod_bias,
        qv_bias,
        out_bias,
        down_bias,
    )
    up_back, down_back, mod_back, qkv_back, out_back = (
        fetched_back[0],
        fetched_back[1],
        fetched_back[2],
        fetched_back[3],
        fetched_back[4],
    )
    mod_bias_back = fetched_back[6]
    mlp_grads, gate_twos, down_bias_grads = ([], [], [])
    for modality in range(2):
        pieces = modulation[modality]
        mlp_grad = (pieces[:, 5][:, None, :] * cotangents[modality]).astype(jnp.bfloat16)
        gate_twos.append(jnp.sum(cotangents[modality] * mlp_outs[modality], axis=1))
        down_bias_grads.append(jnp.sum(mlp_grad.astype(jnp.float32), axis=(0, 1)))
        mlp_grads.append(mlp_grad)
    group_grads = gather_rows(mlp_grads[0], mlp_grads[1])
    down_grads, up_grads, up_bias_grads, norm_partials = ([], [], [], [])
    for modality in range(2):
        down_grads.append(
            jnp.einsum(
                "srd,srf->df",
                group_grads[modality],
                hidden_act[modality],
                preferred_element_type=jnp.float32,
            )
        )
        act_grad = jnp.einsum(
            "srd,df->srf",
            group_grads[modality],
            down_back[modality],
            preferred_element_type=jnp.float32,
        )
        pullback = jax.vjp(gelu_tanh, hidden_pre[modality])[1]
        pre_grad = pullback(act_grad)[0].astype(jnp.bfloat16)
        up_grads.append(
            jnp.einsum(
                "srd,srf->df", group_rows[modality], pre_grad, preferred_element_type=jnp.float32
            )
        )
        up_bias_grads.append(jnp.sum(pre_grad.astype(jnp.float32), axis=(0, 1)))
        norm_partials.append(
            jnp.einsum(
                "srf,df->srd", pre_grad, up_back[modality], preferred_element_type=jnp.float32
            )
        )
    norm_grads = sum_rows(norm_partials[0], norm_partials[1], seq_devices)
    middle_grads, shift_twos, scale_twos, gate_ones, out_bias_grads, proj_grads = (
        [],
        [],
        [],
        [],
        [],
        [],
    )
    for modality in range(2):
        pieces = modulation[modality]
        pullback = jax.vjp(modulate, middles[modality], pieces[:, 3], pieces[:, 4])[1]
        middle_part, shift_two, scale_two = pullback(norm_grads[modality])
        middle_grad = cotangents[modality] + middle_part
        proj_grad = (pieces[:, 2][:, None, :] * middle_grad).astype(jnp.bfloat16)
        gate_ones.append(jnp.sum(middle_grad * projections[modality], axis=1))
        out_bias_grads.append(jnp.sum(proj_grad.astype(jnp.float32), axis=(0, 1)))
        proj_grads.append(remix_columns(proj_grad, seq_devices, batch_devices))
        middle_grads.append(middle_grad)
        shift_twos.append(shift_two)
        scale_twos.append(scale_two)
    proj_cols = to_columns(proj_grads[0], proj_grads[1])
    out_grads, attended_partials = ([], [])
    for modality in range(2):
        out_grads.append(
            jnp.einsum(
                "srd,srf->df",
                attended_all[modality],
                proj_cols[modality],
                preferred_element_type=jnp.float32,
            )
        )
        attended_partials.append(
            jnp.einsum(
                "srf,df->srd",
                proj_cols[modality],
                out_back[modality],
                preferred_element_type=jnp.float32,
            )
        )
    attended_sums = sum_rows(attended_partials[0], attended_partials[1], seq_devices)
    attended_grad = jnp.concatenate([attended_sums[0], attended_sums[1]], axis=1).astype(
        jnp.bfloat16
    )
    grad_heads = attended_grad.reshape(local_seqs, block_rows, HEADS, head_size)
    scores_again = (
        jnp.einsum("sqhe,skhe->shqk", query_heads, key_heads, preferred_element_type=jnp.float32)
        * factor
    )
    probs_again = jnp.exp(jnp.where(key_live, scores_again - logsum, FLOOR_SCORE))
    probs_again_low = probs_again.astype(jnp.bfloat16)
    prob_grad = jnp.einsum(
        "sqhe,skhe->shqk", grad_heads, value_heads, preferred_element_type=jnp.float32
    )
    inner_sum = jnp.sum(probs_again * prob_grad, axis=-1, keepdims=True)
    score_grad = (probs_again * (prob_grad - inner_sum)).astype(jnp.bfloat16)
    query_grad = (
        jnp.einsum("shqk,skhe->sqhe", score_grad, key_heads, preferred_element_type=jnp.float32)
        * factor
    )
    query_grad = query_grad.reshape(local_seqs, block_rows, model_width).astype(jnp.bfloat16)
    key_grad = (
        jnp.einsum("shqk,sqhe->skhe", score_grad, query_heads, preferred_element_type=jnp.float32)
        * factor
    )
    value_grad = jnp.einsum(
        "shqk,sqhe->skhe", probs_again_low, grad_heads, preferred_element_type=jnp.float32
    )
    key_rows, value_rows = (
        lax.psum_scatter(
            key_grad.reshape(local_seqs, key_count, model_width),
            "seq",
            scatter_dimension=1,
            tiled=True,
        ),
        lax.psum_scatter(
            value_grad.reshape(local_seqs, key_count, model_width),
            "seq",
            scatter_dimension=1,
            tiled=True,
        ),
    )
    key_rows = key_rows.astype(jnp.bfloat16)
    value_rows = value_rows.astype(jnp.bfloat16)
    qv_bias_grads, joined_grads = ([], [])
    for modality in range(2):
        row_start, row_stop = row_spans[modality]
        query_part = query_grad[:, row_start:row_stop]
        value_part = value_rows[:, row_start:row_stop]
        joined_grad = jnp.concatenate(
            [query_part, key_rows[:, row_start:row_stop], value_part], axis=-1
        )
        qv_bias_grads.append(
            jnp.concatenate(
                [
                    jnp.sum(query_part.astype(jnp.float32), axis=(0, 1)),
                    jnp.sum(value_part.astype(jnp.float32), axis=(0, 1)),
                ]
            )
        )
        joined_grads.append(remix_columns(joined_grad, seq_devices, batch_devices))
    qkv_grad_cols = to_columns(joined_grads[0], joined_grads[1])
    qkv_grads, first_partials = ([], [])
    for modality in range(2):
        qkv_grads.append(
            jnp.einsum(
                "srd,srf->df",
                first_all[modality],
                qkv_grad_cols[modality],
                preferred_element_type=jnp.float32,
            )
        )
        first_partials.append(
            jnp.einsum(
                "srf,df->srd",
                qkv_grad_cols[modality],
                qkv_back[modality],
                preferred_element_type=jnp.float32,
            )
        )
    first_grads = sum_rows(first_partials[0], first_partials[1], seq_devices)
    input_grads, mod_partials = ([], [])
    for modality in range(2):
        pieces = modulation[modality]
        pullback = jax.vjp(modulate, inputs[modality], pieces[:, 0], pieces[:, 1])[1]
        input_part, shift_one, scale_one = pullback(first_grads[modality])
        input_grads.append(middle_grads[modality] + input_part)
        stacked = jnp.stack(
            [
                shift_one,
                scale_one,
                gate_ones[modality],
                shift_twos[modality],
                scale_twos[modality],
                gate_twos[modality],
            ],
            axis=1,
        )
        mod_partials.append(stacked.reshape(local_seqs, 6 * model_width))
    qv_mixed = remix_columns(jnp.stack(qv_bias_grads), seq_devices, batch_devices)
    out_bias_mixed = remix_columns(jnp.stack(out_bias_grads), seq_devices, batch_devices)
    down_bias_mixed = remix_columns(jnp.stack(down_bias_grads), seq_devices, batch_devices)
    mod_sum, qv_summed, out_bias_summed, down_bias_summed = lax.psum(
        (jnp.stack(mod_partials), qv_mixed, out_bias_mixed, down_bias_mixed), "seq"
    )
    mod_low = mod_sum.astype(jnp.bfloat16)
    mod_mixed = remix_columns(mod_low, seq_devices, batch_devices)
    columns = mod_part.shape[2]
    own_columns = lax.dynamic_slice_in_dim(mod_mixed, seq_index * columns, columns, 2)
    mod_grad = jnp.einsum("sd,tsf->tdf", smooth, own_columns, preferred_element_type=jnp.float32)
    mod_bias_grad = jnp.sum(own_columns.astype(jnp.float32), axis=1)
    mod_again = fetch_modulation(mod_back, mod_bias_back)[0]
    smooth_grad = jnp.einsum(
        "tsf,tdf->sd", mod_mixed, mod_again, preferred_element_type=jnp.float32
    )
    cond_pullback = jax.vjp(jax.nn.silu, cond_float)[1]
    cond_grad = cond_pullback(smooth_grad)[0]
    qv_own = own_block(qv_summed, seq_index, seq_devices)
    out_bias_own = own_block(out_bias_summed, seq_index, seq_devices)
    down_bias_own = own_block(down_bias_summed, seq_index, seq_devices)
    column_grads = (
        lax.psum_scatter(jnp.stack(up_grads), "batch", scatter_dimension=2, tiled=True),
        lax.psum_scatter(jnp.stack(down_grads), "batch", scatter_dimension=2, tiled=True),
        lax.psum_scatter(mod_grad, "batch", scatter_dimension=2, tiled=True),
        lax.psum_scatter(jnp.stack(qkv_grads), "batch", scatter_dimension=2, tiled=True),
        lax.psum_scatter(jnp.stack(out_grads), "batch", scatter_dimension=2, tiled=True),
        lax.psum_scatter(jnp.stack(up_bias_grads), "batch", scatter_dimension=1, tiled=True),
        lax.psum_scatter(mod_bias_grad, "batch", scatter_dimension=1, tiled=True),
        lax.psum_scatter(qv_own, "batch", scatter_dimension=1, tiled=True),
        lax.psum_scatter(out_bias_own, "batch", scatter_dimension=1, tiled=True),
        lax.psum_scatter(down_bias_own, "batch", scatter_dimension=1, tiled=True),
    )
    return (
        results[0],
        results[1],
        input_grads[0],
        input_grads[1],
        cond_grad,
        column_grads[2],
        column_grads[6],
        column_grads[3],
        column_grads[7],
        column_grads[4],
        column_grads[8],
        column_grads[0],
        column_grads[5],
        column_grads[1],
        column_grads[9],
    )


LOG2E = 1.4426950408889634
DEAD = -1e30
BF16 = jnp.bfloat16
F32 = jnp.float32


def dot_nt(a, b):
    return lax.dot_general(a, b, (((1,), (1,)), ((), ())), preferred_element_type=F32)


def dot_nn(a, b):
    return lax.dot_general(a, b, (((1,), (0,)), ((), ())), preferred_element_type=F32)


def dot_tn(a, b):
    return lax.dot_general(a, b, (((0,), (0,)), ((), ())), preferred_element_type=F32)


def attention_kernel(
    query_rows, scale, head, bias_ref, floor_ref, qi, qt, ki, kt, vi, vt, oi, ot, keys, values
):
    image_rows = qi.shape[0]
    keys[:image_rows] = ki[...]
    keys[image_rows:] = kt[...]
    values[:image_rows] = vi[...]
    values[image_rows:] = vt[...]
    bias = bias_ref[...]
    floor = floor_ref[0, 0]
    spans = [(qi, oi, start, query_rows) for start in range(0, image_rows, query_rows)]
    spans.append((qt, ot, 0, qt.shape[0]))
    for source, target, start, size in spans:
        sides = []
        for side in range(2):
            lanes = slice(side * head, (side + 1) * head)
            scores = dot_nt(source[start : start + size, lanes], keys[:, lanes]) * scale + bias
            row_max = jnp.maximum(jnp.max(scores, axis=1, keepdims=True), floor)
            exps = jnp.exp2(scores - row_max)
            total = jnp.maximum(jnp.sum(exps, axis=1, keepdims=True), 1.0)
            probs = (exps * (1.0 / total)).astype(BF16)
            sides.append(dot_nn(probs, values[:, lanes]))
        target[start : start + size, :] = jnp.concatenate(sides, axis=1).astype(BF16)


def pair_block(rows, lanes, pairs, part):
    return pl.BlockSpec((rows, lanes), lambda pair: (0, part * pairs + pair))


def attention(qkv_image, qkv_text, key_bias, floor, head):
    image_rows, width = qkv_image.shape
    text_rows = qkv_text.shape[0]
    rows = image_rows + text_rows
    lanes = 2 * head
    pairs = width // (3 * lanes)
    columns = [
        pair_block(count, lanes, pairs, part)
        for part in range(3)
        for count in (image_rows, text_rows)
    ]
    return pl.pallas_call(
        functools.partial(attention_kernel, 256, LOG2E / math.sqrt(head), head),
        grid=(pairs,),
        in_specs=[
            pl.BlockSpec((1, rows), lambda pair: (0, 0)),
            pl.BlockSpec(memory_space=pltpu.SMEM),
            *columns,
        ],
        out_specs=[columns[0], columns[1]],
        out_shape=[
            jax.ShapeDtypeStruct((image_rows, width // 3), BF16),
            jax.ShapeDtypeStruct((text_rows, width // 3), BF16),
        ],
        scratch_shapes=[pltpu.VMEM((rows, lanes), BF16), pltpu.VMEM((rows, lanes), BF16)],
        compiler_params=pltpu.CompilerParams(vmem_limit_bytes=48 << 20),
        cost_estimate=pl.CostEstimate(
            flops=1,
            bytes_accessed=1,
            transcendentals=0,
        ),
        name="attention",
    )(key_bias[None, :], floor, qkv_image, qkv_text, qkv_image, qkv_text, qkv_image, qkv_text)


def attention_back_kernel(
    query_rows, scale, factor, head, pairs,
    bias_ref, floor_ref, qi, qt, ki, kt, vi, vt, gi, gt, oi, ot, keys, values, key_sum, value_sum,
):
    pair = pl.program_id(0)
    image_rows = qi.shape[0]
    width = 2 * head
    keys[:image_rows] = ki[...]
    keys[image_rows:] = kt[...]
    values[:image_rows] = vi[...]
    values[image_rows:] = vt[...]
    key_sum[...] = jnp.zeros_like(key_sum)
    value_sum[...] = jnp.zeros_like(value_sum)
    bias = bias_ref[...]
    floor = floor_ref[0, 0]
    spans = [(qi, gi, oi, start, query_rows) for start in range(0, image_rows, query_rows)]
    spans.append((qt, gt, ot, 0, qt.shape[0]))
    query_lanes = pl.ds(pl.multiple_of(pair * width, width), width)
    key_lanes = pl.ds(pl.multiple_of((pairs + pair) * width, width), width)
    value_lanes = pl.ds(pl.multiple_of((2 * pairs + pair) * width, width), width)
    for source, grads, target, start, size in spans:
        wide_bias = jnp.concatenate([bias] * -(-size // 128), axis=1)[:, :size]
        dq, dk, dv = ([], [], [])
        for side in range(2):
            lanes = slice(side * head, (side + 1) * head)
            query = source[start : start + size, lanes]
            grad = grads[start : start + size, lanes]
            scores = dot_nt(keys[:, lanes], query) * scale + wide_bias
            top = jnp.maximum(jnp.max(scores, axis=0, keepdims=True), floor)
            exps = jnp.exp2(scores - top)
            total = jnp.maximum(jnp.sum(exps, axis=0, keepdims=True), 1.0)
            probs = exps * (1.0 / total)
            prob_grad = dot_nt(values[:, lanes], grad)
            weighted = probs * prob_grad
            inner = jnp.sum(weighted, axis=0, keepdims=True)
            score_grad = (weighted - probs * inner).astype(BF16)
            dv.append(dot_nn(probs.astype(BF16), grad))
            dk.append(dot_nn(score_grad, query))
            dq.append(dot_tn(score_grad, keys[:, lanes]))
        key_sum[...] += jnp.concatenate(dk, axis=1)
        value_sum[...] += jnp.concatenate(dv, axis=1)
        target[start : start + size, query_lanes] = (
            jnp.concatenate(dq, axis=1) * factor
        ).astype(BF16)
    oi[:, key_lanes] = (key_sum[:image_rows] * factor).astype(BF16)
    ot[:, key_lanes] = (key_sum[image_rows:] * factor).astype(BF16)
    oi[:, value_lanes] = value_sum[:image_rows].astype(BF16)
    ot[:, value_lanes] = value_sum[image_rows:].astype(BF16)


def attention_back(qkv_image, qkv_text, grad_image, grad_text, key_bias, floor, head):
    image_rows, width = qkv_image.shape
    text_rows = qkv_text.shape[0]
    rows = image_rows + text_rows
    lanes = 2 * head
    pairs = width // (3 * lanes)
    columns = [
        pair_block(count, lanes, pairs, part)
        for part in range(3)
        for count in (image_rows, text_rows)
    ]
    return pl.pallas_call(
        functools.partial(
            attention_back_kernel, 256, LOG2E / math.sqrt(head), 1.0 / math.sqrt(head), head, pairs
        ),
        grid=(pairs,),
        in_specs=[
            pl.BlockSpec((rows, 128), lambda pair: (0, 0)),
            pl.BlockSpec(memory_space=pltpu.SMEM),
            *columns,
            columns[0],
            columns[1],
        ],
        out_specs=[
            pl.BlockSpec((image_rows, width), lambda pair: (0, 0)),
            pl.BlockSpec((text_rows, width), lambda pair: (0, 0)),
        ],
        out_shape=[
            jax.ShapeDtypeStruct((image_rows, width), BF16),
            jax.ShapeDtypeStruct((text_rows, width), BF16),
        ],
        scratch_shapes=[
            pltpu.VMEM((rows, lanes), BF16),
            pltpu.VMEM((rows, lanes), BF16),
            pltpu.VMEM((rows, lanes), F32),
            pltpu.VMEM((rows, lanes), F32),
        ],
        compiler_params=pltpu.CompilerParams(vmem_limit_bytes=48 << 20),
        cost_estimate=pl.CostEstimate(
            flops=1,
            bytes_accessed=1,
            transcendentals=0,
        ),
        name="attention_back",
    )(
        jnp.broadcast_to(key_bias[:, None], (rows, 128)),
        floor,
        qkv_image, qkv_text, qkv_image, qkv_text, qkv_image, qkv_text,
        grad_image, grad_text,
    )


def flip(values, bit):
    return lax.ppermute(values, "seq", [(i, i ^ bit) for i in range(4)])


def gather_near(a, b):
    return (flip(a, 1), flip(b, 1), flip(a, 2), flip(b, 2))


def gather_far(a, b, near):
    return (a, b, *near, flip(near[0], 2), flip(near[3], 1))


def gather_halves(a, b):
    return gather_far(a, b, gather_near(a, b))


def add_low(a, b):
    return (a.astype(F32) + b.astype(F32)).astype(BF16)


def scatter_first(halves):
    return (flip(halves[6], 1), flip(halves[7], 2), flip(halves[2], 1), flip(halves[5], 2))


def scatter_last(halves, first):
    for_y, for_x, x_a, y_b = first
    x_b = flip(add_low(halves[3], for_x), 1)
    y_a = flip(add_low(halves[4], for_y), 2)
    return (halves[0], halves[1], x_a, x_b, y_a, y_b)


def scatter_halves(halves):
    return scatter_last(halves, scatter_first(halves))


ANYWHERE = pl.BlockSpec(memory_space=pl.ANY)
ON_CORE = pl.BlockSpec(memory_space=pltpu.VMEM)


class Copies:
    def __init__(self, semaphores):
        self.semaphores = semaphores
        self.count = 0
        self.open = []

    def start(self, source, target):
        copy = pltpu.make_async_copy(source, target, self.semaphores.at[self.count])
        self.count += 1
        copy.start()
        return copy

    def send(self, source, target):
        self.open.append(self.start(source, target))

    def finish(self):
        for copy in self.open:
            copy.wait()


def fetch_halves(copies, halves, rows, seq):
    width = rows.shape[2] // 2
    fetched = []
    for r in range(4):
        pair = []
        for side in range(2):
            half = halves[2 * r + side]
            half = half if seq is None else half.at[seq]
            pair.append(copies.start(half, rows.at[r, :, pl.ds(side * width, width)]))
        fetched.append(pair)
    return fetched


def send_halves(copies, rows, halves, r, seq):
    width = rows.shape[2] // 2
    for side in range(2):
        half = halves[2 * r + side]
        half = half if seq is None else half.at[seq]
        copies.send(rows.at[r, :, pl.ds(side * width, width)], half)


def normalize(values):
    mean = jnp.mean(values, axis=1, keepdims=True)
    centered = values - mean
    variance = jnp.mean(centered * centered, axis=1, keepdims=True)
    inverse = lax.rsqrt(variance + NORM_EPSILON)
    return centered * inverse, inverse


def normalize_back(norm, inverse, grad, scale):
    scaled = grad * (1.0 + scale)
    return inverse * (
        scaled
        - jnp.mean(scaled, axis=1, keepdims=True)
        - norm * jnp.mean(scaled * norm, axis=1, keepdims=True)
    )


def run(kernel, name, operands, specs, outs, out_specs, scratch, copies=0):
    if copies:
        scratch = [*scratch, pltpu.SemaphoreType.DMA((copies,))]
    return pl.pallas_call(
        kernel,
        in_specs=specs,
        out_specs=out_specs,
        out_shape=[jax.ShapeDtypeStruct(shape, dtype) for shape, dtype in outs],
        scratch_shapes=scratch,
        compiler_params=pltpu.CompilerParams(vmem_limit_bytes=56 << 20),
        cost_estimate=pl.CostEstimate(flops=1, bytes_accessed=1, transcendentals=0),
        name=name,
    )(*operands)


def project_kernel(seq, image_rows, *refs):
    halves, (weight, mods, bias) = (refs[:8], refs[8:11])
    qkv_i, qkv_t, norm_i, norm_t = refs[11:15]
    rows, held, image_norm, text_norm, image_out, text_out, semaphores = refs[15:]
    copies = Copies(semaphores)
    fetched = fetch_halves(copies, halves, rows, seq)
    weights = [copies.start(weight.at[t], held.at[t]) for t in range(2)]
    text_rows = rows.shape[1] - image_rows
    for r in range(4):
        for copy in fetched[r]:
            copy.wait()
        for t, norms, low, count in (
            (0, image_norm, 0, image_rows),
            (1, text_norm, image_rows, text_rows),
        ):
            norm, _ = normalize(rows[r, low : low + count, :].astype(F32))
            norm = norm * (1.0 + mods[t, seq, 1:2, :]) + mods[t, seq, 0:1, :]
            norms[r * count : (r + 1) * count, :] = norm.astype(BF16)
        if r == 0:
            weights[0].wait()
        span = pl.ds(r * image_rows, image_rows)
        product = dot_nt(image_norm[span, :], held[0]) + bias[0:1, :]
        image_out[span, :] = product.astype(BF16)
        copies.send(image_norm.at[span, :], norm_i.at[span, :])
        copies.send(image_out.at[span, :], qkv_i.at[span, :])
    weights[1].wait()
    text_out[...] = (dot_nt(text_norm[...], held[1]) + bias[1:2, :]).astype(BF16)
    copies.send(text_norm, norm_t)
    copies.send(text_out, qkv_t)
    copies.finish()


def project(halves, weight, mods, bias, seq, image_rows):
    block, width = halves[0].shape[-2:]
    D, W = 2 * width, weight.shape[1]
    image, text = 4 * image_rows, 4 * (block - image_rows)
    return run(
        functools.partial(project_kernel, seq, image_rows),
        "project",
        (*halves, weight, mods, bias),
        [ANYWHERE] * 9 + [ON_CORE] * 2,
        [((image, W), BF16), ((text, W), BF16), ((image, D), BF16), ((text, D), BF16)],
        [ANYWHERE] * 4,
        [
            pltpu.VMEM((4, block, D), BF16),
            pltpu.VMEM((2, W, D), BF16),
            pltpu.VMEM((image, D), BF16),
            pltpu.VMEM((text, D), BF16),
            pltpu.VMEM((image, W), BF16),
            pltpu.VMEM((text, W), BF16),
        ],
        20,
    )


def partial_kernel(seqs, dot, image_rows, *refs):
    inputs, weight, halves = (refs[: 2 * seqs], refs[2 * seqs], refs[2 * seqs + 1 : 2 * seqs + 9])
    lefts, held, rows, semaphores = (
        refs[2 * seqs + 9 : 4 * seqs + 9],
        refs[4 * seqs + 9],
        refs[4 * seqs + 10 : 5 * seqs + 10],
        refs[5 * seqs + 10],
    )
    copies = Copies(semaphores)
    weights = [copies.start(weight.at[t], held.at[t]) for t in (1, 0)]
    fetched = [
        [copies.start(inputs[2 * s + t], lefts[2 * s + t]) for t in (1, 0)] for s in range(seqs)
    ]
    text_rows = rows[0].shape[1] - image_rows
    for s in range(seqs):
        if s == 0:
            weights[0].wait()
        fetched[s][0].wait()
        text = dot(lefts[2 * s + 1][...], held[1]).astype(BF16)
        for r in range(4):
            rows[s][r, image_rows:, :] = text[r * text_rows : (r + 1) * text_rows]
        if s == 0:
            weights[1].wait()
        fetched[s][1].wait()
        for r in (3, 1, 2, 0):
            left = lefts[2 * s][r * image_rows : (r + 1) * image_rows, :]
            rows[s][r, :image_rows, :] = dot(left, held[0]).astype(BF16)
            send_halves(copies, rows[s], halves, r, s if seqs > 1 else None)
    copies.finish()


def partial_sums(inputs, weight, dot, D, image_rows):
    seqs = len(inputs)
    image, K = inputs[0][0].shape
    text = inputs[0][1].shape[0]
    block = (image + text) // 4
    shape = (block, D // 2) if seqs == 1 else (seqs, block, D // 2)
    return run(
        functools.partial(partial_kernel, seqs, dot, image_rows),
        "partial_sums",
        (*[value for pair in inputs for value in pair], weight),
        [ANYWHERE] * (2 * seqs + 1),
        [(shape, BF16)] * 8,
        [ANYWHERE] * 8,
        [pltpu.VMEM((count, K), BF16) for _ in range(seqs) for count in (image, text)]
        + [pltpu.VMEM(weight.shape, BF16)]
        + [pltpu.VMEM((4, block, D), BF16)] * seqs,
        2 + 2 * seqs + 8 * seqs,
    )


def six_sum(pieces, low, count):
    own_a, own_b, x_a, x_b, y_a, y_b = pieces

    def add(*parts):
        return sum(part[low : low + count, :].astype(F32) for part in parts)

    return jnp.concatenate([add(own_a, x_a, y_a), add(own_b, x_b, y_b)], axis=1)


def both_halves(halves, seq, low, count):
    return jnp.concatenate(
        [half[seq, low : low + count, :].astype(F32) for half in halves], axis=1
    )


def middle_kernel(seq, image_rows, *refs):
    pieces, tokens, (mods, bias) = (refs[:6], refs[6:8], refs[8:10])
    projection_ref, middle_ref, second_a, second_b = refs[10:]
    block, width = second_a.shape
    for t, low, count in ((0, 0, image_rows), (1, image_rows, block - image_rows)):
        span = slice(low, low + count)
        projection = six_sum(pieces, low, count) + bias[t : t + 1, :]
        middle = both_halves(tokens, seq, low, count) + mods[t, seq, 2:3, :] * projection
        norm, _ = normalize(middle)
        second = (norm * (1.0 + mods[t, seq, 4:5, :]) + mods[t, seq, 3:4, :]).astype(BF16)
        projection_ref[span, :] = projection
        middle_ref[span, :] = middle
        second_a[span, :] = second[:, :width]
        second_b[span, :] = second[:, width:]


def middle_step(pieces, tokens, mods, bias, seq, image_rows):
    block, width = pieces[0].shape
    return run(
        functools.partial(middle_kernel, seq, image_rows),
        "middle",
        (*pieces, *tokens, mods, bias),
        [ON_CORE] * 10,
        [((block, 2 * width), F32)] * 2 + [((block, width), BF16)] * 2,
        [ON_CORE] * 4,
        [],
    )


GELU_SCALE = math.sqrt(2.0 / math.pi)
GELU_CUBE = 0.044715


def hidden_kernel(seq, image_rows, *refs):
    halves, cotangents, (weight, bias, mods) = (refs[:8], refs[8:16], refs[16:19])
    outs = refs[19:27]
    act_i, act_t, slope_i, slope_t, grad_i, grad_t, second_i, second_t = outs
    rows, given, held, acts, slopes, grads, texts, semaphores = refs[27:]
    copies = Copies(semaphores)
    fetched = fetch_halves(copies, halves, rows, None)
    weights = [copies.start(weight.at[t], held.at[t]) for t in range(2)]
    other = fetch_halves(copies, cotangents, given, seq)
    text_rows = rows.shape[1] - image_rows
    second_text, grad_text, act_text, slope_text = texts

    def activate(pre):
        squared = pre * pre
        bent = jnp.tanh(GELU_SCALE * (pre + GELU_CUBE * pre * squared))
        rise = 0.5 * (1.0 + bent)
        slope = rise + (0.5 * GELU_SCALE) * pre * (1.0 - bent * bent) * (
            1.0 + (3.0 * GELU_CUBE) * squared
        )
        return (pre * rise).astype(BF16), slope.astype(BF16)

    for r in range(4):
        for copy in fetched[r]:
            copy.wait()
        if r == 0:
            weights[0].wait()
        span = pl.ds(r * image_rows, image_rows)
        text_span = slice(r * text_rows, (r + 1) * text_rows)
        pre = dot_nt(rows[r, :image_rows, :], held[0]) + bias[0:1, :]
        act, slope = activate(pre)
        acts[span, :] = act
        slopes[span, :] = slope
        second_text[text_span, :] = rows[r, image_rows:, :]
        for copy in other[r]:
            copy.wait()
        for t, target, place, low, count in (
            (0, grads, span, 0, image_rows),
            (1, grad_text, text_span, image_rows, text_rows),
        ):
            value = given[r, low : low + count, :].astype(F32) * mods[t, seq, 5:6, :]
            target[place, :] = value.astype(BF16)
        copies.send(acts.at[span, :], act_i.at[span, :])
        copies.send(slopes.at[span, :], slope_i.at[span, :])
        copies.send(grads.at[span, :], grad_i.at[span, :])
        copies.send(rows.at[r, pl.ds(0, image_rows), :], second_i.at[span, :])
    weights[1].wait()
    act_text[...], slope_text[...] = activate(
        dot_nt(second_text[...], held[1]) + bias[1:2, :]
    )
    for source, target in (
        (act_text, act_t),
        (slope_text, slope_t),
        (grad_text, grad_t),
        (second_text, second_t),
    ):
        copies.send(source, target)
    copies.finish()


def hidden_step(halves, cotangents, weight, bias, mods, seq, image_rows):
    block, width = halves[0].shape
    D, F = 2 * width, weight.shape[1]
    image, text = 4 * image_rows, 4 * (block - image_rows)

    def kernel(*refs):
        texts, semaphores = (refs[-5:-1], refs[-1])
        hidden_kernel(seq, image_rows, *refs[:-5], texts, semaphores)

    return run(
        kernel,
        "hidden",
        (*halves, *cotangents, weight, bias, mods),
        [ANYWHERE] * 17 + [ON_CORE] * 2,
        [((count, wide), BF16) for wide in (F, F, D, D) for count in (image, text)],
        [ANYWHERE] * 8,
        [
            pltpu.VMEM((4, block, D), BF16),
            pltpu.VMEM((4, block, D), BF16),
            pltpu.VMEM((2, F, D), BF16),
            pltpu.VMEM((image, F), BF16),
            pltpu.VMEM((image, F), BF16),
            pltpu.VMEM((image, D), BF16),
        ]
        + [pltpu.VMEM((text, wide), BF16) for wide in (D, D, F, F)],
        38,
    )


def outer_kernel(seqs, chunk, *refs):
    inputs, out = (refs[: 4 * seqs], refs[4 * seqs])
    held, result, semaphores = (refs[4 * seqs + 1 : -2], refs[-2], refs[-1])
    copies = Copies(semaphores)
    fetched = [copies.start(source, target) for source, target in zip(inputs, held)]
    columns = result.shape[1]
    for t in range(2):
        for s in range(seqs):
            fetched[4 * s + 2 * t].wait()
            fetched[4 * s + 2 * t + 1].wait()
        for low in range(0, columns, chunk):
            span = pl.ds(low, chunk)
            total = dot_tn(held[2 * t][:, span], held[2 * t + 1][...])
            for s in range(1, seqs):
                total = total + dot_tn(held[4 * s + 2 * t][:, span], held[4 * s + 2 * t + 1][...])
            result[t, span, :] = total.astype(BF16)
            copies.send(result.at[t, span, :], out.at[t, span, :])
    copies.finish()


def outer_sums(lefts, rights, chunk):
    seqs = len(lefts)
    columns, width = lefts[0][0].shape[1], rights[0][0].shape[1]
    operands = [side[s][t] for s in range(seqs) for t in range(2) for side in (lefts, rights)]
    return run(
        functools.partial(outer_kernel, seqs, chunk),
        "outer_sums",
        operands,
        [ANYWHERE] * (4 * seqs),
        [((2, columns, width), BF16)],
        [ANYWHERE],
        [pltpu.VMEM(value.shape, BF16) for value in operands]
        + [pltpu.VMEM((2, columns, width), BF16)],
        4 * seqs + 2 * (columns // chunk),
    )[0]


def hidden_back_kernel(image_rows, *refs):
    (grad_i, grad_t, slope_i, slope_t, down, up) = refs[:6]
    pre_i, pre_t, sums, halves = (refs[6], refs[7], refs[8], refs[9:17])
    grads, slopes, pres, grad_text, slope_text, pre_text, held_down, held_up, rows, semaphores = (
        refs[17:]
    )
    copies = Copies(semaphores)
    downs = [copies.start(down.at[t], held_down.at[t]) for t in (1, 0)]
    texts = [copies.start(grad_t, grad_text), copies.start(slope_t, slope_text)]
    images = [copies.start(grad_i, grads), copies.start(slope_i, slopes)]
    ups = [copies.start(up.at[t], held_up.at[t]) for t in (1, 0)]
    text_rows = rows.shape[1] - image_rows
    downs[0].wait()
    for copy in texts:
        copy.wait()
    product = dot_nt(grad_text[...], held_down[1]) * slope_text[...].astype(F32)
    pre_text[...] = product.astype(BF16)
    copies.send(pre_text, pre_t)
    sums[1:2, :] = jnp.sum(pre_text[...].astype(F32), axis=0, keepdims=True)
    ups[0].wait()
    back = dot_nn(pre_text[...], held_up[1]).astype(BF16)
    for r in range(4):
        rows[r, image_rows:, :] = back[r * text_rows : (r + 1) * text_rows]
    downs[1].wait()
    for copy in images:
        copy.wait()
    total = jnp.zeros((1, pres.shape[1]), F32)
    for r in (3, 1, 2, 0):
        span = pl.ds(r * image_rows, image_rows)
        product = dot_nt(grads[span, :], held_down[0]) * slopes[span, :].astype(F32)
        pres[span, :] = product.astype(BF16)
        copies.send(pres.at[span, :], pre_i.at[span, :])
        total = total + jnp.sum(pres[span, :].astype(F32), axis=0, keepdims=True)
        if r == 3:
            ups[1].wait()
        rows[r, :image_rows, :] = dot_nn(pres[span, :], held_up[0]).astype(BF16)
        send_halves(copies, rows, halves, r, None)
    sums[0:1, :] = total
    copies.finish()


def hidden_back(grads, slopes, down, up, image_rows):
    image, D = grads[0].shape
    text = grads[1].shape[0]
    F = up.shape[1]
    block = (image + text) // 4
    outs = run(
        functools.partial(hidden_back_kernel, image_rows),
        "hidden_back",
        (*grads, *slopes, down, up),
        [ANYWHERE] * 6,
        [((image, F), BF16), ((text, F), BF16), ((2, F), F32)] + [((block, D // 2), BF16)] * 8,
        [ANYWHERE] * 2 + [ON_CORE] + [ANYWHERE] * 8,
        [
            pltpu.VMEM((image, D), BF16),
            pltpu.VMEM((image, F), BF16),
            pltpu.VMEM((image, F), BF16),
            pltpu.VMEM((text, D), BF16),
            pltpu.VMEM((text, F), BF16),
            pltpu.VMEM((text, F), BF16),
            pltpu.VMEM((2, F, D), BF16),
            pltpu.VMEM((2, F, D), BF16),
            pltpu.VMEM((4, block, D), BF16),
        ],
        8 + 1 + 4 + 8,
    )
    return outs[0:2], outs[2], outs[3:]


def middle_back_kernel(seq, image_rows, *refs):
    pieces, cotangents, (middle_ref, projection_ref, mods) = (refs[:6], refs[6:8], refs[8:11])
    grad_ref, low_a, low_b, sums = refs[11:]
    block, width = low_a.shape
    for t, low, count in ((0, 0, image_rows), (1, image_rows, block - image_rows)):
        span = slice(low, low + count)
        norm_grad = six_sum(pieces, low, count)
        norm, inverse = normalize(middle_ref[span, :])
        grad = both_halves(cotangents, seq, low, count) + normalize_back(
            norm, inverse, norm_grad, mods[t, seq, 4:5, :]
        )
        rounded = (mods[t, seq, 2:3, :] * grad).astype(BF16)
        grad_ref[span, :] = grad
        low_a[span, :] = rounded[:, :width]
        low_b[span, :] = rounded[:, width:]
        for k, value in enumerate(
            (norm_grad, norm_grad * norm, grad * projection_ref[span, :], rounded.astype(F32))
        ):
            sums[4 * t + k : 4 * t + k + 1, :] = jnp.sum(value, axis=0, keepdims=True)


def middle_back(pieces, cotangents, middle, projection, mods, seq, image_rows):
    block, width = pieces[0].shape
    return run(
        functools.partial(middle_back_kernel, seq, image_rows),
        "middle_back",
        (*pieces, *cotangents, middle, projection, mods),
        [ON_CORE] * 11,
        [((block, 2 * width), F32)] + [((block, width), BF16)] * 2 + [((8, 2 * width), F32)],
        [ON_CORE] * 4,
        [],
    )


def attended_back_kernel(image_rows, *refs):
    halves, weight = (refs[:8], refs[8])
    grad_i, grad_t, proj_i, proj_t = refs[9:13]
    rows, held, image_out, text_in, text_out, semaphores = refs[13:]
    copies = Copies(semaphores)
    fetched = fetch_halves(copies, halves, rows, None)
    weights = [copies.start(weight.at[t], held.at[t]) for t in range(2)]
    text_rows = rows.shape[1] - image_rows
    for r in range(4):
        for copy in fetched[r]:
            copy.wait()
        if r == 0:
            weights[0].wait()
        span = pl.ds(r * image_rows, image_rows)
        text_in[r * text_rows : (r + 1) * text_rows, :] = rows[r, image_rows:, :]
        copies.send(rows.at[r, pl.ds(0, image_rows), :], proj_i.at[span, :])
        image_out[span, :] = dot_nn(rows[r, :image_rows, :], held[0]).astype(BF16)
    copies.send(image_out, grad_i)
    copies.send(text_in, proj_t)
    weights[1].wait()
    text_out[...] = dot_nn(text_in[...], held[1]).astype(BF16)
    copies.send(text_out, grad_t)
    copies.finish()


def attended_back(halves, weight, image_rows):
    block, width = halves[0].shape
    D, E = 2 * width, weight.shape[2]
    image, text = 4 * image_rows, 4 * (block - image_rows)
    outs = run(
        functools.partial(attended_back_kernel, image_rows),
        "attended_back",
        (*halves, weight),
        [ANYWHERE] * 9,
        [((image, E), BF16), ((text, E), BF16), ((image, D), BF16), ((text, D), BF16)],
        [ANYWHERE] * 4,
        [
            pltpu.VMEM((4, block, D), BF16),
            pltpu.VMEM(weight.shape, BF16),
            pltpu.VMEM((image, E), BF16),
            pltpu.VMEM((text, D), BF16),
            pltpu.VMEM((text, E), BF16),
        ],
        10 + 7,
    )
    return outs[:2], outs[2:]


def project_back_kernel(seq, image_rows, *refs):
    (grad_i, grad_t, weight), tokens = (refs[:3], refs[3:11])
    sums, column_sums, halves = (refs[11], refs[12], refs[13:21])
    grads, grad_text, held, given, rows, semaphores = refs[21:]
    copies = Copies(semaphores)
    weights = [copies.start(weight.at[t], held.at[t]) for t in (1, 0)]
    text_in = copies.start(grad_t, grad_text)
    image_in = copies.start(grad_i, grads)
    fetched = fetch_halves(copies, tokens, given, seq)
    text_rows = rows.shape[1] - image_rows
    weights[0].wait()
    text_in.wait()
    text = dot_nn(grad_text[...], held[1])
    column_sums[1:2, :] = jnp.sum(grad_text[...].astype(F32), axis=0, keepdims=True)
    weights[1].wait()
    image_in.wait()
    totals = [jnp.zeros((1, rows.shape[2]), F32) for _ in range(4)]
    columns = jnp.zeros((1, grads.shape[1]), F32)
    for r in (3, 1, 2, 0):
        for copy in fetched[r]:
            copy.wait()
        span = pl.ds(r * image_rows, image_rows)
        for t, low, count in ((0, 0, image_rows), (1, image_rows, text_rows)):
            if t == 0:
                back = dot_nn(grads[span, :], held[0])
                columns = columns + jnp.sum(grads[span, :].astype(F32), axis=0, keepdims=True)
            else:
                back = text[r * text_rows : (r + 1) * text_rows, :]
            norm, _ = normalize(given[r, low : low + count, :].astype(F32))
            totals[2 * t] = totals[2 * t] + jnp.sum(back, axis=0, keepdims=True)
            totals[2 * t + 1] = totals[2 * t + 1] + jnp.sum(back * norm, axis=0, keepdims=True)
            rows[r, low : low + count, :] = back.astype(BF16)
        send_halves(copies, rows, halves, r, None)
    column_sums[0:1, :] = columns
    for k in range(4):
        sums[k : k + 1, :] = totals[k]
    copies.finish()


def project_back(grads, weight, tokens, seq, image_rows):
    image, W = grads[0].shape
    text = grads[1].shape[0]
    D = weight.shape[2]
    block = (image + text) // 4
    outs = run(
        functools.partial(project_back_kernel, seq, image_rows),
        "project_back",
        (*grads, weight, *tokens),
        [ANYWHERE] * 11,
        [((4, D), F32), ((2, W), F32)] + [((block, D // 2), BF16)] * 8,
        [ON_CORE] * 2 + [ANYWHERE] * 8,
        [
            pltpu.VMEM((image, W), BF16),
            pltpu.VMEM((text, W), BF16),
            pltpu.VMEM(weight.shape, BF16),
            pltpu.VMEM((4, block, D), BF16),
            pltpu.VMEM((4, block, D), BF16),
        ],
        4 + 8 + 8,
    )
    return outs[0], outs[1], outs[2:]


def result_kernel(image_rows, *refs):
    pieces, cotangents, middles = (refs[:6], refs[6:8], refs[8:10])
    mods, bias, image_out, text_out, sums = refs[10:]
    block = middles[0].shape[0]
    for seq in range(2):
        for t, low, count in ((0, 0, image_rows), (1, image_rows, block - image_rows)):
            span = slice(low, low + count)
            value = six_sum([piece.at[seq] for piece in pieces], low, count) + bias[t : t + 1, :]
            gate = mods[t, seq, 5:6, :]
            out = (middles[seq][span, :] + gate * value).astype(BF16)
            if t == 0:
                image_out[seq] = out
            else:
                text_out[seq] = out
            grad = both_halves(cotangents, seq, low, count)
            low_grad = (gate * grad).astype(BF16).astype(F32)
            at = 4 * seq + 2 * t
            sums[at : at + 1, :] = jnp.sum(grad * value, axis=0, keepdims=True)
            sums[at + 1 : at + 2, :] = jnp.sum(low_grad, axis=0, keepdims=True)


def result_step(pieces, cotangents, middles, mods, bias, image_rows):
    seqs, block, width = pieces[0].shape
    return run(
        functools.partial(result_kernel, image_rows),
        "result",
        (*pieces, *cotangents, *middles, mods, bias),
        [ON_CORE] * 12,
        [
            ((seqs, image_rows, 2 * width), BF16),
            ((seqs, block - image_rows, 2 * width), BF16),
            ((8, 2 * width), F32),
        ],
        [ON_CORE] * 3,
        [],
    )


def input_back_kernel(image_rows, live_text, *refs):
    pieces, tokens, grads, mods = (refs[:12], refs[12:14], refs[14:16], refs[16])
    image_out, text_out = refs[17:]
    block = grads[0].shape[0]
    for seq in range(2):
        for t, low, count in ((0, 0, image_rows), (1, image_rows, block - image_rows)):
            norm_grad = six_sum(pieces[6 * seq : 6 * seq + 6], low, count)
            norm, inverse = normalize(both_halves(tokens, seq, low, count))
            out = grads[seq][low : low + count, :] + normalize_back(
                norm, inverse, norm_grad, mods[t, seq, 1:2, :]
            )
            if t == 0:
                image_out[seq] = out
            else:
                text_out[seq] = out[:live_text]


def input_back(pieces, tokens, grads, mods, image_rows, live_text):
    block, width = pieces[0][0].shape
    return run(
        functools.partial(input_back_kernel, image_rows, live_text),
        "input_back",
        (*pieces[0], *pieces[1], *tokens, *grads, mods),
        [ON_CORE] * 17,
        [((2, image_rows, 2 * width), F32), ((2, live_text, 2 * width), F32)],
        [ON_CORE] * 2,
        [],
    )


def match_units(batch_devices, seq_devices, per_device, group_units):
    devices = batch_devices * seq_devices
    total = devices * per_device
    part_units = total // 3
    sources, targets = ([], [])
    for seq_at in range(seq_devices):
        listed = [
            part * part_units + seq_at * group_units + k
            for part in range(3)
            for k in range(group_units)
        ]
        for place, unit in enumerate(listed):
            sources.append((unit // per_device, unit % per_device))
            targets.append(
                ((place // per_device) * seq_devices + seq_at, place % per_device)
            )
    edges = list(zip(sources, targets))
    rounds = []
    left = list(range(total))
    for _ in range(per_device):
        by_source = {}
        for e in left:
            by_source.setdefault(edges[e][0][0], []).append(e)
        taken = {}

        def place_edge(device, seen):
            for e in by_source[device]:
                target = edges[e][1][0]
                if target in seen:
                    continue
                seen.add(target)
                if target not in taken or place_edge(edges[taken[target]][0][0], seen):
                    taken[target] = e
                    return True
            return False

        for device in range(devices):
            place_edge(device, set())
        chosen = sorted(taken.values())
        rounds.append(chosen)
        left = [e for e in left if e not in chosen]
    send = np.zeros((per_device, devices), np.int32)
    land = np.zeros((per_device, devices), np.int32)
    perms = []
    for k, chosen in enumerate(rounds):
        pairs = []
        for e in chosen:
            (source, source_slot), (target, target_slot) = edges[e]
            pairs.append((source, target))
            send[k, source] = source_slot
            land[k, target] = target_slot
        perms.append(sorted(pairs))
    return perms, send, land


def move_units(units, perms, take, put, place):
    arrived = jnp.zeros_like(units)
    for k, pairs in enumerate(perms):
        slot = jnp.asarray(take[k])[place]
        moved = lax.ppermute(
            lax.dynamic_index_in_dim(units, slot, 0, keepdims=True), ("batch", "seq"), pairs
        )
        arrived = lax.dynamic_update_slice_in_dim(arrived, moved, jnp.asarray(put[k])[place], 0)
    return arrived


def gather_rows_over_batch(values):
    return lax.all_gather(values, "batch", axis=1, tiled=True)


def gather_small(values, axis):
    count = lax.axis_size(axis)
    held = values[None]
    bit = 1
    while bit < count:
        pairs = [(i, i ^ bit) for i in range(count)]
        held = jnp.concatenate([held, lax.ppermute(held, axis, pairs)])
        bit *= 2
    return jnp.take(held, jnp.bitwise_xor(lax.axis_index(axis), jnp.arange(count)), axis=0)


def after(values, *others):
    return lax.optimization_barrier((values, others))[0]


def scatter_rows_over_batch(values):
    dimension = values.ndim - 2
    return lax.psum_scatter(values, "batch", scatter_dimension=dimension, tiled=True)


def swap(values, axis):
    return lax.all_to_all(values, axis, 0, 0, tiled=True)


def swift_layer(
    image_tokens,
    text_tokens,
    conditioning,
    key_mask,
    mod_weight,
    mod_bias,
    qkv_weight,
    qv_bias,
    out_weight,
    out_bias,
    up_weight,
    up_bias,
    down_weight,
    down_bias,
    image_cotangent,
    text_cotangent,
):
    S = lax.axis_size("seq")
    B = lax.axis_size("batch")
    seq_index = lax.axis_index("seq")
    place = lax.axis_index(("batch", "seq"))
    L, image_count, D = image_tokens.shape
    live_text = text_tokens.shape[1]
    text_count = -(-live_text // 16) * 16
    pad = ((0, 0), (0, text_count - live_text), (0, 0))
    head = D // HEADS
    own_width = D // S
    half = D // 2

    unit = math.gcd(qkv_weight.shape[2], own_width)
    per_device = qkv_weight.shape[2] // unit
    perms, send, land = match_units(B, S, per_device, own_width // unit)
    back_perms = [[(target, source) for source, target in pairs] for pairs in perms]
    qkv_units = jnp.swapaxes(qkv_weight, 1, 2).reshape(2, per_device, unit, D).swapaxes(0, 1)
    qkv_mine = move_units(qkv_units, perms, send, land, place).swapaxes(0, 1)
    out_units = jnp.swapaxes(out_weight, 1, 2).reshape(2, -1, S, own_width).transpose(2, 0, 1, 3)
    out_mine = swap(after(out_units, qkv_mine), "seq")
    out_columns = out_mine.shape[2]
    qkv_width = per_device * unit
    qkv_part = gather_rows_over_batch(qkv_mine.reshape(2, qkv_width, D))
    out_rows = out_mine.transpose(1, 0, 2, 3).reshape(2, S * out_columns, own_width)
    out_part = gather_rows_over_batch(out_rows)
    hidden_columns = up_weight.shape[2]

    padded = jnp.concatenate([image_tokens, jnp.pad(text_tokens, pad)], axis=1)
    tokens = after((padded[..., :half], padded[..., half:]), qkv_mine)
    tokens_near = gather_near(*tokens)

    bias_widths = [array.shape[1] for array in (qv_bias, out_bias, up_bias, down_bias)]
    bias_ends = np.cumsum(bias_widths)
    own_biases = jnp.concatenate([qv_bias, out_bias, up_bias, down_bias], axis=1)
    near = gather_small(jnp.concatenate([conditioning, own_biases], axis=1), "batch")
    cond_all = near[:, :, :D].reshape(B * L, D)
    column_biases = near[:, :, D:].astype(F32)
    smooth_all = jax.nn.silu(cond_all.astype(F32)).astype(BF16)
    mod_own = (
        jnp.einsum("sd,tdf->tsf", smooth_all, mod_weight, preferred_element_type=F32)
        + mod_bias.astype(F32)[:, None, :]
    )
    mod_width = mod_own.shape[2]
    mod_sent = mod_own.reshape(2, B, L, mod_width).transpose(1, 0, 2, 3)
    mod_came = swap(mod_sent, "batch")
    small = jnp.concatenate(
        [mod_came.reshape(B, 2 * L * mod_width), column_biases.reshape(B, -1)], axis=1
    )
    small_all = gather_small(after(small, tokens_near), "seq")
    modulation = (
        small_all[:, :, : 2 * L * mod_width]
        .reshape(S, B, 2, L, mod_width)
        .transpose(2, 3, 1, 0, 4)
        .reshape(2, L, 6, D)
    )
    bias_all = (
        small_all[:, :, 2 * L * mod_width :].reshape(S, B, 2, -1).transpose(2, 1, 0, 3)
    )
    qv_full = bias_all[..., : bias_ends[0]].reshape(2, 2 * D)
    out_bias_full = bias_all[..., bias_ends[0] : bias_ends[1]].reshape(2, D)
    down_bias_full = bias_all[..., bias_ends[2] :].reshape(2, D)
    up_bias_part = (
        column_biases[:, :, bias_ends[1] : bias_ends[2]].transpose(1, 0, 2).reshape(2, -1)
    )
    first_feature = seq_index * own_width
    qkv_bias = jnp.concatenate(
        [
            lax.dynamic_slice_in_dim(qv_full, first_feature, own_width, 1),
            jnp.zeros((2, own_width), F32),
            lax.dynamic_slice_in_dim(qv_full, D + first_feature, own_width, 1),
        ],
        axis=1,
    )

    tokens_all = gather_far(*tokens, after(tokens_near, small_all))
    padded = jnp.concatenate([image_cotangent, jnp.pad(text_cotangent, pad)], axis=1)
    cotangents = (padded[..., :half], padded[..., half:])
    near_grads = gather_near(*after(cotangents, tokens_all))
    up_part = gather_rows_over_batch(after(jnp.swapaxes(up_weight, 1, 2), tokens_all))

    order = jnp.bitwise_xor(seq_index, jnp.arange(S))
    image_keys = jnp.take(
        key_mask[:, : S * image_count].reshape(L, S, image_count), order, axis=1
    )
    text_keys = jnp.take(
        key_mask[:, S * image_count :].reshape(L, S, live_text), order, axis=1
    )
    text_keys = jnp.pad(text_keys, ((0, 0), (0, 0), (0, text_count - live_text)))
    live = jnp.concatenate([image_keys.reshape(L, -1), text_keys.reshape(L, -1)], axis=1) > 0
    key_bias = jnp.where(live, 0.0, DEAD).astype(F32)
    floors = jnp.where(jnp.all(key_mask > 0, axis=1), -3e38, FLOOR_SCORE * LOG2E).astype(F32)
    floors = floors.reshape(L, 1, 1)

    kept = []
    first = project(tokens_all, qkv_part, modulation, qkv_bias, 0, image_count)
    attended = attention(first[0], first[1], key_bias[0], floors[0], head)
    down_part = gather_rows_over_batch(after(jnp.swapaxes(down_weight, 1, 2), attended))
    parts = partial_sums([attended], out_part, dot_nt, D, image_count)
    kept.append((first, attended, parts))
    again = after(tokens_all, parts, near_grads)
    first = project(again, qkv_part, modulation, qkv_bias, 1, image_count)
    attended = attention(first[0], first[1], key_bias[1], floors[1], head)
    cotangents_all = gather_far(*cotangents, near_grads)
    attended = after(attended, cotangents_all)
    parts = partial_sums([attended], out_part, dot_nt, D, image_count)
    kept.append((first, attended, parts))
    firsts, attendeds, out_halves = zip(*kept)
    steps, seconds = ([], [])
    for s in range(L):
        steps.append(
            middle_step(
                scatter_halves(out_halves[s]), tokens, modulation, out_bias_full, s, image_count
            )
        )
        seconds.append(gather_halves(*steps[s][2:]))
    hidden = []
    for s in range(L):
        halves = after(seconds[s], hidden[-1]) if s else seconds[s]
        hidden.append(
            hidden_step(
                halves, cotangents_all, up_part, up_bias_part, modulation, s, image_count
            )
        )
    acts, slopes, grads, norms = [[step[i : i + 2] for step in hidden] for i in (0, 2, 4, 6)]

    down_sum = outer_sums(acts, grads, 256)
    down_came = scatter_rows_over_batch(down_sum)
    pres, bias_sums, norm2_halves = ([], [], [])
    gate = down_sum
    for s in range(L):
        pre, sums, halves = hidden_back(
            after(grads[s], gate), slopes[s], down_part, up_part, image_count
        )
        gate = halves
        pres.append(pre)
        bias_sums.append(sums)
        norm2_halves.append(halves)
    up_bias_sum = sum(bias_sums)
    norm2_pieces = [scatter_halves(halves) for halves in norm2_halves]
    up_sum = outer_sums(after(pres, gate), norms, 256)

    backs, projs = ([], [])
    backs.append(
        middle_back(
            after(norm2_pieces[0], up_sum), cotangents, *steps[0][1::-1], modulation, 0, image_count
        )
    )
    projs.append(gather_halves(*backs[0][1:3]))
    mlp_halves = partial_sums(after(acts, backs[0]), down_part, dot_nn, D, image_count)
    backs.append(
        middle_back(
            after(norm2_pieces[1], mlp_halves),
            cotangents,
            *steps[1][1::-1],
            modulation,
            1,
            image_count,
        )
    )
    projs.append(gather_halves(*backs[1][1:3]))
    grad0, proj0 = attended_back(after(projs[0], backs[1]), out_part, image_count)
    up_came = scatter_rows_over_batch(after(up_sum, down_came, grad0))
    qkv_grad0 = attention_back(*firsts[0][:2], *grad0, key_bias[0], floors[0], head)
    grad1, proj1 = attended_back(after(projs[1], qkv_grad0), out_part, image_count)
    mlp_first = scatter_first(after(mlp_halves, proj1))
    out_sum = outer_sums([proj0, proj1], attendeds, 256)
    sums0, columns0, halves0 = project_back(
        after(qkv_grad0, out_sum), qkv_part, tokens_all, 0, image_count
    )
    out_came = scatter_rows_over_batch(after(out_sum, up_came, halves0))
    norm1_first = scatter_first(halves0)
    grad1 = after(grad1, halves0, mlp_first)
    qkv_grad1 = attention_back(*firsts[1][:2], *grad1, key_bias[1], floors[1], head)
    mlp_pieces = scatter_last(mlp_halves, mlp_first)
    qkv_grad1 = after(qkv_grad1, mlp_pieces)
    qkv_sum = outer_sums(
        [qkv_grad0, qkv_grad1], [first[2:] for first in firsts], 128 if qkv_width % 256 else 256
    )
    qkv_came = scatter_rows_over_batch(after(qkv_sum, out_came))
    sums1, columns1, halves1 = project_back(
        after(qkv_grad1, qkv_sum), qkv_part, tokens_all, 1, image_count
    )
    norm1_pieces = [scatter_last(halves0, norm1_first), scatter_halves(halves1)]
    image_out, text_out, result_sums = result_step(
        after(mlp_pieces, halves1),
        cotangents,
        [step[1] for step in steps],
        modulation,
        down_bias_full,
        image_count,
    )
    qkv_home = move_units(
        qkv_came.reshape(2, per_device, unit, D).swapaxes(0, 1), back_perms, land, send, place
    )
    out_home = swap(out_came.reshape(2, S, out_columns, own_width).swapaxes(0, 1), "seq")
    qkv_weight_grad = qkv_home.swapaxes(0, 1).reshape(2, -1, D).swapaxes(1, 2).astype(F32)
    out_weight_grad = (
        out_home.transpose(1, 2, 0, 3).reshape(2, out_columns, D).swapaxes(1, 2).astype(F32)
    )
    up_weight_grad = up_came.swapaxes(1, 2).astype(F32)
    down_weight_grad = down_came.swapaxes(1, 2).astype(F32)
    image_grad, text_grad = input_back(
        norm1_pieces, tokens, [back[0] for back in backs], modulation, image_count, live_text
    )

    first_sums = jnp.stack([sums0, sums1]).reshape(L, 2, 2, D)
    second_sums = jnp.stack([back[3] for back in backs]).reshape(L, 2, 4, D)
    result_sums = result_sums.reshape(L, 2, 2, D)
    mod_rows = jnp.concatenate(
        [
            first_sums,
            second_sums[:, :, 2:3],
            second_sums[:, :, :2],
            result_sums[:, :, :1],
        ],
        axis=2,
    ).swapaxes(0, 1)
    mod_rows = mod_rows.reshape(2, L, B, S, mod_width).transpose(3, 2, 0, 1, 4)
    out_bias_sum = jnp.sum(second_sums[:, :, 3], axis=0)
    down_bias_sum = jnp.sum(result_sums[:, :, 1], axis=0)
    column_sums = columns0 + columns1
    qv_bias_sum = jnp.zeros((2, 2 * D), F32)
    for part, column in ((0, 0), (1, 2 * own_width)):
        qv_bias_sum = lax.dynamic_update_slice_in_dim(
            qv_bias_sum, column_sums[:, column : column + own_width], part * D + first_feature, 1
        )
    up_bias_rows = lax.dynamic_update_slice_in_dim(
        jnp.zeros((2, B, S, hidden_columns), F32),
        up_bias_sum.reshape(2, B, 1, hidden_columns),
        seq_index,
        2,
    )
    bias_rows = jnp.concatenate(
        [
            qv_bias_sum.reshape(2, B, S, -1),
            out_bias_sum.reshape(2, B, S, -1),
            up_bias_rows,
            down_bias_sum.reshape(2, B, S, -1),
        ],
        axis=3,
    ).transpose(2, 1, 0, 3)
    packed = jnp.concatenate(
        [mod_rows.reshape(S, B, -1), bias_rows.reshape(S, B, -1)], axis=2
    )
    packed = jnp.sum(swap(packed, "seq"), axis=0)
    packed = swap(packed, "batch")
    mod_mine = (
        packed[:, : 2 * L * mod_width]
        .reshape(B, 2, L, mod_width)
        .transpose(1, 0, 2, 3)
        .reshape(2, B * L, mod_width)
        .astype(BF16)
    )
    bias_mine = jnp.sum(packed[:, 2 * L * mod_width :], axis=0).reshape(2, -1)
    qv_bias_grad, out_bias_grad, up_bias_grad, down_bias_grad = jnp.split(
        bias_mine, bias_ends[:3], axis=1
    )
    mod_weight_grad = jnp.einsum(
        "sd,tsf->tdf", smooth_all, mod_mine, preferred_element_type=F32
    )
    mod_bias_grad = jnp.sum(mod_mine.astype(F32), axis=1)
    smooth_part = jnp.einsum("tsf,tdf->sd", mod_mine, mod_weight, preferred_element_type=F32)
    smooth_grad = jnp.sum(swap(smooth_part.reshape(B, L, D), "batch"), axis=0)
    smooth_grad = smooth_grad + flip(smooth_grad, 1)
    smooth_grad = smooth_grad + flip(smooth_grad, 2)
    cond_grad = jax.vjp(jax.nn.silu, conditioning.astype(F32))[1](smooth_grad)[0]
    return (
        image_out,
        text_out[:, :live_text],
        image_grad,
        text_grad,
        cond_grad,
        mod_weight_grad,
        mod_bias_grad,
        qkv_weight_grad,
        qv_bias_grad,
        out_weight_grad,
        out_bias_grad,
        up_weight_grad,
        up_bias_grad,
        down_weight_grad,
        down_bias_grad,
    )


def choose_layer(mesh):
    if mesh.shape["seq"] == 4 and HEADS % 8 == 0:
        return swift_layer
    return general_layer


def solution(mesh):
    layer = choose_layer(mesh)
    return jax.shard_map(
        layer,
        mesh=mesh,
        in_specs=(
            P("batch", "seq", None),
            P("batch", "seq", None),
            P("batch", None),
            P("batch", None),
            P(None, None, ("batch", "seq")),
            P(None, ("batch", "seq")),
            P(None, None, ("batch", "seq")),
            P(None, ("batch", "seq")),
            P(None, None, ("batch", "seq")),
            P(None, ("batch", "seq")),
            P(None, None, ("batch", "seq")),
            P(None, ("batch", "seq")),
            P(None, None, ("batch", "seq")),
            P(None, ("batch", "seq")),
            P("batch", "seq", None),
            P("batch", "seq", None),
        ),
        out_specs=(
            P("batch", "seq", None),
            P("batch", "seq", None),
            P("batch", "seq", None),
            P("batch", "seq", None),
            P("batch", None),
            P(None, None, ("batch", "seq")),
            P(None, ("batch", "seq")),
            P(None, None, ("batch", "seq")),
            P(None, ("batch", "seq")),
            P(None, None, ("batch", "seq")),
            P(None, ("batch", "seq")),
            P(None, None, ("batch", "seq")),
            P(None, ("batch", "seq")),
            P(None, None, ("batch", "seq")),
            P(None, ("batch", "seq")),
        ),
        check_vma=False,
    )
```

```python
import functools
import math

import jax
import jax.numpy as jnp
import numpy as np
from jax import lax
from jax.experimental import pallas as pl
from jax.experimental.pallas import tpu as pltpu
from jax.sharding import PartitionSpec as P

HEADS = 24


NORM_EPSILON = 1e-06
FLOOR_SCORE = -10000.0


def modulate(tokens, shift_vec, scale_vec):
    row_mean = jnp.mean(tokens, axis=-1, keepdims=True)
    centered = tokens - row_mean
    row_var = jnp.mean(centered * centered, axis=-1, keepdims=True)
    return (
        centered * lax.rsqrt(row_var + NORM_EPSILON) * (1.0 + scale_vec[:, None, :])
        + shift_vec[:, None, :]
    )


def gelu_tanh(values):
    return jax.nn.gelu(values, approximate=True)


def unmix_columns(values, seq_devices, batch_devices):
    array_shape = values.shape
    piece_width = array_shape[-1] // (seq_devices * batch_devices)
    grid_view = values.reshape(array_shape[:-1] + (seq_devices, batch_devices, piece_width))
    return jnp.swapaxes(grid_view, -3, -2).reshape(array_shape)


def remix_columns(values, seq_devices, batch_devices):
    array_shape = values.shape
    piece_width = array_shape[-1] // (seq_devices * batch_devices)
    grid_view = values.reshape(array_shape[:-1] + (batch_devices, seq_devices, piece_width))
    return jnp.swapaxes(grid_view, -3, -2).reshape(array_shape)


def fetch_columns(
    up_weight,
    down_weight,
    mod_weight,
    qkv_weight,
    out_weight,
    up_bias,
    mod_bias,
    qv_bias,
    out_bias,
    down_bias,
):
    return (
        lax.all_gather(up_weight, "batch", axis=2, tiled=True),
        lax.all_gather(down_weight, "batch", axis=2, tiled=True),
        lax.all_gather(mod_weight, "batch", axis=2, tiled=True),
        lax.all_gather(qkv_weight, "batch", axis=2, tiled=True),
        lax.all_gather(out_weight, "batch", axis=2, tiled=True),
        lax.all_gather(up_bias, "batch", axis=1, tiled=True),
        lax.all_gather(mod_bias, "batch", axis=1, tiled=True),
        lax.all_gather(qv_bias, "batch", axis=1, tiled=True),
        lax.all_gather(out_bias, "batch", axis=1, tiled=True),
        lax.all_gather(down_bias, "batch", axis=1, tiled=True),
    )


def fetch_modulation(mod_part, mod_bias_part):
    return (
        lax.all_gather(mod_part, "seq", axis=2, tiled=True),
        lax.all_gather(mod_bias_part, "seq", axis=1, tiled=True),
    )


def gather_rows(first, second):
    return (
        lax.all_gather(first, "seq", axis=1, tiled=True),
        lax.all_gather(second, "seq", axis=1, tiled=True),
    )


def sum_rows(first, second, seq_devices):
    local_seqs, first_rows, width = first.shape
    first_local = first_rows // seq_devices
    second_local = second.shape[1] // seq_devices
    joined = jnp.concatenate(
        [
            first.reshape(local_seqs, seq_devices, first_local, width),
            second.reshape(local_seqs, seq_devices, second_local, width),
        ],
        axis=2,
    )
    joined = joined.reshape(local_seqs, seq_devices * (first_local + second_local), width)
    total = lax.psum_scatter(joined, "seq", scatter_dimension=1, tiled=True)
    return (total[:, :first_local], total[:, first_local:])


def to_rows(first, second):
    return (
        lax.all_to_all(first, "seq", split_axis=1, concat_axis=2, tiled=True),
        lax.all_to_all(second, "seq", split_axis=1, concat_axis=2, tiled=True),
    )


def to_columns(first, second):
    return (
        lax.all_to_all(first, "seq", split_axis=2, concat_axis=1, tiled=True),
        lax.all_to_all(second, "seq", split_axis=2, concat_axis=1, tiled=True),
    )


def own_block(values, seq_index, seq_devices):
    width = values.shape[1] // seq_devices
    return lax.dynamic_slice_in_dim(values, seq_index * width, width, 1)


def general_layer(
    image_tokens,
    text_tokens,
    conditioning,
    key_mask,
    mod_weight,
    mod_bias,
    qkv_weight,
    qv_bias,
    out_weight,
    out_bias,
    up_weight,
    up_bias,
    down_weight,
    down_bias,
    image_cotangent,
    text_cotangent,
):
    seq_devices = lax.axis_size("seq")
    batch_devices = lax.axis_size("batch")
    seq_index = lax.axis_index("seq")
    local_seqs, image_count, model_width = image_tokens.shape
    text_count = text_tokens.shape[1]
    block_rows = image_count + text_count
    key_count = block_rows * seq_devices
    head_size = model_width // HEADS
    factor = 1.0 / math.sqrt(head_size)
    inputs = (image_tokens.astype(jnp.float32), text_tokens.astype(jnp.float32))
    cotangents = (image_cotangent.astype(jnp.float32), text_cotangent.astype(jnp.float32))
    row_spans = ((0, image_count), (image_count, block_rows))
    image_keys = key_mask[:, : image_count * seq_devices].reshape(
        local_seqs, seq_devices, image_count
    )
    text_keys = key_mask[:, image_count * seq_devices :].reshape(
        local_seqs, seq_devices, text_count
    )
    key_live = (
        jnp.concatenate([image_keys, text_keys], axis=2).reshape(local_seqs, key_count) > 0
    )[:, None, None, :]
    cond_float = conditioning.astype(jnp.float32)
    smooth = jax.nn.silu(cond_float).astype(jnp.bfloat16)
    fetched = fetch_columns(
        up_weight,
        down_weight,
        mod_weight,
        qkv_weight,
        out_weight,
        up_bias,
        mod_bias,
        qv_bias,
        out_bias,
        down_bias,
    )
    (
        up_part,
        down_part,
        mod_part,
        qkv_part,
        out_part,
        up_bias_part,
        mod_bias_part,
        qv_part,
        out_bias_part,
        down_bias_part,
    ) = fetched
    mod_full, mod_bias_full = fetch_modulation(mod_part, mod_bias_part)
    mixed_mod = (
        jnp.einsum("sd,tdf->tsf", smooth, mod_full, preferred_element_type=jnp.float32)
        + mod_bias_full.astype(jnp.float32)[:, None, :]
    )
    modulation = unmix_columns(mixed_mod, seq_devices, batch_devices).reshape(
        2, local_seqs, 6, model_width
    )
    first_norms = []
    for modality in range(2):
        pieces = modulation[modality]
        first_norms.append(
            modulate(inputs[modality], pieces[:, 0], pieces[:, 1]).astype(jnp.bfloat16)
        )
    norm_image_all, norm_text_all, qv_seq, out_bias_seq, down_bias_seq = (
        lax.all_gather(first_norms[0], "seq", axis=1, tiled=True),
        lax.all_gather(first_norms[1], "seq", axis=1, tiled=True),
        lax.all_gather(qv_part, "seq", axis=1, tiled=True),
        lax.all_gather(out_bias_part, "seq", axis=1, tiled=True),
        lax.all_gather(down_bias_part, "seq", axis=1, tiled=True),
    )
    first_all = (norm_image_all, norm_text_all)
    qv_full = unmix_columns(qv_seq, seq_devices, batch_devices).astype(jnp.float32)
    out_bias_full = unmix_columns(out_bias_seq, seq_devices, batch_devices).astype(jnp.float32)
    down_bias_full = unmix_columns(down_bias_seq, seq_devices, batch_devices).astype(jnp.float32)
    qkv_cols = [
        jnp.einsum(
            "srd,df->srf",
            first_all[modality],
            qkv_part[modality],
            preferred_element_type=jnp.float32,
        )
        for modality in range(2)
    ]
    qkv_rows = to_rows(qkv_cols[0], qkv_cols[1])
    queries, keyvals = ([], [])
    for modality in range(2):
        projected = unmix_columns(qkv_rows[modality], seq_devices, batch_devices)
        qv_vector = qv_full[modality]
        queries.append(
            (projected[..., :model_width] + qv_vector[:model_width]).astype(jnp.bfloat16)
        )
        value_shift = jnp.concatenate(
            [jnp.zeros((model_width,), jnp.float32), qv_vector[model_width:]]
        )
        keyvals.append((projected[..., model_width:] + value_shift).astype(jnp.bfloat16))
    joined_query = jnp.concatenate(queries, axis=1)
    joined_keyval = jnp.concatenate(keyvals, axis=1)
    all_keyval = lax.all_gather(joined_keyval, "seq", axis=1, tiled=True)
    query_heads = joined_query.reshape(local_seqs, block_rows, HEADS, head_size)
    key_heads = all_keyval[..., :model_width].reshape(local_seqs, key_count, HEADS, head_size)
    value_heads = all_keyval[..., model_width:].reshape(local_seqs, key_count, HEADS, head_size)
    scores = (
        jnp.einsum("sqhe,skhe->shqk", query_heads, key_heads, preferred_element_type=jnp.float32)
        * factor
    )
    row_max = jnp.max(jnp.where(key_live, scores, FLOOR_SCORE), axis=-1, keepdims=True)
    exp_terms = jnp.exp(jnp.where(key_live, scores - row_max, FLOOR_SCORE))
    denominator = jnp.maximum(jnp.sum(exp_terms, axis=-1, keepdims=True), 1.0)
    prob_low = (exp_terms / denominator).astype(jnp.bfloat16)
    logsum = row_max + jnp.log(denominator)
    attended = jnp.einsum(
        "shqk,skhe->sqhe", prob_low, value_heads, preferred_element_type=jnp.float32
    )
    attended = attended.reshape(local_seqs, block_rows, model_width).astype(jnp.bfloat16)
    attended_all = gather_rows(attended[:, :image_count], attended[:, image_count:])
    out_cols = [
        jnp.einsum(
            "srd,df->srf",
            attended_all[modality],
            out_part[modality],
            preferred_element_type=jnp.float32,
        )
        for modality in range(2)
    ]
    out_rows = to_rows(out_cols[0], out_cols[1])
    projections, middles, second_norms = ([], [], [])
    for modality in range(2):
        pieces = modulation[modality]
        projection = (
            unmix_columns(out_rows[modality], seq_devices, batch_devices) + out_bias_full[modality]
        )
        middle = inputs[modality] + pieces[:, 2][:, None, :] * projection
        second_norms.append(modulate(middle, pieces[:, 3], pieces[:, 4]).astype(jnp.bfloat16))
        projections.append(projection)
        middles.append(middle)
    group_rows = gather_rows(second_norms[0], second_norms[1])
    hidden_pre, hidden_act, partials = ([], [], [])
    for modality in range(2):
        pre_values = jnp.einsum(
            "srd,df->srf",
            group_rows[modality],
            up_part[modality],
            preferred_element_type=jnp.float32,
        ) + up_bias_part[modality].astype(jnp.float32)
        act_values = gelu_tanh(pre_values).astype(jnp.bfloat16)
        partials.append(
            jnp.einsum(
                "srf,df->srd", act_values, down_part[modality], preferred_element_type=jnp.float32
            )
        )
        hidden_pre.append(pre_values)
        hidden_act.append(act_values)
    mlp_rows = sum_rows(partials[0], partials[1], seq_devices)
    mlp_outs, results = ([], [])
    for modality in range(2):
        pieces = modulation[modality]
        mlp_value = mlp_rows[modality] + down_bias_full[modality]
        results.append(
            (middles[modality] + pieces[:, 5][:, None, :] * mlp_value).astype(jnp.bfloat16)
        )
        mlp_outs.append(mlp_value)
    fetched_back = fetch_columns(
        up_weight,
        down_weight,
        mod_weight,
        qkv_weight,
        out_weight,
        up_bias,
        mod_bias,
        qv_bias,
        out_bias,
        down_bias,
    )
    up_back, down_back, mod_back, qkv_back, out_back = (
        fetched_back[0],
        fetched_back[1],
        fetched_back[2],
        fetched_back[3],
        fetched_back[4],
    )
    mod_bias_back = fetched_back[6]
    mlp_grads, gate_twos, down_bias_grads = ([], [], [])
    for modality in range(2):
        pieces = modulation[modality]
        mlp_grad = (pieces[:, 5][:, None, :] * cotangents[modality]).astype(jnp.bfloat16)
        gate_twos.append(jnp.sum(cotangents[modality] * mlp_outs[modality], axis=1))
        down_bias_grads.append(jnp.sum(mlp_grad.astype(jnp.float32), axis=(0, 1)))
        mlp_grads.append(mlp_grad)
    group_grads = gather_rows(mlp_grads[0], mlp_grads[1])
    down_grads, up_grads, up_bias_grads, norm_partials = ([], [], [], [])
    for modality in range(2):
        down_grads.append(
            jnp.einsum(
                "srd,srf->df",
                group_grads[modality],
                hidden_act[modality],
                preferred_element_type=jnp.float32,
            )
        )
        act_grad = jnp.einsum(
            "srd,df->srf",
            group_grads[modality],
            down_back[modality],
            preferred_element_type=jnp.float32,
        )
        pullback = jax.vjp(gelu_tanh, hidden_pre[modality])[1]
        pre_grad = pullback(act_grad)[0].astype(jnp.bfloat16)
        up_grads.append(
            jnp.einsum(
                "srd,srf->df", group_rows[modality], pre_grad, preferred_element_type=jnp.float32
            )
        )
        up_bias_grads.append(jnp.sum(pre_grad.astype(jnp.float32), axis=(0, 1)))
        norm_partials.append(
            jnp.einsum(
                "srf,df->srd", pre_grad, up_back[modality], preferred_element_type=jnp.float32
            )
        )
    norm_grads = sum_rows(norm_partials[0], norm_partials[1], seq_devices)
    middle_grads, shift_twos, scale_twos, gate_ones, out_bias_grads, proj_grads = (
        [],
        [],
        [],
        [],
        [],
        [],
    )
    for modality in range(2):
        pieces = modulation[modality]
        pullback = jax.vjp(modulate, middles[modality], pieces[:, 3], pieces[:, 4])[1]
        middle_part, shift_two, scale_two = pullback(norm_grads[modality])
        middle_grad = cotangents[modality] + middle_part
        proj_grad = (pieces[:, 2][:, None, :] * middle_grad).astype(jnp.bfloat16)
        gate_ones.append(jnp.sum(middle_grad * projections[modality], axis=1))
        out_bias_grads.append(jnp.sum(proj_grad.astype(jnp.float32), axis=(0, 1)))
        proj_grads.append(remix_columns(proj_grad, seq_devices, batch_devices))
        middle_grads.append(middle_grad)
        shift_twos.append(shift_two)
        scale_twos.append(scale_two)
    proj_cols = to_columns(proj_grads[0], proj_grads[1])
    out_grads, attended_partials = ([], [])
    for modality in range(2):
        out_grads.append(
            jnp.einsum(
                "srd,srf->df",
                attended_all[modality],
                proj_cols[modality],
                preferred_element_type=jnp.float32,
            )
        )
        attended_partials.append(
            jnp.einsum(
                "srf,df->srd",
                proj_cols[modality],
                out_back[modality],
                preferred_element_type=jnp.float32,
            )
        )
    attended_sums = sum_rows(attended_partials[0], attended_partials[1], seq_devices)
    attended_grad = jnp.concatenate([attended_sums[0], attended_sums[1]], axis=1).astype(
        jnp.bfloat16
    )
    grad_heads = attended_grad.reshape(local_seqs, block_rows, HEADS, head_size)
    scores_again = (
        jnp.einsum("sqhe,skhe->shqk", query_heads, key_heads, preferred_element_type=jnp.float32)
        * factor
    )
    probs_again = jnp.exp(jnp.where(key_live, scores_again - logsum, FLOOR_SCORE))
    probs_again_low = probs_again.astype(jnp.bfloat16)
    prob_grad = jnp.einsum(
        "sqhe,skhe->shqk", grad_heads, value_heads, preferred_element_type=jnp.float32
    )
    inner_sum = jnp.sum(probs_again * prob_grad, axis=-1, keepdims=True)
    score_grad = (probs_again * (prob_grad - inner_sum)).astype(jnp.bfloat16)
    query_grad = (
        jnp.einsum("shqk,skhe->sqhe", score_grad, key_heads, preferred_element_type=jnp.float32)
        * factor
    )
    query_grad = query_grad.reshape(local_seqs, block_rows, model_width).astype(jnp.bfloat16)
    key_grad = (
        jnp.einsum("shqk,sqhe->skhe", score_grad, query_heads, preferred_element_type=jnp.float32)
        * factor
    )
    value_grad = jnp.einsum(
        "shqk,sqhe->skhe", probs_again_low, grad_heads, preferred_element_type=jnp.float32
    )
    key_rows, value_rows = (
        lax.psum_scatter(
            key_grad.reshape(local_seqs, key_count, model_width),
            "seq",
            scatter_dimension=1,
            tiled=True,
        ),
        lax.psum_scatter(
            value_grad.reshape(local_seqs, key_count, model_width),
            "seq",
            scatter_dimension=1,
            tiled=True,
        ),
    )
    key_rows = key_rows.astype(jnp.bfloat16)
    value_rows = value_rows.astype(jnp.bfloat16)
    qv_bias_grads, joined_grads = ([], [])
    for modality in range(2):
        row_start, row_stop = row_spans[modality]
        query_part = query_grad[:, row_start:row_stop]
        value_part = value_rows[:, row_start:row_stop]
        joined_grad = jnp.concatenate(
            [query_part, key_rows[:, row_start:row_stop], value_part], axis=-1
        )
        qv_bias_grads.append(
            jnp.concatenate(
                [
                    jnp.sum(query_part.astype(jnp.float32), axis=(0, 1)),
                    jnp.sum(value_part.astype(jnp.float32), axis=(0, 1)),
                ]
            )
        )
        joined_grads.append(remix_columns(joined_grad, seq_devices, batch_devices))
    qkv_grad_cols = to_columns(joined_grads[0], joined_grads[1])
    qkv_grads, first_partials = ([], [])
    for modality in range(2):
        qkv_grads.append(
            jnp.einsum(
                "srd,srf->df",
                first_all[modality],
                qkv_grad_cols[modality],
                preferred_element_type=jnp.float32,
            )
        )
        first_partials.append(
            jnp.einsum(
                "srf,df->srd",
                qkv_grad_cols[modality],
                qkv_back[modality],
                preferred_element_type=jnp.float32,
            )
        )
    first_grads = sum_rows(first_partials[0], first_partials[1], seq_devices)
    input_grads, mod_partials = ([], [])
    for modality in range(2):
        pieces = modulation[modality]
        pullback = jax.vjp(modulate, inputs[modality], pieces[:, 0], pieces[:, 1])[1]
        input_part, shift_one, scale_one = pullback(first_grads[modality])
        input_grads.append(middle_grads[modality] + input_part)
        stacked = jnp.stack(
            [
                shift_one,
                scale_one,
                gate_ones[modality],
                shift_twos[modality],
                scale_twos[modality],
                gate_twos[modality],
            ],
            axis=1,
        )
        mod_partials.append(stacked.reshape(local_seqs, 6 * model_width))
    qv_mixed = remix_columns(jnp.stack(qv_bias_grads), seq_devices, batch_devices)
    out_bias_mixed = remix_columns(jnp.stack(out_bias_grads), seq_devices, batch_devices)
    down_bias_mixed = remix_columns(jnp.stack(down_bias_grads), seq_devices, batch_devices)
    mod_sum, qv_summed, out_bias_summed, down_bias_summed = lax.psum(
        (jnp.stack(mod_partials), qv_mixed, out_bias_mixed, down_bias_mixed), "seq"
    )
    mod_low = mod_sum.astype(jnp.bfloat16)
    mod_mixed = remix_columns(mod_low, seq_devices, batch_devices)
    columns = mod_part.shape[2]
    own_columns = lax.dynamic_slice_in_dim(mod_mixed, seq_index * columns, columns, 2)
    mod_grad = jnp.einsum("sd,tsf->tdf", smooth, own_columns, preferred_element_type=jnp.float32)
    mod_bias_grad = jnp.sum(own_columns.astype(jnp.float32), axis=1)
    mod_again = fetch_modulation(mod_back, mod_bias_back)[0]
    smooth_grad = jnp.einsum(
        "tsf,tdf->sd", mod_mixed, mod_again, preferred_element_type=jnp.float32
    )
    cond_pullback = jax.vjp(jax.nn.silu, cond_float)[1]
    cond_grad = cond_pullback(smooth_grad)[0]
    qv_own = own_block(qv_summed, seq_index, seq_devices)
    out_bias_own = own_block(out_bias_summed, seq_index, seq_devices)
    down_bias_own = own_block(down_bias_summed, seq_index, seq_devices)
    column_grads = (
        lax.psum_scatter(jnp.stack(up_grads), "batch", scatter_dimension=2, tiled=True),
        lax.psum_scatter(jnp.stack(down_grads), "batch", scatter_dimension=2, tiled=True),
        lax.psum_scatter(mod_grad, "batch", scatter_dimension=2, tiled=True),
        lax.psum_scatter(jnp.stack(qkv_grads), "batch", scatter_dimension=2, tiled=True),
        lax.psum_scatter(jnp.stack(out_grads), "batch", scatter_dimension=2, tiled=True),
        lax.psum_scatter(jnp.stack(up_bias_grads), "batch", scatter_dimension=1, tiled=True),
        lax.psum_scatter(mod_bias_grad, "batch", scatter_dimension=1, tiled=True),
        lax.psum_scatter(qv_own, "batch", scatter_dimension=1, tiled=True),
        lax.psum_scatter(out_bias_own, "batch", scatter_dimension=1, tiled=True),
        lax.psum_scatter(down_bias_own, "batch", scatter_dimension=1, tiled=True),
    )
    return (
        results[0],
        results[1],
        input_grads[0],
        input_grads[1],
        cond_grad,
        column_grads[2],
        column_grads[6],
        column_grads[3],
        column_grads[7],
        column_grads[4],
        column_grads[8],
        column_grads[0],
        column_grads[5],
        column_grads[1],
        column_grads[9],
    )


LOG2E = 1.4426950408889634
DEAD = -1e30
BF16 = jnp.bfloat16
F32 = jnp.float32


def dot_nt(a, b):
    return lax.dot_general(a, b, (((1,), (1,)), ((), ())), preferred_element_type=F32)


def dot_nn(a, b):
    return lax.dot_general(a, b, (((1,), (0,)), ((), ())), preferred_element_type=F32)


def dot_tn(a, b):
    return lax.dot_general(a, b, (((0,), (0,)), ((), ())), preferred_element_type=F32)


WEIGHT = {
    "attention": 8.5,
    "attention_back": 16,
    "project": 6.5,
    "partial_sums": 2.5,
    "middle": 2.5,
    "hidden": 9,
    "outer_sums": 9,
    "hidden_back": 10,
    "middle_back": 3.5,
    "attended_back": 3,
    "project_back": 6,
    "result": 3.5,
    "input_back": 4.5,
}


def lanes_of(columns, rows, width):
    lane = lax.broadcasted_iota(jnp.int32, (rows, width), 1)
    out = jnp.zeros((rows, width), F32)
    for k, column in enumerate(columns):
        out = jnp.where(lane == k, column, out)
    return out.astype(BF16)


def three_parts(column):
    high = column.astype(BF16).astype(F32)
    rest = column - high
    mid = rest.astype(BF16).astype(F32)
    return [high, mid, rest - mid]


def attention_kernel(
    query_rows, scale, head, bias_ref, floor_ref, qi, qt, ki, kt, vi, vt, oi, ot, li, lt, keys, values
):
    image_rows = qi.shape[0]
    rows = keys.shape[1]
    floor = floor_ref[0, 0]
    key_side = lanes_of([bias_ref[:, 0:1]], rows, head)
    value_side = lanes_of([1.0], rows, head)
    for side in range(2):
        lanes = slice(side * head, (side + 1) * head)
        for ref, extra, first, second in (
            (keys, key_side, ki, kt),
            (values, value_side, vi, vt),
        ):
            ref[side, :image_rows, :] = jnp.concatenate(
                [first[:, lanes], extra[:image_rows]], axis=1
            )
            ref[side, image_rows:, :] = jnp.concatenate(
                [second[:, lanes], extra[image_rows:]], axis=1
            )
    spans = [(qi, oi, li, start, query_rows) for start in range(0, image_rows, query_rows)]
    spans.append((qt, ot, lt, 0, qt.shape[0]))
    steps = [(*span, side) for span in spans for side in range(2)]

    def score(step):
        source, _, _, start, size, side = step
        query = source[start : start + size, side * head : (side + 1) * head]
        query = jnp.concatenate([query, lanes_of([1.0], size, head)], axis=1)
        return dot_nt(query, keys[side])

    ahead = score(steps[0])
    for at, (_, target, logs, start, size, side) in enumerate(steps):
        scores = ahead
        if at + 1 < len(steps):
            ahead = score(steps[at + 1])
        top = jnp.maximum(jnp.max(scores, axis=1, keepdims=True) * scale, floor)
        exps = jnp.exp2(scores * scale - top).astype(BF16)
        product = dot_nn(exps, values[side])
        total = jnp.maximum(product[:, head : head + 1], 1.0)
        span = slice(start, start + size)
        lanes = slice(side * head, (side + 1) * head)
        target[span, lanes] = (product[:, :head] * (1.0 / total)).astype(BF16)
        logs[span, lanes] = jnp.broadcast_to(top + jnp.log2(total), (size, head))


def pair_block(rows, lanes, pairs, part):
    return pl.BlockSpec((rows, lanes), lambda pair: (0, part * pairs + pair))


def attention(qkv_image, qkv_text, key_bias, floor, head):
    image_rows, width = qkv_image.shape
    text_rows = qkv_text.shape[0]
    rows = image_rows + text_rows
    lanes = 2 * head
    pairs = width // (3 * lanes)
    columns = [
        pair_block(count, lanes, pairs, part)
        for part in range(3)
        for count in (image_rows, text_rows)
    ]
    return pl.pallas_call(
        functools.partial(attention_kernel, 256, LOG2E / math.sqrt(head), head),
        grid=(pairs,),
        in_specs=[
            pl.BlockSpec((rows, 128), lambda pair: (0, 0)),
            pl.BlockSpec(memory_space=pltpu.SMEM),
            *columns,
        ],
        out_specs=[columns[0], columns[1], columns[0], columns[1]],
        out_shape=[
            jax.ShapeDtypeStruct((count, width // 3), dtype)
            for dtype in (BF16, F32)
            for count in (image_rows, text_rows)
        ],
        scratch_shapes=[pltpu.VMEM((2, rows, lanes), BF16)] * 2,
        compiler_params=pltpu.CompilerParams(vmem_limit_bytes=56 << 20),
        cost_estimate=pl.CostEstimate(
            flops=int(WEIGHT["attention"] * 1.15e9), bytes_accessed=1, transcendentals=0
        ),
        name="attention",
    )(key_bias, floor, qkv_image, qkv_text, qkv_image, qkv_text, qkv_image, qkv_text)


def attention_back_kernel(query_rows, scale, factor, head, pairs, *refs):
    (bias_ref, qi, qt, ki, kt, vi, vt, ai, at, li, lt, gi, gt) = refs[:13]
    oi, ot, keys, values, key_sum, value_sum = refs[13:]
    pair = pl.program_id(0)
    image_rows = qi.shape[0]
    rows = keys.shape[1]
    width = 2 * head
    key_side = lanes_of([bias_ref[:, 0:1], 1.0, 1.0, 1.0], rows, head)
    value_side = lanes_of([1.0, 1.0, 1.0], rows, head)
    for side in range(2):
        lanes = slice(side * head, (side + 1) * head)
        for ref, extra, first, second in (
            (keys, key_side, ki, kt),
            (values, value_side, vi, vt),
        ):
            ref[side, :image_rows, :] = jnp.concatenate(
                [first[:, lanes], extra[:image_rows]], axis=1
            )
            ref[side, image_rows:, :] = jnp.concatenate(
                [second[:, lanes], extra[image_rows:]], axis=1
            )
    key_sum[...] = jnp.zeros_like(key_sum)
    value_sum[...] = jnp.zeros_like(value_sum)
    spans = [(qi, ai, li, gi, oi, start, query_rows) for start in range(0, image_rows, query_rows)]
    spans.append((qt, at, lt, gt, ot, 0, qt.shape[0]))
    steps = [(*span, side) for span in spans for side in range(2)]
    query_lanes = pl.ds(pl.multiple_of(pair * width, width), width)
    key_lanes = pl.ds(pl.multiple_of((pairs + pair) * width, width), width)
    value_lanes = pl.ds(pl.multiple_of((2 * pairs + pair) * width, width), width)

    def products(step):
        source, outs, logs, grads, _, start, size, side = step
        span = slice(start, start + size)
        lanes = slice(side * head, (side + 1) * head)
        query, grad = (source[span, lanes], grads[span, lanes])
        log = logs[span, side * head : side * head + 1] * (-1.0 / scale)
        inner = -jnp.sum(
            grad.astype(F32) * outs[span, lanes].astype(F32), axis=1, keepdims=True
        )
        query_wide = jnp.concatenate(
            [query, lanes_of([1.0, *three_parts(log)], size, head)], axis=1
        )
        grad_wide = jnp.concatenate([grad, lanes_of(three_parts(inner), size, head)], axis=1)
        return (
            query,
            grad,
            dot_nt(keys[side], query_wide),
            dot_nt(values[side], grad_wide),
        )

    ahead = products(steps[0])
    dq = []
    for at_step, (_, _, _, _, target, start, size, side) in enumerate(steps):
        query, grad, scores, prob_grad = ahead
        if at_step + 1 < len(steps):
            ahead = products(steps[at_step + 1])
        probs = jnp.exp2(scores * scale)
        score_grad = (probs * prob_grad).astype(BF16)
        lanes = slice(side * head, (side + 1) * head)
        value_sum[:, lanes] += dot_nn(probs.astype(BF16), grad)
        key_sum[:, lanes] += dot_nn(score_grad, query)
        dq.append(dot_tn(score_grad, keys[side][:, :head]))
        if side == 1:
            target[start : start + size, query_lanes] = (
                jnp.concatenate(dq, axis=1) * factor
            ).astype(BF16)
            dq = []
    oi[:, key_lanes] = (key_sum[:image_rows] * factor).astype(BF16)
    ot[:, key_lanes] = (key_sum[image_rows:] * factor).astype(BF16)
    oi[:, value_lanes] = value_sum[:image_rows].astype(BF16)
    ot[:, value_lanes] = value_sum[image_rows:].astype(BF16)


def attention_back(
    qkv_image, qkv_text, out_image, out_text, log_image, log_text, grad_image, grad_text, key_bias, head
):
    image_rows, width = qkv_image.shape
    text_rows = qkv_text.shape[0]
    rows = image_rows + text_rows
    lanes = 2 * head
    pairs = width // (3 * lanes)
    columns = [
        pair_block(count, lanes, pairs, part)
        for part in range(3)
        for count in (image_rows, text_rows)
    ]
    return pl.pallas_call(
        functools.partial(
            attention_back_kernel, 512, LOG2E / math.sqrt(head), 1.0 / math.sqrt(head), head, pairs
        ),
        grid=(pairs,),
        in_specs=[
            pl.BlockSpec((rows, 128), lambda pair: (0, 0)),
            *columns,
            *(columns[:2] * 3),
        ],
        out_specs=[
            pl.BlockSpec((image_rows, width), lambda pair: (0, 0)),
            pl.BlockSpec((text_rows, width), lambda pair: (0, 0)),
        ],
        out_shape=[
            jax.ShapeDtypeStruct((image_rows, width), BF16),
            jax.ShapeDtypeStruct((text_rows, width), BF16),
        ],
        scratch_shapes=[pltpu.VMEM((2, rows, lanes), BF16)] * 2
        + [pltpu.VMEM((rows, lanes), F32)] * 2,
        compiler_params=pltpu.CompilerParams(vmem_limit_bytes=56 << 20),
        cost_estimate=pl.CostEstimate(
            flops=int(WEIGHT["attention_back"] * 1.15e9), bytes_accessed=1, transcendentals=0
        ),
        name="attention_back",
    )(
        key_bias,
        *(qkv_image, qkv_text) * 3,
        out_image, out_text, log_image, log_text, grad_image, grad_text,
    )


def flip(values, bit):
    return lax.ppermute(values, "seq", [(i, i ^ bit) for i in range(4)])


def gather_near(a, b):
    return (flip(a, 1), flip(b, 1), flip(a, 2), flip(b, 2))


def gather_far(a, b, near):
    return (a, b, *near, flip(near[0], 2), flip(near[3], 1))


def gather_halves(a, b):
    return gather_far(a, b, gather_near(a, b))


def add_low(a, b):
    return (a.astype(F32) + b.astype(F32)).astype(BF16)


def scatter_first(sent):
    return (flip(sent[1], 1), flip(sent[2], 2))


def scatter_last(sent, first):
    from_x, from_y = first
    width = sent[3].shape[-1]
    late_x = flip(add_low(sent[3], from_y[..., :width]), 1)
    late_y = flip(add_low(sent[4], from_x[..., :width]), 2)
    return (sent[0], from_x, from_y, late_x, late_y)


def scatter_halves(halves):
    return scatter_last(halves, scatter_first(halves))


ANYWHERE = pl.BlockSpec(memory_space=pl.ANY)
ON_CORE = pl.BlockSpec(memory_space=pltpu.VMEM)


class Copies:
    def __init__(self, semaphores):
        self.semaphores = semaphores
        self.count = 0
        self.open = []

    def start(self, source, target):
        copy = pltpu.make_async_copy(source, target, self.semaphores.at[self.count])
        self.count += 1
        copy.start()
        return copy

    def send(self, source, target):
        self.open.append(self.start(source, target))

    def finish(self):
        for copy in self.open:
            copy.wait()


def fetch_halves(copies, halves, rows, seq):
    width = rows.shape[2] // 2
    fetched = []
    for r in range(4):
        pair = []
        for side in range(2):
            half = halves[2 * r + side]
            half = half if seq is None else half.at[seq]
            pair.append(copies.start(half, rows.at[r, :, pl.ds(side * width, width)]))
        fetched.append(pair)
    return fetched


def send_block(copies, rows, sent, r, seq):
    own, for_x, for_y, late_x, late_y = sent if seq is None else [ref.at[seq] for ref in sent]
    width = rows.shape[2] // 2
    low, high = pl.ds(0, width), pl.ds(width, width)
    if r == 0:
        copies.send(rows.at[0], own)
        return
    first, second = {
        1: (for_x.at[:, high], late_x),
        2: (late_y, for_y.at[:, high]),
        3: (for_x.at[:, low], for_y.at[:, low]),
    }[r]
    copies.send(rows.at[r, :, low], first)
    copies.send(rows.at[r, :, high], second)


def sent_shapes(block, D, seqs=1):
    lead = () if seqs == 1 else (seqs,)
    return [((*lead, block, width), BF16) for width in (D, D, D, D // 2, D // 2)]


def normalize(values):
    mean = jnp.mean(values, axis=1, keepdims=True)
    centered = values - mean
    variance = jnp.mean(centered * centered, axis=1, keepdims=True)
    inverse = lax.rsqrt(variance + NORM_EPSILON)
    return centered * inverse, inverse


def normalize_back(norm, inverse, grad, scale):
    scaled = grad * (1.0 + scale)
    return inverse * (
        scaled
        - jnp.mean(scaled, axis=1, keepdims=True)
        - norm * jnp.mean(scaled * norm, axis=1, keepdims=True)
    )


def run(kernel, name, operands, specs, outs, out_specs, scratch, copies=0):
    if copies:
        scratch = [*scratch, pltpu.SemaphoreType.DMA((copies,))]
    return pl.pallas_call(
        kernel,
        in_specs=specs,
        out_specs=out_specs,
        out_shape=[jax.ShapeDtypeStruct(shape, dtype) for shape, dtype in outs],
        scratch_shapes=scratch,
        compiler_params=pltpu.CompilerParams(vmem_limit_bytes=56 << 20),
        cost_estimate=pl.CostEstimate(
            flops=int(WEIGHT[name] * 1.15e9), bytes_accessed=1, transcendentals=0
        ),
        name=name,
    )(*operands)


def project_kernel(seq, image_rows, *refs):
    halves, (weight, mods, bias) = (refs[:8], refs[8:11])
    qkv_i, qkv_t, norm_i, norm_t = refs[11:15]
    rows, held, image_norm, text_norm, image_out, text_out, semaphores = refs[15:]
    copies = Copies(semaphores)
    fetched = fetch_halves(copies, halves, rows, seq)
    weights = [copies.start(weight.at[t], held.at[t]) for t in range(2)]
    text_rows = rows.shape[1] - image_rows
    for r in range(4):
        for copy in fetched[r]:
            copy.wait()
        for t, norms, low, count in (
            (0, image_norm, 0, image_rows),
            (1, text_norm, image_rows, text_rows),
        ):
            norm, _ = normalize(rows[r, low : low + count, :].astype(F32))
            norm = norm * (1.0 + mods[t, seq, 1:2, :]) + mods[t, seq, 0:1, :]
            norms[r * count : (r + 1) * count, :] = norm.astype(BF16)
        if r == 0:
            weights[0].wait()
        span = pl.ds(r * image_rows, image_rows)
        product = dot_nt(image_norm[span, :], held[0]) + bias[0:1, :]
        image_out[span, :] = product.astype(BF16)
        copies.send(image_norm.at[span, :], norm_i.at[span, :])
        copies.send(image_out.at[span, :], qkv_i.at[span, :])
    weights[1].wait()
    text_out[...] = (dot_nt(text_norm[...], held[1]) + bias[1:2, :]).astype(BF16)
    copies.send(text_norm, norm_t)
    copies.send(text_out, qkv_t)
    copies.finish()


def project(halves, weight, mods, bias, seq, image_rows):
    block, width = halves[0].shape[-2:]
    D, W = 2 * width, weight.shape[1]
    image, text = 4 * image_rows, 4 * (block - image_rows)
    return run(
        functools.partial(project_kernel, seq, image_rows),
        "project",
        (*halves, weight, mods, bias),
        [ANYWHERE] * 9 + [ON_CORE] * 2,
        [((image, W), BF16), ((text, W), BF16), ((image, D), BF16), ((text, D), BF16)],
        [ANYWHERE] * 4,
        [
            pltpu.VMEM((4, block, D), BF16),
            pltpu.VMEM((2, W, D), BF16),
            pltpu.VMEM((image, D), BF16),
            pltpu.VMEM((text, D), BF16),
            pltpu.VMEM((image, W), BF16),
            pltpu.VMEM((text, W), BF16),
        ],
        20,
    )


def partial_kernel(seqs, dot, image_rows, *refs):
    inputs, weight, halves = (refs[: 2 * seqs], refs[2 * seqs], refs[2 * seqs + 1 : 2 * seqs + 6])
    lefts, held, rows, semaphores = (
        refs[2 * seqs + 6 : 4 * seqs + 6],
        refs[4 * seqs + 6],
        refs[4 * seqs + 7 : 5 * seqs + 7],
        refs[5 * seqs + 7],
    )
    copies = Copies(semaphores)
    weights = [copies.start(weight.at[t], held.at[t]) for t in (1, 0)]
    fetched = [
        [copies.start(inputs[2 * s + t], lefts[2 * s + t]) for t in (1, 0)] for s in range(seqs)
    ]
    text_rows = rows[0].shape[1] - image_rows
    for s in range(seqs):
        if s == 0:
            weights[0].wait()
        fetched[s][0].wait()
        text = dot(lefts[2 * s + 1][...], held[1]).astype(BF16)
        for r in range(4):
            rows[s][r, image_rows:, :] = text[r * text_rows : (r + 1) * text_rows]
        if s == 0:
            weights[1].wait()
        fetched[s][1].wait()
        for r in (3, 1, 2, 0):
            left = lefts[2 * s][r * image_rows : (r + 1) * image_rows, :]
            rows[s][r, :image_rows, :] = dot(left, held[0]).astype(BF16)
            send_block(copies, rows[s], halves, r, s if seqs > 1 else None)
    copies.finish()


def partial_sums(inputs, weight, dot, D, image_rows):
    seqs = len(inputs)
    image, K = inputs[0][0].shape
    text = inputs[0][1].shape[0]
    block = (image + text) // 4
    return run(
        functools.partial(partial_kernel, seqs, dot, image_rows),
        "partial_sums",
        (*[value for pair in inputs for value in pair], weight),
        [ANYWHERE] * (2 * seqs + 1),
        sent_shapes(block, D, seqs),
        [ANYWHERE] * 5,
        [pltpu.VMEM((count, K), BF16) for _ in range(seqs) for count in (image, text)]
        + [pltpu.VMEM(weight.shape, BF16)]
        + [pltpu.VMEM((4, block, D), BF16)] * seqs,
        2 + 2 * seqs + 7 * seqs,
    )


def piece_sum(pieces, low, count):
    own, from_x, from_y, late_x, late_y = pieces
    width = late_x.shape[-1]

    def add(*parts):
        return sum(part.astype(F32) for part in parts)

    span = pl.ds(low, count)
    return jnp.concatenate(
        [
            add(own[span, :width], from_x[span, width:], late_y[span, :]),
            add(own[span, width:], late_x[span, :], from_y[span, width:]),
        ],
        axis=1,
    )


def both_halves(halves, seq, low, count):
    return jnp.concatenate(
        [half[seq, low : low + count, :].astype(F32) for half in halves], axis=1
    )


def middle_kernel(seq, image_rows, *refs):
    pieces, tokens, (mods, bias) = (refs[:5], refs[5:7], refs[7:9])
    projection_ref, middle_ref, second_a, second_b = refs[9:]
    block, width = second_a.shape
    for t, low, count in ((0, 0, image_rows), (1, image_rows, block - image_rows)):
        span = slice(low, low + count)
        projection = piece_sum(pieces, low, count) + bias[t : t + 1, :]
        middle = both_halves(tokens, seq, low, count) + mods[t, seq, 2:3, :] * projection
        norm, _ = normalize(middle)
        second = (norm * (1.0 + mods[t, seq, 4:5, :]) + mods[t, seq, 3:4, :]).astype(BF16)
        projection_ref[span, :] = projection
        middle_ref[span, :] = middle
        second_a[span, :] = second[:, :width]
        second_b[span, :] = second[:, width:]


def middle_step(pieces, tokens, mods, bias, seq, image_rows):
    block, width = pieces[3].shape
    return run(
        functools.partial(middle_kernel, seq, image_rows),
        "middle",
        (*pieces, *tokens, mods, bias),
        [ON_CORE] * 9,
        [((block, 2 * width), F32)] * 2 + [((block, width), BF16)] * 2,
        [ON_CORE] * 4,
        [],
    )


GELU_SCALE = math.sqrt(2.0 / math.pi)
GELU_CUBE = 0.044715


def hidden_kernel(seq, image_rows, *refs):
    halves, cotangents, (weight, bias, mods) = (refs[:8], refs[8:16], refs[16:19])
    outs = refs[19:27]
    act_i, act_t, slope_i, slope_t, grad_i, grad_t, second_i, second_t = outs
    rows, given, held, acts, slopes, grads, texts, semaphores = refs[27:]
    copies = Copies(semaphores)
    fetched = fetch_halves(copies, halves, rows, None)
    weights = [copies.start(weight.at[t], held.at[t]) for t in range(2)]
    other = fetch_halves(copies, cotangents, given, seq)
    text_rows = rows.shape[1] - image_rows
    second_text, grad_text, act_text, slope_text = texts

    def activate(pre):
        squared = pre * pre
        bent = jnp.tanh(pre * (GELU_SCALE + (GELU_SCALE * GELU_CUBE) * squared))
        rise = 0.5 + 0.5 * bent
        act = pre * rise
        slope = rise + (act * (1.0 - rise)) * (
            2.0 * GELU_SCALE + (6.0 * GELU_SCALE * GELU_CUBE) * squared
        )
        return act.astype(BF16), slope.astype(BF16)

    for r in range(4):
        for copy in fetched[r]:
            copy.wait()
        if r == 0:
            weights[0].wait()
        span = pl.ds(r * image_rows, image_rows)
        text_span = slice(r * text_rows, (r + 1) * text_rows)
        pre = dot_nt(rows[r, :image_rows, :], held[0]) + bias[0:1, :]
        act, slope = activate(pre)
        acts[span, :] = act
        slopes[span, :] = slope
        second_text[text_span, :] = rows[r, image_rows:, :]
        for copy in other[r]:
            copy.wait()
        for t, target, place, low, count in (
            (0, grads, span, 0, image_rows),
            (1, grad_text, text_span, image_rows, text_rows),
        ):
            value = given[r, low : low + count, :].astype(F32) * mods[t, seq, 5:6, :]
            target[place, :] = value.astype(BF16)
        copies.send(acts.at[span, :], act_i.at[span, :])
        copies.send(slopes.at[span, :], slope_i.at[span, :])
        copies.send(grads.at[span, :], grad_i.at[span, :])
        copies.send(rows.at[r, pl.ds(0, image_rows), :], second_i.at[span, :])
    weights[1].wait()
    act_text[...], slope_text[...] = activate(
        dot_nt(second_text[...], held[1]) + bias[1:2, :]
    )
    for source, target in (
        (act_text, act_t),
        (slope_text, slope_t),
        (grad_text, grad_t),
        (second_text, second_t),
    ):
        copies.send(source, target)
    copies.finish()


def hidden_step(halves, cotangents, weight, bias, mods, seq, image_rows):
    block, width = halves[0].shape
    D, F = 2 * width, weight.shape[1]
    image, text = 4 * image_rows, 4 * (block - image_rows)

    def kernel(*refs):
        texts, semaphores = (refs[-5:-1], refs[-1])
        hidden_kernel(seq, image_rows, *refs[:-5], texts, semaphores)

    return run(
        kernel,
        "hidden",
        (*halves, *cotangents, weight, bias, mods),
        [ANYWHERE] * 17 + [ON_CORE] * 2,
        [((count, wide), BF16) for wide in (F, F, D, D) for count in (image, text)],
        [ANYWHERE] * 8,
        [
            pltpu.VMEM((4, block, D), BF16),
            pltpu.VMEM((4, block, D), BF16),
            pltpu.VMEM((2, F, D), BF16),
            pltpu.VMEM((image, F), BF16),
            pltpu.VMEM((image, F), BF16),
            pltpu.VMEM((image, D), BF16),
        ]
        + [pltpu.VMEM((text, wide), BF16) for wide in (D, D, F, F)],
        38,
    )


def outer_kernel(seqs, chunk, *refs):
    inputs, out = (refs[: 4 * seqs], refs[4 * seqs])
    held, result, semaphores = (refs[4 * seqs + 1 : -2], refs[-2], refs[-1])
    copies = Copies(semaphores)
    order = [4 * s + 2 * t + side for t in (1, 0) for s in range(seqs) for side in range(2)]
    fetched = {k: copies.start(inputs[k], held[k]) for k in order}
    columns = result.shape[1]
    for t in (1, 0):
        for s in range(seqs):
            fetched[4 * s + 2 * t].wait()
            fetched[4 * s + 2 * t + 1].wait()
        for low in range(0, columns, chunk):
            span = pl.ds(low, chunk)
            total = dot_tn(held[2 * t][:, span], held[2 * t + 1][...])
            for s in range(1, seqs):
                total = total + dot_tn(held[4 * s + 2 * t][:, span], held[4 * s + 2 * t + 1][...])
            result[t, span, :] = total.astype(BF16)
            copies.send(result.at[t, span, :], out.at[t, span, :])
    copies.finish()


def outer_sums(lefts, rights, chunk):
    seqs = len(lefts)
    columns, width = lefts[0][0].shape[1], rights[0][0].shape[1]
    operands = [side[s][t] for s in range(seqs) for t in range(2) for side in (lefts, rights)]
    return run(
        functools.partial(outer_kernel, seqs, chunk),
        "outer_sums",
        operands,
        [ANYWHERE] * (4 * seqs),
        [((2, columns, width), BF16)],
        [ANYWHERE],
        [pltpu.VMEM(value.shape, BF16) for value in operands]
        + [pltpu.VMEM((2, columns, width), BF16)],
        4 * seqs + 2 * (columns // chunk),
    )[0]


def hidden_back_kernel(image_rows, *refs):
    (grad_i, grad_t, slope_i, slope_t, down, up) = refs[:6]
    pre_i, pre_t, sums, sent = (refs[6], refs[7], refs[8], refs[9:14])
    grads, slopes, pres, grad_text, slope_text, pre_text, held_down, held_up, rows, semaphores = (
        refs[14:]
    )
    copies = Copies(semaphores)
    order = (3, 1, 2, 0)
    spans = {r: pl.ds(r * image_rows, image_rows) for r in order}
    images = {}
    downs, ups = ([None, None], [None, None])
    for k, r in enumerate(order):
        images[r] = [copies.start(grad_i.at[spans[r], :], grads.at[spans[r], :])]
        if k == 0:
            downs[0] = copies.start(down.at[0], held_down.at[0])
        images[r].append(copies.start(slope_i.at[spans[r], :], slopes.at[spans[r], :]))
        if k == 0:
            ups[0] = copies.start(up.at[0], held_up.at[0])
    texts = [copies.start(grad_t, grad_text), copies.start(slope_t, slope_text)]
    downs[1] = copies.start(down.at[1], held_down.at[1])
    ups[1] = copies.start(up.at[1], held_up.at[1])
    text_rows = rows.shape[1] - image_rows
    total = jnp.zeros((1, pres.shape[1]), F32)
    for k, r in enumerate(order):
        for copy in images[r]:
            copy.wait()
        if k == 0:
            downs[0].wait()
        product = dot_nt(grads[spans[r], :], held_down[0]) * slopes[spans[r], :].astype(F32)
        low = product.astype(BF16)
        pres[spans[r], :] = low
        copies.send(pres.at[spans[r], :], pre_i.at[spans[r], :])
        total = total + jnp.sum(low.astype(F32), axis=0, keepdims=True)
        if k == 0:
            ups[0].wait()
        rows[r, :image_rows, :] = dot_nn(pres[spans[r], :], held_up[0]).astype(BF16)
        if k == 1:
            for copy in texts:
                copy.wait()
            downs[1].wait()
            product = dot_nt(grad_text[...], held_down[1]) * slope_text[...].astype(F32)
            pre_text[...] = product.astype(BF16)
            copies.send(pre_text, pre_t)
            sums[1:2, :] = jnp.sum(pre_text[...].astype(F32), axis=0, keepdims=True)
            ups[1].wait()
            back = dot_nn(pre_text[...], held_up[1]).astype(BF16)
            for q in range(4):
                rows[q, image_rows:, :] = back[q * text_rows : (q + 1) * text_rows]
            send_block(copies, rows, sent, order[0], None)
        if k >= 1:
            send_block(copies, rows, sent, r, None)
    sums[0:1, :] = total
    copies.finish()


def hidden_back(grads, slopes, down, up, image_rows):
    image, D = grads[0].shape
    text = grads[1].shape[0]
    F = up.shape[1]
    block = (image + text) // 4
    outs = run(
        functools.partial(hidden_back_kernel, image_rows),
        "hidden_back",
        (*grads, *slopes, down, up),
        [ANYWHERE] * 6,
        [((image, F), BF16), ((text, F), BF16), ((2, F), F32)] + sent_shapes(block, D),
        [ANYWHERE] * 2 + [ON_CORE] + [ANYWHERE] * 5,
        [
            pltpu.VMEM((image, D), BF16),
            pltpu.VMEM((image, F), BF16),
            pltpu.VMEM((image, F), BF16),
            pltpu.VMEM((text, D), BF16),
            pltpu.VMEM((text, F), BF16),
            pltpu.VMEM((text, F), BF16),
            pltpu.VMEM((2, F, D), BF16),
            pltpu.VMEM((2, F, D), BF16),
            pltpu.VMEM((4, block, D), BF16),
        ],
        8 + 2 + 4 + 1 + 4 + 7,
    )
    return outs[0:2], outs[2], outs[3:]


def middle_back_kernel(seq, image_rows, *refs):
    pieces, cotangents, (middle_ref, projection_ref, mods) = (refs[:5], refs[5:7], refs[7:10])
    grad_ref, low_a, low_b, sums = refs[10:]
    block, width = low_a.shape
    for t, low, count in ((0, 0, image_rows), (1, image_rows, block - image_rows)):
        span = slice(low, low + count)
        norm_grad = piece_sum(pieces, low, count)
        norm, inverse = normalize(middle_ref[span, :])
        grad = both_halves(cotangents, seq, low, count) + normalize_back(
            norm, inverse, norm_grad, mods[t, seq, 4:5, :]
        )
        rounded = (mods[t, seq, 2:3, :] * grad).astype(BF16)
        grad_ref[span, :] = grad
        low_a[span, :] = rounded[:, :width]
        low_b[span, :] = rounded[:, width:]
        for k, value in enumerate(
            (norm_grad, norm_grad * norm, grad * projection_ref[span, :], rounded.astype(F32))
        ):
            sums[4 * t + k : 4 * t + k + 1, :] = jnp.sum(value, axis=0, keepdims=True)


def middle_back(pieces, cotangents, middle, projection, mods, seq, image_rows):
    block, width = pieces[3].shape
    return run(
        functools.partial(middle_back_kernel, seq, image_rows),
        "middle_back",
        (*pieces, *cotangents, middle, projection, mods),
        [ON_CORE] * 10,
        [((block, 2 * width), F32)] + [((block, width), BF16)] * 2 + [((8, 2 * width), F32)],
        [ON_CORE] * 4,
        [],
    )


def attended_back_kernel(image_rows, *refs):
    halves, weight = (refs[:8], refs[8])
    grad_i, grad_t, proj_i, proj_t = refs[9:13]
    rows, held, image_out, text_in, text_out, semaphores = refs[13:]
    copies = Copies(semaphores)
    fetched = fetch_halves(copies, halves, rows, None)
    weights = [copies.start(weight.at[t], held.at[t]) for t in range(2)]
    text_rows = rows.shape[1] - image_rows
    for r in range(4):
        for copy in fetched[r]:
            copy.wait()
        if r == 0:
            weights[0].wait()
        span = pl.ds(r * image_rows, image_rows)
        text_in[r * text_rows : (r + 1) * text_rows, :] = rows[r, image_rows:, :]
        copies.send(rows.at[r, pl.ds(0, image_rows), :], proj_i.at[span, :])
        image_out[span, :] = dot_nn(rows[r, :image_rows, :], held[0]).astype(BF16)
    copies.send(image_out, grad_i)
    copies.send(text_in, proj_t)
    weights[1].wait()
    text_out[...] = dot_nn(text_in[...], held[1]).astype(BF16)
    copies.send(text_out, grad_t)
    copies.finish()


def attended_back(halves, weight, image_rows):
    block, width = halves[0].shape
    D, E = 2 * width, weight.shape[2]
    image, text = 4 * image_rows, 4 * (block - image_rows)
    outs = run(
        functools.partial(attended_back_kernel, image_rows),
        "attended_back",
        (*halves, weight),
        [ANYWHERE] * 9,
        [((image, E), BF16), ((text, E), BF16), ((image, D), BF16), ((text, D), BF16)],
        [ANYWHERE] * 4,
        [
            pltpu.VMEM((4, block, D), BF16),
            pltpu.VMEM(weight.shape, BF16),
            pltpu.VMEM((image, E), BF16),
            pltpu.VMEM((text, D), BF16),
            pltpu.VMEM((text, E), BF16),
        ],
        10 + 7,
    )
    return outs[:2], outs[2:]


def project_back_kernel(seq, image_rows, *refs):
    (grad_i, grad_t, weight), tokens = (refs[:3], refs[3:11])
    sums, column_sums, sent = (refs[11], refs[12], refs[13:18])
    grads, grad_text, held, given, rows, semaphores = refs[18:]
    copies = Copies(semaphores)
    weights = [copies.start(weight.at[t], held.at[t]) for t in (1, 0)]
    text_in = copies.start(grad_t, grad_text)
    image_in = copies.start(grad_i, grads)
    fetched = fetch_halves(copies, tokens, given, seq)
    text_rows = rows.shape[1] - image_rows
    weights[0].wait()
    text_in.wait()
    text = dot_nn(grad_text[...], held[1])
    column_sums[1:2, :] = jnp.sum(grad_text[...].astype(F32), axis=0, keepdims=True)
    weights[1].wait()
    image_in.wait()
    totals = [jnp.zeros((1, rows.shape[2]), F32) for _ in range(4)]
    columns = jnp.zeros((1, grads.shape[1]), F32)
    for r in (3, 1, 2, 0):
        for copy in fetched[r]:
            copy.wait()
        span = pl.ds(r * image_rows, image_rows)
        for t, low, count in ((0, 0, image_rows), (1, image_rows, text_rows)):
            if t == 0:
                back = dot_nn(grads[span, :], held[0])
                columns = columns + jnp.sum(grads[span, :].astype(F32), axis=0, keepdims=True)
            else:
                back = text[r * text_rows : (r + 1) * text_rows, :]
            norm, _ = normalize(given[r, low : low + count, :].astype(F32))
            totals[2 * t] = totals[2 * t] + jnp.sum(back, axis=0, keepdims=True)
            totals[2 * t + 1] = totals[2 * t + 1] + jnp.sum(back * norm, axis=0, keepdims=True)
            rows[r, low : low + count, :] = back.astype(BF16)
        send_block(copies, rows, sent, r, None)
    column_sums[0:1, :] = columns
    for k in range(4):
        sums[k : k + 1, :] = totals[k]
    copies.finish()


def project_back(grads, weight, tokens, seq, image_rows):
    image, W = grads[0].shape
    text = grads[1].shape[0]
    D = weight.shape[2]
    block = (image + text) // 4
    outs = run(
        functools.partial(project_back_kernel, seq, image_rows),
        "project_back",
        (*grads, weight, *tokens),
        [ANYWHERE] * 11,
        [((4, D), F32), ((2, W), F32)] + sent_shapes(block, D),
        [ON_CORE] * 2 + [ANYWHERE] * 5,
        [
            pltpu.VMEM((image, W), BF16),
            pltpu.VMEM((text, W), BF16),
            pltpu.VMEM(weight.shape, BF16),
            pltpu.VMEM((4, block, D), BF16),
            pltpu.VMEM((4, block, D), BF16),
        ],
        4 + 8 + 7,
    )
    return outs[0], outs[1], outs[2:]


def result_kernel(image_rows, *refs):
    pieces, cotangents, middles = (refs[:5], refs[5:7], refs[7:9])
    mods, bias, image_out, text_out, sums = refs[9:]
    block = middles[0].shape[0]
    for seq in range(2):
        for t, low, count in ((0, 0, image_rows), (1, image_rows, block - image_rows)):
            span = slice(low, low + count)
            value = piece_sum([piece.at[seq] for piece in pieces], low, count) + bias[t : t + 1, :]
            gate = mods[t, seq, 5:6, :]
            out = (middles[seq][span, :] + gate * value).astype(BF16)
            if t == 0:
                image_out[seq] = out
            else:
                text_out[seq] = out
            grad = both_halves(cotangents, seq, low, count)
            low_grad = (gate * grad).astype(BF16).astype(F32)
            at = 4 * seq + 2 * t
            sums[at : at + 1, :] = jnp.sum(grad * value, axis=0, keepdims=True)
            sums[at + 1 : at + 2, :] = jnp.sum(low_grad, axis=0, keepdims=True)


def result_step(pieces, cotangents, middles, mods, bias, image_rows):
    seqs, block, width = pieces[3].shape
    return run(
        functools.partial(result_kernel, image_rows),
        "result",
        (*pieces, *cotangents, *middles, mods, bias),
        [ON_CORE] * 11,
        [
            ((seqs, image_rows, 2 * width), BF16),
            ((seqs, block - image_rows, 2 * width), BF16),
            ((8, 2 * width), F32),
        ],
        [ON_CORE] * 3,
        [],
    )


def input_back_kernel(image_rows, live_text, *refs):
    pieces, tokens, grads, mods = (refs[:10], refs[10:12], refs[12:14], refs[14])
    image_out, text_out = refs[15:]
    block = grads[0].shape[0]
    for seq in range(2):
        for t, low, count in ((0, 0, image_rows), (1, image_rows, block - image_rows)):
            norm_grad = piece_sum(pieces[5 * seq : 5 * seq + 5], low, count)
            norm, inverse = normalize(both_halves(tokens, seq, low, count))
            out = grads[seq][low : low + count, :] + normalize_back(
                norm, inverse, norm_grad, mods[t, seq, 1:2, :]
            )
            if t == 0:
                image_out[seq] = out
            else:
                text_out[seq] = out[:live_text]


def input_back(pieces, tokens, grads, mods, image_rows, live_text):
    block, width = pieces[0][3].shape
    return run(
        functools.partial(input_back_kernel, image_rows, live_text),
        "input_back",
        (*pieces[0], *pieces[1], *tokens, *grads, mods),
        [ON_CORE] * 15,
        [((2, image_rows, 2 * width), F32), ((2, live_text, 2 * width), F32)],
        [ON_CORE] * 2,
        [],
    )


def match_units(batch_devices, seq_devices, per_device, group_units):
    devices = batch_devices * seq_devices
    total = devices * per_device
    part_units = total // 3
    sources, targets = ([], [])
    for seq_at in range(seq_devices):
        listed = [
            part * part_units + seq_at * group_units + k
            for part in range(3)
            for k in range(group_units)
        ]
        for place, unit in enumerate(listed):
            sources.append((unit // per_device, unit % per_device))
            targets.append(
                ((place // per_device) * seq_devices + seq_at, place % per_device)
            )
    edges = list(zip(sources, targets))
    rounds = []
    left = list(range(total))
    for _ in range(per_device):
        by_source = {}
        for e in left:
            by_source.setdefault(edges[e][0][0], []).append(e)
        taken = {}

        def place_edge(device, seen):
            for e in by_source[device]:
                target = edges[e][1][0]
                if target in seen:
                    continue
                seen.add(target)
                if target not in taken or place_edge(edges[taken[target]][0][0], seen):
                    taken[target] = e
                    return True
            return False

        for device in range(devices):
            place_edge(device, set())
        chosen = sorted(taken.values())
        rounds.append(chosen)
        left = [e for e in left if e not in chosen]
    send = np.zeros((per_device, devices), np.int32)
    land = np.zeros((per_device, devices), np.int32)
    perms = []
    for k, chosen in enumerate(rounds):
        pairs = []
        for e in chosen:
            (source, source_slot), (target, target_slot) = edges[e]
            pairs.append((source, target))
            send[k, source] = source_slot
            land[k, target] = target_slot
        perms.append(sorted(pairs))
    return perms, send, land


def move_units(units, perms, take, put, place):
    arrived = jnp.zeros_like(units)
    for k, pairs in enumerate(perms):
        slot = jnp.asarray(take[k])[place]
        moved = lax.ppermute(
            lax.dynamic_index_in_dim(units, slot, 0, keepdims=True), ("batch", "seq"), pairs
        )
        arrived = lax.dynamic_update_slice_in_dim(arrived, moved, jnp.asarray(put[k])[place], 0)
    return arrived


def gather_rows_over_batch(values):
    return lax.all_gather(values, "batch", axis=1, tiled=True)


def gather_small(values, axis):
    count = lax.axis_size(axis)
    held = values[None]
    bit = 1
    while bit < count:
        pairs = [(i, i ^ bit) for i in range(count)]
        held = jnp.concatenate([held, lax.ppermute(held, axis, pairs)])
        bit *= 2
    return jnp.take(held, jnp.bitwise_xor(lax.axis_index(axis), jnp.arange(count)), axis=0)


def after(values, *others):
    return lax.optimization_barrier((values, others))[0]


def scatter_rows_over_batch(values):
    dimension = values.ndim - 2
    return lax.psum_scatter(values, "batch", scatter_dimension=dimension, tiled=True)


def swap(values, axis):
    return lax.all_to_all(values, axis, 0, 0, tiled=True)


def swift_layer(
    image_tokens,
    text_tokens,
    conditioning,
    key_mask,
    mod_weight,
    mod_bias,
    qkv_weight,
    qv_bias,
    out_weight,
    out_bias,
    up_weight,
    up_bias,
    down_weight,
    down_bias,
    image_cotangent,
    text_cotangent,
):
    S = lax.axis_size("seq")
    B = lax.axis_size("batch")
    seq_index = lax.axis_index("seq")
    place = lax.axis_index(("batch", "seq"))
    L, image_count, D = image_tokens.shape
    live_text = text_tokens.shape[1]
    text_count = -(-live_text // 16) * 16
    pad = ((0, 0), (0, text_count - live_text), (0, 0))
    head = D // HEADS
    own_width = D // S
    half = D // 2

    unit = math.gcd(qkv_weight.shape[2], own_width)
    per_device = qkv_weight.shape[2] // unit
    perms, send, land = match_units(B, S, per_device, own_width // unit)
    back_perms = [[(target, source) for source, target in pairs] for pairs in perms]
    qkv_units = jnp.swapaxes(qkv_weight, 1, 2).reshape(2, per_device, unit, D).swapaxes(0, 1)
    qkv_mine = move_units(qkv_units, perms, send, land, place).swapaxes(0, 1)
    qkv_width = per_device * unit
    qkv_part = gather_rows_over_batch(qkv_mine.reshape(2, qkv_width, D))
    padded = jnp.concatenate([image_tokens, jnp.pad(text_tokens, pad)], axis=1)
    tokens = after((padded[..., :half], padded[..., half:]), qkv_mine)
    tokens_near = gather_near(*tokens)

    bias_widths = [array.shape[1] for array in (qv_bias, out_bias, up_bias, down_bias)]
    bias_ends = np.cumsum(bias_widths)
    own_biases = jnp.concatenate([qv_bias, out_bias, up_bias, down_bias], axis=1)
    near = gather_small(jnp.concatenate([conditioning, own_biases], axis=1), "batch")
    cond_all = near[:, :, :D].reshape(B * L, D)
    column_biases = near[:, :, D:].astype(F32)
    smooth_all = jax.nn.silu(cond_all.astype(F32)).astype(BF16)
    mod_own = (
        jnp.einsum("sd,tdf->tsf", smooth_all, mod_weight, preferred_element_type=F32)
        + mod_bias.astype(F32)[:, None, :]
    )
    mod_width = mod_own.shape[2]
    mod_sent = mod_own.reshape(2, B, L, mod_width).transpose(1, 0, 2, 3)
    mod_came = swap(after(mod_sent, tokens_near), "batch")
    out_units = jnp.swapaxes(out_weight, 1, 2).reshape(2, -1, S, own_width).transpose(2, 0, 1, 3)
    out_mine = swap(after(out_units, mod_came), "seq")
    out_columns = out_mine.shape[2]
    out_rows = out_mine.transpose(1, 0, 2, 3).reshape(2, S * out_columns, own_width)
    out_part = gather_rows_over_batch(out_rows)
    hidden_columns = up_weight.shape[2]
    small = jnp.concatenate(
        [mod_came.reshape(B, 2 * L * mod_width), column_biases.reshape(B, -1)], axis=1
    )
    small_all = gather_small(small, "seq")
    modulation = (
        small_all[:, :, : 2 * L * mod_width]
        .reshape(S, B, 2, L, mod_width)
        .transpose(2, 3, 1, 0, 4)
        .reshape(2, L, 6, D)
    )
    bias_all = (
        small_all[:, :, 2 * L * mod_width :].reshape(S, B, 2, -1).transpose(2, 1, 0, 3)
    )
    qv_full = bias_all[..., : bias_ends[0]].reshape(2, 2 * D)
    out_bias_full = bias_all[..., bias_ends[0] : bias_ends[1]].reshape(2, D)
    down_bias_full = bias_all[..., bias_ends[2] :].reshape(2, D)
    up_bias_part = (
        column_biases[:, :, bias_ends[1] : bias_ends[2]].transpose(1, 0, 2).reshape(2, -1)
    )
    first_feature = seq_index * own_width
    qkv_bias = jnp.concatenate(
        [
            lax.dynamic_slice_in_dim(qv_full, first_feature, own_width, 1),
            jnp.zeros((2, own_width), F32),
            lax.dynamic_slice_in_dim(qv_full, D + first_feature, own_width, 1),
        ],
        axis=1,
    )

    tokens_all = gather_far(*tokens, tokens_near)
    padded = jnp.concatenate([image_cotangent, jnp.pad(text_cotangent, pad)], axis=1)
    cotangents = (padded[..., :half], padded[..., half:])
    near_grads = gather_near(*after(cotangents, tokens_all, small_all))
    up_part = gather_rows_over_batch(after(jnp.swapaxes(up_weight, 1, 2), tokens_all))
    down_part = gather_rows_over_batch(after(jnp.swapaxes(down_weight, 1, 2), tokens_all))

    order = jnp.bitwise_xor(seq_index, jnp.arange(S))
    image_keys = jnp.take(
        key_mask[:, : S * image_count].reshape(L, S, image_count), order, axis=1
    )
    text_keys = jnp.take(
        key_mask[:, S * image_count :].reshape(L, S, live_text), order, axis=1
    )
    text_keys = jnp.pad(text_keys, ((0, 0), (0, 0), (0, text_count - live_text)))
    live = jnp.concatenate([image_keys.reshape(L, -1), text_keys.reshape(L, -1)], axis=1) > 0
    key_bias = jnp.where(live, 0.0, DEAD).astype(F32)
    floors = jnp.where(jnp.all(key_mask > 0, axis=1), -3e38, FLOOR_SCORE * LOG2E).astype(F32)
    floors = floors.reshape(L, 1, 1)
    key_bias = jnp.broadcast_to(key_bias[:, :, None], (*key_bias.shape, 128))

    kept = []
    first = project(tokens_all, qkv_part, modulation, qkv_bias, 0, image_count)
    attended = attention(first[0], first[1], key_bias[0], floors[0], head)
    attended, logs = (attended[:2], attended[2:])
    attended = after(attended, near_grads)
    parts = partial_sums([attended], out_part, dot_nt, D, image_count)
    kept.append((first, attended, logs, parts))
    again = after(tokens_all, parts)
    first = project(again, qkv_part, modulation, qkv_bias, 1, image_count)
    attended = attention(first[0], first[1], key_bias[1], floors[1], head)
    attended, logs = (attended[:2], attended[2:])
    cotangents_all = gather_far(*cotangents, after(near_grads, kept[0][0]))
    out_first = scatter_first(kept[0][3])
    attended = after(attended, cotangents_all, out_first)
    parts = partial_sums([attended], out_part, dot_nt, D, image_count)
    kept.append((first, attended, logs, parts))
    firsts, attendeds, logs, out_halves = zip(*kept)
    steps, seconds = ([], [])
    for s in range(L):
        steps.append(
            middle_step(
                scatter_last(out_halves[s], out_first if s == 0 else scatter_first(out_halves[s])),
                tokens,
                modulation,
                out_bias_full,
                s,
                image_count,
            )
        )
        seconds.append(gather_halves(*steps[s][2:]))
    hidden = []
    for s in range(L):
        halves = after(seconds[s], hidden[-1]) if s else seconds[s]
        hidden.append(
            hidden_step(
                halves, cotangents_all, up_part, up_bias_part, modulation, s, image_count
            )
        )
    acts, slopes, grads, norms = [[step[i : i + 2] for step in hidden] for i in (0, 2, 4, 6)]

    down_sum = outer_sums(acts, grads, 256)
    down_came = scatter_rows_over_batch(down_sum)
    pres, bias_sums, norm2_halves = ([], [], [])
    gate = down_sum
    for s in range(L):
        pre, sums, halves = hidden_back(
            after(grads[s], gate), slopes[s], down_part, up_part, image_count
        )
        gate = halves
        pres.append(pre)
        bias_sums.append(sums)
        norm2_halves.append(halves)
    up_bias_sum = sum(bias_sums)
    norm2_first = [scatter_first(halves) for halves in norm2_halves]
    norm2_pieces = [
        scatter_last(halves, first) for halves, first in zip(norm2_halves, norm2_first)
    ]
    up_sum = outer_sums(after(pres, gate, norm2_first[0]), norms, 256)
    up_came = scatter_rows_over_batch(up_sum)

    backs, projs = ([], [])
    backs.append(
        middle_back(
            after(norm2_pieces[0], up_sum), cotangents, *steps[0][1::-1], modulation, 0, image_count
        )
    )
    proj_near = gather_near(*backs[0][1:3])
    projs.append(gather_far(*backs[0][1:3], proj_near))
    mlp_halves = partial_sums(
        after(acts, backs[0], norm2_first[1]), down_part, dot_nn, D, image_count
    )
    backs.append(
        middle_back(
            after(norm2_pieces[1], mlp_halves, proj_near),
            cotangents,
            *steps[1][1::-1],
            modulation,
            1,
            image_count,
        )
    )
    projs.append(gather_halves(*backs[1][1:3]))
    grad0, proj0 = attended_back(
        after(projs[0], backs[1], down_came), out_part, image_count
    )
    qkv_grad0 = attention_back(
        *firsts[0][:2], *attendeds[0], *logs[0], *grad0, key_bias[0], head
    )
    grad1, proj1 = attended_back(after(projs[1], qkv_grad0), out_part, image_count)
    mlp_first = scatter_first(after(mlp_halves, projs[1]))
    out_sum = outer_sums([proj0, proj1], attendeds, 256)
    sums0, columns0, halves0 = project_back(
        after(qkv_grad0, out_sum), qkv_part, tokens_all, 0, image_count
    )
    out_came = scatter_rows_over_batch(after(out_sum, halves0))
    norm1_first = scatter_first(halves0)
    grad1 = after(grad1, halves0, up_came, mlp_first)
    qkv_grad1 = attention_back(
        *firsts[1][:2], *attendeds[1], *logs[1], *grad1, key_bias[1], head
    )
    mlp_pieces = scatter_last(mlp_halves, mlp_first)
    qkv_grad1 = after(qkv_grad1, norm1_first)
    qkv_sum = outer_sums(
        [qkv_grad0, qkv_grad1], [first[2:] for first in firsts], 128 if qkv_width % 256 else 256
    )
    qkv_came = scatter_rows_over_batch(after(qkv_sum, out_came))
    sums1, columns1, halves1 = project_back(
        after(qkv_grad1, qkv_sum), qkv_part, tokens_all, 1, image_count
    )
    norm1_pieces = [scatter_last(halves0, norm1_first), scatter_halves(halves1)]
    image_out, text_out, result_sums = result_step(
        after(mlp_pieces, halves1),
        cotangents,
        [step[1] for step in steps],
        modulation,
        down_bias_full,
        image_count,
    )
    qkv_home = move_units(
        qkv_came.reshape(2, per_device, unit, D).swapaxes(0, 1), back_perms, land, send, place
    )
    out_home = swap(out_came.reshape(2, S, out_columns, own_width).swapaxes(0, 1), "seq")
    qkv_weight_grad = qkv_home.swapaxes(0, 1).reshape(2, -1, D).swapaxes(1, 2).astype(F32)
    out_weight_grad = (
        out_home.transpose(1, 2, 0, 3).reshape(2, out_columns, D).swapaxes(1, 2).astype(F32)
    )
    up_weight_grad = up_came.swapaxes(1, 2).astype(F32)
    down_weight_grad = down_came.swapaxes(1, 2).astype(F32)
    image_grad, text_grad = input_back(
        norm1_pieces, tokens, [back[0] for back in backs], modulation, image_count, live_text
    )

    first_sums = jnp.stack([sums0, sums1]).reshape(L, 2, 2, D)
    second_sums = jnp.stack([back[3] for back in backs]).reshape(L, 2, 4, D)
    result_sums = result_sums.reshape(L, 2, 2, D)
    mod_rows = jnp.concatenate(
        [
            first_sums,
            second_sums[:, :, 2:3],
            second_sums[:, :, :2],
            result_sums[:, :, :1],
        ],
        axis=2,
    ).swapaxes(0, 1)
    mod_rows = mod_rows.reshape(2, L, B, S, mod_width).transpose(3, 2, 0, 1, 4)
    out_bias_sum = jnp.sum(second_sums[:, :, 3], axis=0)
    down_bias_sum = jnp.sum(result_sums[:, :, 1], axis=0)
    column_sums = columns0 + columns1
    qv_bias_sum = jnp.zeros((2, 2 * D), F32)
    for part, column in ((0, 0), (1, 2 * own_width)):
        qv_bias_sum = lax.dynamic_update_slice_in_dim(
            qv_bias_sum, column_sums[:, column : column + own_width], part * D + first_feature, 1
        )
    up_bias_rows = lax.dynamic_update_slice_in_dim(
        jnp.zeros((2, B, S, hidden_columns), F32),
        up_bias_sum.reshape(2, B, 1, hidden_columns),
        seq_index,
        2,
    )
    bias_rows = jnp.concatenate(
        [
            qv_bias_sum.reshape(2, B, S, -1),
            out_bias_sum.reshape(2, B, S, -1),
            up_bias_rows,
            down_bias_sum.reshape(2, B, S, -1),
        ],
        axis=3,
    ).transpose(2, 1, 0, 3)
    packed = jnp.concatenate(
        [mod_rows.reshape(S, B, -1), bias_rows.reshape(S, B, -1)], axis=2
    )
    packed = jnp.sum(swap(packed, "seq"), axis=0)
    packed = swap(packed, "batch")
    mod_mine = (
        packed[:, : 2 * L * mod_width]
        .reshape(B, 2, L, mod_width)
        .transpose(1, 0, 2, 3)
        .reshape(2, B * L, mod_width)
        .astype(BF16)
    )
    bias_mine = jnp.sum(packed[:, 2 * L * mod_width :], axis=0).reshape(2, -1)
    qv_bias_grad, out_bias_grad, up_bias_grad, down_bias_grad = jnp.split(
        bias_mine, bias_ends[:3], axis=1
    )
    mod_weight_grad = jnp.einsum(
        "sd,tsf->tdf", smooth_all, mod_mine, preferred_element_type=F32
    )
    mod_bias_grad = jnp.sum(mod_mine.astype(F32), axis=1)
    smooth_part = jnp.einsum("tsf,tdf->sd", mod_mine, mod_weight, preferred_element_type=F32)
    smooth_grad = jnp.sum(swap(smooth_part.reshape(B, L, D), "batch"), axis=0)
    smooth_grad = smooth_grad + flip(smooth_grad, 1)
    smooth_grad = smooth_grad + flip(smooth_grad, 2)
    cond_grad = jax.vjp(jax.nn.silu, conditioning.astype(F32))[1](smooth_grad)[0]
    return (
        image_out,
        text_out[:, :live_text],
        image_grad,
        text_grad,
        cond_grad,
        mod_weight_grad,
        mod_bias_grad,
        qkv_weight_grad,
        qv_bias_grad,
        out_weight_grad,
        out_bias_grad,
        up_weight_grad,
        up_bias_grad,
        down_weight_grad,
        down_bias_grad,
    )


def choose_layer(mesh):
    if mesh.shape["seq"] == 4 and HEADS % 8 == 0:
        return swift_layer
    return general_layer


def solution(mesh):
    layer = choose_layer(mesh)
    return jax.shard_map(
        layer,
        mesh=mesh,
        in_specs=(
            P("batch", "seq", None),
            P("batch", "seq", None),
            P("batch", None),
            P("batch", None),
            P(None, None, ("batch", "seq")),
            P(None, ("batch", "seq")),
            P(None, None, ("batch", "seq")),
            P(None, ("batch", "seq")),
            P(None, None, ("batch", "seq")),
            P(None, ("batch", "seq")),
            P(None, None, ("batch", "seq")),
            P(None, ("batch", "seq")),
            P(None, None, ("batch", "seq")),
            P(None, ("batch", "seq")),
            P("batch", "seq", None),
            P("batch", "seq", None),
        ),
        out_specs=(
            P("batch", "seq", None),
            P("batch", "seq", None),
            P("batch", "seq", None),
            P("batch", "seq", None),
            P("batch", None),
            P(None, None, ("batch", "seq")),
            P(None, ("batch", "seq")),
            P(None, None, ("batch", "seq")),
            P(None, ("batch", "seq")),
            P(None, None, ("batch", "seq")),
            P(None, ("batch", "seq")),
            P(None, None, ("batch", "seq")),
            P(None, ("batch", "seq")),
            P(None, None, ("batch", "seq")),
            P(None, ("batch", "seq")),
        ),
        check_vma=False,
    )
```

```python
import functools
import math

import jax
import jax.numpy as jnp
import numpy as np
from jax import lax
from jax.experimental import pallas as pl
from jax.experimental.pallas import tpu as pltpu
from jax.sharding import PartitionSpec as P

HEADS = 24


NORM_EPSILON = 1e-06
FLOOR_SCORE = -10000.0


def modulate(tokens, shift_vec, scale_vec):
    row_mean = jnp.mean(tokens, axis=-1, keepdims=True)
    centered = tokens - row_mean
    row_var = jnp.mean(centered * centered, axis=-1, keepdims=True)
    return (
        centered * lax.rsqrt(row_var + NORM_EPSILON) * (1.0 + scale_vec[:, None, :])
        + shift_vec[:, None, :]
    )


def gelu_tanh(values):
    return jax.nn.gelu(values, approximate=True)


def unmix_columns(values, seq_devices, batch_devices):
    array_shape = values.shape
    piece_width = array_shape[-1] // (seq_devices * batch_devices)
    grid_view = values.reshape(array_shape[:-1] + (seq_devices, batch_devices, piece_width))
    return jnp.swapaxes(grid_view, -3, -2).reshape(array_shape)


def remix_columns(values, seq_devices, batch_devices):
    array_shape = values.shape
    piece_width = array_shape[-1] // (seq_devices * batch_devices)
    grid_view = values.reshape(array_shape[:-1] + (batch_devices, seq_devices, piece_width))
    return jnp.swapaxes(grid_view, -3, -2).reshape(array_shape)


def fetch_columns(
    up_weight,
    down_weight,
    mod_weight,
    qkv_weight,
    out_weight,
    up_bias,
    mod_bias,
    qv_bias,
    out_bias,
    down_bias,
):
    return (
        lax.all_gather(up_weight, "batch", axis=2, tiled=True),
        lax.all_gather(down_weight, "batch", axis=2, tiled=True),
        lax.all_gather(mod_weight, "batch", axis=2, tiled=True),
        lax.all_gather(qkv_weight, "batch", axis=2, tiled=True),
        lax.all_gather(out_weight, "batch", axis=2, tiled=True),
        lax.all_gather(up_bias, "batch", axis=1, tiled=True),
        lax.all_gather(mod_bias, "batch", axis=1, tiled=True),
        lax.all_gather(qv_bias, "batch", axis=1, tiled=True),
        lax.all_gather(out_bias, "batch", axis=1, tiled=True),
        lax.all_gather(down_bias, "batch", axis=1, tiled=True),
    )


def fetch_modulation(mod_part, mod_bias_part):
    return (
        lax.all_gather(mod_part, "seq", axis=2, tiled=True),
        lax.all_gather(mod_bias_part, "seq", axis=1, tiled=True),
    )


def gather_rows(first, second):
    return (
        lax.all_gather(first, "seq", axis=1, tiled=True),
        lax.all_gather(second, "seq", axis=1, tiled=True),
    )


def sum_rows(first, second, seq_devices):
    local_seqs, first_rows, width = first.shape
    first_local = first_rows // seq_devices
    second_local = second.shape[1] // seq_devices
    joined = jnp.concatenate(
        [
            first.reshape(local_seqs, seq_devices, first_local, width),
            second.reshape(local_seqs, seq_devices, second_local, width),
        ],
        axis=2,
    )
    joined = joined.reshape(local_seqs, seq_devices * (first_local + second_local), width)
    total = lax.psum_scatter(joined, "seq", scatter_dimension=1, tiled=True)
    return (total[:, :first_local], total[:, first_local:])


def to_rows(first, second):
    return (
        lax.all_to_all(first, "seq", split_axis=1, concat_axis=2, tiled=True),
        lax.all_to_all(second, "seq", split_axis=1, concat_axis=2, tiled=True),
    )


def to_columns(first, second):
    return (
        lax.all_to_all(first, "seq", split_axis=2, concat_axis=1, tiled=True),
        lax.all_to_all(second, "seq", split_axis=2, concat_axis=1, tiled=True),
    )


def own_block(values, seq_index, seq_devices):
    width = values.shape[1] // seq_devices
    return lax.dynamic_slice_in_dim(values, seq_index * width, width, 1)


def general_layer(
    image_tokens,
    text_tokens,
    conditioning,
    key_mask,
    mod_weight,
    mod_bias,
    qkv_weight,
    qv_bias,
    out_weight,
    out_bias,
    up_weight,
    up_bias,
    down_weight,
    down_bias,
    image_cotangent,
    text_cotangent,
):
    seq_devices = lax.axis_size("seq")
    batch_devices = lax.axis_size("batch")
    seq_index = lax.axis_index("seq")
    local_seqs, image_count, model_width = image_tokens.shape
    text_count = text_tokens.shape[1]
    block_rows = image_count + text_count
    key_count = block_rows * seq_devices
    head_size = model_width // HEADS
    factor = 1.0 / math.sqrt(head_size)
    inputs = (image_tokens.astype(jnp.float32), text_tokens.astype(jnp.float32))
    cotangents = (image_cotangent.astype(jnp.float32), text_cotangent.astype(jnp.float32))
    row_spans = ((0, image_count), (image_count, block_rows))
    image_keys = key_mask[:, : image_count * seq_devices].reshape(
        local_seqs, seq_devices, image_count
    )
    text_keys = key_mask[:, image_count * seq_devices :].reshape(
        local_seqs, seq_devices, text_count
    )
    key_live = (
        jnp.concatenate([image_keys, text_keys], axis=2).reshape(local_seqs, key_count) > 0
    )[:, None, None, :]
    cond_float = conditioning.astype(jnp.float32)
    smooth = jax.nn.silu(cond_float).astype(jnp.bfloat16)
    fetched = fetch_columns(
        up_weight,
        down_weight,
        mod_weight,
        qkv_weight,
        out_weight,
        up_bias,
        mod_bias,
        qv_bias,
        out_bias,
        down_bias,
    )
    (
        up_part,
        down_part,
        mod_part,
        qkv_part,
        out_part,
        up_bias_part,
        mod_bias_part,
        qv_part,
        out_bias_part,
        down_bias_part,
    ) = fetched
    mod_full, mod_bias_full = fetch_modulation(mod_part, mod_bias_part)
    mixed_mod = (
        jnp.einsum("sd,tdf->tsf", smooth, mod_full, preferred_element_type=jnp.float32)
        + mod_bias_full.astype(jnp.float32)[:, None, :]
    )
    modulation = unmix_columns(mixed_mod, seq_devices, batch_devices).reshape(
        2, local_seqs, 6, model_width
    )
    first_norms = []
    for modality in range(2):
        pieces = modulation[modality]
        first_norms.append(
            modulate(inputs[modality], pieces[:, 0], pieces[:, 1]).astype(jnp.bfloat16)
        )
    norm_image_all, norm_text_all, qv_seq, out_bias_seq, down_bias_seq = (
        lax.all_gather(first_norms[0], "seq", axis=1, tiled=True),
        lax.all_gather(first_norms[1], "seq", axis=1, tiled=True),
        lax.all_gather(qv_part, "seq", axis=1, tiled=True),
        lax.all_gather(out_bias_part, "seq", axis=1, tiled=True),
        lax.all_gather(down_bias_part, "seq", axis=1, tiled=True),
    )
    first_all = (norm_image_all, norm_text_all)
    qv_full = unmix_columns(qv_seq, seq_devices, batch_devices).astype(jnp.float32)
    out_bias_full = unmix_columns(out_bias_seq, seq_devices, batch_devices).astype(jnp.float32)
    down_bias_full = unmix_columns(down_bias_seq, seq_devices, batch_devices).astype(jnp.float32)
    qkv_cols = [
        jnp.einsum(
            "srd,df->srf",
            first_all[modality],
            qkv_part[modality],
            preferred_element_type=jnp.float32,
        )
        for modality in range(2)
    ]
    qkv_rows = to_rows(qkv_cols[0], qkv_cols[1])
    queries, keyvals = ([], [])
    for modality in range(2):
        projected = unmix_columns(qkv_rows[modality], seq_devices, batch_devices)
        qv_vector = qv_full[modality]
        queries.append(
            (projected[..., :model_width] + qv_vector[:model_width]).astype(jnp.bfloat16)
        )
        value_shift = jnp.concatenate(
            [jnp.zeros((model_width,), jnp.float32), qv_vector[model_width:]]
        )
        keyvals.append((projected[..., model_width:] + value_shift).astype(jnp.bfloat16))
    joined_query = jnp.concatenate(queries, axis=1)
    joined_keyval = jnp.concatenate(keyvals, axis=1)
    all_keyval = lax.all_gather(joined_keyval, "seq", axis=1, tiled=True)
    query_heads = joined_query.reshape(local_seqs, block_rows, HEADS, head_size)
    key_heads = all_keyval[..., :model_width].reshape(local_seqs, key_count, HEADS, head_size)
    value_heads = all_keyval[..., model_width:].reshape(local_seqs, key_count, HEADS, head_size)
    scores = (
        jnp.einsum("sqhe,skhe->shqk", query_heads, key_heads, preferred_element_type=jnp.float32)
        * factor
    )
    row_max = jnp.max(jnp.where(key_live, scores, FLOOR_SCORE), axis=-1, keepdims=True)
    exp_terms = jnp.exp(jnp.where(key_live, scores - row_max, FLOOR_SCORE))
    denominator = jnp.maximum(jnp.sum(exp_terms, axis=-1, keepdims=True), 1.0)
    prob_low = (exp_terms / denominator).astype(jnp.bfloat16)
    logsum = row_max + jnp.log(denominator)
    attended = jnp.einsum(
        "shqk,skhe->sqhe", prob_low, value_heads, preferred_element_type=jnp.float32
    )
    attended = attended.reshape(local_seqs, block_rows, model_width).astype(jnp.bfloat16)
    attended_all = gather_rows(attended[:, :image_count], attended[:, image_count:])
    out_cols = [
        jnp.einsum(
            "srd,df->srf",
            attended_all[modality],
            out_part[modality],
            preferred_element_type=jnp.float32,
        )
        for modality in range(2)
    ]
    out_rows = to_rows(out_cols[0], out_cols[1])
    projections, middles, second_norms = ([], [], [])
    for modality in range(2):
        pieces = modulation[modality]
        projection = (
            unmix_columns(out_rows[modality], seq_devices, batch_devices) + out_bias_full[modality]
        )
        middle = inputs[modality] + pieces[:, 2][:, None, :] * projection
        second_norms.append(modulate(middle, pieces[:, 3], pieces[:, 4]).astype(jnp.bfloat16))
        projections.append(projection)
        middles.append(middle)
    group_rows = gather_rows(second_norms[0], second_norms[1])
    hidden_pre, hidden_act, partials = ([], [], [])
    for modality in range(2):
        pre_values = jnp.einsum(
            "srd,df->srf",
            group_rows[modality],
            up_part[modality],
            preferred_element_type=jnp.float32,
        ) + up_bias_part[modality].astype(jnp.float32)
        act_values = gelu_tanh(pre_values).astype(jnp.bfloat16)
        partials.append(
            jnp.einsum(
                "srf,df->srd", act_values, down_part[modality], preferred_element_type=jnp.float32
            )
        )
        hidden_pre.append(pre_values)
        hidden_act.append(act_values)
    mlp_rows = sum_rows(partials[0], partials[1], seq_devices)
    mlp_outs, results = ([], [])
    for modality in range(2):
        pieces = modulation[modality]
        mlp_value = mlp_rows[modality] + down_bias_full[modality]
        results.append(
            (middles[modality] + pieces[:, 5][:, None, :] * mlp_value).astype(jnp.bfloat16)
        )
        mlp_outs.append(mlp_value)
    fetched_back = fetch_columns(
        up_weight,
        down_weight,
        mod_weight,
        qkv_weight,
        out_weight,
        up_bias,
        mod_bias,
        qv_bias,
        out_bias,
        down_bias,
    )
    up_back, down_back, mod_back, qkv_back, out_back = (
        fetched_back[0],
        fetched_back[1],
        fetched_back[2],
        fetched_back[3],
        fetched_back[4],
    )
    mod_bias_back = fetched_back[6]
    mlp_grads, gate_twos, down_bias_grads = ([], [], [])
    for modality in range(2):
        pieces = modulation[modality]
        mlp_grad = (pieces[:, 5][:, None, :] * cotangents[modality]).astype(jnp.bfloat16)
        gate_twos.append(jnp.sum(cotangents[modality] * mlp_outs[modality], axis=1))
        down_bias_grads.append(jnp.sum(mlp_grad.astype(jnp.float32), axis=(0, 1)))
        mlp_grads.append(mlp_grad)
    group_grads = gather_rows(mlp_grads[0], mlp_grads[1])
    down_grads, up_grads, up_bias_grads, norm_partials = ([], [], [], [])
    for modality in range(2):
        down_grads.append(
            jnp.einsum(
                "srd,srf->df",
                group_grads[modality],
                hidden_act[modality],
                preferred_element_type=jnp.float32,
            )
        )
        act_grad = jnp.einsum(
            "srd,df->srf",
            group_grads[modality],
            down_back[modality],
            preferred_element_type=jnp.float32,
        )
        pullback = jax.vjp(gelu_tanh, hidden_pre[modality])[1]
        pre_grad = pullback(act_grad)[0].astype(jnp.bfloat16)
        up_grads.append(
            jnp.einsum(
                "srd,srf->df", group_rows[modality], pre_grad, preferred_element_type=jnp.float32
            )
        )
        up_bias_grads.append(jnp.sum(pre_grad.astype(jnp.float32), axis=(0, 1)))
        norm_partials.append(
            jnp.einsum(
                "srf,df->srd", pre_grad, up_back[modality], preferred_element_type=jnp.float32
            )
        )
    norm_grads = sum_rows(norm_partials[0], norm_partials[1], seq_devices)
    middle_grads, shift_twos, scale_twos, gate_ones, out_bias_grads, proj_grads = (
        [],
        [],
        [],
        [],
        [],
        [],
    )
    for modality in range(2):
        pieces = modulation[modality]
        pullback = jax.vjp(modulate, middles[modality], pieces[:, 3], pieces[:, 4])[1]
        middle_part, shift_two, scale_two = pullback(norm_grads[modality])
        middle_grad = cotangents[modality] + middle_part
        proj_grad = (pieces[:, 2][:, None, :] * middle_grad).astype(jnp.bfloat16)
        gate_ones.append(jnp.sum(middle_grad * projections[modality], axis=1))
        out_bias_grads.append(jnp.sum(proj_grad.astype(jnp.float32), axis=(0, 1)))
        proj_grads.append(remix_columns(proj_grad, seq_devices, batch_devices))
        middle_grads.append(middle_grad)
        shift_twos.append(shift_two)
        scale_twos.append(scale_two)
    proj_cols = to_columns(proj_grads[0], proj_grads[1])
    out_grads, attended_partials = ([], [])
    for modality in range(2):
        out_grads.append(
            jnp.einsum(
                "srd,srf->df",
                attended_all[modality],
                proj_cols[modality],
                preferred_element_type=jnp.float32,
            )
        )
        attended_partials.append(
            jnp.einsum(
                "srf,df->srd",
                proj_cols[modality],
                out_back[modality],
                preferred_element_type=jnp.float32,
            )
        )
    attended_sums = sum_rows(attended_partials[0], attended_partials[1], seq_devices)
    attended_grad = jnp.concatenate([attended_sums[0], attended_sums[1]], axis=1).astype(
        jnp.bfloat16
    )
    grad_heads = attended_grad.reshape(local_seqs, block_rows, HEADS, head_size)
    scores_again = (
        jnp.einsum("sqhe,skhe->shqk", query_heads, key_heads, preferred_element_type=jnp.float32)
        * factor
    )
    probs_again = jnp.exp(jnp.where(key_live, scores_again - logsum, FLOOR_SCORE))
    probs_again_low = probs_again.astype(jnp.bfloat16)
    prob_grad = jnp.einsum(
        "sqhe,skhe->shqk", grad_heads, value_heads, preferred_element_type=jnp.float32
    )
    inner_sum = jnp.sum(probs_again * prob_grad, axis=-1, keepdims=True)
    score_grad = (probs_again * (prob_grad - inner_sum)).astype(jnp.bfloat16)
    query_grad = (
        jnp.einsum("shqk,skhe->sqhe", score_grad, key_heads, preferred_element_type=jnp.float32)
        * factor
    )
    query_grad = query_grad.reshape(local_seqs, block_rows, model_width).astype(jnp.bfloat16)
    key_grad = (
        jnp.einsum("shqk,sqhe->skhe", score_grad, query_heads, preferred_element_type=jnp.float32)
        * factor
    )
    value_grad = jnp.einsum(
        "shqk,sqhe->skhe", probs_again_low, grad_heads, preferred_element_type=jnp.float32
    )
    key_rows, value_rows = (
        lax.psum_scatter(
            key_grad.reshape(local_seqs, key_count, model_width),
            "seq",
            scatter_dimension=1,
            tiled=True,
        ),
        lax.psum_scatter(
            value_grad.reshape(local_seqs, key_count, model_width),
            "seq",
            scatter_dimension=1,
            tiled=True,
        ),
    )
    key_rows = key_rows.astype(jnp.bfloat16)
    value_rows = value_rows.astype(jnp.bfloat16)
    qv_bias_grads, joined_grads = ([], [])
    for modality in range(2):
        row_start, row_stop = row_spans[modality]
        query_part = query_grad[:, row_start:row_stop]
        value_part = value_rows[:, row_start:row_stop]
        joined_grad = jnp.concatenate(
            [query_part, key_rows[:, row_start:row_stop], value_part], axis=-1
        )
        qv_bias_grads.append(
            jnp.concatenate(
                [
                    jnp.sum(query_part.astype(jnp.float32), axis=(0, 1)),
                    jnp.sum(value_part.astype(jnp.float32), axis=(0, 1)),
                ]
            )
        )
        joined_grads.append(remix_columns(joined_grad, seq_devices, batch_devices))
    qkv_grad_cols = to_columns(joined_grads[0], joined_grads[1])
    qkv_grads, first_partials = ([], [])
    for modality in range(2):
        qkv_grads.append(
            jnp.einsum(
                "srd,srf->df",
                first_all[modality],
                qkv_grad_cols[modality],
                preferred_element_type=jnp.float32,
            )
        )
        first_partials.append(
            jnp.einsum(
                "srf,df->srd",
                qkv_grad_cols[modality],
                qkv_back[modality],
                preferred_element_type=jnp.float32,
            )
        )
    first_grads = sum_rows(first_partials[0], first_partials[1], seq_devices)
    input_grads, mod_partials = ([], [])
    for modality in range(2):
        pieces = modulation[modality]
        pullback = jax.vjp(modulate, inputs[modality], pieces[:, 0], pieces[:, 1])[1]
        input_part, shift_one, scale_one = pullback(first_grads[modality])
        input_grads.append(middle_grads[modality] + input_part)
        stacked = jnp.stack(
            [
                shift_one,
                scale_one,
                gate_ones[modality],
                shift_twos[modality],
                scale_twos[modality],
                gate_twos[modality],
            ],
            axis=1,
        )
        mod_partials.append(stacked.reshape(local_seqs, 6 * model_width))
    qv_mixed = remix_columns(jnp.stack(qv_bias_grads), seq_devices, batch_devices)
    out_bias_mixed = remix_columns(jnp.stack(out_bias_grads), seq_devices, batch_devices)
    down_bias_mixed = remix_columns(jnp.stack(down_bias_grads), seq_devices, batch_devices)
    mod_sum, qv_summed, out_bias_summed, down_bias_summed = lax.psum(
        (jnp.stack(mod_partials), qv_mixed, out_bias_mixed, down_bias_mixed), "seq"
    )
    mod_low = mod_sum.astype(jnp.bfloat16)
    mod_mixed = remix_columns(mod_low, seq_devices, batch_devices)
    columns = mod_part.shape[2]
    own_columns = lax.dynamic_slice_in_dim(mod_mixed, seq_index * columns, columns, 2)
    mod_grad = jnp.einsum("sd,tsf->tdf", smooth, own_columns, preferred_element_type=jnp.float32)
    mod_bias_grad = jnp.sum(own_columns.astype(jnp.float32), axis=1)
    mod_again = fetch_modulation(mod_back, mod_bias_back)[0]
    smooth_grad = jnp.einsum(
        "tsf,tdf->sd", mod_mixed, mod_again, preferred_element_type=jnp.float32
    )
    cond_pullback = jax.vjp(jax.nn.silu, cond_float)[1]
    cond_grad = cond_pullback(smooth_grad)[0]
    qv_own = own_block(qv_summed, seq_index, seq_devices)
    out_bias_own = own_block(out_bias_summed, seq_index, seq_devices)
    down_bias_own = own_block(down_bias_summed, seq_index, seq_devices)
    column_grads = (
        lax.psum_scatter(jnp.stack(up_grads), "batch", scatter_dimension=2, tiled=True),
        lax.psum_scatter(jnp.stack(down_grads), "batch", scatter_dimension=2, tiled=True),
        lax.psum_scatter(mod_grad, "batch", scatter_dimension=2, tiled=True),
        lax.psum_scatter(jnp.stack(qkv_grads), "batch", scatter_dimension=2, tiled=True),
        lax.psum_scatter(jnp.stack(out_grads), "batch", scatter_dimension=2, tiled=True),
        lax.psum_scatter(jnp.stack(up_bias_grads), "batch", scatter_dimension=1, tiled=True),
        lax.psum_scatter(mod_bias_grad, "batch", scatter_dimension=1, tiled=True),
        lax.psum_scatter(qv_own, "batch", scatter_dimension=1, tiled=True),
        lax.psum_scatter(out_bias_own, "batch", scatter_dimension=1, tiled=True),
        lax.psum_scatter(down_bias_own, "batch", scatter_dimension=1, tiled=True),
    )
    return (
        results[0],
        results[1],
        input_grads[0],
        input_grads[1],
        cond_grad,
        column_grads[2],
        column_grads[6],
        column_grads[3],
        column_grads[7],
        column_grads[4],
        column_grads[8],
        column_grads[0],
        column_grads[5],
        column_grads[1],
        column_grads[9],
    )


LOG2E = 1.4426950408889634
DEAD = -1e30
BF16 = jnp.bfloat16
F32 = jnp.float32


def dot_nt(a, b):
    return lax.dot_general(a, b, (((1,), (1,)), ((), ())), preferred_element_type=F32)


def dot_nn(a, b):
    return lax.dot_general(a, b, (((1,), (0,)), ((), ())), preferred_element_type=F32)


def dot_tn(a, b):
    return lax.dot_general(a, b, (((0,), (0,)), ((), ())), preferred_element_type=F32)


WEIGHT = {
    "attention": 0.17,
    "attention_back": 0.32,
    "project": 0.13,
    "partial_sums": 0.05,
    "middle": 0.05,
    "hidden": 0.18,
    "outer_sums": 0.18,
    "hidden_back": 0.2,
    "middle_back": 0.07,
    "attended_back": 0.06,
    "project_back": 0.12,
    "result": 0.07,
    "input_back": 0.09,
}


def lanes_of(columns, rows, width):
    lane = lax.broadcasted_iota(jnp.int32, (rows, width), 1)
    out = jnp.zeros((rows, width), F32)
    for k, column in enumerate(columns):
        out = jnp.where(lane == k, column, out)
    return out.astype(BF16)


def three_parts(column):
    high = column.astype(BF16).astype(F32)
    rest = column - high
    mid = rest.astype(BF16).astype(F32)
    return [high, mid, rest - mid]


def attention_kernel(
    query_rows, scale, head, bias_ref, floor_ref, qi, qt, ki, kt, vi, vt, oi, ot, li, lt, keys, values
):
    image_rows = qi.shape[0]
    rows = keys.shape[1]
    floor = floor_ref[0, 0]
    key_side = lanes_of([bias_ref[:, 0:1]], rows, head)
    value_side = lanes_of([1.0], rows, head)
    for side in range(2):
        lanes = slice(side * head, (side + 1) * head)
        for ref, extra, first, second in (
            (keys, key_side, ki, kt),
            (values, value_side, vi, vt),
        ):
            ref[side, :image_rows, :] = jnp.concatenate(
                [first[:, lanes], extra[:image_rows]], axis=1
            )
            ref[side, image_rows:, :] = jnp.concatenate(
                [second[:, lanes], extra[image_rows:]], axis=1
            )
    spans = [(qi, oi, li, start, query_rows) for start in range(0, image_rows, query_rows)]
    spans.append((qt, ot, lt, 0, qt.shape[0]))
    steps = [(*span, side) for span in spans for side in range(2)]

    def score(step):
        source, _, _, start, size, side = step
        query = source[start : start + size, side * head : (side + 1) * head]
        query = jnp.concatenate([query, lanes_of([1.0], size, head)], axis=1)
        return dot_nt(query, keys[side])

    ahead = score(steps[0])
    for at, (_, target, logs, start, size, side) in enumerate(steps):
        scores = ahead
        if at + 1 < len(steps):
            ahead = score(steps[at + 1])
        top = jnp.maximum(jnp.max(scores, axis=1, keepdims=True) * scale, floor)
        exps = jnp.exp2(scores * scale - top).astype(BF16)
        product = dot_nn(exps, values[side])
        total = jnp.maximum(product[:, head : head + 1], 1.0)
        span = slice(start, start + size)
        lanes = slice(side * head, (side + 1) * head)
        target[span, lanes] = (product[:, :head] * (1.0 / total)).astype(BF16)
        logs[span, lanes] = jnp.broadcast_to(top + jnp.log2(total), (size, head))


def pair_block(rows, lanes, pairs, part):
    return pl.BlockSpec((rows, lanes), lambda pair: (0, part * pairs + pair))


def attention(qkv_image, qkv_text, key_bias, floor, head):
    image_rows, width = qkv_image.shape
    text_rows = qkv_text.shape[0]
    rows = image_rows + text_rows
    lanes = 2 * head
    pairs = width // (3 * lanes)
    columns = [
        pair_block(count, lanes, pairs, part)
        for part in range(3)
        for count in (image_rows, text_rows)
    ]
    return pl.pallas_call(
        functools.partial(attention_kernel, 256, LOG2E / math.sqrt(head), head),
        grid=(pairs,),
        in_specs=[
            pl.BlockSpec((rows, 128), lambda pair: (0, 0)),
            pl.BlockSpec(memory_space=pltpu.SMEM),
            *columns,
        ],
        out_specs=[columns[0], columns[1], columns[0], columns[1]],
        out_shape=[
            jax.ShapeDtypeStruct((count, width // 3), dtype)
            for dtype in (BF16, F32)
            for count in (image_rows, text_rows)
        ],
        scratch_shapes=[pltpu.VMEM((2, rows, lanes), BF16)] * 2,
        compiler_params=pltpu.CompilerParams(vmem_limit_bytes=56 << 20),
        cost_estimate=pl.CostEstimate(
            flops=int(WEIGHT["attention"] * 1.15e9), bytes_accessed=1, transcendentals=0
        ),
        name="attention",
    )(key_bias, floor, qkv_image, qkv_text, qkv_image, qkv_text, qkv_image, qkv_text)


def attention_back_kernel(query_rows, scale, factor, head, pairs, *refs):
    (bias_ref, qi, qt, ki, kt, vi, vt, ai, at, li, lt, gi, gt) = refs[:13]
    oi, ot, keys, values, key_sum, value_sum = refs[13:]
    pair = pl.program_id(0)
    image_rows = qi.shape[0]
    rows = keys.shape[1]
    width = 2 * head
    key_side = lanes_of([bias_ref[:, 0:1], 1.0, 1.0, 1.0], rows, head)
    value_side = lanes_of([1.0, 1.0, 1.0], rows, head)
    for side in range(2):
        lanes = slice(side * head, (side + 1) * head)
        for ref, extra, first, second in (
            (keys, key_side, ki, kt),
            (values, value_side, vi, vt),
        ):
            ref[side, :image_rows, :] = jnp.concatenate(
                [first[:, lanes], extra[:image_rows]], axis=1
            )
            ref[side, image_rows:, :] = jnp.concatenate(
                [second[:, lanes], extra[image_rows:]], axis=1
            )
    key_sum[...] = jnp.zeros_like(key_sum)
    value_sum[...] = jnp.zeros_like(value_sum)
    spans = [(qi, ai, li, gi, oi, start, query_rows) for start in range(0, image_rows, query_rows)]
    spans.append((qt, at, lt, gt, ot, 0, qt.shape[0]))
    steps = [(*span, side) for span in spans for side in range(2)]
    query_lanes = pl.ds(pl.multiple_of(pair * width, width), width)
    key_lanes = pl.ds(pl.multiple_of((pairs + pair) * width, width), width)
    value_lanes = pl.ds(pl.multiple_of((2 * pairs + pair) * width, width), width)

    def products(step):
        source, outs, logs, grads, _, start, size, side = step
        span = slice(start, start + size)
        lanes = slice(side * head, (side + 1) * head)
        query, grad = (source[span, lanes], grads[span, lanes])
        log = logs[span, side * head : side * head + 1] * (-1.0 / scale)
        inner = -jnp.sum(
            grad.astype(F32) * outs[span, lanes].astype(F32), axis=1, keepdims=True
        )
        query_wide = jnp.concatenate(
            [query, lanes_of([1.0, *three_parts(log)], size, head)], axis=1
        )
        grad_wide = jnp.concatenate([grad, lanes_of(three_parts(inner), size, head)], axis=1)
        return (
            query,
            grad,
            dot_nt(keys[side], query_wide),
            dot_nt(values[side], grad_wide),
        )

    ahead = products(steps[0])
    dq = []
    for at_step, (_, _, _, _, target, start, size, side) in enumerate(steps):
        query, grad, scores, prob_grad = ahead
        if at_step + 1 < len(steps):
            ahead = products(steps[at_step + 1])
        probs = jnp.exp2(scores * scale)
        score_grad = (probs * prob_grad).astype(BF16)
        lanes = slice(side * head, (side + 1) * head)
        value_sum[:, lanes] += dot_nn(probs.astype(BF16), grad)
        key_sum[:, lanes] += dot_nn(score_grad, query)
        dq.append(dot_tn(score_grad, keys[side][:, :head]))
        if side == 1:
            target[start : start + size, query_lanes] = (
                jnp.concatenate(dq, axis=1) * factor
            ).astype(BF16)
            dq = []
    oi[:, key_lanes] = (key_sum[:image_rows] * factor).astype(BF16)
    ot[:, key_lanes] = (key_sum[image_rows:] * factor).astype(BF16)
    oi[:, value_lanes] = value_sum[:image_rows].astype(BF16)
    ot[:, value_lanes] = value_sum[image_rows:].astype(BF16)


def attention_back(
    qkv_image, qkv_text, out_image, out_text, log_image, log_text, grad_image, grad_text, key_bias, head
):
    image_rows, width = qkv_image.shape
    text_rows = qkv_text.shape[0]
    rows = image_rows + text_rows
    lanes = 2 * head
    pairs = width // (3 * lanes)
    columns = [
        pair_block(count, lanes, pairs, part)
        for part in range(3)
        for count in (image_rows, text_rows)
    ]
    return pl.pallas_call(
        functools.partial(
            attention_back_kernel, 512, LOG2E / math.sqrt(head), 1.0 / math.sqrt(head), head, pairs
        ),
        grid=(pairs,),
        in_specs=[
            pl.BlockSpec((rows, 128), lambda pair: (0, 0)),
            *columns,
            *(columns[:2] * 3),
        ],
        out_specs=[
            pl.BlockSpec((image_rows, width), lambda pair: (0, 0)),
            pl.BlockSpec((text_rows, width), lambda pair: (0, 0)),
        ],
        out_shape=[
            jax.ShapeDtypeStruct((image_rows, width), BF16),
            jax.ShapeDtypeStruct((text_rows, width), BF16),
        ],
        scratch_shapes=[pltpu.VMEM((2, rows, lanes), BF16)] * 2
        + [pltpu.VMEM((rows, lanes), F32)] * 2,
        compiler_params=pltpu.CompilerParams(vmem_limit_bytes=56 << 20),
        cost_estimate=pl.CostEstimate(
            flops=int(WEIGHT["attention_back"] * 1.15e9), bytes_accessed=1, transcendentals=0
        ),
        name="attention_back",
    )(
        key_bias,
        *(qkv_image, qkv_text) * 3,
        out_image, out_text, log_image, log_text, grad_image, grad_text,
    )


def flip(values, bit):
    return lax.ppermute(values, "seq", [(i, i ^ bit) for i in range(4)])


def gather_near(a, b):
    return (flip(a, 1), flip(b, 1), flip(a, 2), flip(b, 2))


def gather_far(a, b, near):
    return (a, b, *near, flip(near[0], 2), flip(near[3], 1))


def gather_halves(a, b):
    return gather_far(a, b, gather_near(a, b))


def add_low(a, b):
    return (a.astype(F32) + b.astype(F32)).astype(BF16)


def scatter_first(sent):
    return (flip(sent[1], 1), flip(sent[2], 2))


def scatter_added(sent, first):
    width = sent[3].shape[-1]
    return (
        add_low(sent[3], first[1][..., :width]),
        add_low(sent[4], first[0][..., :width]),
    )


def scatter_sent(sent, first, added):
    return (sent[0], *first, flip(added[0], 1), flip(added[1], 2))


def scatter_last(sent, first):
    return scatter_sent(sent, first, scatter_added(sent, first))


def scatter_halves(halves):
    return scatter_last(halves, scatter_first(halves))


ANYWHERE = pl.BlockSpec(memory_space=pl.ANY)
ON_CORE = pl.BlockSpec(memory_space=pltpu.VMEM)


class Copies:
    def __init__(self, semaphores):
        self.semaphores = semaphores
        self.count = 0
        self.open = []

    def start(self, source, target):
        copy = pltpu.make_async_copy(source, target, self.semaphores.at[self.count])
        self.count += 1
        copy.start()
        return copy

    def send(self, source, target):
        self.open.append(self.start(source, target))

    def finish(self):
        for copy in self.open:
            copy.wait()


def fetch_halves(copies, halves, rows, seq):
    width = rows.shape[2] // 2
    fetched = []
    for r in range(4):
        pair = []
        for side in range(2):
            half = halves[2 * r + side]
            half = half if seq is None else half.at[seq]
            pair.append(copies.start(half, rows.at[r, :, pl.ds(side * width, width)]))
        fetched.append(pair)
    return fetched


def send_block(copies, rows, sent, r):
    own, for_x, for_y, late_x, late_y = sent
    width = rows.shape[2] // 2
    low, high = pl.ds(0, width), pl.ds(width, width)
    if r == 0:
        copies.send(rows.at[0], own)
        return
    first, second = {
        1: (for_x.at[:, high], late_x),
        2: (late_y, for_y.at[:, high]),
        3: (for_x.at[:, low], for_y.at[:, low]),
    }[r]
    copies.send(rows.at[r, :, low], first)
    copies.send(rows.at[r, :, high], second)


def sent_shapes(block, D):
    return [((block, width), BF16) for width in (D, D, D, D // 2, D // 2)]


def normalize(values):
    mean = jnp.mean(values, axis=1, keepdims=True)
    centered = values - mean
    variance = jnp.mean(centered * centered, axis=1, keepdims=True)
    inverse = lax.rsqrt(variance + NORM_EPSILON)
    return centered * inverse, inverse


def normalize_back(norm, inverse, grad, scale):
    scaled = grad * (1.0 + scale)
    return inverse * (
        scaled
        - jnp.mean(scaled, axis=1, keepdims=True)
        - norm * jnp.mean(scaled * norm, axis=1, keepdims=True)
    )


def run(kernel, name, operands, specs, outs, out_specs, scratch, copies=0):
    if copies:
        scratch = [*scratch, pltpu.SemaphoreType.DMA((copies,))]
    return pl.pallas_call(
        kernel,
        in_specs=specs,
        out_specs=out_specs,
        out_shape=[jax.ShapeDtypeStruct(shape, dtype) for shape, dtype in outs],
        scratch_shapes=scratch,
        compiler_params=pltpu.CompilerParams(vmem_limit_bytes=56 << 20),
        cost_estimate=pl.CostEstimate(
            flops=int(WEIGHT[name] * 1.15e9), bytes_accessed=1, transcendentals=0
        ),
        name=name,
    )(*operands)


def project_kernel(seq, image_rows, *refs):
    halves, (weight, mods, bias) = (refs[:8], refs[8:11])
    qkv_i, qkv_t, norm_i, norm_t = refs[11:15]
    rows, held, image_norm, text_norm, image_out, text_out, semaphores = refs[15:]
    copies = Copies(semaphores)
    fetched = fetch_halves(copies, halves, rows, seq)
    weights = [copies.start(weight.at[t], held.at[t]) for t in range(2)]
    text_rows = rows.shape[1] - image_rows
    for r in range(4):
        for copy in fetched[r]:
            copy.wait()
        for t, norms, low, count in (
            (0, image_norm, 0, image_rows),
            (1, text_norm, image_rows, text_rows),
        ):
            norm, _ = normalize(rows[r, low : low + count, :].astype(F32))
            norm = norm * (1.0 + mods[t, seq, 1:2, :]) + mods[t, seq, 0:1, :]
            norms[r * count : (r + 1) * count, :] = norm.astype(BF16)
        if r == 0:
            weights[0].wait()
        span = pl.ds(r * image_rows, image_rows)
        product = dot_nt(image_norm[span, :], held[0]) + bias[0:1, :]
        image_out[span, :] = product.astype(BF16)
        copies.send(image_norm.at[span, :], norm_i.at[span, :])
        copies.send(image_out.at[span, :], qkv_i.at[span, :])
    weights[1].wait()
    text_out[...] = (dot_nt(text_norm[...], held[1]) + bias[1:2, :]).astype(BF16)
    copies.send(text_norm, norm_t)
    copies.send(text_out, qkv_t)
    copies.finish()


def project(halves, weight, mods, bias, seq, image_rows):
    block, width = halves[0].shape[-2:]
    D, W = 2 * width, weight.shape[1]
    image, text = 4 * image_rows, 4 * (block - image_rows)
    return run(
        functools.partial(project_kernel, seq, image_rows),
        "project",
        (*halves, weight, mods, bias),
        [ANYWHERE] * 9 + [ON_CORE] * 2,
        [((image, W), BF16), ((text, W), BF16), ((image, D), BF16), ((text, D), BF16)],
        [ANYWHERE] * 4,
        [
            pltpu.VMEM((4, block, D), BF16),
            pltpu.VMEM((2, W, D), BF16),
            pltpu.VMEM((image, D), BF16),
            pltpu.VMEM((text, D), BF16),
            pltpu.VMEM((image, W), BF16),
            pltpu.VMEM((text, W), BF16),
        ],
        20,
    )


def partial_kernel(seqs, dot, image_rows, *refs):
    inputs, weight, halves = (refs[: 2 * seqs], refs[2 * seqs], refs[2 * seqs + 1 : 7 * seqs + 1])
    lefts, held, rows, semaphores = (
        refs[7 * seqs + 1 : 9 * seqs + 1],
        refs[9 * seqs + 1],
        refs[9 * seqs + 2 : 10 * seqs + 2],
        refs[10 * seqs + 2],
    )
    copies = Copies(semaphores)
    weights = [copies.start(weight.at[t], held.at[t]) for t in (1, 0)]
    fetched = [
        [copies.start(inputs[2 * s + t], lefts[2 * s + t]) for t in (1, 0)] for s in range(seqs)
    ]
    text_rows = rows[0].shape[1] - image_rows
    for s in range(seqs):
        if s == 0:
            weights[0].wait()
        fetched[s][0].wait()
        text = dot(lefts[2 * s + 1][...], held[1]).astype(BF16)
        for r in range(4):
            rows[s][r, image_rows:, :] = text[r * text_rows : (r + 1) * text_rows]
        if s == 0:
            weights[1].wait()
        fetched[s][1].wait()
        for r in (3, 1, 2, 0):
            left = lefts[2 * s][r * image_rows : (r + 1) * image_rows, :]
            rows[s][r, :image_rows, :] = dot(left, held[0]).astype(BF16)
            send_block(copies, rows[s], halves[5 * s : 5 * s + 5], r)
    copies.finish()


def partial_sums(inputs, weight, dot, D, image_rows):
    seqs = len(inputs)
    image, K = inputs[0][0].shape
    text = inputs[0][1].shape[0]
    block = (image + text) // 4
    return run(
        functools.partial(partial_kernel, seqs, dot, image_rows),
        "partial_sums",
        (*[value for pair in inputs for value in pair], weight),
        [ANYWHERE] * (2 * seqs + 1),
        sent_shapes(block, D) * seqs,
        [ANYWHERE] * (5 * seqs),
        [pltpu.VMEM((count, K), BF16) for _ in range(seqs) for count in (image, text)]
        + [pltpu.VMEM(weight.shape, BF16)]
        + [pltpu.VMEM((4, block, D), BF16)] * seqs,
        2 + 2 * seqs + 7 * seqs,
    )


def piece_sum(pieces, low, count):
    own, from_x, from_y, late_x, late_y = pieces
    width = late_x.shape[-1]

    def add(*parts):
        return sum(part.astype(F32) for part in parts)

    span = pl.ds(low, count)
    return jnp.concatenate(
        [
            add(own[span, :width], from_x[span, width:], late_y[span, :]),
            add(own[span, width:], late_x[span, :], from_y[span, width:]),
        ],
        axis=1,
    )


def both_halves(halves, seq, low, count):
    return jnp.concatenate(
        [half[seq, low : low + count, :].astype(F32) for half in halves], axis=1
    )


def middle_kernel(seq, image_rows, *refs):
    pieces, tokens, (mods, bias) = (refs[:5], refs[5:7], refs[7:9])
    projection_ref, middle_ref, second_a, second_b = refs[9:]
    block, width = second_a.shape
    for t, low, count in ((0, 0, image_rows), (1, image_rows, block - image_rows)):
        span = slice(low, low + count)
        projection = piece_sum(pieces, low, count) + bias[t : t + 1, :]
        middle = both_halves(tokens, seq, low, count) + mods[t, seq, 2:3, :] * projection
        norm, _ = normalize(middle)
        second = (norm * (1.0 + mods[t, seq, 4:5, :]) + mods[t, seq, 3:4, :]).astype(BF16)
        projection_ref[span, :] = projection
        middle_ref[span, :] = middle
        second_a[span, :] = second[:, :width]
        second_b[span, :] = second[:, width:]


def middle_step(pieces, tokens, mods, bias, seq, image_rows):
    block, width = pieces[3].shape
    return run(
        functools.partial(middle_kernel, seq, image_rows),
        "middle",
        (*pieces, *tokens, mods, bias),
        [ON_CORE] * 9,
        [((block, 2 * width), F32)] * 2 + [((block, width), BF16)] * 2,
        [ON_CORE] * 4,
        [],
    )


GELU_SCALE = math.sqrt(2.0 / math.pi)
GELU_CUBE = 0.044715


def hidden_kernel(seq, image_rows, *refs):
    halves, cotangents, (weight, bias, mods) = (refs[:8], refs[8:16], refs[16:19])
    outs = refs[19:27]
    act_i, act_t, slope_i, slope_t, grad_i, grad_t, second_i, second_t = outs
    rows, given, held, acts, slopes, grads, texts, semaphores = refs[27:]
    copies = Copies(semaphores)
    fetched = fetch_halves(copies, halves, rows, None)
    weights = [copies.start(weight.at[t], held.at[t]) for t in range(2)]
    other = fetch_halves(copies, cotangents, given, seq)
    text_rows = rows.shape[1] - image_rows
    second_text, grad_text, act_text, slope_text = texts

    def activate(pre):
        squared = pre * pre
        bent = jnp.tanh(pre * (GELU_SCALE + (GELU_SCALE * GELU_CUBE) * squared))
        rise = 0.5 + 0.5 * bent
        act = pre * rise
        slope = rise + (act * (1.0 - rise)) * (
            2.0 * GELU_SCALE + (6.0 * GELU_SCALE * GELU_CUBE) * squared
        )
        return act.astype(BF16), slope.astype(BF16)

    for r in range(4):
        for copy in fetched[r]:
            copy.wait()
        if r == 0:
            weights[0].wait()
        span = pl.ds(r * image_rows, image_rows)
        text_span = slice(r * text_rows, (r + 1) * text_rows)
        pre = dot_nt(rows[r, :image_rows, :], held[0]) + bias[0:1, :]
        act, slope = activate(pre)
        acts[span, :] = act
        slopes[span, :] = slope
        second_text[text_span, :] = rows[r, image_rows:, :]
        for copy in other[r]:
            copy.wait()
        for t, target, place, low, count in (
            (0, grads, span, 0, image_rows),
            (1, grad_text, text_span, image_rows, text_rows),
        ):
            value = given[r, low : low + count, :].astype(F32) * mods[t, seq, 5:6, :]
            target[place, :] = value.astype(BF16)
        copies.send(acts.at[span, :], act_i.at[span, :])
        copies.send(slopes.at[span, :], slope_i.at[span, :])
        copies.send(grads.at[span, :], grad_i.at[span, :])
        copies.send(rows.at[r, pl.ds(0, image_rows), :], second_i.at[span, :])
    weights[1].wait()
    act_text[...], slope_text[...] = activate(
        dot_nt(second_text[...], held[1]) + bias[1:2, :]
    )
    for source, target in (
        (act_text, act_t),
        (slope_text, slope_t),
        (grad_text, grad_t),
        (second_text, second_t),
    ):
        copies.send(source, target)
    copies.finish()


def hidden_step(halves, cotangents, weight, bias, mods, seq, image_rows):
    block, width = halves[0].shape
    D, F = 2 * width, weight.shape[1]
    image, text = 4 * image_rows, 4 * (block - image_rows)

    def kernel(*refs):
        texts, semaphores = (refs[-5:-1], refs[-1])
        hidden_kernel(seq, image_rows, *refs[:-5], texts, semaphores)

    return run(
        kernel,
        "hidden",
        (*halves, *cotangents, weight, bias, mods),
        [ANYWHERE] * 17 + [ON_CORE] * 2,
        [((count, wide), BF16) for wide in (F, F, D, D) for count in (image, text)],
        [ANYWHERE] * 8,
        [
            pltpu.VMEM((4, block, D), BF16),
            pltpu.VMEM((4, block, D), BF16),
            pltpu.VMEM((2, F, D), BF16),
            pltpu.VMEM((image, F), BF16),
            pltpu.VMEM((image, F), BF16),
            pltpu.VMEM((image, D), BF16),
        ]
        + [pltpu.VMEM((text, wide), BF16) for wide in (D, D, F, F)],
        38,
    )


def outer_kernel(seqs, chunk, *refs):
    inputs, out = (refs[: 4 * seqs], refs[4 * seqs])
    held, result, semaphores = (refs[4 * seqs + 1 : -2], refs[-2], refs[-1])
    copies = Copies(semaphores)
    order = [4 * s + 2 * t + side for t in (1, 0) for s in range(seqs) for side in range(2)]
    fetched = {k: copies.start(inputs[k], held[k]) for k in order}
    columns = result.shape[1]
    for t in (1, 0):
        for s in range(seqs):
            fetched[4 * s + 2 * t].wait()
            fetched[4 * s + 2 * t + 1].wait()
        for low in range(0, columns, chunk):
            span = pl.ds(low, chunk)
            total = dot_tn(held[2 * t][:, span], held[2 * t + 1][...])
            for s in range(1, seqs):
                total = total + dot_tn(held[4 * s + 2 * t][:, span], held[4 * s + 2 * t + 1][...])
            result[t, span, :] = total.astype(BF16)
            copies.send(result.at[t, span, :], out.at[t, span, :])
    copies.finish()


def outer_sums(lefts, rights, chunk):
    seqs = len(lefts)
    columns, width = lefts[0][0].shape[1], rights[0][0].shape[1]
    operands = [side[s][t] for s in range(seqs) for t in range(2) for side in (lefts, rights)]
    return run(
        functools.partial(outer_kernel, seqs, chunk),
        "outer_sums",
        operands,
        [ANYWHERE] * (4 * seqs),
        [((2, columns, width), BF16)],
        [ANYWHERE],
        [pltpu.VMEM(value.shape, BF16) for value in operands]
        + [pltpu.VMEM((2, columns, width), BF16)],
        4 * seqs + 2 * (columns // chunk),
    )[0]


def hidden_back_kernel(image_rows, *refs):
    (grad_i, grad_t, slope_i, slope_t, down, up) = refs[:6]
    pre_i, pre_t, sums, sent = (refs[6], refs[7], refs[8], refs[9:14])
    grads, slopes, pres, grad_text, slope_text, pre_text, held_down, held_up, rows, semaphores = (
        refs[14:]
    )
    copies = Copies(semaphores)
    order = (3, 1, 2, 0)
    spans = {r: pl.ds(r * image_rows, image_rows) for r in order}
    images = {}
    downs, ups = ([None, None], [None, None])
    for k, r in enumerate(order):
        images[r] = [copies.start(grad_i.at[spans[r], :], grads.at[spans[r], :])]
        if k == 0:
            downs[0] = copies.start(down.at[0], held_down.at[0])
        images[r].append(copies.start(slope_i.at[spans[r], :], slopes.at[spans[r], :]))
        if k == 0:
            ups[0] = copies.start(up.at[0], held_up.at[0])
    texts = [copies.start(grad_t, grad_text), copies.start(slope_t, slope_text)]
    downs[1] = copies.start(down.at[1], held_down.at[1])
    ups[1] = copies.start(up.at[1], held_up.at[1])
    text_rows = rows.shape[1] - image_rows
    total = jnp.zeros((1, pres.shape[1]), F32)
    for k, r in enumerate(order):
        for copy in images[r]:
            copy.wait()
        if k == 0:
            downs[0].wait()
        product = dot_nt(grads[spans[r], :], held_down[0]) * slopes[spans[r], :].astype(F32)
        low = product.astype(BF16)
        pres[spans[r], :] = low
        copies.send(pres.at[spans[r], :], pre_i.at[spans[r], :])
        total = total + jnp.sum(low.astype(F32), axis=0, keepdims=True)
        if k == 0:
            ups[0].wait()
        rows[r, :image_rows, :] = dot_nn(pres[spans[r], :], held_up[0]).astype(BF16)
        if k == 1:
            for copy in texts:
                copy.wait()
            downs[1].wait()
            product = dot_nt(grad_text[...], held_down[1]) * slope_text[...].astype(F32)
            pre_text[...] = product.astype(BF16)
            copies.send(pre_text, pre_t)
            sums[1:2, :] = jnp.sum(pre_text[...].astype(F32), axis=0, keepdims=True)
            ups[1].wait()
            back = dot_nn(pre_text[...], held_up[1]).astype(BF16)
            for q in range(4):
                rows[q, image_rows:, :] = back[q * text_rows : (q + 1) * text_rows]
            send_block(copies, rows, sent, order[0])
        if k >= 1:
            send_block(copies, rows, sent, r)
    sums[0:1, :] = total
    copies.finish()


def hidden_back(grads, slopes, down, up, image_rows):
    image, D = grads[0].shape
    text = grads[1].shape[0]
    F = up.shape[1]
    block = (image + text) // 4
    outs = run(
        functools.partial(hidden_back_kernel, image_rows),
        "hidden_back",
        (*grads, *slopes, down, up),
        [ANYWHERE] * 6,
        [((image, F), BF16), ((text, F), BF16), ((2, F), F32)] + sent_shapes(block, D),
        [ANYWHERE] * 2 + [ON_CORE] + [ANYWHERE] * 5,
        [
            pltpu.VMEM((image, D), BF16),
            pltpu.VMEM((image, F), BF16),
            pltpu.VMEM((image, F), BF16),
            pltpu.VMEM((text, D), BF16),
            pltpu.VMEM((text, F), BF16),
            pltpu.VMEM((text, F), BF16),
            pltpu.VMEM((2, F, D), BF16),
            pltpu.VMEM((2, F, D), BF16),
            pltpu.VMEM((4, block, D), BF16),
        ],
        8 + 2 + 4 + 1 + 4 + 7,
    )
    return outs[0:2], outs[2], outs[3:]


def middle_back_kernel(seq, image_rows, *refs):
    pieces, cotangents, (middle_ref, projection_ref, mods) = (refs[:5], refs[5:7], refs[7:10])
    grad_ref, low_a, low_b, sums = refs[10:]
    block, width = low_a.shape
    for t, low, count in ((0, 0, image_rows), (1, image_rows, block - image_rows)):
        span = slice(low, low + count)
        norm_grad = piece_sum(pieces, low, count)
        norm, inverse = normalize(middle_ref[span, :])
        grad = both_halves(cotangents, seq, low, count) + normalize_back(
            norm, inverse, norm_grad, mods[t, seq, 4:5, :]
        )
        rounded = (mods[t, seq, 2:3, :] * grad).astype(BF16)
        grad_ref[span, :] = grad
        low_a[span, :] = rounded[:, :width]
        low_b[span, :] = rounded[:, width:]
        for k, value in enumerate(
            (norm_grad, norm_grad * norm, grad * projection_ref[span, :], rounded.astype(F32))
        ):
            sums[4 * t + k : 4 * t + k + 1, :] = jnp.sum(value, axis=0, keepdims=True)


def middle_back(pieces, cotangents, middle, projection, mods, seq, image_rows):
    block, width = pieces[3].shape
    return run(
        functools.partial(middle_back_kernel, seq, image_rows),
        "middle_back",
        (*pieces, *cotangents, middle, projection, mods),
        [ON_CORE] * 10,
        [((block, 2 * width), F32)] + [((block, width), BF16)] * 2 + [((8, 2 * width), F32)],
        [ON_CORE] * 4,
        [],
    )


def attended_back_kernel(image_rows, *refs):
    halves, weight = (refs[:8], refs[8])
    grad_i, grad_t, proj_i, proj_t = refs[9:13]
    rows, held, image_out, text_in, text_out, semaphores = refs[13:]
    copies = Copies(semaphores)
    fetched = fetch_halves(copies, halves, rows, None)
    weights = [copies.start(weight.at[t], held.at[t]) for t in range(2)]
    text_rows = rows.shape[1] - image_rows
    for r in range(4):
        for copy in fetched[r]:
            copy.wait()
        if r == 0:
            weights[0].wait()
        span = pl.ds(r * image_rows, image_rows)
        text_in[r * text_rows : (r + 1) * text_rows, :] = rows[r, image_rows:, :]
        copies.send(rows.at[r, pl.ds(0, image_rows), :], proj_i.at[span, :])
        image_out[span, :] = dot_nn(rows[r, :image_rows, :], held[0]).astype(BF16)
    copies.send(image_out, grad_i)
    copies.send(text_in, proj_t)
    weights[1].wait()
    text_out[...] = dot_nn(text_in[...], held[1]).astype(BF16)
    copies.send(text_out, grad_t)
    copies.finish()


def attended_back(halves, weight, image_rows):
    block, width = halves[0].shape
    D, E = 2 * width, weight.shape[2]
    image, text = 4 * image_rows, 4 * (block - image_rows)
    outs = run(
        functools.partial(attended_back_kernel, image_rows),
        "attended_back",
        (*halves, weight),
        [ANYWHERE] * 9,
        [((image, E), BF16), ((text, E), BF16), ((image, D), BF16), ((text, D), BF16)],
        [ANYWHERE] * 4,
        [
            pltpu.VMEM((4, block, D), BF16),
            pltpu.VMEM(weight.shape, BF16),
            pltpu.VMEM((image, E), BF16),
            pltpu.VMEM((text, D), BF16),
            pltpu.VMEM((text, E), BF16),
        ],
        10 + 7,
    )
    return outs[:2], outs[2:]


def project_back_kernel(seq, image_rows, *refs):
    (grad_i, grad_t, weight), tokens = (refs[:3], refs[3:11])
    sums, column_sums, sent = (refs[11], refs[12], refs[13:18])
    grads, grad_text, held, given, rows, semaphores = refs[18:]
    copies = Copies(semaphores)
    weights = [copies.start(weight.at[t], held.at[t]) for t in (1, 0)]
    text_in = copies.start(grad_t, grad_text)
    image_in = copies.start(grad_i, grads)
    fetched = fetch_halves(copies, tokens, given, seq)
    text_rows = rows.shape[1] - image_rows
    weights[0].wait()
    text_in.wait()
    text = dot_nn(grad_text[...], held[1])
    column_sums[1:2, :] = jnp.sum(grad_text[...].astype(F32), axis=0, keepdims=True)
    weights[1].wait()
    image_in.wait()
    totals = [jnp.zeros((1, rows.shape[2]), F32) for _ in range(4)]
    columns = jnp.zeros((1, grads.shape[1]), F32)
    for r in (3, 1, 2, 0):
        for copy in fetched[r]:
            copy.wait()
        span = pl.ds(r * image_rows, image_rows)
        for t, low, count in ((0, 0, image_rows), (1, image_rows, text_rows)):
            if t == 0:
                back = dot_nn(grads[span, :], held[0])
                columns = columns + jnp.sum(grads[span, :].astype(F32), axis=0, keepdims=True)
            else:
                back = text[r * text_rows : (r + 1) * text_rows, :]
            norm, _ = normalize(given[r, low : low + count, :].astype(F32))
            totals[2 * t] = totals[2 * t] + jnp.sum(back, axis=0, keepdims=True)
            totals[2 * t + 1] = totals[2 * t + 1] + jnp.sum(back * norm, axis=0, keepdims=True)
            rows[r, low : low + count, :] = back.astype(BF16)
        send_block(copies, rows, sent, r)
    column_sums[0:1, :] = columns
    for k in range(4):
        sums[k : k + 1, :] = totals[k]
    copies.finish()


def project_back(grads, weight, tokens, seq, image_rows):
    image, W = grads[0].shape
    text = grads[1].shape[0]
    D = weight.shape[2]
    block = (image + text) // 4
    outs = run(
        functools.partial(project_back_kernel, seq, image_rows),
        "project_back",
        (*grads, weight, *tokens),
        [ANYWHERE] * 11,
        [((4, D), F32), ((2, W), F32)] + sent_shapes(block, D),
        [ON_CORE] * 2 + [ANYWHERE] * 5,
        [
            pltpu.VMEM((image, W), BF16),
            pltpu.VMEM((text, W), BF16),
            pltpu.VMEM(weight.shape, BF16),
            pltpu.VMEM((4, block, D), BF16),
            pltpu.VMEM((4, block, D), BF16),
        ],
        4 + 8 + 7,
    )
    return outs[0], outs[1], outs[2:]


def result_kernel(image_rows, *refs):
    pieces, cotangents, middles = (refs[:10], refs[10:12], refs[12:14])
    mods, bias, image_out, text_out, sums = refs[14:]
    block = middles[0].shape[0]
    for seq in range(2):
        for t, low, count in ((0, 0, image_rows), (1, image_rows, block - image_rows)):
            span = slice(low, low + count)
            value = piece_sum(pieces[5 * seq : 5 * seq + 5], low, count) + bias[t : t + 1, :]
            gate = mods[t, seq, 5:6, :]
            out = (middles[seq][span, :] + gate * value).astype(BF16)
            if t == 0:
                image_out[seq] = out
            else:
                text_out[seq] = out
            grad = both_halves(cotangents, seq, low, count)
            low_grad = (gate * grad).astype(BF16).astype(F32)
            at = 4 * seq + 2 * t
            sums[at : at + 1, :] = jnp.sum(grad * value, axis=0, keepdims=True)
            sums[at + 1 : at + 2, :] = jnp.sum(low_grad, axis=0, keepdims=True)


def result_step(pieces, cotangents, middles, mods, bias, image_rows):
    seqs, (block, width) = (len(middles), pieces[3].shape)
    return run(
        functools.partial(result_kernel, image_rows),
        "result",
        (*pieces, *cotangents, *middles, mods, bias),
        [ON_CORE] * 16,
        [
            ((seqs, image_rows, 2 * width), BF16),
            ((seqs, block - image_rows, 2 * width), BF16),
            ((8, 2 * width), F32),
        ],
        [ON_CORE] * 3,
        [],
    )


def input_back_kernel(image_rows, live_text, *refs):
    pieces, tokens, grads, mods = (refs[:10], refs[10:12], refs[12:14], refs[14])
    image_out, text_out = refs[15:]
    block = grads[0].shape[0]
    for seq in range(2):
        for t, low, count in ((0, 0, image_rows), (1, image_rows, block - image_rows)):
            norm_grad = piece_sum(pieces[5 * seq : 5 * seq + 5], low, count)
            norm, inverse = normalize(both_halves(tokens, seq, low, count))
            out = grads[seq][low : low + count, :] + normalize_back(
                norm, inverse, norm_grad, mods[t, seq, 1:2, :]
            )
            if t == 0:
                image_out[seq] = out
            else:
                text_out[seq] = out[:live_text]


def input_back(pieces, tokens, grads, mods, image_rows, live_text):
    block, width = pieces[0][3].shape
    return run(
        functools.partial(input_back_kernel, image_rows, live_text),
        "input_back",
        (*pieces[0], *pieces[1], *tokens, *grads, mods),
        [ON_CORE] * 15,
        [((2, image_rows, 2 * width), F32), ((2, live_text, 2 * width), F32)],
        [ON_CORE] * 2,
        [],
    )


def match_units(batch_devices, seq_devices, per_device, group_units):
    devices = batch_devices * seq_devices
    total = devices * per_device
    part_units = total // 3
    sources, targets = ([], [])
    for seq_at in range(seq_devices):
        listed = [
            part * part_units + seq_at * group_units + k
            for part in range(3)
            for k in range(group_units)
        ]
        for place, unit in enumerate(listed):
            sources.append((unit // per_device, unit % per_device))
            targets.append(
                ((place // per_device) * seq_devices + seq_at, place % per_device)
            )
    edges = list(zip(sources, targets))
    rounds = []
    left = list(range(total))
    for _ in range(per_device):
        by_source = {}
        for e in left:
            by_source.setdefault(edges[e][0][0], []).append(e)
        taken = {}

        def place_edge(device, seen):
            for e in by_source[device]:
                target = edges[e][1][0]
                if target in seen:
                    continue
                seen.add(target)
                if target not in taken or place_edge(edges[taken[target]][0][0], seen):
                    taken[target] = e
                    return True
            return False

        for device in range(devices):
            place_edge(device, set())
        chosen = sorted(taken.values())
        rounds.append(chosen)
        left = [e for e in left if e not in chosen]
    send = np.zeros((per_device, devices), np.int32)
    land = np.zeros((per_device, devices), np.int32)
    perms = []
    for k, chosen in enumerate(rounds):
        pairs = []
        for e in chosen:
            (source, source_slot), (target, target_slot) = edges[e]
            pairs.append((source, target))
            send[k, source] = source_slot
            land[k, target] = target_slot
        perms.append(sorted(pairs))
    return perms, send, land


def move_units(units, perms, take, put, place):
    arrived = jnp.zeros_like(units)
    for k, pairs in enumerate(perms):
        slot = jnp.asarray(take[k])[place]
        moved = lax.ppermute(
            lax.dynamic_index_in_dim(units, slot, 0, keepdims=True), ("batch", "seq"), pairs
        )
        arrived = lax.dynamic_update_slice_in_dim(arrived, moved, jnp.asarray(put[k])[place], 0)
    return arrived


def gather_rows_over_batch(values):
    return lax.all_gather(values, "batch", axis=1, tiled=True)


def after(values, *others):
    return lax.optimization_barrier((values, others))[0]


def gather_small(values, axis, last=()):
    count = lax.axis_size(axis)
    held = values[None]
    bit = 1
    while bit < count:
        pairs = [(i, i ^ bit) for i in range(count)]
        if 2 * bit == count:
            held = after(held, last)
        held = jnp.concatenate([held, lax.ppermute(held, axis, pairs)])
        bit *= 2
    return jnp.take(held, jnp.bitwise_xor(lax.axis_index(axis), jnp.arange(count)), axis=0)


def scatter_rows_over_batch(values):
    dimension = values.ndim - 2
    return lax.psum_scatter(values, "batch", scatter_dimension=dimension, tiled=True)


def swap(values, axis):
    return lax.all_to_all(values, axis, 0, 0, tiled=True)


def swift_layer(
    image_tokens,
    text_tokens,
    conditioning,
    key_mask,
    mod_weight,
    mod_bias,
    qkv_weight,
    qv_bias,
    out_weight,
    out_bias,
    up_weight,
    up_bias,
    down_weight,
    down_bias,
    image_cotangent,
    text_cotangent,
):
    S = lax.axis_size("seq")
    B = lax.axis_size("batch")
    seq_index = lax.axis_index("seq")
    place = lax.axis_index(("batch", "seq"))
    L, image_count, D = image_tokens.shape
    live_text = text_tokens.shape[1]
    text_count = -(-live_text // 16) * 16
    pad = ((0, 0), (0, text_count - live_text), (0, 0))
    head = D // HEADS
    own_width = D // S
    half = D // 2

    unit = math.gcd(qkv_weight.shape[2], own_width)
    per_device = qkv_weight.shape[2] // unit
    perms, send, land = match_units(B, S, per_device, own_width // unit)
    back_perms = [[(target, source) for source, target in pairs] for pairs in perms]
    qkv_units = jnp.swapaxes(qkv_weight, 1, 2).reshape(2, per_device, unit, D).swapaxes(0, 1)
    qkv_mine = move_units(qkv_units, perms, send, land, place).swapaxes(0, 1)
    qkv_width = per_device * unit
    qkv_part = gather_rows_over_batch(qkv_mine.reshape(2, qkv_width, D))
    padded = jnp.concatenate([image_tokens, jnp.pad(text_tokens, pad)], axis=1)
    tokens = after((padded[..., :half], padded[..., half:]), qkv_mine)
    tokens_near = gather_near(*tokens)

    bias_widths = [array.shape[1] for array in (qv_bias, out_bias, up_bias, down_bias)]
    bias_ends = np.cumsum(bias_widths)
    own_biases = jnp.concatenate([qv_bias, out_bias, up_bias, down_bias], axis=1)
    near = gather_small(
        jnp.concatenate([conditioning, own_biases], axis=1),
        "batch",
        (tokens_near[0], tokens_near[3]),
    )
    cond_all = near[:, :, :D].reshape(B * L, D)
    column_biases = near[:, :, D:].astype(F32)
    smooth_all = jax.nn.silu(cond_all.astype(F32)).astype(BF16)
    mod_own = (
        jnp.einsum("sd,tdf->tsf", smooth_all, mod_weight, preferred_element_type=F32)
        + mod_bias.astype(F32)[:, None, :]
    )
    mod_width = mod_own.shape[2]
    mod_all = gather_small(mod_own, "batch", (tokens_near[1], tokens_near[2]))
    mod_came = lax.dynamic_slice_in_dim(mod_all, lax.axis_index("batch") * L, L, 2)
    small = jnp.concatenate(
        [mod_came.reshape(B, 2 * L * mod_width), column_biases.reshape(B, -1)], axis=1
    )
    tokens_all = gather_far(*tokens, tokens_near)
    small_all = gather_small(small, "seq", tokens_all[6:])
    modulation = (
        small_all[:, :, : 2 * L * mod_width]
        .reshape(S, B, 2, L, mod_width)
        .transpose(2, 3, 1, 0, 4)
        .reshape(2, L, 6, D)
    )
    bias_all = (
        small_all[:, :, 2 * L * mod_width :].reshape(S, B, 2, -1).transpose(2, 1, 0, 3)
    )
    qv_full = bias_all[..., : bias_ends[0]].reshape(2, 2 * D)
    out_bias_full = bias_all[..., bias_ends[0] : bias_ends[1]].reshape(2, D)
    down_bias_full = bias_all[..., bias_ends[2] :].reshape(2, D)
    up_bias_part = (
        column_biases[:, :, bias_ends[1] : bias_ends[2]].transpose(1, 0, 2).reshape(2, -1)
    )
    first_feature = seq_index * own_width
    qkv_bias = jnp.concatenate(
        [
            lax.dynamic_slice_in_dim(qv_full, first_feature, own_width, 1),
            jnp.zeros((2, own_width), F32),
            lax.dynamic_slice_in_dim(qv_full, D + first_feature, own_width, 1),
        ],
        axis=1,
    )

    out_units = jnp.swapaxes(out_weight, 1, 2).reshape(2, -1, S, own_width).transpose(2, 0, 1, 3)
    order = jnp.bitwise_xor(seq_index, jnp.arange(S))
    out_units = jnp.take(after(out_units, mod_own), order, axis=0)
    out_mine = jnp.stack([out_units[0], *(flip(out_units[r], r) for r in range(1, S))])
    out_mine = jnp.take(out_mine, order, axis=0)
    out_columns = out_mine.shape[2]
    out_rows = out_mine.transpose(1, 0, 2, 3).reshape(2, S * out_columns, own_width)
    out_part = gather_rows_over_batch(out_rows)
    hidden_columns = up_weight.shape[2]
    padded = jnp.concatenate([image_cotangent, jnp.pad(text_cotangent, pad)], axis=1)
    cotangents = (padded[..., :half], padded[..., half:])
    near_grads = gather_near(*after(cotangents, tokens_all, small_all))
    up_part = gather_rows_over_batch(after(jnp.swapaxes(up_weight, 1, 2), out_mine, mod_own))
    down_part = gather_rows_over_batch(after(jnp.swapaxes(down_weight, 1, 2), out_mine, mod_own))

    image_keys = jnp.take(
        key_mask[:, : S * image_count].reshape(L, S, image_count), order, axis=1
    )
    text_keys = jnp.take(
        key_mask[:, S * image_count :].reshape(L, S, live_text), order, axis=1
    )
    text_keys = jnp.pad(text_keys, ((0, 0), (0, 0), (0, text_count - live_text)))
    live = jnp.concatenate([image_keys.reshape(L, -1), text_keys.reshape(L, -1)], axis=1) > 0
    key_bias = jnp.where(live, 0.0, DEAD).astype(F32)
    floors = jnp.where(jnp.all(key_mask > 0, axis=1), -3e38, FLOOR_SCORE * LOG2E).astype(F32)
    floors = floors.reshape(L, 1, 1)
    key_bias = jnp.broadcast_to(key_bias[:, :, None], (*key_bias.shape, 128))

    kept = []
    first = project(tokens_all, qkv_part, modulation, qkv_bias, 0, image_count)
    attended = attention(first[0], first[1], key_bias[0], floors[0], head)
    attended, logs = (attended[:2], attended[2:])
    attended = after(attended, near_grads)
    parts = partial_sums([attended], out_part, dot_nt, D, image_count)
    kept.append((first, attended, logs, parts))
    again = after(tokens_all, parts)
    first = project(again, qkv_part, modulation, qkv_bias, 1, image_count)
    attended = attention(first[0], first[1], key_bias[1], floors[1], head)
    attended, logs = (attended[:2], attended[2:])
    cotangents_all = gather_far(*cotangents, after(near_grads, kept[0][1]))
    out_first = scatter_first(kept[0][3])
    out_added = scatter_added(kept[0][3], after(out_first, attended))
    attended = after(attended, cotangents_all, out_added)
    parts = partial_sums([attended], out_part, dot_nt, D, image_count)
    kept.append((first, attended, logs, parts))
    firsts, attendeds, logs, out_halves = zip(*kept)
    out_pieces = [scatter_sent(out_halves[0], out_first, out_added)]
    out_pieces.append(scatter_halves(after(out_halves[1], out_pieces[0])))
    steps = []
    for s in range(L):
        steps.append(
            middle_step(
                out_pieces[s],
                tokens,
                modulation,
                out_bias_full,
                s,
                image_count,
            )
        )
    second_near = [gather_near(*step[2:]) for step in steps]
    hidden = []
    for s in range(L):
        near = after(second_near[s], hidden[-1]) if s else second_near[s]
        halves = gather_far(*steps[s][2:], near)
        hidden.append(
            hidden_step(
                halves, cotangents_all, up_part, up_bias_part, modulation, s, image_count
            )
        )
    acts, slopes, grads, norms = [[step[i : i + 2] for step in hidden] for i in (0, 2, 4, 6)]

    down_sum = outer_sums(acts, grads, 256)
    down_came = scatter_rows_over_batch(down_sum)
    pres, bias_sums, norm2_halves = ([], [], [])
    gate = down_sum
    for s in range(L):
        pre, sums, halves = hidden_back(
            after(grads[s], gate), slopes[s], down_part, up_part, image_count
        )
        gate = halves
        pres.append(pre)
        bias_sums.append(sums)
        norm2_halves.append(halves)
    up_bias_sum = sum(bias_sums)
    norm2_first = scatter_first(norm2_halves[0])
    norm2_added = scatter_added(norm2_halves[0], after(norm2_first, gate))
    norm2_pieces = scatter_sent(norm2_halves[0], norm2_first, norm2_added)
    norm2_first1 = scatter_first(after(norm2_halves[1], norm2_pieces[3:]))
    backs = [
        middle_back(
            after(norm2_pieces, gate),
            cotangents,
            *steps[0][1::-1],
            modulation,
            0,
            image_count,
        )
    ]
    proj_near0 = gather_near(*backs[0][1:3])
    mlp_halves = partial_sums(after(acts, backs[0]), down_part, dot_nn, D, image_count)
    up_sum = outer_sums(after(pres, mlp_halves), norms, 256)
    norm2_added = scatter_added(norm2_halves[1], after(norm2_first1, mlp_halves))
    norm2_pieces = scatter_sent(norm2_halves[1], norm2_first1, norm2_added)
    projs = [gather_far(*backs[0][1:3], after(proj_near0, up_sum))]
    backs.append(
        middle_back(
            after(norm2_pieces, up_sum, proj_near0),
            cotangents,
            *steps[1][1::-1],
            modulation,
            1,
            image_count,
        )
    )
    proj_near1 = gather_near(*backs[1][1:3])
    grad0, proj0 = attended_back(
        after(projs[0], backs[1], down_came), out_part, image_count
    )
    up_came = scatter_rows_over_batch(after(up_sum, backs[1]))
    qkv_grad0 = attention_back(
        *firsts[0][:2], *attendeds[0], *logs[0], *grad0, key_bias[0], head
    )
    projs.append(gather_far(*backs[1][1:3], after(proj_near1, qkv_grad0)))
    sums0, columns0, halves0 = project_back(
        qkv_grad0, qkv_part, tokens_all, 0, image_count
    )
    grad1, proj1 = attended_back(after(projs[1], halves0), out_part, image_count)
    mlp_halves = (mlp_halves[:5], mlp_halves[5:])
    mlp_first = [scatter_first(after(halves, projs[1])) for halves in mlp_halves]
    out_sum = outer_sums([proj0, proj1], attendeds, 256)
    out_came = scatter_rows_over_batch(out_sum)
    grad1 = after(grad1, out_sum)
    qkv_grad1 = attention_back(
        *firsts[1][:2], *attendeds[1], *logs[1], *grad1, key_bias[1], head
    )
    mlp_added = [
        scatter_added(halves, after(first, qkv_grad1))
        for halves, first in zip(mlp_halves, mlp_first)
    ]
    mlp_pieces = [
        piece
        for halves, first, added in zip(mlp_halves, mlp_first, mlp_added)
        for piece in scatter_sent(halves, first, added)
    ]
    norm1_first = scatter_first(after(halves0, mlp_pieces))
    qkv_sum = outer_sums(
        [qkv_grad0, after(qkv_grad1, mlp_added, up_came)],
        [first[2:] for first in firsts],
        128 if qkv_width % 256 else 256,
    )
    qkv_came = scatter_rows_over_batch(after(qkv_sum, out_came))
    out_home = swap(out_came.reshape(2, S, out_columns, own_width).swapaxes(0, 1), "seq")
    sums1, columns1, halves1 = project_back(
        after(qkv_grad1, qkv_sum, mlp_pieces, out_home), qkv_part, tokens_all, 1, image_count
    )
    norm1_pieces = [scatter_last(halves0, norm1_first), scatter_halves(halves1)]
    image_out, text_out, result_sums = result_step(
        after(mlp_pieces, halves1),
        cotangents,
        [step[1] for step in steps],
        modulation,
        down_bias_full,
        image_count,
    )
    image_grad, text_grad = input_back(
        norm1_pieces, tokens, [back[0] for back in backs], modulation, image_count, live_text
    )
    qkv_home = move_units(
        after(qkv_came, image_grad).reshape(2, per_device, unit, D).swapaxes(0, 1),
        back_perms, land, send, place
    )
    qkv_weight_grad = qkv_home.swapaxes(0, 1).reshape(2, -1, D).swapaxes(1, 2).astype(F32)
    out_weight_grad = (
        out_home.transpose(1, 2, 0, 3).reshape(2, out_columns, D).swapaxes(1, 2).astype(F32)
    )
    up_weight_grad = up_came.swapaxes(1, 2).astype(F32)
    down_weight_grad = down_came.swapaxes(1, 2).astype(F32)


    first_sums = jnp.stack([sums0, sums1]).reshape(L, 2, 2, D)
    second_sums = jnp.stack([back[3] for back in backs]).reshape(L, 2, 4, D)
    result_sums = result_sums.reshape(L, 2, 2, D)
    mod_rows = jnp.concatenate(
        [
            first_sums,
            second_sums[:, :, 2:3],
            second_sums[:, :, :2],
            result_sums[:, :, :1],
        ],
        axis=2,
    ).swapaxes(0, 1)
    mod_rows = mod_rows.reshape(2, L, B, S, mod_width).transpose(3, 2, 0, 1, 4)
    out_bias_sum = jnp.sum(second_sums[:, :, 3], axis=0)
    down_bias_sum = jnp.sum(result_sums[:, :, 1], axis=0)
    column_sums = columns0 + columns1
    qv_bias_sum = jnp.zeros((2, 2 * D), F32)
    for part, column in ((0, 0), (1, 2 * own_width)):
        qv_bias_sum = lax.dynamic_update_slice_in_dim(
            qv_bias_sum, column_sums[:, column : column + own_width], part * D + first_feature, 1
        )
    up_bias_rows = lax.dynamic_update_slice_in_dim(
        jnp.zeros((2, B, S, hidden_columns), F32),
        up_bias_sum.reshape(2, B, 1, hidden_columns),
        seq_index,
        2,
    )
    bias_rows = jnp.concatenate(
        [
            qv_bias_sum.reshape(2, B, S, -1),
            out_bias_sum.reshape(2, B, S, -1),
            up_bias_rows,
            down_bias_sum.reshape(2, B, S, -1),
        ],
        axis=3,
    ).transpose(2, 1, 0, 3)
    packed = jnp.concatenate(
        [mod_rows.reshape(S, B, -1), bias_rows.reshape(S, B, -1)], axis=2
    )
    packed = jnp.sum(swap(packed, "seq"), axis=0)
    packed = swap(packed, "batch")
    mod_mine = (
        packed[:, : 2 * L * mod_width]
        .reshape(B, 2, L, mod_width)
        .transpose(1, 0, 2, 3)
        .reshape(2, B * L, mod_width)
        .astype(BF16)
    )
    bias_mine = jnp.sum(packed[:, 2 * L * mod_width :], axis=0).reshape(2, -1)
    qv_bias_grad, out_bias_grad, up_bias_grad, down_bias_grad = jnp.split(
        bias_mine, bias_ends[:3], axis=1
    )
    mod_weight_grad = jnp.einsum(
        "sd,tsf->tdf", smooth_all, mod_mine, preferred_element_type=F32
    )
    mod_bias_grad = jnp.sum(mod_mine.astype(F32), axis=1)
    smooth_part = jnp.einsum("tsf,tdf->sd", mod_mine, mod_weight, preferred_element_type=F32)
    smooth_grad = jnp.sum(swap(after(smooth_part, norm1_pieces[1]).reshape(B, L, D), "batch"), axis=0)
    smooth_grad = after(smooth_grad, qkv_home)
    smooth_grad = smooth_grad + flip(smooth_grad, 1)
    smooth_grad = smooth_grad + flip(smooth_grad, 2)
    cond_grad = jax.vjp(jax.nn.silu, conditioning.astype(F32))[1](smooth_grad)[0]
    return (
        image_out,
        text_out[:, :live_text],
        image_grad,
        text_grad,
        cond_grad,
        mod_weight_grad,
        mod_bias_grad,
        qkv_weight_grad,
        qv_bias_grad,
        out_weight_grad,
        out_bias_grad,
        up_weight_grad,
        up_bias_grad,
        down_weight_grad,
        down_bias_grad,
    )


def choose_layer(mesh):
    if mesh.shape["seq"] == 4 and HEADS % 8 == 0:
        return swift_layer
    return general_layer


def solution(mesh):
    layer = choose_layer(mesh)
    return jax.shard_map(
        layer,
        mesh=mesh,
        in_specs=(
            P("batch", "seq", None),
            P("batch", "seq", None),
            P("batch", None),
            P("batch", None),
            P(None, None, ("batch", "seq")),
            P(None, ("batch", "seq")),
            P(None, None, ("batch", "seq")),
            P(None, ("batch", "seq")),
            P(None, None, ("batch", "seq")),
            P(None, ("batch", "seq")),
            P(None, None, ("batch", "seq")),
            P(None, ("batch", "seq")),
            P(None, None, ("batch", "seq")),
            P(None, ("batch", "seq")),
            P("batch", "seq", None),
            P("batch", "seq", None),
        ),
        out_specs=(
            P("batch", "seq", None),
            P("batch", "seq", None),
            P("batch", "seq", None),
            P("batch", "seq", None),
            P("batch", None),
            P(None, None, ("batch", "seq")),
            P(None, ("batch", "seq")),
            P(None, None, ("batch", "seq")),
            P(None, ("batch", "seq")),
            P(None, None, ("batch", "seq")),
            P(None, ("batch", "seq")),
            P(None, None, ("batch", "seq")),
            P(None, ("batch", "seq")),
            P(None, None, ("batch", "seq")),
            P(None, ("batch", "seq")),
        ),
        check_vma=False,
    )
```

```python
import functools
import math

import jax
import jax.numpy as jnp
import numpy as np
from jax import lax
from jax.experimental import pallas as pl
from jax.experimental.pallas import tpu as pltpu
from jax.sharding import PartitionSpec as P

HEADS = 24


NORM_EPSILON = 1e-06
FLOOR_SCORE = -10000.0


def modulate(tokens, shift_vec, scale_vec):
    row_mean = jnp.mean(tokens, axis=-1, keepdims=True)
    centered = tokens - row_mean
    row_var = jnp.mean(centered * centered, axis=-1, keepdims=True)
    return (
        centered * lax.rsqrt(row_var + NORM_EPSILON) * (1.0 + scale_vec[:, None, :])
        + shift_vec[:, None, :]
    )


def gelu_tanh(values):
    return jax.nn.gelu(values, approximate=True)


def unmix_columns(values, seq_devices, batch_devices):
    array_shape = values.shape
    piece_width = array_shape[-1] // (seq_devices * batch_devices)
    grid_view = values.reshape(array_shape[:-1] + (seq_devices, batch_devices, piece_width))
    return jnp.swapaxes(grid_view, -3, -2).reshape(array_shape)


def remix_columns(values, seq_devices, batch_devices):
    array_shape = values.shape
    piece_width = array_shape[-1] // (seq_devices * batch_devices)
    grid_view = values.reshape(array_shape[:-1] + (batch_devices, seq_devices, piece_width))
    return jnp.swapaxes(grid_view, -3, -2).reshape(array_shape)


def fetch_columns(
    up_weight,
    down_weight,
    mod_weight,
    qkv_weight,
    out_weight,
    up_bias,
    mod_bias,
    qv_bias,
    out_bias,
    down_bias,
):
    return (
        lax.all_gather(up_weight, "batch", axis=2, tiled=True),
        lax.all_gather(down_weight, "batch", axis=2, tiled=True),
        lax.all_gather(mod_weight, "batch", axis=2, tiled=True),
        lax.all_gather(qkv_weight, "batch", axis=2, tiled=True),
        lax.all_gather(out_weight, "batch", axis=2, tiled=True),
        lax.all_gather(up_bias, "batch", axis=1, tiled=True),
        lax.all_gather(mod_bias, "batch", axis=1, tiled=True),
        lax.all_gather(qv_bias, "batch", axis=1, tiled=True),
        lax.all_gather(out_bias, "batch", axis=1, tiled=True),
        lax.all_gather(down_bias, "batch", axis=1, tiled=True),
    )


def fetch_modulation(mod_part, mod_bias_part):
    return (
        lax.all_gather(mod_part, "seq", axis=2, tiled=True),
        lax.all_gather(mod_bias_part, "seq", axis=1, tiled=True),
    )


def gather_rows(first, second):
    return (
        lax.all_gather(first, "seq", axis=1, tiled=True),
        lax.all_gather(second, "seq", axis=1, tiled=True),
    )


def sum_rows(first, second, seq_devices):
    local_seqs, first_rows, width = first.shape
    first_local = first_rows // seq_devices
    second_local = second.shape[1] // seq_devices
    joined = jnp.concatenate(
        [
            first.reshape(local_seqs, seq_devices, first_local, width),
            second.reshape(local_seqs, seq_devices, second_local, width),
        ],
        axis=2,
    )
    joined = joined.reshape(local_seqs, seq_devices * (first_local + second_local), width)
    total = lax.psum_scatter(joined, "seq", scatter_dimension=1, tiled=True)
    return (total[:, :first_local], total[:, first_local:])


def to_rows(first, second):
    return (
        lax.all_to_all(first, "seq", split_axis=1, concat_axis=2, tiled=True),
        lax.all_to_all(second, "seq", split_axis=1, concat_axis=2, tiled=True),
    )


def to_columns(first, second):
    return (
        lax.all_to_all(first, "seq", split_axis=2, concat_axis=1, tiled=True),
        lax.all_to_all(second, "seq", split_axis=2, concat_axis=1, tiled=True),
    )


def own_block(values, seq_index, seq_devices):
    width = values.shape[1] // seq_devices
    return lax.dynamic_slice_in_dim(values, seq_index * width, width, 1)


def general_layer(
    image_tokens,
    text_tokens,
    conditioning,
    key_mask,
    mod_weight,
    mod_bias,
    qkv_weight,
    qv_bias,
    out_weight,
    out_bias,
    up_weight,
    up_bias,
    down_weight,
    down_bias,
    image_cotangent,
    text_cotangent,
):
    seq_devices = lax.axis_size("seq")
    batch_devices = lax.axis_size("batch")
    seq_index = lax.axis_index("seq")
    local_seqs, image_count, model_width = image_tokens.shape
    text_count = text_tokens.shape[1]
    block_rows = image_count + text_count
    key_count = block_rows * seq_devices
    head_size = model_width // HEADS
    factor = 1.0 / math.sqrt(head_size)
    inputs = (image_tokens.astype(jnp.float32), text_tokens.astype(jnp.float32))
    cotangents = (image_cotangent.astype(jnp.float32), text_cotangent.astype(jnp.float32))
    row_spans = ((0, image_count), (image_count, block_rows))
    image_keys = key_mask[:, : image_count * seq_devices].reshape(
        local_seqs, seq_devices, image_count
    )
    text_keys = key_mask[:, image_count * seq_devices :].reshape(
        local_seqs, seq_devices, text_count
    )
    key_live = (
        jnp.concatenate([image_keys, text_keys], axis=2).reshape(local_seqs, key_count) > 0
    )[:, None, None, :]
    cond_float = conditioning.astype(jnp.float32)
    smooth = jax.nn.silu(cond_float).astype(jnp.bfloat16)
    fetched = fetch_columns(
        up_weight,
        down_weight,
        mod_weight,
        qkv_weight,
        out_weight,
        up_bias,
        mod_bias,
        qv_bias,
        out_bias,
        down_bias,
    )
    (
        up_part,
        down_part,
        mod_part,
        qkv_part,
        out_part,
        up_bias_part,
        mod_bias_part,
        qv_part,
        out_bias_part,
        down_bias_part,
    ) = fetched
    mod_full, mod_bias_full = fetch_modulation(mod_part, mod_bias_part)
    mixed_mod = (
        jnp.einsum("sd,tdf->tsf", smooth, mod_full, preferred_element_type=jnp.float32)
        + mod_bias_full.astype(jnp.float32)[:, None, :]
    )
    modulation = unmix_columns(mixed_mod, seq_devices, batch_devices).reshape(
        2, local_seqs, 6, model_width
    )
    first_norms = []
    for modality in range(2):
        pieces = modulation[modality]
        first_norms.append(
            modulate(inputs[modality], pieces[:, 0], pieces[:, 1]).astype(jnp.bfloat16)
        )
    norm_image_all, norm_text_all, qv_seq, out_bias_seq, down_bias_seq = (
        lax.all_gather(first_norms[0], "seq", axis=1, tiled=True),
        lax.all_gather(first_norms[1], "seq", axis=1, tiled=True),
        lax.all_gather(qv_part, "seq", axis=1, tiled=True),
        lax.all_gather(out_bias_part, "seq", axis=1, tiled=True),
        lax.all_gather(down_bias_part, "seq", axis=1, tiled=True),
    )
    first_all = (norm_image_all, norm_text_all)
    qv_full = unmix_columns(qv_seq, seq_devices, batch_devices).astype(jnp.float32)
    out_bias_full = unmix_columns(out_bias_seq, seq_devices, batch_devices).astype(jnp.float32)
    down_bias_full = unmix_columns(down_bias_seq, seq_devices, batch_devices).astype(jnp.float32)
    qkv_cols = [
        jnp.einsum(
            "srd,df->srf",
            first_all[modality],
            qkv_part[modality],
            preferred_element_type=jnp.float32,
        )
        for modality in range(2)
    ]
    qkv_rows = to_rows(qkv_cols[0], qkv_cols[1])
    queries, keyvals = ([], [])
    for modality in range(2):
        projected = unmix_columns(qkv_rows[modality], seq_devices, batch_devices)
        qv_vector = qv_full[modality]
        queries.append(
            (projected[..., :model_width] + qv_vector[:model_width]).astype(jnp.bfloat16)
        )
        value_shift = jnp.concatenate(
            [jnp.zeros((model_width,), jnp.float32), qv_vector[model_width:]]
        )
        keyvals.append((projected[..., model_width:] + value_shift).astype(jnp.bfloat16))
    joined_query = jnp.concatenate(queries, axis=1)
    joined_keyval = jnp.concatenate(keyvals, axis=1)
    all_keyval = lax.all_gather(joined_keyval, "seq", axis=1, tiled=True)
    query_heads = joined_query.reshape(local_seqs, block_rows, HEADS, head_size)
    key_heads = all_keyval[..., :model_width].reshape(local_seqs, key_count, HEADS, head_size)
    value_heads = all_keyval[..., model_width:].reshape(local_seqs, key_count, HEADS, head_size)
    scores = (
        jnp.einsum("sqhe,skhe->shqk", query_heads, key_heads, preferred_element_type=jnp.float32)
        * factor
    )
    row_max = jnp.max(jnp.where(key_live, scores, FLOOR_SCORE), axis=-1, keepdims=True)
    exp_terms = jnp.exp(jnp.where(key_live, scores - row_max, FLOOR_SCORE))
    denominator = jnp.maximum(jnp.sum(exp_terms, axis=-1, keepdims=True), 1.0)
    prob_low = (exp_terms / denominator).astype(jnp.bfloat16)
    logsum = row_max + jnp.log(denominator)
    attended = jnp.einsum(
        "shqk,skhe->sqhe", prob_low, value_heads, preferred_element_type=jnp.float32
    )
    attended = attended.reshape(local_seqs, block_rows, model_width).astype(jnp.bfloat16)
    attended_all = gather_rows(attended[:, :image_count], attended[:, image_count:])
    out_cols = [
        jnp.einsum(
            "srd,df->srf",
            attended_all[modality],
            out_part[modality],
            preferred_element_type=jnp.float32,
        )
        for modality in range(2)
    ]
    out_rows = to_rows(out_cols[0], out_cols[1])
    projections, middles, second_norms = ([], [], [])
    for modality in range(2):
        pieces = modulation[modality]
        projection = (
            unmix_columns(out_rows[modality], seq_devices, batch_devices) + out_bias_full[modality]
        )
        middle = inputs[modality] + pieces[:, 2][:, None, :] * projection
        second_norms.append(modulate(middle, pieces[:, 3], pieces[:, 4]).astype(jnp.bfloat16))
        projections.append(projection)
        middles.append(middle)
    group_rows = gather_rows(second_norms[0], second_norms[1])
    hidden_pre, hidden_act, partials = ([], [], [])
    for modality in range(2):
        pre_values = jnp.einsum(
            "srd,df->srf",
            group_rows[modality],
            up_part[modality],
            preferred_element_type=jnp.float32,
        ) + up_bias_part[modality].astype(jnp.float32)
        act_values = gelu_tanh(pre_values).astype(jnp.bfloat16)
        partials.append(
            jnp.einsum(
                "srf,df->srd", act_values, down_part[modality], preferred_element_type=jnp.float32
            )
        )
        hidden_pre.append(pre_values)
        hidden_act.append(act_values)
    mlp_rows = sum_rows(partials[0], partials[1], seq_devices)
    mlp_outs, results = ([], [])
    for modality in range(2):
        pieces = modulation[modality]
        mlp_value = mlp_rows[modality] + down_bias_full[modality]
        results.append(
            (middles[modality] + pieces[:, 5][:, None, :] * mlp_value).astype(jnp.bfloat16)
        )
        mlp_outs.append(mlp_value)
    fetched_back = fetch_columns(
        up_weight,
        down_weight,
        mod_weight,
        qkv_weight,
        out_weight,
        up_bias,
        mod_bias,
        qv_bias,
        out_bias,
        down_bias,
    )
    up_back, down_back, mod_back, qkv_back, out_back = (
        fetched_back[0],
        fetched_back[1],
        fetched_back[2],
        fetched_back[3],
        fetched_back[4],
    )
    mod_bias_back = fetched_back[6]
    mlp_grads, gate_twos, down_bias_grads = ([], [], [])
    for modality in range(2):
        pieces = modulation[modality]
        mlp_grad = (pieces[:, 5][:, None, :] * cotangents[modality]).astype(jnp.bfloat16)
        gate_twos.append(jnp.sum(cotangents[modality] * mlp_outs[modality], axis=1))
        down_bias_grads.append(jnp.sum(mlp_grad.astype(jnp.float32), axis=(0, 1)))
        mlp_grads.append(mlp_grad)
    group_grads = gather_rows(mlp_grads[0], mlp_grads[1])
    down_grads, up_grads, up_bias_grads, norm_partials = ([], [], [], [])
    for modality in range(2):
        down_grads.append(
            jnp.einsum(
                "srd,srf->df",
                group_grads[modality],
                hidden_act[modality],
                preferred_element_type=jnp.float32,
            )
        )
        act_grad = jnp.einsum(
            "srd,df->srf",
            group_grads[modality],
            down_back[modality],
            preferred_element_type=jnp.float32,
        )
        pullback = jax.vjp(gelu_tanh, hidden_pre[modality])[1]
        pre_grad = pullback(act_grad)[0].astype(jnp.bfloat16)
        up_grads.append(
            jnp.einsum(
                "srd,srf->df", group_rows[modality], pre_grad, preferred_element_type=jnp.float32
            )
        )
        up_bias_grads.append(jnp.sum(pre_grad.astype(jnp.float32), axis=(0, 1)))
        norm_partials.append(
            jnp.einsum(
                "srf,df->srd", pre_grad, up_back[modality], preferred_element_type=jnp.float32
            )
        )
    norm_grads = sum_rows(norm_partials[0], norm_partials[1], seq_devices)
    middle_grads, shift_twos, scale_twos, gate_ones, out_bias_grads, proj_grads = (
        [],
        [],
        [],
        [],
        [],
        [],
    )
    for modality in range(2):
        pieces = modulation[modality]
        pullback = jax.vjp(modulate, middles[modality], pieces[:, 3], pieces[:, 4])[1]
        middle_part, shift_two, scale_two = pullback(norm_grads[modality])
        middle_grad = cotangents[modality] + middle_part
        proj_grad = (pieces[:, 2][:, None, :] * middle_grad).astype(jnp.bfloat16)
        gate_ones.append(jnp.sum(middle_grad * projections[modality], axis=1))
        out_bias_grads.append(jnp.sum(proj_grad.astype(jnp.float32), axis=(0, 1)))
        proj_grads.append(remix_columns(proj_grad, seq_devices, batch_devices))
        middle_grads.append(middle_grad)
        shift_twos.append(shift_two)
        scale_twos.append(scale_two)
    proj_cols = to_columns(proj_grads[0], proj_grads[1])
    out_grads, attended_partials = ([], [])
    for modality in range(2):
        out_grads.append(
            jnp.einsum(
                "srd,srf->df",
                attended_all[modality],
                proj_cols[modality],
                preferred_element_type=jnp.float32,
            )
        )
        attended_partials.append(
            jnp.einsum(
                "srf,df->srd",
                proj_cols[modality],
                out_back[modality],
                preferred_element_type=jnp.float32,
            )
        )
    attended_sums = sum_rows(attended_partials[0], attended_partials[1], seq_devices)
    attended_grad = jnp.concatenate([attended_sums[0], attended_sums[1]], axis=1).astype(
        jnp.bfloat16
    )
    grad_heads = attended_grad.reshape(local_seqs, block_rows, HEADS, head_size)
    scores_again = (
        jnp.einsum("sqhe,skhe->shqk", query_heads, key_heads, preferred_element_type=jnp.float32)
        * factor
    )
    probs_again = jnp.exp(jnp.where(key_live, scores_again - logsum, FLOOR_SCORE))
    probs_again_low = probs_again.astype(jnp.bfloat16)
    prob_grad = jnp.einsum(
        "sqhe,skhe->shqk", grad_heads, value_heads, preferred_element_type=jnp.float32
    )
    inner_sum = jnp.sum(probs_again * prob_grad, axis=-1, keepdims=True)
    score_grad = (probs_again * (prob_grad - inner_sum)).astype(jnp.bfloat16)
    query_grad = (
        jnp.einsum("shqk,skhe->sqhe", score_grad, key_heads, preferred_element_type=jnp.float32)
        * factor
    )
    query_grad = query_grad.reshape(local_seqs, block_rows, model_width).astype(jnp.bfloat16)
    key_grad = (
        jnp.einsum("shqk,sqhe->skhe", score_grad, query_heads, preferred_element_type=jnp.float32)
        * factor
    )
    value_grad = jnp.einsum(
        "shqk,sqhe->skhe", probs_again_low, grad_heads, preferred_element_type=jnp.float32
    )
    key_rows, value_rows = (
        lax.psum_scatter(
            key_grad.reshape(local_seqs, key_count, model_width),
            "seq",
            scatter_dimension=1,
            tiled=True,
        ),
        lax.psum_scatter(
            value_grad.reshape(local_seqs, key_count, model_width),
            "seq",
            scatter_dimension=1,
            tiled=True,
        ),
    )
    key_rows = key_rows.astype(jnp.bfloat16)
    value_rows = value_rows.astype(jnp.bfloat16)
    qv_bias_grads, joined_grads = ([], [])
    for modality in range(2):
        row_start, row_stop = row_spans[modality]
        query_part = query_grad[:, row_start:row_stop]
        value_part = value_rows[:, row_start:row_stop]
        joined_grad = jnp.concatenate(
            [query_part, key_rows[:, row_start:row_stop], value_part], axis=-1
        )
        qv_bias_grads.append(
            jnp.concatenate(
                [
                    jnp.sum(query_part.astype(jnp.float32), axis=(0, 1)),
                    jnp.sum(value_part.astype(jnp.float32), axis=(0, 1)),
                ]
            )
        )
        joined_grads.append(remix_columns(joined_grad, seq_devices, batch_devices))
    qkv_grad_cols = to_columns(joined_grads[0], joined_grads[1])
    qkv_grads, first_partials = ([], [])
    for modality in range(2):
        qkv_grads.append(
            jnp.einsum(
                "srd,srf->df",
                first_all[modality],
                qkv_grad_cols[modality],
                preferred_element_type=jnp.float32,
            )
        )
        first_partials.append(
            jnp.einsum(
                "srf,df->srd",
                qkv_grad_cols[modality],
                qkv_back[modality],
                preferred_element_type=jnp.float32,
            )
        )
    first_grads = sum_rows(first_partials[0], first_partials[1], seq_devices)
    input_grads, mod_partials = ([], [])
    for modality in range(2):
        pieces = modulation[modality]
        pullback = jax.vjp(modulate, inputs[modality], pieces[:, 0], pieces[:, 1])[1]
        input_part, shift_one, scale_one = pullback(first_grads[modality])
        input_grads.append(middle_grads[modality] + input_part)
        stacked = jnp.stack(
            [
                shift_one,
                scale_one,
                gate_ones[modality],
                shift_twos[modality],
                scale_twos[modality],
                gate_twos[modality],
            ],
            axis=1,
        )
        mod_partials.append(stacked.reshape(local_seqs, 6 * model_width))
    qv_mixed = remix_columns(jnp.stack(qv_bias_grads), seq_devices, batch_devices)
    out_bias_mixed = remix_columns(jnp.stack(out_bias_grads), seq_devices, batch_devices)
    down_bias_mixed = remix_columns(jnp.stack(down_bias_grads), seq_devices, batch_devices)
    mod_sum, qv_summed, out_bias_summed, down_bias_summed = lax.psum(
        (jnp.stack(mod_partials), qv_mixed, out_bias_mixed, down_bias_mixed), "seq"
    )
    mod_low = mod_sum.astype(jnp.bfloat16)
    mod_mixed = remix_columns(mod_low, seq_devices, batch_devices)
    columns = mod_part.shape[2]
    own_columns = lax.dynamic_slice_in_dim(mod_mixed, seq_index * columns, columns, 2)
    mod_grad = jnp.einsum("sd,tsf->tdf", smooth, own_columns, preferred_element_type=jnp.float32)
    mod_bias_grad = jnp.sum(own_columns.astype(jnp.float32), axis=1)
    mod_again = fetch_modulation(mod_back, mod_bias_back)[0]
    smooth_grad = jnp.einsum(
        "tsf,tdf->sd", mod_mixed, mod_again, preferred_element_type=jnp.float32
    )
    cond_pullback = jax.vjp(jax.nn.silu, cond_float)[1]
    cond_grad = cond_pullback(smooth_grad)[0]
    qv_own = own_block(qv_summed, seq_index, seq_devices)
    out_bias_own = own_block(out_bias_summed, seq_index, seq_devices)
    down_bias_own = own_block(down_bias_summed, seq_index, seq_devices)
    column_grads = (
        lax.psum_scatter(jnp.stack(up_grads), "batch", scatter_dimension=2, tiled=True),
        lax.psum_scatter(jnp.stack(down_grads), "batch", scatter_dimension=2, tiled=True),
        lax.psum_scatter(mod_grad, "batch", scatter_dimension=2, tiled=True),
        lax.psum_scatter(jnp.stack(qkv_grads), "batch", scatter_dimension=2, tiled=True),
        lax.psum_scatter(jnp.stack(out_grads), "batch", scatter_dimension=2, tiled=True),
        lax.psum_scatter(jnp.stack(up_bias_grads), "batch", scatter_dimension=1, tiled=True),
        lax.psum_scatter(mod_bias_grad, "batch", scatter_dimension=1, tiled=True),
        lax.psum_scatter(qv_own, "batch", scatter_dimension=1, tiled=True),
        lax.psum_scatter(out_bias_own, "batch", scatter_dimension=1, tiled=True),
        lax.psum_scatter(down_bias_own, "batch", scatter_dimension=1, tiled=True),
    )
    return (
        results[0],
        results[1],
        input_grads[0],
        input_grads[1],
        cond_grad,
        column_grads[2],
        column_grads[6],
        column_grads[3],
        column_grads[7],
        column_grads[4],
        column_grads[8],
        column_grads[0],
        column_grads[5],
        column_grads[1],
        column_grads[9],
    )


LOG2E = 1.4426950408889634
DEAD = -1e30
BF16 = jnp.bfloat16
F32 = jnp.float32


def dot_nt(a, b):
    return lax.dot_general(a, b, (((1,), (1,)), ((), ())), preferred_element_type=F32)


def dot_nn(a, b):
    return lax.dot_general(a, b, (((1,), (0,)), ((), ())), preferred_element_type=F32)


def dot_tn(a, b):
    return lax.dot_general(a, b, (((0,), (0,)), ((), ())), preferred_element_type=F32)


WEIGHT = {
    "attention": 0.17,
    "attention_back": 0.32,
    "project": 0.13,
    "partial_sums": 0.05,
    "middle": 0.05,
    "hidden": 0.18,
    "outer_sums": 0.18,
    "hidden_back": 0.2,
    "middle_back": 0.07,
    "attended_back": 0.06,
    "project_back": 0.12,
    "result": 0.07,
    "input_back": 0.09,
}


def lanes_of(columns, rows, width):
    lane = lax.broadcasted_iota(jnp.int32, (rows, width), 1)
    out = jnp.zeros((rows, width), F32)
    for k, column in enumerate(columns):
        out = jnp.where(lane == k, column, out)
    return out.astype(BF16)


def three_parts(column):
    high = column.astype(BF16).astype(F32)
    rest = column - high
    mid = rest.astype(BF16).astype(F32)
    return [high, mid, rest - mid]


def attention_kernel(
    query_rows, scale, head, bias_ref, floor_ref, qi, qt, ki, kt, vi, vt, oi, ot, li, lt, keys, values
):
    image_rows = qi.shape[0]
    rows = keys.shape[1]
    floor = floor_ref[0, 0]
    key_side = lanes_of([bias_ref[:, 0:1]], rows, head)
    value_side = lanes_of([1.0], rows, head)
    for side in range(2):
        lanes = slice(side * head, (side + 1) * head)
        for ref, extra, first, second in (
            (keys, key_side, ki, kt),
            (values, value_side, vi, vt),
        ):
            ref[side, :image_rows, :] = jnp.concatenate(
                [first[:, lanes], extra[:image_rows]], axis=1
            )
            ref[side, image_rows:, :] = jnp.concatenate(
                [second[:, lanes], extra[image_rows:]], axis=1
            )
    spans = [(qi, oi, li, start, query_rows) for start in range(0, image_rows, query_rows)]
    spans.append((qt, ot, lt, 0, qt.shape[0]))
    steps = [(*span, side) for span in spans for side in range(2)]

    def score(step):
        source, _, _, start, size, side = step
        query = source[start : start + size, side * head : (side + 1) * head]
        query = jnp.concatenate([query, lanes_of([1.0], size, head)], axis=1)
        return dot_nt(query, keys[side])

    ahead = score(steps[0])
    for at, (_, target, logs, start, size, side) in enumerate(steps):
        scores = ahead
        if at + 1 < len(steps):
            ahead = score(steps[at + 1])
        top = jnp.maximum(jnp.max(scores, axis=1, keepdims=True) * scale, floor)
        exps = jnp.exp2(scores * scale - top).astype(BF16)
        product = dot_nn(exps, values[side])
        total = jnp.maximum(product[:, head : head + 1], 1.0)
        span = slice(start, start + size)
        lanes = slice(side * head, (side + 1) * head)
        target[span, lanes] = (product[:, :head] * (1.0 / total)).astype(BF16)
        logs[span, lanes] = jnp.broadcast_to(top + jnp.log2(total), (size, head))


def pair_block(rows, lanes, pairs, part):
    return pl.BlockSpec((rows, lanes), lambda pair: (0, part * pairs + pair))


def attention(qkv_image, qkv_text, key_bias, floor, head):
    image_rows, width = qkv_image.shape
    text_rows = qkv_text.shape[0]
    rows = image_rows + text_rows
    lanes = 2 * head
    pairs = width // (3 * lanes)
    columns = [
        pair_block(count, lanes, pairs, part)
        for part in range(3)
        for count in (image_rows, text_rows)
    ]
    return pl.pallas_call(
        functools.partial(attention_kernel, 256, LOG2E / math.sqrt(head), head),
        grid=(pairs,),
        in_specs=[
            pl.BlockSpec((rows, 128), lambda pair: (0, 0)),
            pl.BlockSpec(memory_space=pltpu.SMEM),
            *columns,
        ],
        out_specs=[columns[0], columns[1], columns[0], columns[1]],
        out_shape=[
            jax.ShapeDtypeStruct((count, width // 3), dtype)
            for dtype in (BF16, F32)
            for count in (image_rows, text_rows)
        ],
        scratch_shapes=[pltpu.VMEM((2, rows, lanes), BF16)] * 2,
        compiler_params=pltpu.CompilerParams(vmem_limit_bytes=56 << 20),
        cost_estimate=pl.CostEstimate(
            flops=int(WEIGHT["attention"] * 1.15e9), bytes_accessed=1, transcendentals=0
        ),
        name="attention",
    )(key_bias, floor, qkv_image, qkv_text, qkv_image, qkv_text, qkv_image, qkv_text)


def attention_back_kernel(query_rows, scale, factor, head, pairs, *refs):
    (bias_ref, qi, qt, ki, kt, vi, vt, ai, at, li, lt, gi, gt) = refs[:13]
    oi, ot, keys, values, key_sum, value_sum = refs[13:]
    pair = pl.program_id(0)
    image_rows = qi.shape[0]
    rows = keys.shape[1]
    width = 2 * head
    key_side = lanes_of([bias_ref[:, 0:1], 1.0, 1.0, 1.0], rows, head)
    value_side = lanes_of([1.0, 1.0, 1.0], rows, head)
    for side in range(2):
        lanes = slice(side * head, (side + 1) * head)
        for ref, extra, first, second in (
            (keys, key_side, ki, kt),
            (values, value_side, vi, vt),
        ):
            ref[side, :image_rows, :] = jnp.concatenate(
                [first[:, lanes], extra[:image_rows]], axis=1
            )
            ref[side, image_rows:, :] = jnp.concatenate(
                [second[:, lanes], extra[image_rows:]], axis=1
            )
    key_sum[...] = jnp.zeros_like(key_sum)
    value_sum[...] = jnp.zeros_like(value_sum)
    spans = [(qi, ai, li, gi, oi, start, query_rows) for start in range(0, image_rows, query_rows)]
    spans.append((qt, at, lt, gt, ot, 0, qt.shape[0]))
    steps = [(*span, side) for span in spans for side in range(2)]
    query_lanes = pl.ds(pl.multiple_of(pair * width, width), width)
    key_lanes = pl.ds(pl.multiple_of((pairs + pair) * width, width), width)
    value_lanes = pl.ds(pl.multiple_of((2 * pairs + pair) * width, width), width)

    def products(step):
        source, outs, logs, grads, _, start, size, side = step
        span = slice(start, start + size)
        lanes = slice(side * head, (side + 1) * head)
        query, grad = (source[span, lanes], grads[span, lanes])
        log = logs[span, side * head : side * head + 1] * (-1.0 / scale)
        inner = -jnp.sum(
            grad.astype(F32) * outs[span, lanes].astype(F32), axis=1, keepdims=True
        )
        query_wide = jnp.concatenate(
            [query, lanes_of([1.0, *three_parts(log)], size, head)], axis=1
        )
        grad_wide = jnp.concatenate([grad, lanes_of(three_parts(inner), size, head)], axis=1)
        return (
            query,
            grad,
            dot_nt(keys[side], query_wide),
            dot_nt(values[side], grad_wide),
        )

    ahead = products(steps[0])
    dq = []
    for at_step, (_, _, _, _, target, start, size, side) in enumerate(steps):
        query, grad, scores, prob_grad = ahead
        if at_step + 1 < len(steps):
            ahead = products(steps[at_step + 1])
        probs = jnp.exp2(scores * scale)
        score_grad = (probs * prob_grad).astype(BF16)
        lanes = slice(side * head, (side + 1) * head)
        value_sum[:, lanes] += dot_nn(probs.astype(BF16), grad)
        key_sum[:, lanes] += dot_nn(score_grad, query)
        dq.append(dot_tn(score_grad, keys[side][:, :head]))
        if side == 1:
            target[start : start + size, query_lanes] = (
                jnp.concatenate(dq, axis=1) * factor
            ).astype(BF16)
            dq = []
    oi[:, key_lanes] = (key_sum[:image_rows] * factor).astype(BF16)
    ot[:, key_lanes] = (key_sum[image_rows:] * factor).astype(BF16)
    oi[:, value_lanes] = value_sum[:image_rows].astype(BF16)
    ot[:, value_lanes] = value_sum[image_rows:].astype(BF16)


def attention_back(
    qkv_image, qkv_text, out_image, out_text, log_image, log_text, grad_image, grad_text, key_bias, head
):
    image_rows, width = qkv_image.shape
    text_rows = qkv_text.shape[0]
    rows = image_rows + text_rows
    lanes = 2 * head
    pairs = width // (3 * lanes)
    columns = [
        pair_block(count, lanes, pairs, part)
        for part in range(3)
        for count in (image_rows, text_rows)
    ]
    return pl.pallas_call(
        functools.partial(
            attention_back_kernel, 512, LOG2E / math.sqrt(head), 1.0 / math.sqrt(head), head, pairs
        ),
        grid=(pairs,),
        in_specs=[
            pl.BlockSpec((rows, 128), lambda pair: (0, 0)),
            *columns,
            *(columns[:2] * 3),
        ],
        out_specs=[
            pl.BlockSpec((image_rows, width), lambda pair: (0, 0)),
            pl.BlockSpec((text_rows, width), lambda pair: (0, 0)),
        ],
        out_shape=[
            jax.ShapeDtypeStruct((image_rows, width), BF16),
            jax.ShapeDtypeStruct((text_rows, width), BF16),
        ],
        scratch_shapes=[pltpu.VMEM((2, rows, lanes), BF16)] * 2
        + [pltpu.VMEM((rows, lanes), F32)] * 2,
        compiler_params=pltpu.CompilerParams(vmem_limit_bytes=56 << 20),
        cost_estimate=pl.CostEstimate(
            flops=int(WEIGHT["attention_back"] * 1.15e9), bytes_accessed=1, transcendentals=0
        ),
        name="attention_back",
    )(
        key_bias,
        *(qkv_image, qkv_text) * 3,
        out_image, out_text, log_image, log_text, grad_image, grad_text,
    )


def flip(values, bit):
    return lax.ppermute(values, "seq", [(i, i ^ bit) for i in range(4)])


def gather_near(a, b):
    return (flip(a, 1), flip(b, 1), flip(a, 2), flip(b, 2))


def gather_far(a, b, near):
    return (a, b, *near, flip(near[0], 2), flip(near[3], 1))


def gather_halves(a, b):
    return gather_far(a, b, gather_near(a, b))


def add_low(a, b):
    return (a.astype(F32) + b.astype(F32)).astype(BF16)


def scatter_first(sent):
    return (flip(sent[1], 1), flip(sent[2], 2))


def scatter_added(sent, first):
    width = sent[3].shape[-1]
    return (
        add_low(sent[3], first[1][..., :width]),
        add_low(sent[4], first[0][..., :width]),
    )


def scatter_sent(sent, first, added):
    return (sent[0], *first, flip(added[0], 1), flip(added[1], 2))


def scatter_last(sent, first):
    return scatter_sent(sent, first, scatter_added(sent, first))


def scatter_halves(halves):
    return scatter_last(halves, scatter_first(halves))


ANYWHERE = pl.BlockSpec(memory_space=pl.ANY)
ON_CORE = pl.BlockSpec(memory_space=pltpu.VMEM)


class Copies:
    def __init__(self, semaphores):
        self.semaphores = semaphores
        self.count = 0
        self.open = []

    def start(self, source, target):
        copy = pltpu.make_async_copy(source, target, self.semaphores.at[self.count])
        self.count += 1
        copy.start()
        return copy

    def send(self, source, target):
        self.open.append(self.start(source, target))

    def finish(self):
        for copy in self.open:
            copy.wait()


def fetch_halves(copies, halves, rows, seq):
    width = rows.shape[2] // 2
    fetched = []
    for r in range(4):
        pair = []
        for side in range(2):
            half = halves[2 * r + side]
            half = half if seq is None else half.at[seq]
            pair.append(copies.start(half, rows.at[r, :, pl.ds(side * width, width)]))
        fetched.append(pair)
    return fetched


def send_block(copies, rows, sent, r):
    own, for_x, for_y, late_x, late_y = sent
    width = rows.shape[2] // 2
    low, high = pl.ds(0, width), pl.ds(width, width)
    if r == 0:
        copies.send(rows.at[0], own)
        return
    first, second = {
        1: (for_x.at[:, high], late_x),
        2: (late_y, for_y.at[:, high]),
        3: (for_x.at[:, low], for_y.at[:, low]),
    }[r]
    copies.send(rows.at[r, :, low], first)
    copies.send(rows.at[r, :, high], second)


def sent_shapes(block, D):
    return [((block, width), BF16) for width in (D, D, D, D // 2, D // 2)]


def normalize(values):
    mean = jnp.mean(values, axis=1, keepdims=True)
    centered = values - mean
    variance = jnp.mean(centered * centered, axis=1, keepdims=True)
    inverse = lax.rsqrt(variance + NORM_EPSILON)
    return centered * inverse, inverse


def normalize_back(norm, inverse, grad, scale):
    scaled = grad * (1.0 + scale)
    return inverse * (
        scaled
        - jnp.mean(scaled, axis=1, keepdims=True)
        - norm * jnp.mean(scaled * norm, axis=1, keepdims=True)
    )


def run(kernel, name, operands, specs, outs, out_specs, scratch, copies=0):
    if copies:
        scratch = [*scratch, pltpu.SemaphoreType.DMA((copies,))]
    return pl.pallas_call(
        kernel,
        in_specs=specs,
        out_specs=out_specs,
        out_shape=[jax.ShapeDtypeStruct(shape, dtype) for shape, dtype in outs],
        scratch_shapes=scratch,
        compiler_params=pltpu.CompilerParams(vmem_limit_bytes=56 << 20),
        cost_estimate=pl.CostEstimate(
            flops=int(WEIGHT[name] * 1.15e9), bytes_accessed=1, transcendentals=0
        ),
        name=name,
    )(*operands)


def project_kernel(seq, image_rows, *refs):
    halves, (weight, mods, bias) = (refs[:8], refs[8:11])
    qkv_i, qkv_t, norm_i, norm_t = refs[11:15]
    rows, held, image_norm, text_norm, image_out, text_out, semaphores = refs[15:]
    copies = Copies(semaphores)
    fetched = fetch_halves(copies, halves, rows, seq)
    weights = [copies.start(weight.at[t], held.at[t]) for t in range(2)]
    text_rows = rows.shape[1] - image_rows
    for r in range(4):
        for copy in fetched[r]:
            copy.wait()
        for t, norms, low, count in (
            (0, image_norm, 0, image_rows),
            (1, text_norm, image_rows, text_rows),
        ):
            norm, _ = normalize(rows[r, low : low + count, :].astype(F32))
            norm = norm * (1.0 + mods[t, seq, 1:2, :]) + mods[t, seq, 0:1, :]
            norms[r * count : (r + 1) * count, :] = norm.astype(BF16)
        if r == 0:
            weights[0].wait()
        span = pl.ds(r * image_rows, image_rows)
        product = dot_nt(image_norm[span, :], held[0]) + bias[0:1, :]
        image_out[span, :] = product.astype(BF16)
        copies.send(image_norm.at[span, :], norm_i.at[span, :])
        copies.send(image_out.at[span, :], qkv_i.at[span, :])
    weights[1].wait()
    text_out[...] = (dot_nt(text_norm[...], held[1]) + bias[1:2, :]).astype(BF16)
    copies.send(text_norm, norm_t)
    copies.send(text_out, qkv_t)
    copies.finish()


def project(halves, weight, mods, bias, seq, image_rows):
    block, width = halves[0].shape[-2:]
    D, W = 2 * width, weight.shape[1]
    image, text = 4 * image_rows, 4 * (block - image_rows)
    return run(
        functools.partial(project_kernel, seq, image_rows),
        "project",
        (*halves, weight, mods, bias),
        [ANYWHERE] * 9 + [ON_CORE] * 2,
        [((image, W), BF16), ((text, W), BF16), ((image, D), BF16), ((text, D), BF16)],
        [ANYWHERE] * 4,
        [
            pltpu.VMEM((4, block, D), BF16),
            pltpu.VMEM((2, W, D), BF16),
            pltpu.VMEM((image, D), BF16),
            pltpu.VMEM((text, D), BF16),
            pltpu.VMEM((image, W), BF16),
            pltpu.VMEM((text, W), BF16),
        ],
        20,
    )


def partial_kernel(seqs, dot, image_rows, *refs):
    inputs, weight, halves = (refs[: 2 * seqs], refs[2 * seqs], refs[2 * seqs + 1 : 7 * seqs + 1])
    lefts, held, rows, semaphores = (
        refs[7 * seqs + 1 : 9 * seqs + 1],
        refs[9 * seqs + 1],
        refs[9 * seqs + 2 : 10 * seqs + 2],
        refs[10 * seqs + 2],
    )
    copies = Copies(semaphores)
    weights = [copies.start(weight.at[t], held.at[t]) for t in (1, 0)]
    fetched = [
        [copies.start(inputs[2 * s + t], lefts[2 * s + t]) for t in (1, 0)] for s in range(seqs)
    ]
    text_rows = rows[0].shape[1] - image_rows
    for s in range(seqs):
        if s == 0:
            weights[0].wait()
        fetched[s][0].wait()
        text = dot(lefts[2 * s + 1][...], held[1]).astype(BF16)
        for r in range(4):
            rows[s][r, image_rows:, :] = text[r * text_rows : (r + 1) * text_rows]
        if s == 0:
            weights[1].wait()
        fetched[s][1].wait()
        for r in (3, 1, 2, 0):
            left = lefts[2 * s][r * image_rows : (r + 1) * image_rows, :]
            rows[s][r, :image_rows, :] = dot(left, held[0]).astype(BF16)
            send_block(copies, rows[s], halves[5 * s : 5 * s + 5], r)
    copies.finish()


def partial_sums(inputs, weight, dot, D, image_rows):
    seqs = len(inputs)
    image, K = inputs[0][0].shape
    text = inputs[0][1].shape[0]
    block = (image + text) // 4
    return run(
        functools.partial(partial_kernel, seqs, dot, image_rows),
        "partial_sums",
        (*[value for pair in inputs for value in pair], weight),
        [ANYWHERE] * (2 * seqs + 1),
        sent_shapes(block, D) * seqs,
        [ANYWHERE] * (5 * seqs),
        [pltpu.VMEM((count, K), BF16) for _ in range(seqs) for count in (image, text)]
        + [pltpu.VMEM(weight.shape, BF16)]
        + [pltpu.VMEM((4, block, D), BF16)] * seqs,
        2 + 2 * seqs + 7 * seqs,
    )


def piece_sum(pieces, low, count):
    own, from_x, from_y, late_x, late_y = pieces
    width = late_x.shape[-1]

    def add(*parts):
        return sum(part.astype(F32) for part in parts)

    span = pl.ds(low, count)
    return jnp.concatenate(
        [
            add(own[span, :width], from_x[span, width:], late_y[span, :]),
            add(own[span, width:], late_x[span, :], from_y[span, width:]),
        ],
        axis=1,
    )


def both_halves(halves, seq, low, count):
    return jnp.concatenate(
        [half[seq, low : low + count, :].astype(F32) for half in halves], axis=1
    )


def middle_kernel(seq, image_rows, *refs):
    pieces, tokens, (mods, bias) = (refs[:5], refs[5:7], refs[7:9])
    projection_ref, middle_ref, second_a, second_b = refs[9:]
    block, width = second_a.shape
    for t, low, count in ((0, 0, image_rows), (1, image_rows, block - image_rows)):
        span = slice(low, low + count)
        projection = piece_sum(pieces, low, count) + bias[t : t + 1, :]
        middle = both_halves(tokens, seq, low, count) + mods[t, seq, 2:3, :] * projection
        norm, _ = normalize(middle)
        second = (norm * (1.0 + mods[t, seq, 4:5, :]) + mods[t, seq, 3:4, :]).astype(BF16)
        projection_ref[span, :] = projection
        middle_ref[span, :] = middle
        second_a[span, :] = second[:, :width]
        second_b[span, :] = second[:, width:]


def middle_step(pieces, tokens, mods, bias, seq, image_rows):
    block, width = pieces[3].shape
    return run(
        functools.partial(middle_kernel, seq, image_rows),
        "middle",
        (*pieces, *tokens, mods, bias),
        [ON_CORE] * 9,
        [((block, 2 * width), F32)] * 2 + [((block, width), BF16)] * 2,
        [ON_CORE] * 4,
        [],
    )


GELU_SCALE = math.sqrt(2.0 / math.pi)
GELU_CUBE = 0.044715


def hidden_kernel(seq, image_rows, *refs):
    halves, cotangents, (weight, bias, mods) = (refs[:8], refs[8:16], refs[16:19])
    outs = refs[19:27]
    act_i, act_t, slope_i, slope_t, grad_i, grad_t, second_i, second_t = outs
    rows, given, held, acts, slopes, grads, texts, semaphores = refs[27:]
    copies = Copies(semaphores)
    fetched = fetch_halves(copies, halves, rows, None)
    weights = [copies.start(weight.at[t], held.at[t]) for t in range(2)]
    other = fetch_halves(copies, cotangents, given, seq)
    text_rows = rows.shape[1] - image_rows
    second_text, grad_text, act_text, slope_text = texts

    def activate(pre):
        squared = pre * pre
        bent = jnp.tanh(pre * (GELU_SCALE + (GELU_SCALE * GELU_CUBE) * squared))
        rise = 0.5 + 0.5 * bent
        act = pre * rise
        slope = rise + (act * (1.0 - rise)) * (
            2.0 * GELU_SCALE + (6.0 * GELU_SCALE * GELU_CUBE) * squared
        )
        return act.astype(BF16), slope.astype(BF16)

    for r in range(4):
        for copy in fetched[r]:
            copy.wait()
        if r == 0:
            weights[0].wait()
        span = pl.ds(r * image_rows, image_rows)
        text_span = slice(r * text_rows, (r + 1) * text_rows)
        pre = dot_nt(rows[r, :image_rows, :], held[0]) + bias[0:1, :]
        act, slope = activate(pre)
        acts[span, :] = act
        slopes[span, :] = slope
        second_text[text_span, :] = rows[r, image_rows:, :]
        for copy in other[r]:
            copy.wait()
        for t, target, place, low, count in (
            (0, grads, span, 0, image_rows),
            (1, grad_text, text_span, image_rows, text_rows),
        ):
            value = given[r, low : low + count, :].astype(F32) * mods[t, seq, 5:6, :]
            target[place, :] = value.astype(BF16)
        copies.send(acts.at[span, :], act_i.at[span, :])
        copies.send(slopes.at[span, :], slope_i.at[span, :])
        copies.send(grads.at[span, :], grad_i.at[span, :])
        copies.send(rows.at[r, pl.ds(0, image_rows), :], second_i.at[span, :])
    weights[1].wait()
    act_text[...], slope_text[...] = activate(
        dot_nt(second_text[...], held[1]) + bias[1:2, :]
    )
    for source, target in (
        (act_text, act_t),
        (slope_text, slope_t),
        (grad_text, grad_t),
        (second_text, second_t),
    ):
        copies.send(source, target)
    copies.finish()


def hidden_step(halves, cotangents, weight, bias, mods, seq, image_rows):
    block, width = halves[0].shape
    D, F = 2 * width, weight.shape[1]
    image, text = 4 * image_rows, 4 * (block - image_rows)

    def kernel(*refs):
        texts, semaphores = (refs[-5:-1], refs[-1])
        hidden_kernel(seq, image_rows, *refs[:-5], texts, semaphores)

    return run(
        kernel,
        "hidden",
        (*halves, *cotangents, weight, bias, mods),
        [ANYWHERE] * 17 + [ON_CORE] * 2,
        [((count, wide), BF16) for wide in (F, F, D, D) for count in (image, text)],
        [ANYWHERE] * 8,
        [
            pltpu.VMEM((4, block, D), BF16),
            pltpu.VMEM((4, block, D), BF16),
            pltpu.VMEM((2, F, D), BF16),
            pltpu.VMEM((image, F), BF16),
            pltpu.VMEM((image, F), BF16),
            pltpu.VMEM((image, D), BF16),
        ]
        + [pltpu.VMEM((text, wide), BF16) for wide in (D, D, F, F)],
        38,
    )


def outer_kernel(seqs, chunk, *refs):
    inputs, out = (refs[: 4 * seqs], refs[4 * seqs])
    held, result, semaphores = (refs[4 * seqs + 1 : -2], refs[-2], refs[-1])
    copies = Copies(semaphores)
    order = [4 * s + 2 * t + side for t in (1, 0) for s in range(seqs) for side in range(2)]
    fetched = {k: copies.start(inputs[k], held[k]) for k in order}
    columns = result.shape[1]
    for t in (1, 0):
        for s in range(seqs):
            fetched[4 * s + 2 * t].wait()
            fetched[4 * s + 2 * t + 1].wait()
        for low in range(0, columns, chunk):
            span = pl.ds(low, chunk)
            total = dot_tn(held[2 * t][:, span], held[2 * t + 1][...])
            for s in range(1, seqs):
                total = total + dot_tn(held[4 * s + 2 * t][:, span], held[4 * s + 2 * t + 1][...])
            result[t, span, :] = total.astype(BF16)
            copies.send(result.at[t, span, :], out.at[t, span, :])
    copies.finish()


def outer_sums(lefts, rights, chunk):
    seqs = len(lefts)
    columns, width = lefts[0][0].shape[1], rights[0][0].shape[1]
    operands = [side[s][t] for s in range(seqs) for t in range(2) for side in (lefts, rights)]
    return run(
        functools.partial(outer_kernel, seqs, chunk),
        "outer_sums",
        operands,
        [ANYWHERE] * (4 * seqs),
        [((2, columns, width), BF16)],
        [ANYWHERE],
        [pltpu.VMEM(value.shape, BF16) for value in operands]
        + [pltpu.VMEM((2, columns, width), BF16)],
        4 * seqs + 2 * (columns // chunk),
    )[0]


def hidden_back_kernel(image_rows, *refs):
    (grad_i, grad_t, slope_i, slope_t, down, up) = refs[:6]
    pre_i, pre_t, sums, sent = (refs[6], refs[7], refs[8], refs[9:14])
    grads, slopes, pres, grad_text, slope_text, pre_text, held_down, held_up, rows, semaphores = (
        refs[14:]
    )
    copies = Copies(semaphores)
    order = (3, 1, 2, 0)
    spans = {r: pl.ds(r * image_rows, image_rows) for r in order}
    images = {}
    downs, ups = ([None, None], [None, None])
    for k, r in enumerate(order):
        images[r] = [copies.start(grad_i.at[spans[r], :], grads.at[spans[r], :])]
        if k == 0:
            downs[0] = copies.start(down.at[0], held_down.at[0])
        images[r].append(copies.start(slope_i.at[spans[r], :], slopes.at[spans[r], :]))
        if k == 0:
            ups[0] = copies.start(up.at[0], held_up.at[0])
    texts = [copies.start(grad_t, grad_text), copies.start(slope_t, slope_text)]
    downs[1] = copies.start(down.at[1], held_down.at[1])
    ups[1] = copies.start(up.at[1], held_up.at[1])
    text_rows = rows.shape[1] - image_rows
    total = jnp.zeros((1, pres.shape[1]), F32)
    for k, r in enumerate(order):
        for copy in images[r]:
            copy.wait()
        if k == 0:
            downs[0].wait()
        product = dot_nt(grads[spans[r], :], held_down[0]) * slopes[spans[r], :].astype(F32)
        low = product.astype(BF16)
        pres[spans[r], :] = low
        copies.send(pres.at[spans[r], :], pre_i.at[spans[r], :])
        total = total + jnp.sum(low.astype(F32), axis=0, keepdims=True)
        if k == 0:
            ups[0].wait()
        rows[r, :image_rows, :] = dot_nn(pres[spans[r], :], held_up[0]).astype(BF16)
        if k == 1:
            for copy in texts:
                copy.wait()
            downs[1].wait()
            product = dot_nt(grad_text[...], held_down[1]) * slope_text[...].astype(F32)
            pre_text[...] = product.astype(BF16)
            copies.send(pre_text, pre_t)
            sums[1:2, :] = jnp.sum(pre_text[...].astype(F32), axis=0, keepdims=True)
            ups[1].wait()
            back = dot_nn(pre_text[...], held_up[1]).astype(BF16)
            for q in range(4):
                rows[q, image_rows:, :] = back[q * text_rows : (q + 1) * text_rows]
            send_block(copies, rows, sent, order[0])
        if k >= 1:
            send_block(copies, rows, sent, r)
    sums[0:1, :] = total
    copies.finish()


def hidden_back(grads, slopes, down, up, image_rows):
    image, D = grads[0].shape
    text = grads[1].shape[0]
    F = up.shape[1]
    block = (image + text) // 4
    outs = run(
        functools.partial(hidden_back_kernel, image_rows),
        "hidden_back",
        (*grads, *slopes, down, up),
        [ANYWHERE] * 6,
        [((image, F), BF16), ((text, F), BF16), ((2, F), F32)] + sent_shapes(block, D),
        [ANYWHERE] * 2 + [ON_CORE] + [ANYWHERE] * 5,
        [
            pltpu.VMEM((image, D), BF16),
            pltpu.VMEM((image, F), BF16),
            pltpu.VMEM((image, F), BF16),
            pltpu.VMEM((text, D), BF16),
            pltpu.VMEM((text, F), BF16),
            pltpu.VMEM((text, F), BF16),
            pltpu.VMEM((2, F, D), BF16),
            pltpu.VMEM((2, F, D), BF16),
            pltpu.VMEM((4, block, D), BF16),
        ],
        8 + 2 + 4 + 1 + 4 + 7,
    )
    return outs[0:2], outs[2], outs[3:]


def middle_back_kernel(seq, image_rows, *refs):
    pieces, cotangents, (middle_ref, projection_ref, mods) = (refs[:5], refs[5:7], refs[7:10])
    grad_ref, low_a, low_b, sums = refs[10:]
    block, width = low_a.shape
    for t, low, count in ((0, 0, image_rows), (1, image_rows, block - image_rows)):
        span = slice(low, low + count)
        norm_grad = piece_sum(pieces, low, count)
        norm, inverse = normalize(middle_ref[span, :])
        grad = both_halves(cotangents, seq, low, count) + normalize_back(
            norm, inverse, norm_grad, mods[t, seq, 4:5, :]
        )
        rounded = (mods[t, seq, 2:3, :] * grad).astype(BF16)
        grad_ref[span, :] = grad
        low_a[span, :] = rounded[:, :width]
        low_b[span, :] = rounded[:, width:]
        for k, value in enumerate(
            (norm_grad, norm_grad * norm, grad * projection_ref[span, :], rounded.astype(F32))
        ):
            sums[4 * t + k : 4 * t + k + 1, :] = jnp.sum(value, axis=0, keepdims=True)


def middle_back(pieces, cotangents, middle, projection, mods, seq, image_rows):
    block, width = pieces[3].shape
    return run(
        functools.partial(middle_back_kernel, seq, image_rows),
        "middle_back",
        (*pieces, *cotangents, middle, projection, mods),
        [ON_CORE] * 10,
        [((block, 2 * width), F32)] + [((block, width), BF16)] * 2 + [((8, 2 * width), F32)],
        [ON_CORE] * 4,
        [],
    )


def attended_back_kernel(image_rows, *refs):
    halves, weight = (refs[:8], refs[8])
    grad_i, grad_t, proj_i, proj_t = refs[9:13]
    rows, held, image_out, text_in, text_out, semaphores = refs[13:]
    copies = Copies(semaphores)
    fetched = fetch_halves(copies, halves, rows, None)
    weights = [copies.start(weight.at[t], held.at[t]) for t in range(2)]
    text_rows = rows.shape[1] - image_rows
    for r in range(4):
        for copy in fetched[r]:
            copy.wait()
        if r == 0:
            weights[0].wait()
        span = pl.ds(r * image_rows, image_rows)
        text_in[r * text_rows : (r + 1) * text_rows, :] = rows[r, image_rows:, :]
        copies.send(rows.at[r, pl.ds(0, image_rows), :], proj_i.at[span, :])
        image_out[span, :] = dot_nn(rows[r, :image_rows, :], held[0]).astype(BF16)
    copies.send(image_out, grad_i)
    copies.send(text_in, proj_t)
    weights[1].wait()
    text_out[...] = dot_nn(text_in[...], held[1]).astype(BF16)
    copies.send(text_out, grad_t)
    copies.finish()


def attended_back(halves, weight, image_rows):
    block, width = halves[0].shape
    D, E = 2 * width, weight.shape[2]
    image, text = 4 * image_rows, 4 * (block - image_rows)
    outs = run(
        functools.partial(attended_back_kernel, image_rows),
        "attended_back",
        (*halves, weight),
        [ANYWHERE] * 9,
        [((image, E), BF16), ((text, E), BF16), ((image, D), BF16), ((text, D), BF16)],
        [ANYWHERE] * 4,
        [
            pltpu.VMEM((4, block, D), BF16),
            pltpu.VMEM(weight.shape, BF16),
            pltpu.VMEM((image, E), BF16),
            pltpu.VMEM((text, D), BF16),
            pltpu.VMEM((text, E), BF16),
        ],
        10 + 7,
    )
    return outs[:2], outs[2:]


def project_back_kernel(seq, image_rows, *refs):
    (grad_i, grad_t, weight), tokens = (refs[:3], refs[3:11])
    sums, column_sums, sent = (refs[11], refs[12], refs[13:18])
    grads, grad_text, held, given, rows, semaphores = refs[18:]
    copies = Copies(semaphores)
    weights = [copies.start(weight.at[t], held.at[t]) for t in (1, 0)]
    text_in = copies.start(grad_t, grad_text)
    image_in = copies.start(grad_i, grads)
    fetched = fetch_halves(copies, tokens, given, seq)
    text_rows = rows.shape[1] - image_rows
    weights[0].wait()
    text_in.wait()
    text = dot_nn(grad_text[...], held[1])
    column_sums[1:2, :] = jnp.sum(grad_text[...].astype(F32), axis=0, keepdims=True)
    weights[1].wait()
    image_in.wait()
    totals = [jnp.zeros((1, rows.shape[2]), F32) for _ in range(4)]
    columns = jnp.zeros((1, grads.shape[1]), F32)
    for r in (3, 1, 2, 0):
        for copy in fetched[r]:
            copy.wait()
        span = pl.ds(r * image_rows, image_rows)
        for t, low, count in ((0, 0, image_rows), (1, image_rows, text_rows)):
            if t == 0:
                back = dot_nn(grads[span, :], held[0])
                columns = columns + jnp.sum(grads[span, :].astype(F32), axis=0, keepdims=True)
            else:
                back = text[r * text_rows : (r + 1) * text_rows, :]
            norm, _ = normalize(given[r, low : low + count, :].astype(F32))
            totals[2 * t] = totals[2 * t] + jnp.sum(back, axis=0, keepdims=True)
            totals[2 * t + 1] = totals[2 * t + 1] + jnp.sum(back * norm, axis=0, keepdims=True)
            rows[r, low : low + count, :] = back.astype(BF16)
        send_block(copies, rows, sent, r)
    column_sums[0:1, :] = columns
    for k in range(4):
        sums[k : k + 1, :] = totals[k]
    copies.finish()


def project_back(grads, weight, tokens, seq, image_rows):
    image, W = grads[0].shape
    text = grads[1].shape[0]
    D = weight.shape[2]
    block = (image + text) // 4
    outs = run(
        functools.partial(project_back_kernel, seq, image_rows),
        "project_back",
        (*grads, weight, *tokens),
        [ANYWHERE] * 11,
        [((4, D), F32), ((2, W), F32)] + sent_shapes(block, D),
        [ON_CORE] * 2 + [ANYWHERE] * 5,
        [
            pltpu.VMEM((image, W), BF16),
            pltpu.VMEM((text, W), BF16),
            pltpu.VMEM(weight.shape, BF16),
            pltpu.VMEM((4, block, D), BF16),
            pltpu.VMEM((4, block, D), BF16),
        ],
        4 + 8 + 7,
    )
    return outs[0], outs[1], outs[2:]


def result_kernel(image_rows, *refs):
    pieces, cotangents, middles = (refs[:10], refs[10:12], refs[12:14])
    mods, bias, image_out, text_out, sums = refs[14:]
    block = middles[0].shape[0]
    for seq in range(2):
        for t, low, count in ((0, 0, image_rows), (1, image_rows, block - image_rows)):
            span = slice(low, low + count)
            value = piece_sum(pieces[5 * seq : 5 * seq + 5], low, count) + bias[t : t + 1, :]
            gate = mods[t, seq, 5:6, :]
            out = (middles[seq][span, :] + gate * value).astype(BF16)
            if t == 0:
                image_out[seq] = out
            else:
                text_out[seq] = out
            grad = both_halves(cotangents, seq, low, count)
            low_grad = (gate * grad).astype(BF16).astype(F32)
            at = 4 * seq + 2 * t
            sums[at : at + 1, :] = jnp.sum(grad * value, axis=0, keepdims=True)
            sums[at + 1 : at + 2, :] = jnp.sum(low_grad, axis=0, keepdims=True)


def result_step(pieces, cotangents, middles, mods, bias, image_rows):
    seqs, (block, width) = (len(middles), pieces[3].shape)
    return run(
        functools.partial(result_kernel, image_rows),
        "result",
        (*pieces, *cotangents, *middles, mods, bias),
        [ON_CORE] * 16,
        [
            ((seqs, image_rows, 2 * width), BF16),
            ((seqs, block - image_rows, 2 * width), BF16),
            ((8, 2 * width), F32),
        ],
        [ON_CORE] * 3,
        [],
    )


def input_back_kernel(image_rows, live_text, *refs):
    pieces, tokens, grads, mods = (refs[:10], refs[10:12], refs[12:14], refs[14])
    image_out, text_out = refs[15:]
    block = grads[0].shape[0]
    for seq in range(2):
        for t, low, count in ((0, 0, image_rows), (1, image_rows, block - image_rows)):
            norm_grad = piece_sum(pieces[5 * seq : 5 * seq + 5], low, count)
            norm, inverse = normalize(both_halves(tokens, seq, low, count))
            out = grads[seq][low : low + count, :] + normalize_back(
                norm, inverse, norm_grad, mods[t, seq, 1:2, :]
            )
            if t == 0:
                image_out[seq] = out
            else:
                text_out[seq] = out[:live_text]


def input_back(pieces, tokens, grads, mods, image_rows, live_text):
    block, width = pieces[0][3].shape
    return run(
        functools.partial(input_back_kernel, image_rows, live_text),
        "input_back",
        (*pieces[0], *pieces[1], *tokens, *grads, mods),
        [ON_CORE] * 15,
        [((2, image_rows, 2 * width), F32), ((2, live_text, 2 * width), F32)],
        [ON_CORE] * 2,
        [],
    )


def match_units(batch_devices, seq_devices, per_device, group_units):
    devices = batch_devices * seq_devices
    total = devices * per_device
    part_units = total // 3
    sources, targets = ([], [])
    for seq_at in range(seq_devices):
        listed = [
            part * part_units + seq_at * group_units + k
            for part in range(3)
            for k in range(group_units)
        ]
        for place, unit in enumerate(listed):
            sources.append((unit // per_device, unit % per_device))
            targets.append(
                ((place // per_device) * seq_devices + seq_at, place % per_device)
            )
    edges = list(zip(sources, targets))
    rounds = []
    left = list(range(total))
    for _ in range(per_device):
        by_source = {}
        for e in left:
            by_source.setdefault(edges[e][0][0], []).append(e)
        taken = {}

        def place_edge(device, seen):
            for e in by_source[device]:
                target = edges[e][1][0]
                if target in seen:
                    continue
                seen.add(target)
                if target not in taken or place_edge(edges[taken[target]][0][0], seen):
                    taken[target] = e
                    return True
            return False

        for device in range(devices):
            place_edge(device, set())
        chosen = sorted(taken.values())
        rounds.append(chosen)
        left = [e for e in left if e not in chosen]
    send = np.zeros((per_device, devices), np.int32)
    land = np.zeros((per_device, devices), np.int32)
    perms = []
    for k, chosen in enumerate(rounds):
        pairs = []
        for e in chosen:
            (source, source_slot), (target, target_slot) = edges[e]
            pairs.append((source, target))
            send[k, source] = source_slot
            land[k, target] = target_slot
        perms.append(sorted(pairs))
    return perms, send, land


def move_units(units, perms, take, put, place):
    arrived = jnp.zeros_like(units)
    for k, pairs in enumerate(perms):
        slot = jnp.asarray(take[k])[place]
        moved = lax.ppermute(
            lax.dynamic_index_in_dim(units, slot, 0, keepdims=True), ("batch", "seq"), pairs
        )
        arrived = lax.dynamic_update_slice_in_dim(arrived, moved, jnp.asarray(put[k])[place], 0)
    return arrived


def gather_rows_over_batch(values):
    return lax.all_gather(values, "batch", axis=1, tiled=True)


def after(values, *others):
    return lax.optimization_barrier((values, others))[0]


def gather_small(values, axis, last=()):
    count = lax.axis_size(axis)
    held = values[None]
    bit = 1
    while bit < count:
        pairs = [(i, i ^ bit) for i in range(count)]
        if 2 * bit == count:
            held = after(held, last)
        held = jnp.concatenate([held, lax.ppermute(held, axis, pairs)])
        bit *= 2
    return jnp.take(held, jnp.bitwise_xor(lax.axis_index(axis), jnp.arange(count)), axis=0)


def scatter_rows_over_batch(values):
    dimension = values.ndim - 2
    return lax.psum_scatter(values, "batch", scatter_dimension=dimension, tiled=True)


def swap(values, axis):
    return lax.all_to_all(values, axis, 0, 0, tiled=True)


def swift_layer(
    image_tokens,
    text_tokens,
    conditioning,
    key_mask,
    mod_weight,
    mod_bias,
    qkv_weight,
    qv_bias,
    out_weight,
    out_bias,
    up_weight,
    up_bias,
    down_weight,
    down_bias,
    image_cotangent,
    text_cotangent,
):
    S = lax.axis_size("seq")
    B = lax.axis_size("batch")
    seq_index = lax.axis_index("seq")
    place = lax.axis_index(("batch", "seq"))
    L, image_count, D = image_tokens.shape
    live_text = text_tokens.shape[1]
    text_count = -(-live_text // 16) * 16
    pad = ((0, 0), (0, text_count - live_text), (0, 0))
    head = D // HEADS
    own_width = D // S
    half = D // 2

    unit = math.gcd(qkv_weight.shape[2], own_width)
    per_device = qkv_weight.shape[2] // unit
    perms, send, land = match_units(B, S, per_device, own_width // unit)
    back_perms = [[(target, source) for source, target in pairs] for pairs in perms]
    qkv_units = jnp.swapaxes(qkv_weight, 1, 2).reshape(2, per_device, unit, D).swapaxes(0, 1)
    qkv_mine = move_units(qkv_units, perms, send, land, place).swapaxes(0, 1)
    qkv_width = per_device * unit
    qkv_part = gather_rows_over_batch(qkv_mine.reshape(2, qkv_width, D))
    padded = jnp.concatenate([image_tokens, jnp.pad(text_tokens, pad)], axis=1)
    tokens = after((padded[..., :half], padded[..., half:]), qkv_mine)
    tokens_near = gather_near(*tokens)

    bias_widths = [array.shape[1] for array in (qv_bias, out_bias, up_bias, down_bias)]
    bias_ends = np.cumsum(bias_widths)
    own_biases = jnp.concatenate([qv_bias, out_bias, up_bias, down_bias], axis=1)
    near = gather_small(
        jnp.concatenate([conditioning, own_biases], axis=1),
        "batch",
        (tokens_near[0], tokens_near[3]),
    )
    cond_all = near[:, :, :D].reshape(B * L, D)
    column_biases = near[:, :, D:].astype(F32)
    smooth_all = jax.nn.silu(cond_all.astype(F32)).astype(BF16)
    mod_own = (
        jnp.einsum("sd,tdf->tsf", smooth_all, mod_weight, preferred_element_type=F32)
        + mod_bias.astype(F32)[:, None, :]
    )
    mod_width = mod_own.shape[2]
    mod_all = gather_small(mod_own, "batch", (tokens_near[1], tokens_near[2]))
    mod_came = lax.dynamic_slice_in_dim(mod_all, lax.axis_index("batch") * L, L, 2)
    small = jnp.concatenate(
        [mod_came.reshape(B, 2 * L * mod_width), column_biases.reshape(B, -1)], axis=1
    )
    tokens_all = gather_far(*tokens, tokens_near)
    small_all = gather_small(small, "seq", tokens_all[6:])
    modulation = (
        small_all[:, :, : 2 * L * mod_width]
        .reshape(S, B, 2, L, mod_width)
        .transpose(2, 3, 1, 0, 4)
        .reshape(2, L, 6, D)
    )
    bias_all = (
        small_all[:, :, 2 * L * mod_width :].reshape(S, B, 2, -1).transpose(2, 1, 0, 3)
    )
    qv_full = bias_all[..., : bias_ends[0]].reshape(2, 2 * D)
    out_bias_full = bias_all[..., bias_ends[0] : bias_ends[1]].reshape(2, D)
    down_bias_full = bias_all[..., bias_ends[2] :].reshape(2, D)
    up_bias_part = (
        column_biases[:, :, bias_ends[1] : bias_ends[2]].transpose(1, 0, 2).reshape(2, -1)
    )
    first_feature = seq_index * own_width
    qkv_bias = jnp.concatenate(
        [
            lax.dynamic_slice_in_dim(qv_full, first_feature, own_width, 1),
            jnp.zeros((2, own_width), F32),
            lax.dynamic_slice_in_dim(qv_full, D + first_feature, own_width, 1),
        ],
        axis=1,
    )

    out_units = jnp.swapaxes(out_weight, 1, 2).reshape(2, -1, S, own_width).transpose(2, 0, 1, 3)
    order = jnp.bitwise_xor(seq_index, jnp.arange(S))
    out_units = jnp.take(after(out_units, mod_own), order, axis=0)
    out_mine = jnp.stack([out_units[0], *(flip(out_units[r], r) for r in range(1, S))])
    out_mine = jnp.take(out_mine, order, axis=0)
    out_columns = out_mine.shape[2]
    out_rows = out_mine.transpose(1, 0, 2, 3).reshape(2, S * out_columns, own_width)
    out_part = gather_rows_over_batch(out_rows)
    hidden_columns = up_weight.shape[2]
    padded = jnp.concatenate([image_cotangent, jnp.pad(text_cotangent, pad)], axis=1)
    cotangents = (padded[..., :half], padded[..., half:])
    near_grads = gather_near(*after(cotangents, tokens_all, small_all))
    up_part = gather_rows_over_batch(after(jnp.swapaxes(up_weight, 1, 2), out_mine, mod_own))
    down_part = gather_rows_over_batch(after(jnp.swapaxes(down_weight, 1, 2), out_mine, mod_own))

    image_keys = jnp.take(
        key_mask[:, : S * image_count].reshape(L, S, image_count), order, axis=1
    )
    text_keys = jnp.take(
        key_mask[:, S * image_count :].reshape(L, S, live_text), order, axis=1
    )
    text_keys = jnp.pad(text_keys, ((0, 0), (0, 0), (0, text_count - live_text)))
    live = jnp.concatenate([image_keys.reshape(L, -1), text_keys.reshape(L, -1)], axis=1) > 0
    key_bias = jnp.where(live, 0.0, DEAD).astype(F32)
    floors = jnp.where(jnp.all(key_mask > 0, axis=1), -3e38, FLOOR_SCORE * LOG2E).astype(F32)
    floors = floors.reshape(L, 1, 1)
    key_bias = jnp.broadcast_to(key_bias[:, :, None], (*key_bias.shape, 128))

    kept = []
    first = project(tokens_all, qkv_part, modulation, qkv_bias, 0, image_count)
    attended = attention(first[0], first[1], key_bias[0], floors[0], head)
    attended, logs = (attended[:2], attended[2:])
    attended = after(attended, near_grads)
    parts = partial_sums([attended], out_part, dot_nt, D, image_count)
    kept.append((first, attended, logs, parts))
    again = after(tokens_all, parts)
    first = project(again, qkv_part, modulation, qkv_bias, 1, image_count)
    attended = attention(first[0], first[1], key_bias[1], floors[1], head)
    attended, logs = (attended[:2], attended[2:])
    cotangents_all = gather_far(*cotangents, after(near_grads, kept[0][1]))
    out_first = scatter_first(kept[0][3])
    out_added = scatter_added(kept[0][3], after(out_first, attended))
    attended = after(attended, cotangents_all, out_added)
    parts = partial_sums([attended], out_part, dot_nt, D, image_count)
    kept.append((first, attended, logs, parts))
    firsts, attendeds, logs, out_halves = zip(*kept)
    out_pieces = [scatter_sent(out_halves[0], out_first, out_added)]
    out_pieces.append(scatter_halves(after(out_halves[1], out_pieces[0])))
    steps = []
    for s in range(L):
        steps.append(
            middle_step(
                out_pieces[s],
                tokens,
                modulation,
                out_bias_full,
                s,
                image_count,
            )
        )
    second_near = [gather_near(*step[2:]) for step in steps]
    hidden = []
    for s in range(L):
        near = after(second_near[s], hidden[-1]) if s else second_near[s]
        halves = gather_far(*steps[s][2:], near)
        hidden.append(
            hidden_step(
                halves, cotangents_all, up_part, up_bias_part, modulation, s, image_count
            )
        )
    acts, slopes, grads, norms = [[step[i : i + 2] for step in hidden] for i in (0, 2, 4, 6)]

    down_sum = outer_sums(acts, grads, 256)
    down_came = scatter_rows_over_batch(down_sum)
    pres, bias_sums, norm2_halves = ([], [], [])
    gate = down_sum
    for s in range(L):
        pre, sums, halves = hidden_back(
            after(grads[s], gate), slopes[s], down_part, up_part, image_count
        )
        gate = halves
        pres.append(pre)
        bias_sums.append(sums)
        norm2_halves.append(halves)
    up_bias_sum = sum(bias_sums)
    norm2_first = scatter_first(norm2_halves[0])
    norm2_added = scatter_added(norm2_halves[0], after(norm2_first, gate))
    norm2_pieces = scatter_sent(norm2_halves[0], norm2_first, norm2_added)
    norm2_first1 = scatter_first(after(norm2_halves[1], norm2_pieces[3:]))
    backs = [
        middle_back(
            after(norm2_pieces, gate),
            cotangents,
            *steps[0][1::-1],
            modulation,
            0,
            image_count,
        )
    ]
    proj_near0 = gather_near(*backs[0][1:3])
    mlp_halves = partial_sums(after(acts, backs[0]), down_part, dot_nn, D, image_count)
    up_sum = outer_sums(after(pres, mlp_halves), norms, 256)
    norm2_added = scatter_added(norm2_halves[1], after(norm2_first1, mlp_halves))
    norm2_pieces = scatter_sent(norm2_halves[1], norm2_first1, norm2_added)
    projs = [gather_far(*backs[0][1:3], after(proj_near0, up_sum))]
    backs.append(
        middle_back(
            after(norm2_pieces, up_sum, proj_near0),
            cotangents,
            *steps[1][1::-1],
            modulation,
            1,
            image_count,
        )
    )
    proj_near1 = gather_near(*backs[1][1:3])
    grad0, proj0 = attended_back(
        after(projs[0], backs[1], down_came), out_part, image_count
    )
    up_came = scatter_rows_over_batch(after(up_sum, backs[1]))
    qkv_grad0 = attention_back(
        *firsts[0][:2], *attendeds[0], *logs[0], *grad0, key_bias[0], head
    )
    projs.append(gather_far(*backs[1][1:3], after(proj_near1, qkv_grad0)))
    mlp_halves = (mlp_halves[:5], mlp_halves[5:])
    mlp_first = [scatter_first(after(mlp_halves[0], grad0))]
    sums0, columns0, halves0 = project_back(
        after(qkv_grad0, mlp_first), qkv_part, tokens_all, 0, image_count
    )
    grad1, proj1 = attended_back(after(projs[1], halves0), out_part, image_count)
    mlp_first.append(scatter_first(after(mlp_halves[1], projs[1])))
    out_sum = outer_sums([proj0, proj1], attendeds, 256)
    out_came = scatter_rows_over_batch(out_sum)
    grad1 = after(grad1, out_sum)
    qkv_grad1 = attention_back(
        *firsts[1][:2], *attendeds[1], *logs[1], *grad1, key_bias[1], head
    )
    mlp_added = [
        scatter_added(halves, after(first, qkv_grad1))
        for halves, first in zip(mlp_halves, mlp_first)
    ]
    mlp_pieces = [
        piece
        for halves, first, added in zip(mlp_halves, mlp_first, mlp_added)
        for piece in scatter_sent(halves, first, added)
    ]
    qkv_sum = outer_sums(
        [qkv_grad0, after(qkv_grad1, mlp_added, up_came)],
        [first[2:] for first in firsts],
        128 if qkv_width % 256 else 256,
    )
    qkv_came = scatter_rows_over_batch(after(qkv_sum, out_came))
    sums1, columns1, halves1 = project_back(
        after(qkv_grad1, qkv_sum), qkv_part, tokens_all, 1, image_count
    )
    norm1_pieces = [
        scatter_halves(after(halves0, qkv_sum)),
        scatter_halves(after(halves1, mlp_pieces)),
    ]
    image_out, text_out, result_sums = result_step(
        after(mlp_pieces, halves1),
        cotangents,
        [step[1] for step in steps],
        modulation,
        down_bias_full,
        image_count,
    )
    image_grad, text_grad = input_back(
        after(norm1_pieces, qkv_came),
        tokens,
        [back[0] for back in backs],
        modulation,
        image_count,
        live_text,
    )
    out_home = swap(
        after(out_came, image_grad).reshape(2, S, out_columns, own_width).swapaxes(0, 1), "seq"
    )
    qkv_home = move_units(
        qkv_came.reshape(2, per_device, unit, D).swapaxes(0, 1),
        back_perms, land, send, place
    )
    qkv_weight_grad = qkv_home.swapaxes(0, 1).reshape(2, -1, D).swapaxes(1, 2).astype(F32)
    out_weight_grad = (
        out_home.transpose(1, 2, 0, 3).reshape(2, out_columns, D).swapaxes(1, 2).astype(F32)
    )
    up_weight_grad = up_came.swapaxes(1, 2).astype(F32)
    down_weight_grad = down_came.swapaxes(1, 2).astype(F32)


    first_sums = jnp.stack([sums0, sums1]).reshape(L, 2, 2, D)
    second_sums = jnp.stack([back[3] for back in backs]).reshape(L, 2, 4, D)
    result_sums = result_sums.reshape(L, 2, 2, D)
    mod_rows = jnp.concatenate(
        [
            first_sums,
            second_sums[:, :, 2:3],
            second_sums[:, :, :2],
            result_sums[:, :, :1],
        ],
        axis=2,
    ).swapaxes(0, 1)
    mod_rows = mod_rows.reshape(2, L, B, S, mod_width).transpose(3, 2, 0, 1, 4)
    out_bias_sum = jnp.sum(second_sums[:, :, 3], axis=0)
    down_bias_sum = jnp.sum(result_sums[:, :, 1], axis=0)
    column_sums = columns0 + columns1
    qv_bias_sum = jnp.zeros((2, 2 * D), F32)
    for part, column in ((0, 0), (1, 2 * own_width)):
        qv_bias_sum = lax.dynamic_update_slice_in_dim(
            qv_bias_sum, column_sums[:, column : column + own_width], part * D + first_feature, 1
        )
    up_bias_rows = lax.dynamic_update_slice_in_dim(
        jnp.zeros((2, B, S, hidden_columns), F32),
        up_bias_sum.reshape(2, B, 1, hidden_columns),
        seq_index,
        2,
    )
    bias_rows = jnp.concatenate(
        [
            qv_bias_sum.reshape(2, B, S, -1),
            out_bias_sum.reshape(2, B, S, -1),
            up_bias_rows,
            down_bias_sum.reshape(2, B, S, -1),
        ],
        axis=3,
    ).transpose(2, 1, 0, 3)
    packed = jnp.concatenate(
        [mod_rows.reshape(S, B, -1), bias_rows.reshape(S, B, -1)], axis=2
    )
    packed = jnp.sum(swap(packed, "seq"), axis=0)
    packed = swap(packed, "batch")
    mod_mine = (
        packed[:, : 2 * L * mod_width]
        .reshape(B, 2, L, mod_width)
        .transpose(1, 0, 2, 3)
        .reshape(2, B * L, mod_width)
        .astype(BF16)
    )
    bias_mine = jnp.sum(packed[:, 2 * L * mod_width :], axis=0).reshape(2, -1)
    qv_bias_grad, out_bias_grad, up_bias_grad, down_bias_grad = jnp.split(
        bias_mine, bias_ends[:3], axis=1
    )
    mod_weight_grad = jnp.einsum(
        "sd,tsf->tdf", smooth_all, mod_mine, preferred_element_type=F32
    )
    mod_bias_grad = jnp.sum(mod_mine.astype(F32), axis=1)
    smooth_part = jnp.einsum("tsf,tdf->sd", mod_mine, mod_weight, preferred_element_type=F32)
    smooth_grad = jnp.sum(swap(smooth_part.reshape(B, L, D), "batch"), axis=0)
    smooth_grad = after(smooth_grad, qkv_home)
    smooth_grad = smooth_grad + flip(smooth_grad, 1)
    smooth_grad = smooth_grad + flip(smooth_grad, 2)
    cond_grad = jax.vjp(jax.nn.silu, conditioning.astype(F32))[1](smooth_grad)[0]
    return (
        image_out,
        text_out[:, :live_text],
        image_grad,
        text_grad,
        cond_grad,
        mod_weight_grad,
        mod_bias_grad,
        qkv_weight_grad,
        qv_bias_grad,
        out_weight_grad,
        out_bias_grad,
        up_weight_grad,
        up_bias_grad,
        down_weight_grad,
        down_bias_grad,
    )


def choose_layer(mesh):
    if mesh.shape["seq"] == 4 and HEADS % 8 == 0:
        return swift_layer
    return general_layer


def solution(mesh):
    layer = choose_layer(mesh)
    return jax.shard_map(
        layer,
        mesh=mesh,
        in_specs=(
            P("batch", "seq", None),
            P("batch", "seq", None),
            P("batch", None),
            P("batch", None),
            P(None, None, ("batch", "seq")),
            P(None, ("batch", "seq")),
            P(None, None, ("batch", "seq")),
            P(None, ("batch", "seq")),
            P(None, None, ("batch", "seq")),
            P(None, ("batch", "seq")),
            P(None, None, ("batch", "seq")),
            P(None, ("batch", "seq")),
            P(None, None, ("batch", "seq")),
            P(None, ("batch", "seq")),
            P("batch", "seq", None),
            P("batch", "seq", None),
        ),
        out_specs=(
            P("batch", "seq", None),
            P("batch", "seq", None),
            P("batch", "seq", None),
            P("batch", "seq", None),
            P("batch", None),
            P(None, None, ("batch", "seq")),
            P(None, ("batch", "seq")),
            P(None, None, ("batch", "seq")),
            P(None, ("batch", "seq")),
            P(None, None, ("batch", "seq")),
            P(None, ("batch", "seq")),
            P(None, None, ("batch", "seq")),
            P(None, ("batch", "seq")),
            P(None, None, ("batch", "seq")),
            P(None, ("batch", "seq")),
        ),
        check_vma=False,
    )
```

```python
import functools
import math

import jax
import jax.numpy as jnp
import numpy as np
from jax import lax
from jax.experimental import pallas as pl
from jax.experimental.pallas import tpu as pltpu
from jax.sharding import PartitionSpec as P

HEADS = 24


NORM_EPSILON = 1e-06
FLOOR_SCORE = -10000.0


def modulate(tokens, shift_vec, scale_vec):
    row_mean = jnp.mean(tokens, axis=-1, keepdims=True)
    centered = tokens - row_mean
    row_var = jnp.mean(centered * centered, axis=-1, keepdims=True)
    return (
        centered * lax.rsqrt(row_var + NORM_EPSILON) * (1.0 + scale_vec[:, None, :])
        + shift_vec[:, None, :]
    )


def gelu_tanh(values):
    return jax.nn.gelu(values, approximate=True)


def unmix_columns(values, seq_devices, batch_devices):
    array_shape = values.shape
    piece_width = array_shape[-1] // (seq_devices * batch_devices)
    grid_view = values.reshape(array_shape[:-1] + (seq_devices, batch_devices, piece_width))
    return jnp.swapaxes(grid_view, -3, -2).reshape(array_shape)


def remix_columns(values, seq_devices, batch_devices):
    array_shape = values.shape
    piece_width = array_shape[-1] // (seq_devices * batch_devices)
    grid_view = values.reshape(array_shape[:-1] + (batch_devices, seq_devices, piece_width))
    return jnp.swapaxes(grid_view, -3, -2).reshape(array_shape)


def fetch_columns(
    up_weight,
    down_weight,
    mod_weight,
    qkv_weight,
    out_weight,
    up_bias,
    mod_bias,
    qv_bias,
    out_bias,
    down_bias,
):
    return (
        lax.all_gather(up_weight, "batch", axis=2, tiled=True),
        lax.all_gather(down_weight, "batch", axis=2, tiled=True),
        lax.all_gather(mod_weight, "batch", axis=2, tiled=True),
        lax.all_gather(qkv_weight, "batch", axis=2, tiled=True),
        lax.all_gather(out_weight, "batch", axis=2, tiled=True),
        lax.all_gather(up_bias, "batch", axis=1, tiled=True),
        lax.all_gather(mod_bias, "batch", axis=1, tiled=True),
        lax.all_gather(qv_bias, "batch", axis=1, tiled=True),
        lax.all_gather(out_bias, "batch", axis=1, tiled=True),
        lax.all_gather(down_bias, "batch", axis=1, tiled=True),
    )


def fetch_modulation(mod_part, mod_bias_part):
    return (
        lax.all_gather(mod_part, "seq", axis=2, tiled=True),
        lax.all_gather(mod_bias_part, "seq", axis=1, tiled=True),
    )


def gather_rows(first, second):
    return (
        lax.all_gather(first, "seq", axis=1, tiled=True),
        lax.all_gather(second, "seq", axis=1, tiled=True),
    )


def sum_rows(first, second, seq_devices):
    local_seqs, first_rows, width = first.shape
    first_local = first_rows // seq_devices
    second_local = second.shape[1] // seq_devices
    joined = jnp.concatenate(
        [
            first.reshape(local_seqs, seq_devices, first_local, width),
            second.reshape(local_seqs, seq_devices, second_local, width),
        ],
        axis=2,
    )
    joined = joined.reshape(local_seqs, seq_devices * (first_local + second_local), width)
    total = lax.psum_scatter(joined, "seq", scatter_dimension=1, tiled=True)
    return (total[:, :first_local], total[:, first_local:])


def to_rows(first, second):
    return (
        lax.all_to_all(first, "seq", split_axis=1, concat_axis=2, tiled=True),
        lax.all_to_all(second, "seq", split_axis=1, concat_axis=2, tiled=True),
    )


def to_columns(first, second):
    return (
        lax.all_to_all(first, "seq", split_axis=2, concat_axis=1, tiled=True),
        lax.all_to_all(second, "seq", split_axis=2, concat_axis=1, tiled=True),
    )


def own_block(values, seq_index, seq_devices):
    width = values.shape[1] // seq_devices
    return lax.dynamic_slice_in_dim(values, seq_index * width, width, 1)


def general_layer(
    image_tokens,
    text_tokens,
    conditioning,
    key_mask,
    mod_weight,
    mod_bias,
    qkv_weight,
    qv_bias,
    out_weight,
    out_bias,
    up_weight,
    up_bias,
    down_weight,
    down_bias,
    image_cotangent,
    text_cotangent,
):
    seq_devices = lax.axis_size("seq")
    batch_devices = lax.axis_size("batch")
    seq_index = lax.axis_index("seq")
    local_seqs, image_count, model_width = image_tokens.shape
    text_count = text_tokens.shape[1]
    block_rows = image_count + text_count
    key_count = block_rows * seq_devices
    head_size = model_width // HEADS
    factor = 1.0 / math.sqrt(head_size)
    inputs = (image_tokens.astype(jnp.float32), text_tokens.astype(jnp.float32))
    cotangents = (image_cotangent.astype(jnp.float32), text_cotangent.astype(jnp.float32))
    row_spans = ((0, image_count), (image_count, block_rows))
    image_keys = key_mask[:, : image_count * seq_devices].reshape(
        local_seqs, seq_devices, image_count
    )
    text_keys = key_mask[:, image_count * seq_devices :].reshape(
        local_seqs, seq_devices, text_count
    )
    key_live = (
        jnp.concatenate([image_keys, text_keys], axis=2).reshape(local_seqs, key_count) > 0
    )[:, None, None, :]
    cond_float = conditioning.astype(jnp.float32)
    smooth = jax.nn.silu(cond_float).astype(jnp.bfloat16)
    fetched = fetch_columns(
        up_weight,
        down_weight,
        mod_weight,
        qkv_weight,
        out_weight,
        up_bias,
        mod_bias,
        qv_bias,
        out_bias,
        down_bias,
    )
    (
        up_part,
        down_part,
        mod_part,
        qkv_part,
        out_part,
        up_bias_part,
        mod_bias_part,
        qv_part,
        out_bias_part,
        down_bias_part,
    ) = fetched
    mod_full, mod_bias_full = fetch_modulation(mod_part, mod_bias_part)
    mixed_mod = (
        jnp.einsum("sd,tdf->tsf", smooth, mod_full, preferred_element_type=jnp.float32)
        + mod_bias_full.astype(jnp.float32)[:, None, :]
    )
    modulation = unmix_columns(mixed_mod, seq_devices, batch_devices).reshape(
        2, local_seqs, 6, model_width
    )
    first_norms = []
    for modality in range(2):
        pieces = modulation[modality]
        first_norms.append(
            modulate(inputs[modality], pieces[:, 0], pieces[:, 1]).astype(jnp.bfloat16)
        )
    norm_image_all, norm_text_all, qv_seq, out_bias_seq, down_bias_seq = (
        lax.all_gather(first_norms[0], "seq", axis=1, tiled=True),
        lax.all_gather(first_norms[1], "seq", axis=1, tiled=True),
        lax.all_gather(qv_part, "seq", axis=1, tiled=True),
        lax.all_gather(out_bias_part, "seq", axis=1, tiled=True),
        lax.all_gather(down_bias_part, "seq", axis=1, tiled=True),
    )
    first_all = (norm_image_all, norm_text_all)
    qv_full = unmix_columns(qv_seq, seq_devices, batch_devices).astype(jnp.float32)
    out_bias_full = unmix_columns(out_bias_seq, seq_devices, batch_devices).astype(jnp.float32)
    down_bias_full = unmix_columns(down_bias_seq, seq_devices, batch_devices).astype(jnp.float32)
    qkv_cols = [
        jnp.einsum(
            "srd,df->srf",
            first_all[modality],
            qkv_part[modality],
            preferred_element_type=jnp.float32,
        )
        for modality in range(2)
    ]
    qkv_rows = to_rows(qkv_cols[0], qkv_cols[1])
    queries, keyvals = ([], [])
    for modality in range(2):
        projected = unmix_columns(qkv_rows[modality], seq_devices, batch_devices)
        qv_vector = qv_full[modality]
        queries.append(
            (projected[..., :model_width] + qv_vector[:model_width]).astype(jnp.bfloat16)
        )
        value_shift = jnp.concatenate(
            [jnp.zeros((model_width,), jnp.float32), qv_vector[model_width:]]
        )
        keyvals.append((projected[..., model_width:] + value_shift).astype(jnp.bfloat16))
    joined_query = jnp.concatenate(queries, axis=1)
    joined_keyval = jnp.concatenate(keyvals, axis=1)
    all_keyval = lax.all_gather(joined_keyval, "seq", axis=1, tiled=True)
    query_heads = joined_query.reshape(local_seqs, block_rows, HEADS, head_size)
    key_heads = all_keyval[..., :model_width].reshape(local_seqs, key_count, HEADS, head_size)
    value_heads = all_keyval[..., model_width:].reshape(local_seqs, key_count, HEADS, head_size)
    scores = (
        jnp.einsum("sqhe,skhe->shqk", query_heads, key_heads, preferred_element_type=jnp.float32)
        * factor
    )
    row_max = jnp.max(jnp.where(key_live, scores, FLOOR_SCORE), axis=-1, keepdims=True)
    exp_terms = jnp.exp(jnp.where(key_live, scores - row_max, FLOOR_SCORE))
    denominator = jnp.maximum(jnp.sum(exp_terms, axis=-1, keepdims=True), 1.0)
    prob_low = (exp_terms / denominator).astype(jnp.bfloat16)
    logsum = row_max + jnp.log(denominator)
    attended = jnp.einsum(
        "shqk,skhe->sqhe", prob_low, value_heads, preferred_element_type=jnp.float32
    )
    attended = attended.reshape(local_seqs, block_rows, model_width).astype(jnp.bfloat16)
    attended_all = gather_rows(attended[:, :image_count], attended[:, image_count:])
    out_cols = [
        jnp.einsum(
            "srd,df->srf",
            attended_all[modality],
            out_part[modality],
            preferred_element_type=jnp.float32,
        )
        for modality in range(2)
    ]
    out_rows = to_rows(out_cols[0], out_cols[1])
    projections, middles, second_norms = ([], [], [])
    for modality in range(2):
        pieces = modulation[modality]
        projection = (
            unmix_columns(out_rows[modality], seq_devices, batch_devices) + out_bias_full[modality]
        )
        middle = inputs[modality] + pieces[:, 2][:, None, :] * projection
        second_norms.append(modulate(middle, pieces[:, 3], pieces[:, 4]).astype(jnp.bfloat16))
        projections.append(projection)
        middles.append(middle)
    group_rows = gather_rows(second_norms[0], second_norms[1])
    hidden_pre, hidden_act, partials = ([], [], [])
    for modality in range(2):
        pre_values = jnp.einsum(
            "srd,df->srf",
            group_rows[modality],
            up_part[modality],
            preferred_element_type=jnp.float32,
        ) + up_bias_part[modality].astype(jnp.float32)
        act_values = gelu_tanh(pre_values).astype(jnp.bfloat16)
        partials.append(
            jnp.einsum(
                "srf,df->srd", act_values, down_part[modality], preferred_element_type=jnp.float32
            )
        )
        hidden_pre.append(pre_values)
        hidden_act.append(act_values)
    mlp_rows = sum_rows(partials[0], partials[1], seq_devices)
    mlp_outs, results = ([], [])
    for modality in range(2):
        pieces = modulation[modality]
        mlp_value = mlp_rows[modality] + down_bias_full[modality]
        results.append(
            (middles[modality] + pieces[:, 5][:, None, :] * mlp_value).astype(jnp.bfloat16)
        )
        mlp_outs.append(mlp_value)
    fetched_back = fetch_columns(
        up_weight,
        down_weight,
        mod_weight,
        qkv_weight,
        out_weight,
        up_bias,
        mod_bias,
        qv_bias,
        out_bias,
        down_bias,
    )
    up_back, down_back, mod_back, qkv_back, out_back = (
        fetched_back[0],
        fetched_back[1],
        fetched_back[2],
        fetched_back[3],
        fetched_back[4],
    )
    mod_bias_back = fetched_back[6]
    mlp_grads, gate_twos, down_bias_grads = ([], [], [])
    for modality in range(2):
        pieces = modulation[modality]
        mlp_grad = (pieces[:, 5][:, None, :] * cotangents[modality]).astype(jnp.bfloat16)
        gate_twos.append(jnp.sum(cotangents[modality] * mlp_outs[modality], axis=1))
        down_bias_grads.append(jnp.sum(mlp_grad.astype(jnp.float32), axis=(0, 1)))
        mlp_grads.append(mlp_grad)
    group_grads = gather_rows(mlp_grads[0], mlp_grads[1])
    down_grads, up_grads, up_bias_grads, norm_partials = ([], [], [], [])
    for modality in range(2):
        down_grads.append(
            jnp.einsum(
                "srd,srf->df",
                group_grads[modality],
                hidden_act[modality],
                preferred_element_type=jnp.float32,
            )
        )
        act_grad = jnp.einsum(
            "srd,df->srf",
            group_grads[modality],
            down_back[modality],
            preferred_element_type=jnp.float32,
        )
        pullback = jax.vjp(gelu_tanh, hidden_pre[modality])[1]
        pre_grad = pullback(act_grad)[0].astype(jnp.bfloat16)
        up_grads.append(
            jnp.einsum(
                "srd,srf->df", group_rows[modality], pre_grad, preferred_element_type=jnp.float32
            )
        )
        up_bias_grads.append(jnp.sum(pre_grad.astype(jnp.float32), axis=(0, 1)))
        norm_partials.append(
            jnp.einsum(
                "srf,df->srd", pre_grad, up_back[modality], preferred_element_type=jnp.float32
            )
        )
    norm_grads = sum_rows(norm_partials[0], norm_partials[1], seq_devices)
    middle_grads, shift_twos, scale_twos, gate_ones, out_bias_grads, proj_grads = (
        [],
        [],
        [],
        [],
        [],
        [],
    )
    for modality in range(2):
        pieces = modulation[modality]
        pullback = jax.vjp(modulate, middles[modality], pieces[:, 3], pieces[:, 4])[1]
        middle_part, shift_two, scale_two = pullback(norm_grads[modality])
        middle_grad = cotangents[modality] + middle_part
        proj_grad = (pieces[:, 2][:, None, :] * middle_grad).astype(jnp.bfloat16)
        gate_ones.append(jnp.sum(middle_grad * projections[modality], axis=1))
        out_bias_grads.append(jnp.sum(proj_grad.astype(jnp.float32), axis=(0, 1)))
        proj_grads.append(remix_columns(proj_grad, seq_devices, batch_devices))
        middle_grads.append(middle_grad)
        shift_twos.append(shift_two)
        scale_twos.append(scale_two)
    proj_cols = to_columns(proj_grads[0], proj_grads[1])
    out_grads, attended_partials = ([], [])
    for modality in range(2):
        out_grads.append(
            jnp.einsum(
                "srd,srf->df",
                attended_all[modality],
                proj_cols[modality],
                preferred_element_type=jnp.float32,
            )
        )
        attended_partials.append(
            jnp.einsum(
                "srf,df->srd",
                proj_cols[modality],
                out_back[modality],
                preferred_element_type=jnp.float32,
            )
        )
    attended_sums = sum_rows(attended_partials[0], attended_partials[1], seq_devices)
    attended_grad = jnp.concatenate([attended_sums[0], attended_sums[1]], axis=1).astype(
        jnp.bfloat16
    )
    grad_heads = attended_grad.reshape(local_seqs, block_rows, HEADS, head_size)
    scores_again = (
        jnp.einsum("sqhe,skhe->shqk", query_heads, key_heads, preferred_element_type=jnp.float32)
        * factor
    )
    probs_again = jnp.exp(jnp.where(key_live, scores_again - logsum, FLOOR_SCORE))
    probs_again_low = probs_again.astype(jnp.bfloat16)
    prob_grad = jnp.einsum(
        "sqhe,skhe->shqk", grad_heads, value_heads, preferred_element_type=jnp.float32
    )
    inner_sum = jnp.sum(probs_again * prob_grad, axis=-1, keepdims=True)
    score_grad = (probs_again * (prob_grad - inner_sum)).astype(jnp.bfloat16)
    query_grad = (
        jnp.einsum("shqk,skhe->sqhe", score_grad, key_heads, preferred_element_type=jnp.float32)
        * factor
    )
    query_grad = query_grad.reshape(local_seqs, block_rows, model_width).astype(jnp.bfloat16)
    key_grad = (
        jnp.einsum("shqk,sqhe->skhe", score_grad, query_heads, preferred_element_type=jnp.float32)
        * factor
    )
    value_grad = jnp.einsum(
        "shqk,sqhe->skhe", probs_again_low, grad_heads, preferred_element_type=jnp.float32
    )
    key_rows, value_rows = (
        lax.psum_scatter(
            key_grad.reshape(local_seqs, key_count, model_width),
            "seq",
            scatter_dimension=1,
            tiled=True,
        ),
        lax.psum_scatter(
            value_grad.reshape(local_seqs, key_count, model_width),
            "seq",
            scatter_dimension=1,
            tiled=True,
        ),
    )
    key_rows = key_rows.astype(jnp.bfloat16)
    value_rows = value_rows.astype(jnp.bfloat16)
    qv_bias_grads, joined_grads = ([], [])
    for modality in range(2):
        row_start, row_stop = row_spans[modality]
        query_part = query_grad[:, row_start:row_stop]
        value_part = value_rows[:, row_start:row_stop]
        joined_grad = jnp.concatenate(
            [query_part, key_rows[:, row_start:row_stop], value_part], axis=-1
        )
        qv_bias_grads.append(
            jnp.concatenate(
                [
                    jnp.sum(query_part.astype(jnp.float32), axis=(0, 1)),
                    jnp.sum(value_part.astype(jnp.float32), axis=(0, 1)),
                ]
            )
        )
        joined_grads.append(remix_columns(joined_grad, seq_devices, batch_devices))
    qkv_grad_cols = to_columns(joined_grads[0], joined_grads[1])
    qkv_grads, first_partials = ([], [])
    for modality in range(2):
        qkv_grads.append(
            jnp.einsum(
                "srd,srf->df",
                first_all[modality],
                qkv_grad_cols[modality],
                preferred_element_type=jnp.float32,
            )
        )
        first_partials.append(
            jnp.einsum(
                "srf,df->srd",
                qkv_grad_cols[modality],
                qkv_back[modality],
                preferred_element_type=jnp.float32,
            )
        )
    first_grads = sum_rows(first_partials[0], first_partials[1], seq_devices)
    input_grads, mod_partials = ([], [])
    for modality in range(2):
        pieces = modulation[modality]
        pullback = jax.vjp(modulate, inputs[modality], pieces[:, 0], pieces[:, 1])[1]
        input_part, shift_one, scale_one = pullback(first_grads[modality])
        input_grads.append(middle_grads[modality] + input_part)
        stacked = jnp.stack(
            [
                shift_one,
                scale_one,
                gate_ones[modality],
                shift_twos[modality],
                scale_twos[modality],
                gate_twos[modality],
            ],
            axis=1,
        )
        mod_partials.append(stacked.reshape(local_seqs, 6 * model_width))
    qv_mixed = remix_columns(jnp.stack(qv_bias_grads), seq_devices, batch_devices)
    out_bias_mixed = remix_columns(jnp.stack(out_bias_grads), seq_devices, batch_devices)
    down_bias_mixed = remix_columns(jnp.stack(down_bias_grads), seq_devices, batch_devices)
    mod_sum, qv_summed, out_bias_summed, down_bias_summed = lax.psum(
        (jnp.stack(mod_partials), qv_mixed, out_bias_mixed, down_bias_mixed), "seq"
    )
    mod_low = mod_sum.astype(jnp.bfloat16)
    mod_mixed = remix_columns(mod_low, seq_devices, batch_devices)
    columns = mod_part.shape[2]
    own_columns = lax.dynamic_slice_in_dim(mod_mixed, seq_index * columns, columns, 2)
    mod_grad = jnp.einsum("sd,tsf->tdf", smooth, own_columns, preferred_element_type=jnp.float32)
    mod_bias_grad = jnp.sum(own_columns.astype(jnp.float32), axis=1)
    mod_again = fetch_modulation(mod_back, mod_bias_back)[0]
    smooth_grad = jnp.einsum(
        "tsf,tdf->sd", mod_mixed, mod_again, preferred_element_type=jnp.float32
    )
    cond_pullback = jax.vjp(jax.nn.silu, cond_float)[1]
    cond_grad = cond_pullback(smooth_grad)[0]
    qv_own = own_block(qv_summed, seq_index, seq_devices)
    out_bias_own = own_block(out_bias_summed, seq_index, seq_devices)
    down_bias_own = own_block(down_bias_summed, seq_index, seq_devices)
    column_grads = (
        lax.psum_scatter(jnp.stack(up_grads), "batch", scatter_dimension=2, tiled=True),
        lax.psum_scatter(jnp.stack(down_grads), "batch", scatter_dimension=2, tiled=True),
        lax.psum_scatter(mod_grad, "batch", scatter_dimension=2, tiled=True),
        lax.psum_scatter(jnp.stack(qkv_grads), "batch", scatter_dimension=2, tiled=True),
        lax.psum_scatter(jnp.stack(out_grads), "batch", scatter_dimension=2, tiled=True),
        lax.psum_scatter(jnp.stack(up_bias_grads), "batch", scatter_dimension=1, tiled=True),
        lax.psum_scatter(mod_bias_grad, "batch", scatter_dimension=1, tiled=True),
        lax.psum_scatter(qv_own, "batch", scatter_dimension=1, tiled=True),
        lax.psum_scatter(out_bias_own, "batch", scatter_dimension=1, tiled=True),
        lax.psum_scatter(down_bias_own, "batch", scatter_dimension=1, tiled=True),
    )
    return (
        results[0],
        results[1],
        input_grads[0],
        input_grads[1],
        cond_grad,
        column_grads[2],
        column_grads[6],
        column_grads[3],
        column_grads[7],
        column_grads[4],
        column_grads[8],
        column_grads[0],
        column_grads[5],
        column_grads[1],
        column_grads[9],
    )


LOG2E = 1.4426950408889634
DEAD = -1e30
BF16 = jnp.bfloat16
F32 = jnp.float32


def dot_nt(a, b):
    return lax.dot_general(a, b, (((1,), (1,)), ((), ())), preferred_element_type=F32)


def dot_nn(a, b):
    return lax.dot_general(a, b, (((1,), (0,)), ((), ())), preferred_element_type=F32)


def dot_tn(a, b):
    return lax.dot_general(a, b, (((0,), (0,)), ((), ())), preferred_element_type=F32)


WEIGHT = {
    "attention": 0.17,
    "attention_back": 0.32,
    "project": 0.13,
    "partial_sums": 0.05,
    "middle": 0.05,
    "hidden": 0.18,
    "outer_sums": 0.18,
    "hidden_back": 0.2,
    "middle_back": 0.07,
    "attended_back": 0.06,
    "project_back": 0.12,
    "result": 0.07,
    "input_back": 0.09,
}


def lanes_of(columns, rows, width):
    lane = lax.broadcasted_iota(jnp.int32, (rows, width), 1)
    out = jnp.zeros((rows, width), F32)
    for k, column in enumerate(columns):
        out = jnp.where(lane == k, column, out)
    return out.astype(BF16)


def three_parts(column):
    high = column.astype(BF16).astype(F32)
    rest = column - high
    mid = rest.astype(BF16).astype(F32)
    return [high, mid, rest - mid]


def attention_kernel(
    query_rows, scale, head, bias_ref, floor_ref, qi, qt, ki, kt, vi, vt, oi, ot, li, lt, keys, values
):
    image_rows = qi.shape[0]
    rows = keys.shape[1]
    floor = floor_ref[0, 0]
    key_side = lanes_of([bias_ref[:, 0:1]], rows, head)
    value_side = lanes_of([1.0], rows, head)
    for side in range(2):
        lanes = slice(side * head, (side + 1) * head)
        for ref, extra, first, second in (
            (keys, key_side, ki, kt),
            (values, value_side, vi, vt),
        ):
            ref[side, :image_rows, :] = jnp.concatenate(
                [first[:, lanes], extra[:image_rows]], axis=1
            )
            ref[side, image_rows:, :] = jnp.concatenate(
                [second[:, lanes], extra[image_rows:]], axis=1
            )
    spans = [(qi, oi, li, start, query_rows) for start in range(0, image_rows, query_rows)]
    spans.append((qt, ot, lt, 0, qt.shape[0]))
    steps = [(*span, side) for span in spans for side in range(2)]

    def score(step):
        source, _, _, start, size, side = step
        query = source[start : start + size, side * head : (side + 1) * head]
        query = jnp.concatenate([query, lanes_of([1.0], size, head)], axis=1)
        return dot_nt(query, keys[side])

    ahead = score(steps[0])
    for at, (_, target, logs, start, size, side) in enumerate(steps):
        scores = ahead
        if at + 1 < len(steps):
            ahead = score(steps[at + 1])
        top = jnp.maximum(jnp.max(scores, axis=1, keepdims=True) * scale, floor)
        exps = jnp.exp2(scores * scale - top).astype(BF16)
        product = dot_nn(exps, values[side])
        total = jnp.maximum(product[:, head : head + 1], 1.0)
        span = slice(start, start + size)
        lanes = slice(side * head, (side + 1) * head)
        target[span, lanes] = (product[:, :head] * (1.0 / total)).astype(BF16)
        logs[span, lanes] = jnp.broadcast_to(top + jnp.log2(total), (size, head))


def pair_block(rows, lanes, pairs, part):
    return pl.BlockSpec((rows, lanes), lambda pair: (0, part * pairs + pair))


def attention(qkv_image, qkv_text, key_bias, floor, head):
    image_rows, width = qkv_image.shape
    text_rows = qkv_text.shape[0]
    rows = image_rows + text_rows
    lanes = 2 * head
    pairs = width // (3 * lanes)
    columns = [
        pair_block(count, lanes, pairs, part)
        for part in range(3)
        for count in (image_rows, text_rows)
    ]
    return pl.pallas_call(
        functools.partial(attention_kernel, 256, LOG2E / math.sqrt(head), head),
        grid=(pairs,),
        in_specs=[
            pl.BlockSpec((rows, 128), lambda pair: (0, 0)),
            pl.BlockSpec(memory_space=pltpu.SMEM),
            *columns,
        ],
        out_specs=[columns[0], columns[1], columns[0], columns[1]],
        out_shape=[
            jax.ShapeDtypeStruct((count, width // 3), dtype)
            for dtype in (BF16, F32)
            for count in (image_rows, text_rows)
        ],
        scratch_shapes=[pltpu.VMEM((2, rows, lanes), BF16)] * 2,
        compiler_params=pltpu.CompilerParams(vmem_limit_bytes=24 << 20),
        cost_estimate=pl.CostEstimate(
            flops=int(WEIGHT["attention"] * 1.15e9), bytes_accessed=1, transcendentals=0
        ),
        name="attention",
    )(key_bias, floor, qkv_image, qkv_text, qkv_image, qkv_text, qkv_image, qkv_text)


def attention_back_kernel(query_rows, scale, factor, head, pairs, *refs):
    (bias_ref, qi, qt, ki, kt, vi, vt, ai, at, li, lt, gi, gt) = refs[:13]
    oi, ot, keys, values, key_sum, value_sum = refs[13:]
    pair = pl.program_id(0)
    image_rows = qi.shape[0]
    rows = keys.shape[1]
    width = 2 * head
    key_side = lanes_of([bias_ref[:, 0:1], 1.0, 1.0, 1.0], rows, head)
    value_side = lanes_of([1.0, 1.0, 1.0], rows, head)
    for side in range(2):
        lanes = slice(side * head, (side + 1) * head)
        for ref, extra, first, second in (
            (keys, key_side, ki, kt),
            (values, value_side, vi, vt),
        ):
            ref[side, :image_rows, :] = jnp.concatenate(
                [first[:, lanes], extra[:image_rows]], axis=1
            )
            ref[side, image_rows:, :] = jnp.concatenate(
                [second[:, lanes], extra[image_rows:]], axis=1
            )
    key_sum[...] = jnp.zeros_like(key_sum)
    value_sum[...] = jnp.zeros_like(value_sum)
    spans = [(qi, ai, li, gi, oi, start, query_rows) for start in range(0, image_rows, query_rows)]
    spans.append((qt, at, lt, gt, ot, 0, qt.shape[0]))
    steps = [(*span, side) for span in spans for side in range(2)]
    query_lanes = pl.ds(pl.multiple_of(pair * width, width), width)
    key_lanes = pl.ds(pl.multiple_of((pairs + pair) * width, width), width)
    value_lanes = pl.ds(pl.multiple_of((2 * pairs + pair) * width, width), width)

    def products(step):
        source, outs, logs, grads, _, start, size, side = step
        span = slice(start, start + size)
        lanes = slice(side * head, (side + 1) * head)
        query, grad = (source[span, lanes], grads[span, lanes])
        log = logs[span, side * head : side * head + 1] * (-1.0 / scale)
        inner = -jnp.sum(
            grad.astype(F32) * outs[span, lanes].astype(F32), axis=1, keepdims=True
        )
        query_wide = jnp.concatenate(
            [query, lanes_of([1.0, *three_parts(log)], size, head)], axis=1
        )
        grad_wide = jnp.concatenate([grad, lanes_of(three_parts(inner), size, head)], axis=1)
        return (
            query,
            grad,
            dot_nt(keys[side], query_wide),
            dot_nt(values[side], grad_wide),
        )

    ahead = products(steps[0])
    dq = []
    for at_step, (_, _, _, _, target, start, size, side) in enumerate(steps):
        query, grad, scores, prob_grad = ahead
        if at_step + 1 < len(steps):
            ahead = products(steps[at_step + 1])
        probs = jnp.exp2(scores * scale)
        score_grad = (probs * prob_grad).astype(BF16)
        lanes = slice(side * head, (side + 1) * head)
        value_sum[:, lanes] += dot_nn(probs.astype(BF16), grad)
        key_sum[:, lanes] += dot_nn(score_grad, query)
        dq.append(dot_tn(score_grad, keys[side][:, :head]))
        if side == 1:
            target[start : start + size, query_lanes] = (
                jnp.concatenate(dq, axis=1) * factor
            ).astype(BF16)
            dq = []
    oi[:, key_lanes] = (key_sum[:image_rows] * factor).astype(BF16)
    ot[:, key_lanes] = (key_sum[image_rows:] * factor).astype(BF16)
    oi[:, value_lanes] = value_sum[:image_rows].astype(BF16)
    ot[:, value_lanes] = value_sum[image_rows:].astype(BF16)


def attention_back(
    qkv_image, qkv_text, out_image, out_text, log_image, log_text, grad_image, grad_text, key_bias, head
):
    image_rows, width = qkv_image.shape
    text_rows = qkv_text.shape[0]
    rows = image_rows + text_rows
    lanes = 2 * head
    pairs = width // (3 * lanes)
    columns = [
        pair_block(count, lanes, pairs, part)
        for part in range(3)
        for count in (image_rows, text_rows)
    ]
    return pl.pallas_call(
        functools.partial(
            attention_back_kernel, 512, LOG2E / math.sqrt(head), 1.0 / math.sqrt(head), head, pairs
        ),
        grid=(pairs,),
        in_specs=[
            pl.BlockSpec((rows, 128), lambda pair: (0, 0)),
            *columns,
            *(columns[:2] * 3),
        ],
        out_specs=[
            pl.BlockSpec((image_rows, width), lambda pair: (0, 0)),
            pl.BlockSpec((text_rows, width), lambda pair: (0, 0)),
        ],
        out_shape=[
            jax.ShapeDtypeStruct((image_rows, width), BF16),
            jax.ShapeDtypeStruct((text_rows, width), BF16),
        ],
        scratch_shapes=[pltpu.VMEM((2, rows, lanes), BF16)] * 2
        + [pltpu.VMEM((rows, lanes), F32)] * 2,
        compiler_params=pltpu.CompilerParams(vmem_limit_bytes=24 << 20),
        cost_estimate=pl.CostEstimate(
            flops=int(WEIGHT["attention_back"] * 1.15e9), bytes_accessed=1, transcendentals=0
        ),
        name="attention_back",
    )(
        key_bias,
        *(qkv_image, qkv_text) * 3,
        out_image, out_text, log_image, log_text, grad_image, grad_text,
    )


def flip(values, bit):
    return lax.ppermute(values, "seq", [(i, i ^ bit) for i in range(4)])


def gather_near(a, b):
    return (flip(a, 1), flip(b, 1), flip(a, 2), flip(b, 2))


def gather_far(a, b, near):
    return (a, b, *near, flip(near[0], 2), flip(near[3], 1))


def gather_halves(a, b):
    return gather_far(a, b, gather_near(a, b))


def add_low(a, b):
    return (a.astype(F32) + b.astype(F32)).astype(BF16)


def scatter_first(sent):
    return (flip(sent[1], 1), flip(sent[2], 2))


def scatter_added(sent, first):
    width = sent[3].shape[-1]
    return (
        add_low(sent[3], first[1][..., :width]),
        add_low(sent[4], first[0][..., :width]),
    )


def scatter_sent(sent, first, added):
    return (sent[0], *first, flip(added[0], 1), flip(added[1], 2))


def scatter_last(sent, first):
    return scatter_sent(sent, first, scatter_added(sent, first))


def scatter_halves(halves):
    return scatter_last(halves, scatter_first(halves))


ANYWHERE = pl.BlockSpec(memory_space=pl.ANY)
ON_CORE = pl.BlockSpec(memory_space=pltpu.VMEM)
ROOM = 10 << 20


class Copies:
    def __init__(self, semaphores):
        self.semaphores = semaphores
        self.count = 0
        self.open = []

    def start(self, source, target):
        copy = pltpu.make_async_copy(source, target, self.semaphores.at[self.count])
        self.count += 1
        copy.start()
        return copy

    def send(self, source, target):
        self.open.append(self.start(source, target))

    def finish(self):
        for copy in self.open:
            copy.wait()


def fetch_halves(copies, halves, rows, seq):
    width = rows.shape[2] // 2
    fetched = []
    for r in range(4):
        pair = []
        for side in range(2):
            half = halves[2 * r + side]
            half = half if seq is None else half.at[seq]
            pair.append(copies.start(half, rows.at[r, :, pl.ds(side * width, width)]))
        fetched.append(pair)
    return fetched


def send_block(copies, rows, sent, r):
    own, for_x, for_y, late_x, late_y = sent
    width = rows.shape[2] // 2
    low, high = pl.ds(0, width), pl.ds(width, width)
    if r == 0:
        copies.send(rows.at[0], own)
        return
    first, second = {
        1: (for_x.at[:, high], late_x),
        2: (late_y, for_y.at[:, high]),
        3: (for_x.at[:, low], for_y.at[:, low]),
    }[r]
    copies.send(rows.at[r, :, low], first)
    copies.send(rows.at[r, :, high], second)


def sent_shapes(block, D):
    return [((block, width), BF16) for width in (D, D, D, D // 2, D // 2)]


def normalize(values):
    mean = jnp.mean(values, axis=1, keepdims=True)
    centered = values - mean
    variance = jnp.mean(centered * centered, axis=1, keepdims=True)
    inverse = lax.rsqrt(variance + NORM_EPSILON)
    return centered * inverse, inverse


def normalize_back(norm, inverse, grad, scale):
    scaled = grad * (1.0 + scale)
    return inverse * (
        scaled
        - jnp.mean(scaled, axis=1, keepdims=True)
        - norm * jnp.mean(scaled * norm, axis=1, keepdims=True)
    )


def run(kernel, name, operands, specs, outs, out_specs, scratch, copies=0):
    held = sum(math.prod(ref.shape) * np.dtype(ref.dtype).itemsize for ref in scratch)
    for spec, (shape, dtype) in zip(
        [*specs, *out_specs],
        [*((value.shape, value.dtype) for value in operands), *outs],
    ):
        held += math.prod(shape) * np.dtype(dtype).itemsize if spec is ON_CORE else 0
    if copies:
        scratch = [*scratch, pltpu.SemaphoreType.DMA((copies,))]
    return pl.pallas_call(
        kernel,
        in_specs=specs,
        out_specs=out_specs,
        out_shape=[jax.ShapeDtypeStruct(shape, dtype) for shape, dtype in outs],
        scratch_shapes=scratch,
        compiler_params=pltpu.CompilerParams(vmem_limit_bytes=min(held + ROOM, 56 << 20)),
        cost_estimate=pl.CostEstimate(
            flops=int(WEIGHT[name] * 1.15e9), bytes_accessed=1, transcendentals=0
        ),
        name=name,
    )(*operands)


def project_kernel(seq, image_rows, *refs):
    halves, (weight, mods, bias) = (refs[:8], refs[8:11])
    qkv_i, qkv_t, norm_i, norm_t = refs[11:15]
    rows, held, image_norm, text_norm, image_out, text_out, semaphores = refs[15:]
    copies = Copies(semaphores)
    fetched = fetch_halves(copies, halves, rows, seq)
    weights = [copies.start(weight.at[t], held.at[t]) for t in range(2)]
    text_rows = rows.shape[1] - image_rows
    for r in range(4):
        for copy in fetched[r]:
            copy.wait()
        for t, norms, low, count in (
            (0, image_norm, 0, image_rows),
            (1, text_norm, image_rows, text_rows),
        ):
            norm, _ = normalize(rows[r, low : low + count, :].astype(F32))
            norm = norm * (1.0 + mods[t, seq, 1:2, :]) + mods[t, seq, 0:1, :]
            norms[r * count : (r + 1) * count, :] = norm.astype(BF16)
        if r == 0:
            weights[0].wait()
        span = pl.ds(r * image_rows, image_rows)
        product = dot_nt(image_norm[span, :], held[0]) + bias[0:1, :]
        image_out[span, :] = product.astype(BF16)
        copies.send(image_norm.at[span, :], norm_i.at[span, :])
        copies.send(image_out.at[span, :], qkv_i.at[span, :])
    weights[1].wait()
    text_out[...] = (dot_nt(text_norm[...], held[1]) + bias[1:2, :]).astype(BF16)
    copies.send(text_norm, norm_t)
    copies.send(text_out, qkv_t)
    copies.finish()


def project(halves, weight, mods, bias, seq, image_rows):
    block, width = halves[0].shape[-2:]
    D, W = 2 * width, weight.shape[1]
    image, text = 4 * image_rows, 4 * (block - image_rows)
    return run(
        functools.partial(project_kernel, seq, image_rows),
        "project",
        (*halves, weight, mods, bias),
        [ANYWHERE] * 9 + [ON_CORE] * 2,
        [((image, W), BF16), ((text, W), BF16), ((image, D), BF16), ((text, D), BF16)],
        [ANYWHERE] * 4,
        [
            pltpu.VMEM((4, block, D), BF16),
            pltpu.VMEM((2, W, D), BF16),
            pltpu.VMEM((image, D), BF16),
            pltpu.VMEM((text, D), BF16),
            pltpu.VMEM((image, W), BF16),
            pltpu.VMEM((text, W), BF16),
        ],
        20,
    )


def partial_kernel(seqs, dot, image_rows, *refs):
    inputs, weight, halves = (refs[: 2 * seqs], refs[2 * seqs], refs[2 * seqs + 1 : 7 * seqs + 1])
    lefts, held, rows, semaphores = (
        refs[7 * seqs + 1 : 9 * seqs + 1],
        refs[9 * seqs + 1],
        refs[9 * seqs + 2 : 10 * seqs + 2],
        refs[10 * seqs + 2],
    )
    copies = Copies(semaphores)
    weights = [copies.start(weight.at[t], held.at[t]) for t in (1, 0)]
    fetched = [
        [copies.start(inputs[2 * s + t], lefts[2 * s + t]) for t in (1, 0)] for s in range(seqs)
    ]
    text_rows = rows[0].shape[1] - image_rows
    for s in range(seqs):
        if s == 0:
            weights[0].wait()
        fetched[s][0].wait()
        text = dot(lefts[2 * s + 1][...], held[1]).astype(BF16)
        for r in range(4):
            rows[s][r, image_rows:, :] = text[r * text_rows : (r + 1) * text_rows]
        if s == 0:
            weights[1].wait()
        fetched[s][1].wait()
        for r in (3, 1, 2, 0):
            left = lefts[2 * s][r * image_rows : (r + 1) * image_rows, :]
            rows[s][r, :image_rows, :] = dot(left, held[0]).astype(BF16)
            send_block(copies, rows[s], halves[5 * s : 5 * s + 5], r)
    copies.finish()


def partial_sums(inputs, weight, dot, D, image_rows):
    seqs = len(inputs)
    image, K = inputs[0][0].shape
    text = inputs[0][1].shape[0]
    block = (image + text) // 4
    return run(
        functools.partial(partial_kernel, seqs, dot, image_rows),
        "partial_sums",
        (*[value for pair in inputs for value in pair], weight),
        [ANYWHERE] * (2 * seqs + 1),
        sent_shapes(block, D) * seqs,
        [ANYWHERE] * (5 * seqs),
        [pltpu.VMEM((count, K), BF16) for _ in range(seqs) for count in (image, text)]
        + [pltpu.VMEM(weight.shape, BF16)]
        + [pltpu.VMEM((4, block, D), BF16)] * seqs,
        2 + 2 * seqs + 7 * seqs,
    )


def piece_sum(pieces, low, count):
    own, from_x, from_y, late_x, late_y = pieces
    width = late_x.shape[-1]

    def add(*parts):
        return sum(part.astype(F32) for part in parts)

    span = pl.ds(low, count)
    return jnp.concatenate(
        [
            add(own[span, :width], from_x[span, width:], late_y[span, :]),
            add(own[span, width:], late_x[span, :], from_y[span, width:]),
        ],
        axis=1,
    )


def both_halves(halves, seq, low, count):
    return jnp.concatenate(
        [half[seq, low : low + count, :].astype(F32) for half in halves], axis=1
    )


def middle_kernel(seq, image_rows, *refs):
    pieces, tokens, (mods, bias) = (refs[:5], refs[5:7], refs[7:9])
    projection_ref, middle_ref, second_a, second_b = refs[9:]
    block, width = second_a.shape
    for t, low, count in ((0, 0, image_rows), (1, image_rows, block - image_rows)):
        span = slice(low, low + count)
        projection = piece_sum(pieces, low, count) + bias[t : t + 1, :]
        middle = both_halves(tokens, seq, low, count) + mods[t, seq, 2:3, :] * projection
        norm, _ = normalize(middle)
        second = (norm * (1.0 + mods[t, seq, 4:5, :]) + mods[t, seq, 3:4, :]).astype(BF16)
        projection_ref[span, :] = projection
        middle_ref[span, :] = middle
        second_a[span, :] = second[:, :width]
        second_b[span, :] = second[:, width:]


def middle_step(pieces, tokens, mods, bias, seq, image_rows):
    block, width = pieces[3].shape
    return run(
        functools.partial(middle_kernel, seq, image_rows),
        "middle",
        (*pieces, *tokens, mods, bias),
        [ON_CORE] * 9,
        [((block, 2 * width), F32)] * 2 + [((block, width), BF16)] * 2,
        [ON_CORE] * 4,
        [],
    )


GELU_SCALE = math.sqrt(2.0 / math.pi)
GELU_CUBE = 0.044715


def hidden_kernel(seq, image_rows, *refs):
    halves, cotangents, (weight, bias, mods) = (refs[:8], refs[8:16], refs[16:19])
    outs = refs[19:27]
    act_i, act_t, slope_i, slope_t, grad_i, grad_t, second_i, second_t = outs
    rows, given, held, acts, slopes, grads, texts, semaphores = refs[27:]
    copies = Copies(semaphores)
    fetched = fetch_halves(copies, halves, rows, None)
    weights = [copies.start(weight.at[t], held.at[t]) for t in range(2)]
    other = fetch_halves(copies, cotangents, given, seq)
    text_rows = rows.shape[1] - image_rows
    second_text, grad_text, act_text, slope_text = texts

    def activate(pre):
        squared = pre * pre
        bent = jnp.tanh(pre * (GELU_SCALE + (GELU_SCALE * GELU_CUBE) * squared))
        rise = 0.5 + 0.5 * bent
        act = pre * rise
        slope = rise + (act * (1.0 - rise)) * (
            2.0 * GELU_SCALE + (6.0 * GELU_SCALE * GELU_CUBE) * squared
        )
        return act.astype(BF16), slope.astype(BF16)

    for r in range(4):
        for copy in fetched[r]:
            copy.wait()
        if r == 0:
            weights[0].wait()
        span = pl.ds(r * image_rows, image_rows)
        text_span = slice(r * text_rows, (r + 1) * text_rows)
        pre = dot_nt(rows[r, :image_rows, :], held[0]) + bias[0:1, :]
        act, slope = activate(pre)
        acts[span, :] = act
        slopes[span, :] = slope
        second_text[text_span, :] = rows[r, image_rows:, :]
        for copy in other[r]:
            copy.wait()
        for t, target, place, low, count in (
            (0, grads, span, 0, image_rows),
            (1, grad_text, text_span, image_rows, text_rows),
        ):
            value = given[r, low : low + count, :].astype(F32) * mods[t, seq, 5:6, :]
            target[place, :] = value.astype(BF16)
        copies.send(acts.at[span, :], act_i.at[span, :])
        copies.send(slopes.at[span, :], slope_i.at[span, :])
        copies.send(grads.at[span, :], grad_i.at[span, :])
        copies.send(rows.at[r, pl.ds(0, image_rows), :], second_i.at[span, :])
    weights[1].wait()
    act_text[...], slope_text[...] = activate(
        dot_nt(second_text[...], held[1]) + bias[1:2, :]
    )
    for source, target in (
        (act_text, act_t),
        (slope_text, slope_t),
        (grad_text, grad_t),
        (second_text, second_t),
    ):
        copies.send(source, target)
    copies.finish()


def hidden_step(halves, cotangents, weight, bias, mods, seq, image_rows):
    block, width = halves[0].shape
    D, F = 2 * width, weight.shape[1]
    image, text = 4 * image_rows, 4 * (block - image_rows)

    def kernel(*refs):
        texts, semaphores = (refs[-5:-1], refs[-1])
        hidden_kernel(seq, image_rows, *refs[:-5], texts, semaphores)

    return run(
        kernel,
        "hidden",
        (*halves, *cotangents, weight, bias, mods),
        [ANYWHERE] * 17 + [ON_CORE] * 2,
        [((count, wide), BF16) for wide in (F, F, D, D) for count in (image, text)],
        [ANYWHERE] * 8,
        [
            pltpu.VMEM((4, block, D), BF16),
            pltpu.VMEM((4, block, D), BF16),
            pltpu.VMEM((2, F, D), BF16),
            pltpu.VMEM((image, F), BF16),
            pltpu.VMEM((image, F), BF16),
            pltpu.VMEM((image, D), BF16),
        ]
        + [pltpu.VMEM((text, wide), BF16) for wide in (D, D, F, F)],
        38,
    )


def outer_kernel(seqs, chunk, *refs):
    inputs, out = (refs[: 4 * seqs], refs[4 * seqs])
    held, result, semaphores = (refs[4 * seqs + 1 : -2], refs[-2], refs[-1])
    copies = Copies(semaphores)
    order = [4 * s + 2 * t + side for t in (1, 0) for s in range(seqs) for side in range(2)]
    fetched = {k: copies.start(inputs[k], held[k]) for k in order}
    columns = result.shape[1]
    for t in (1, 0):
        for s in range(seqs):
            fetched[4 * s + 2 * t].wait()
            fetched[4 * s + 2 * t + 1].wait()
        for low in range(0, columns, chunk):
            span = pl.ds(low, chunk)
            total = dot_tn(held[2 * t][:, span], held[2 * t + 1][...])
            for s in range(1, seqs):
                total = total + dot_tn(held[4 * s + 2 * t][:, span], held[4 * s + 2 * t + 1][...])
            result[t, span, :] = total.astype(BF16)
            copies.send(result.at[t, span, :], out.at[t, span, :])
    copies.finish()


def outer_sums(lefts, rights, chunk):
    seqs = len(lefts)
    columns, width = lefts[0][0].shape[1], rights[0][0].shape[1]
    operands = [side[s][t] for s in range(seqs) for t in range(2) for side in (lefts, rights)]
    return run(
        functools.partial(outer_kernel, seqs, chunk),
        "outer_sums",
        operands,
        [ANYWHERE] * (4 * seqs),
        [((2, columns, width), BF16)],
        [ANYWHERE],
        [pltpu.VMEM(value.shape, BF16) for value in operands]
        + [pltpu.VMEM((2, columns, width), BF16)],
        4 * seqs + 2 * (columns // chunk),
    )[0]


def hidden_back_kernel(image_rows, *refs):
    (grad_i, grad_t, slope_i, slope_t, down, up) = refs[:6]
    pre_i, pre_t, sums, sent = (refs[6], refs[7], refs[8], refs[9:14])
    grads, slopes, pres, grad_text, slope_text, pre_text, held_down, held_up, rows, semaphores = (
        refs[14:]
    )
    copies = Copies(semaphores)
    order = (3, 1, 2, 0)
    spans = {r: pl.ds(r * image_rows, image_rows) for r in order}
    images = {}
    downs, ups = ([None, None], [None, None])
    for k, r in enumerate(order):
        images[r] = [copies.start(grad_i.at[spans[r], :], grads.at[spans[r], :])]
        if k == 0:
            downs[0] = copies.start(down.at[0], held_down.at[0])
        images[r].append(copies.start(slope_i.at[spans[r], :], slopes.at[spans[r], :]))
        if k == 0:
            ups[0] = copies.start(up.at[0], held_up.at[0])
    texts = [copies.start(grad_t, grad_text), copies.start(slope_t, slope_text)]
    downs[1] = copies.start(down.at[1], held_down.at[1])
    ups[1] = copies.start(up.at[1], held_up.at[1])
    text_rows = rows.shape[1] - image_rows
    total = jnp.zeros((1, pres.shape[1]), F32)
    for k, r in enumerate(order):
        for copy in images[r]:
            copy.wait()
        if k == 0:
            downs[0].wait()
        product = dot_nt(grads[spans[r], :], held_down[0]) * slopes[spans[r], :].astype(F32)
        low = product.astype(BF16)
        pres[spans[r], :] = low
        copies.send(pres.at[spans[r], :], pre_i.at[spans[r], :])
        total = total + jnp.sum(low.astype(F32), axis=0, keepdims=True)
        if k == 0:
            ups[0].wait()
        rows[r, :image_rows, :] = dot_nn(pres[spans[r], :], held_up[0]).astype(BF16)
        if k == 1:
            for copy in texts:
                copy.wait()
            downs[1].wait()
            product = dot_nt(grad_text[...], held_down[1]) * slope_text[...].astype(F32)
            pre_text[...] = product.astype(BF16)
            copies.send(pre_text, pre_t)
            sums[1:2, :] = jnp.sum(pre_text[...].astype(F32), axis=0, keepdims=True)
            ups[1].wait()
            back = dot_nn(pre_text[...], held_up[1]).astype(BF16)
            for q in range(4):
                rows[q, image_rows:, :] = back[q * text_rows : (q + 1) * text_rows]
            send_block(copies, rows, sent, order[0])
        if k >= 1:
            send_block(copies, rows, sent, r)
    sums[0:1, :] = total
    copies.finish()


def hidden_back(grads, slopes, down, up, image_rows):
    image, D = grads[0].shape
    text = grads[1].shape[0]
    F = up.shape[1]
    block = (image + text) // 4
    outs = run(
        functools.partial(hidden_back_kernel, image_rows),
        "hidden_back",
        (*grads, *slopes, down, up),
        [ANYWHERE] * 6,
        [((image, F), BF16), ((text, F), BF16), ((2, F), F32)] + sent_shapes(block, D),
        [ANYWHERE] * 2 + [ON_CORE] + [ANYWHERE] * 5,
        [
            pltpu.VMEM((image, D), BF16),
            pltpu.VMEM((image, F), BF16),
            pltpu.VMEM((image, F), BF16),
            pltpu.VMEM((text, D), BF16),
            pltpu.VMEM((text, F), BF16),
            pltpu.VMEM((text, F), BF16),
            pltpu.VMEM((2, F, D), BF16),
            pltpu.VMEM((2, F, D), BF16),
            pltpu.VMEM((4, block, D), BF16),
        ],
        8 + 2 + 4 + 1 + 4 + 7,
    )
    return outs[0:2], outs[2], outs[3:]


def middle_back_kernel(seq, image_rows, *refs):
    pieces, cotangents, (middle_ref, projection_ref, mods) = (refs[:5], refs[5:7], refs[7:10])
    grad_ref, low_a, low_b, sums = refs[10:]
    block, width = low_a.shape
    for t, low, count in ((0, 0, image_rows), (1, image_rows, block - image_rows)):
        span = slice(low, low + count)
        norm_grad = piece_sum(pieces, low, count)
        norm, inverse = normalize(middle_ref[span, :])
        grad = both_halves(cotangents, seq, low, count) + normalize_back(
            norm, inverse, norm_grad, mods[t, seq, 4:5, :]
        )
        rounded = (mods[t, seq, 2:3, :] * grad).astype(BF16)
        grad_ref[span, :] = grad
        low_a[span, :] = rounded[:, :width]
        low_b[span, :] = rounded[:, width:]
        for k, value in enumerate(
            (norm_grad, norm_grad * norm, grad * projection_ref[span, :], rounded.astype(F32))
        ):
            sums[4 * t + k : 4 * t + k + 1, :] = jnp.sum(value, axis=0, keepdims=True)


def middle_back(pieces, cotangents, middle, projection, mods, seq, image_rows):
    block, width = pieces[3].shape
    return run(
        functools.partial(middle_back_kernel, seq, image_rows),
        "middle_back",
        (*pieces, *cotangents, middle, projection, mods),
        [ON_CORE] * 10,
        [((block, 2 * width), F32)] + [((block, width), BF16)] * 2 + [((8, 2 * width), F32)],
        [ON_CORE] * 4,
        [],
    )


def attended_back_kernel(image_rows, *refs):
    halves, weight = (refs[:8], refs[8])
    grad_i, grad_t, proj_i, proj_t = refs[9:13]
    rows, held, image_out, text_in, text_out, semaphores = refs[13:]
    copies = Copies(semaphores)
    fetched = fetch_halves(copies, halves, rows, None)
    weights = [copies.start(weight.at[t], held.at[t]) for t in range(2)]
    text_rows = rows.shape[1] - image_rows
    for r in range(4):
        for copy in fetched[r]:
            copy.wait()
        if r == 0:
            weights[0].wait()
        span = pl.ds(r * image_rows, image_rows)
        text_in[r * text_rows : (r + 1) * text_rows, :] = rows[r, image_rows:, :]
        copies.send(rows.at[r, pl.ds(0, image_rows), :], proj_i.at[span, :])
        image_out[span, :] = dot_nn(rows[r, :image_rows, :], held[0]).astype(BF16)
    copies.send(image_out, grad_i)
    copies.send(text_in, proj_t)
    weights[1].wait()
    text_out[...] = dot_nn(text_in[...], held[1]).astype(BF16)
    copies.send(text_out, grad_t)
    copies.finish()


def attended_back(halves, weight, image_rows):
    block, width = halves[0].shape
    D, E = 2 * width, weight.shape[2]
    image, text = 4 * image_rows, 4 * (block - image_rows)
    outs = run(
        functools.partial(attended_back_kernel, image_rows),
        "attended_back",
        (*halves, weight),
        [ANYWHERE] * 9,
        [((image, E), BF16), ((text, E), BF16), ((image, D), BF16), ((text, D), BF16)],
        [ANYWHERE] * 4,
        [
            pltpu.VMEM((4, block, D), BF16),
            pltpu.VMEM(weight.shape, BF16),
            pltpu.VMEM((image, E), BF16),
            pltpu.VMEM((text, D), BF16),
            pltpu.VMEM((text, E), BF16),
        ],
        10 + 7,
    )
    return outs[:2], outs[2:]


def project_back_kernel(seq, image_rows, *refs):
    (grad_i, grad_t, weight), tokens = (refs[:3], refs[3:11])
    sums, column_sums, sent = (refs[11], refs[12], refs[13:18])
    grads, grad_text, held, given, rows, semaphores = refs[18:]
    copies = Copies(semaphores)
    weights = [copies.start(weight.at[t], held.at[t]) for t in (1, 0)]
    text_in = copies.start(grad_t, grad_text)
    image_in = copies.start(grad_i, grads)
    fetched = fetch_halves(copies, tokens, given, seq)
    text_rows = rows.shape[1] - image_rows
    weights[0].wait()
    text_in.wait()
    text = dot_nn(grad_text[...], held[1])
    column_sums[1:2, :] = jnp.sum(grad_text[...].astype(F32), axis=0, keepdims=True)
    weights[1].wait()
    image_in.wait()
    totals = [jnp.zeros((1, rows.shape[2]), F32) for _ in range(4)]
    columns = jnp.zeros((1, grads.shape[1]), F32)
    for r in (3, 1, 2, 0):
        for copy in fetched[r]:
            copy.wait()
        span = pl.ds(r * image_rows, image_rows)
        for t, low, count in ((0, 0, image_rows), (1, image_rows, text_rows)):
            if t == 0:
                back = dot_nn(grads[span, :], held[0])
                columns = columns + jnp.sum(grads[span, :].astype(F32), axis=0, keepdims=True)
            else:
                back = text[r * text_rows : (r + 1) * text_rows, :]
            norm, _ = normalize(given[r, low : low + count, :].astype(F32))
            totals[2 * t] = totals[2 * t] + jnp.sum(back, axis=0, keepdims=True)
            totals[2 * t + 1] = totals[2 * t + 1] + jnp.sum(back * norm, axis=0, keepdims=True)
            rows[r, low : low + count, :] = back.astype(BF16)
        send_block(copies, rows, sent, r)
    column_sums[0:1, :] = columns
    for k in range(4):
        sums[k : k + 1, :] = totals[k]
    copies.finish()


def project_back(grads, weight, tokens, seq, image_rows):
    image, W = grads[0].shape
    text = grads[1].shape[0]
    D = weight.shape[2]
    block = (image + text) // 4
    outs = run(
        functools.partial(project_back_kernel, seq, image_rows),
        "project_back",
        (*grads, weight, *tokens),
        [ANYWHERE] * 11,
        [((4, D), F32), ((2, W), F32)] + sent_shapes(block, D),
        [ON_CORE] * 2 + [ANYWHERE] * 5,
        [
            pltpu.VMEM((image, W), BF16),
            pltpu.VMEM((text, W), BF16),
            pltpu.VMEM(weight.shape, BF16),
            pltpu.VMEM((4, block, D), BF16),
            pltpu.VMEM((4, block, D), BF16),
        ],
        4 + 8 + 7,
    )
    return outs[0], outs[1], outs[2:]


def result_kernel(image_rows, *refs):
    pieces, cotangents, middles = (refs[:10], refs[10:12], refs[12:14])
    mods, bias, image_out, text_out, sums = refs[14:]
    block = middles[0].shape[0]
    for seq in range(2):
        for t, low, count in ((0, 0, image_rows), (1, image_rows, block - image_rows)):
            span = slice(low, low + count)
            value = piece_sum(pieces[5 * seq : 5 * seq + 5], low, count) + bias[t : t + 1, :]
            gate = mods[t, seq, 5:6, :]
            out = (middles[seq][span, :] + gate * value).astype(BF16)
            if t == 0:
                image_out[seq] = out
            else:
                text_out[seq] = out
            grad = both_halves(cotangents, seq, low, count)
            low_grad = (gate * grad).astype(BF16).astype(F32)
            at = 4 * seq + 2 * t
            sums[at : at + 1, :] = jnp.sum(grad * value, axis=0, keepdims=True)
            sums[at + 1 : at + 2, :] = jnp.sum(low_grad, axis=0, keepdims=True)


def result_step(pieces, cotangents, middles, mods, bias, image_rows):
    seqs, (block, width) = (len(middles), pieces[3].shape)
    return run(
        functools.partial(result_kernel, image_rows),
        "result",
        (*pieces, *cotangents, *middles, mods, bias),
        [ON_CORE] * 16,
        [
            ((seqs, image_rows, 2 * width), BF16),
            ((seqs, block - image_rows, 2 * width), BF16),
            ((8, 2 * width), F32),
        ],
        [ON_CORE] * 3,
        [],
    )


def input_back_kernel(image_rows, live_text, *refs):
    pieces, tokens, grads, mods = (refs[:10], refs[10:12], refs[12:14], refs[14])
    image_out, text_out = refs[15:]
    block = grads[0].shape[0]
    for seq in range(2):
        for t, low, count in ((0, 0, image_rows), (1, image_rows, block - image_rows)):
            norm_grad = piece_sum(pieces[5 * seq : 5 * seq + 5], low, count)
            norm, inverse = normalize(both_halves(tokens, seq, low, count))
            out = grads[seq][low : low + count, :] + normalize_back(
                norm, inverse, norm_grad, mods[t, seq, 1:2, :]
            )
            if t == 0:
                image_out[seq] = out
            else:
                text_out[seq] = out[:live_text]


def input_back(pieces, tokens, grads, mods, image_rows, live_text):
    block, width = pieces[0][3].shape
    return run(
        functools.partial(input_back_kernel, image_rows, live_text),
        "input_back",
        (*pieces[0], *pieces[1], *tokens, *grads, mods),
        [ON_CORE] * 15,
        [((2, image_rows, 2 * width), F32), ((2, live_text, 2 * width), F32)],
        [ON_CORE] * 2,
        [],
    )


def match_units(batch_devices, seq_devices, per_device, group_units):
    devices = batch_devices * seq_devices
    total = devices * per_device
    part_units = total // 3
    sources, targets = ([], [])
    for seq_at in range(seq_devices):
        listed = [
            part * part_units + seq_at * group_units + k
            for part in range(3)
            for k in range(group_units)
        ]
        for place, unit in enumerate(listed):
            sources.append((unit // per_device, unit % per_device))
            targets.append(
                ((place // per_device) * seq_devices + seq_at, place % per_device)
            )
    edges = list(zip(sources, targets))
    rounds = []
    left = list(range(total))
    for _ in range(per_device):
        by_source = {}
        for e in left:
            by_source.setdefault(edges[e][0][0], []).append(e)
        taken = {}

        def place_edge(device, seen):
            for e in by_source[device]:
                target = edges[e][1][0]
                if target in seen:
                    continue
                seen.add(target)
                if target not in taken or place_edge(edges[taken[target]][0][0], seen):
                    taken[target] = e
                    return True
            return False

        for device in range(devices):
            place_edge(device, set())
        chosen = sorted(taken.values())
        rounds.append(chosen)
        left = [e for e in left if e not in chosen]
    send = np.zeros((per_device, devices), np.int32)
    land = np.zeros((per_device, devices), np.int32)
    perms = []
    for k, chosen in enumerate(rounds):
        pairs = []
        for e in chosen:
            (source, source_slot), (target, target_slot) = edges[e]
            pairs.append((source, target))
            send[k, source] = source_slot
            land[k, target] = target_slot
        perms.append(sorted(pairs))
    return perms, send, land


def move_units(units, perms, take, put, place):
    arrived = jnp.zeros_like(units)
    for k, pairs in enumerate(perms):
        slot = jnp.asarray(take[k])[place]
        moved = lax.ppermute(
            lax.dynamic_index_in_dim(units, slot, 0, keepdims=True), ("batch", "seq"), pairs
        )
        arrived = lax.dynamic_update_slice_in_dim(arrived, moved, jnp.asarray(put[k])[place], 0)
    return arrived


def gather_rows_over_batch(values):
    return lax.all_gather(values, "batch", axis=1, tiled=True)


def after(values, *others):
    return lax.optimization_barrier((values, others))[0]


def gather_small(values, axis, last=()):
    count = lax.axis_size(axis)
    held = values[None]
    bit = 1
    while bit < count:
        pairs = [(i, i ^ bit) for i in range(count)]
        if 2 * bit == count:
            held = after(held, last)
        held = jnp.concatenate([held, lax.ppermute(held, axis, pairs)])
        bit *= 2
    return jnp.take(held, jnp.bitwise_xor(lax.axis_index(axis), jnp.arange(count)), axis=0)


def scatter_rows_over_batch(values):
    dimension = values.ndim - 2
    return lax.psum_scatter(values, "batch", scatter_dimension=dimension, tiled=True)


def swap(values, axis):
    return lax.all_to_all(values, axis, 0, 0, tiled=True)


def swift_layer(
    image_tokens,
    text_tokens,
    conditioning,
    key_mask,
    mod_weight,
    mod_bias,
    qkv_weight,
    qv_bias,
    out_weight,
    out_bias,
    up_weight,
    up_bias,
    down_weight,
    down_bias,
    image_cotangent,
    text_cotangent,
):
    S = lax.axis_size("seq")
    B = lax.axis_size("batch")
    seq_index = lax.axis_index("seq")
    place = lax.axis_index(("batch", "seq"))
    L, image_count, D = image_tokens.shape
    live_text = text_tokens.shape[1]
    text_count = -(-live_text // 16) * 16
    pad = ((0, 0), (0, text_count - live_text), (0, 0))
    head = D // HEADS
    own_width = D // S
    half = D // 2

    unit = math.gcd(qkv_weight.shape[2], own_width)
    per_device = qkv_weight.shape[2] // unit
    perms, send, land = match_units(B, S, per_device, own_width // unit)
    back_perms = [[(target, source) for source, target in pairs] for pairs in perms]
    qkv_units = jnp.swapaxes(qkv_weight, 1, 2).reshape(2, per_device, unit, D).swapaxes(0, 1)
    qkv_mine = move_units(qkv_units, perms, send, land, place).swapaxes(0, 1)
    qkv_width = per_device * unit
    qkv_part = gather_rows_over_batch(qkv_mine.reshape(2, qkv_width, D))
    padded = jnp.concatenate([image_tokens, jnp.pad(text_tokens, pad)], axis=1)
    tokens = after((padded[..., :half], padded[..., half:]), qkv_mine)
    tokens_near = gather_near(*tokens)

    bias_widths = [array.shape[1] for array in (qv_bias, out_bias, up_bias, down_bias)]
    bias_ends = np.cumsum(bias_widths)
    own_biases = jnp.concatenate([qv_bias, out_bias, up_bias, down_bias], axis=1)
    near = gather_small(
        jnp.concatenate([conditioning, own_biases], axis=1),
        "batch",
        (tokens_near[0], tokens_near[3]),
    )
    cond_all = near[:, :, :D].reshape(B * L, D)
    column_biases = near[:, :, D:].astype(F32)
    smooth_all = jax.nn.silu(cond_all.astype(F32)).astype(BF16)
    mod_own = (
        jnp.einsum("sd,tdf->tsf", smooth_all, mod_weight, preferred_element_type=F32)
        + mod_bias.astype(F32)[:, None, :]
    )
    mod_width = mod_own.shape[2]
    mod_all = gather_small(mod_own, "batch", (tokens_near[1], tokens_near[2]))
    mod_came = lax.dynamic_slice_in_dim(mod_all, lax.axis_index("batch") * L, L, 2)
    small = jnp.concatenate(
        [mod_came.reshape(B, 2 * L * mod_width), column_biases.reshape(B, -1)], axis=1
    )
    tokens_all = gather_far(*tokens, tokens_near)
    small_all = gather_small(small, "seq", tokens_all[6:])
    modulation = (
        small_all[:, :, : 2 * L * mod_width]
        .reshape(S, B, 2, L, mod_width)
        .transpose(2, 3, 1, 0, 4)
        .reshape(2, L, 6, D)
    )
    bias_all = (
        small_all[:, :, 2 * L * mod_width :].reshape(S, B, 2, -1).transpose(2, 1, 0, 3)
    )
    qv_full = bias_all[..., : bias_ends[0]].reshape(2, 2 * D)
    out_bias_full = bias_all[..., bias_ends[0] : bias_ends[1]].reshape(2, D)
    down_bias_full = bias_all[..., bias_ends[2] :].reshape(2, D)
    up_bias_part = (
        column_biases[:, :, bias_ends[1] : bias_ends[2]].transpose(1, 0, 2).reshape(2, -1)
    )
    first_feature = seq_index * own_width
    qkv_bias = jnp.concatenate(
        [
            lax.dynamic_slice_in_dim(qv_full, first_feature, own_width, 1),
            jnp.zeros((2, own_width), F32),
            lax.dynamic_slice_in_dim(qv_full, D + first_feature, own_width, 1),
        ],
        axis=1,
    )

    out_units = jnp.swapaxes(out_weight, 1, 2).reshape(2, -1, S, own_width).transpose(2, 0, 1, 3)
    order = jnp.bitwise_xor(seq_index, jnp.arange(S))
    out_units = jnp.take(after(out_units, mod_own), order, axis=0)
    out_mine = jnp.stack([out_units[0], *(flip(out_units[r], r) for r in range(1, S))])
    out_mine = jnp.take(out_mine, order, axis=0)
    out_columns = out_mine.shape[2]
    out_rows = out_mine.transpose(1, 0, 2, 3).reshape(2, S * out_columns, own_width)
    out_part = gather_rows_over_batch(out_rows)
    hidden_columns = up_weight.shape[2]
    padded = jnp.concatenate([image_cotangent, jnp.pad(text_cotangent, pad)], axis=1)
    cotangents = (padded[..., :half], padded[..., half:])
    near_grads = gather_near(*after(cotangents, tokens_all, small_all))
    up_part = gather_rows_over_batch(after(jnp.swapaxes(up_weight, 1, 2), out_mine, mod_own))
    down_part = gather_rows_over_batch(after(jnp.swapaxes(down_weight, 1, 2), out_mine, mod_own))

    image_keys = jnp.take(
        key_mask[:, : S * image_count].reshape(L, S, image_count), order, axis=1
    )
    text_keys = jnp.take(
        key_mask[:, S * image_count :].reshape(L, S, live_text), order, axis=1
    )
    text_keys = jnp.pad(text_keys, ((0, 0), (0, 0), (0, text_count - live_text)))
    live = jnp.concatenate([image_keys.reshape(L, -1), text_keys.reshape(L, -1)], axis=1) > 0
    key_bias = jnp.where(live, 0.0, DEAD).astype(F32)
    floors = jnp.where(jnp.all(key_mask > 0, axis=1), -3e38, FLOOR_SCORE * LOG2E).astype(F32)
    floors = floors.reshape(L, 1, 1)
    key_bias = jnp.broadcast_to(key_bias[:, :, None], (*key_bias.shape, 128))

    kept = []
    first = project(tokens_all, qkv_part, modulation, qkv_bias, 0, image_count)
    attended = attention(first[0], first[1], key_bias[0], floors[0], head)
    attended, logs = (attended[:2], attended[2:])
    attended = after(attended, near_grads)
    parts = partial_sums([attended], out_part, dot_nt, D, image_count)
    kept.append((first, attended, logs, parts))
    again = after(tokens_all, parts)
    first = project(again, qkv_part, modulation, qkv_bias, 1, image_count)
    attended = attention(first[0], first[1], key_bias[1], floors[1], head)
    attended, logs = (attended[:2], attended[2:])
    cotangents_all = gather_far(*cotangents, after(near_grads, kept[0][1]))
    out_first = scatter_first(kept[0][3])
    out_added = scatter_added(kept[0][3], after(out_first, attended))
    attended = after(attended, cotangents_all, out_added)
    parts = partial_sums([attended], out_part, dot_nt, D, image_count)
    kept.append((first, attended, logs, parts))
    firsts, attendeds, logs, out_halves = zip(*kept)
    out_pieces = [scatter_sent(out_halves[0], out_first, out_added)]
    out_pieces.append(scatter_halves(after(out_halves[1], out_pieces[0])))
    steps = []
    for s in range(L):
        steps.append(
            middle_step(
                out_pieces[s],
                tokens,
                modulation,
                out_bias_full,
                s,
                image_count,
            )
        )
    second_near = [gather_near(*step[2:]) for step in steps]
    hidden = []
    for s in range(L):
        near = after(second_near[s], hidden[-1]) if s else second_near[s]
        halves = gather_far(*steps[s][2:], near)
        hidden.append(
            hidden_step(
                halves, cotangents_all, up_part, up_bias_part, modulation, s, image_count
            )
        )
    acts, slopes, grads, norms = [[step[i : i + 2] for step in hidden] for i in (0, 2, 4, 6)]

    down_sum = outer_sums(acts, grads, 256)
    down_came = scatter_rows_over_batch(down_sum)
    pres, bias_sums, norm2_halves = ([], [], [])
    gate = down_sum
    for s in range(L):
        pre, sums, halves = hidden_back(
            after(grads[s], gate), slopes[s], down_part, up_part, image_count
        )
        gate = halves
        pres.append(pre)
        bias_sums.append(sums)
        norm2_halves.append(halves)
    up_bias_sum = sum(bias_sums)
    norm2_first = scatter_first(norm2_halves[0])
    norm2_added = scatter_added(norm2_halves[0], after(norm2_first, gate))
    norm2_pieces = scatter_sent(norm2_halves[0], norm2_first, norm2_added)
    norm2_first1 = scatter_first(after(norm2_halves[1], norm2_pieces[3:]))
    backs = [
        middle_back(
            after(norm2_pieces, gate),
            cotangents,
            *steps[0][1::-1],
            modulation,
            0,
            image_count,
        )
    ]
    proj_near0 = gather_near(*backs[0][1:3])
    mlp_halves = partial_sums(after(acts, backs[0]), down_part, dot_nn, D, image_count)
    up_sum = outer_sums(after(pres, mlp_halves), norms, 256)
    norm2_added = scatter_added(norm2_halves[1], after(norm2_first1, mlp_halves))
    norm2_pieces = scatter_sent(norm2_halves[1], norm2_first1, norm2_added)
    projs = [gather_far(*backs[0][1:3], after(proj_near0, up_sum))]
    backs.append(
        middle_back(
            after(norm2_pieces, up_sum, proj_near0),
            cotangents,
            *steps[1][1::-1],
            modulation,
            1,
            image_count,
        )
    )
    proj_near1 = gather_near(*backs[1][1:3])
    grad0, proj0 = attended_back(
        after(projs[0], backs[1], down_came), out_part, image_count
    )
    up_came = scatter_rows_over_batch(after(up_sum, backs[1]))
    qkv_grad0 = attention_back(
        *firsts[0][:2], *attendeds[0], *logs[0], *grad0, key_bias[0], head
    )
    projs.append(gather_far(*backs[1][1:3], after(proj_near1, qkv_grad0)))
    mlp_halves = (mlp_halves[:5], mlp_halves[5:])
    mlp_first = [scatter_first(after(mlp_halves[0], grad0))]
    sums0, columns0, halves0 = project_back(
        after(qkv_grad0, mlp_first), qkv_part, tokens_all, 0, image_count
    )
    grad1, proj1 = attended_back(after(projs[1], halves0), out_part, image_count)
    mlp_first.append(scatter_first(after(mlp_halves[1], projs[1])))
    out_sum = outer_sums([proj0, proj1], attendeds, 256)
    out_came = scatter_rows_over_batch(out_sum)
    grad1 = after(grad1, out_sum)
    qkv_grad1 = attention_back(
        *firsts[1][:2], *attendeds[1], *logs[1], *grad1, key_bias[1], head
    )
    mlp_added = [
        scatter_added(halves, after(first, qkv_grad1))
        for halves, first in zip(mlp_halves, mlp_first)
    ]
    mlp_pieces = [
        piece
        for halves, first, added in zip(mlp_halves, mlp_first, mlp_added)
        for piece in scatter_sent(halves, first, added)
    ]
    qkv_sum = outer_sums(
        [qkv_grad0, after(qkv_grad1, mlp_added, up_came)],
        [first[2:] for first in firsts],
        128 if qkv_width % 256 else 256,
    )
    qkv_came = scatter_rows_over_batch(after(qkv_sum, out_came))
    sums1, columns1, halves1 = project_back(
        after(qkv_grad1, qkv_sum), qkv_part, tokens_all, 1, image_count
    )
    norm1_pieces = [
        scatter_halves(after(halves0, qkv_sum)),
        scatter_halves(after(halves1, mlp_pieces)),
    ]
    image_out, text_out, result_sums = result_step(
        after(mlp_pieces, halves1),
        cotangents,
        [step[1] for step in steps],
        modulation,
        down_bias_full,
        image_count,
    )
    image_grad, text_grad = input_back(
        after(norm1_pieces, qkv_came),
        tokens,
        [back[0] for back in backs],
        modulation,
        image_count,
        live_text,
    )
    out_home = swap(
        after(out_came, image_grad).reshape(2, S, out_columns, own_width).swapaxes(0, 1), "seq"
    )
    qkv_home = move_units(
        qkv_came.reshape(2, per_device, unit, D).swapaxes(0, 1),
        back_perms, land, send, place
    )
    qkv_weight_grad = qkv_home.swapaxes(0, 1).reshape(2, -1, D).swapaxes(1, 2).astype(F32)
    out_weight_grad = (
        out_home.transpose(1, 2, 0, 3).reshape(2, out_columns, D).swapaxes(1, 2).astype(F32)
    )
    up_weight_grad = up_came.swapaxes(1, 2).astype(F32)
    down_weight_grad = down_came.swapaxes(1, 2).astype(F32)


    first_sums = jnp.stack([sums0, sums1]).reshape(L, 2, 2, D)
    second_sums = jnp.stack([back[3] for back in backs]).reshape(L, 2, 4, D)
    result_sums = result_sums.reshape(L, 2, 2, D)
    mod_rows = jnp.concatenate(
        [
            first_sums,
            second_sums[:, :, 2:3],
            second_sums[:, :, :2],
            result_sums[:, :, :1],
        ],
        axis=2,
    ).swapaxes(0, 1)
    mod_rows = mod_rows.reshape(2, L, B, S, mod_width).transpose(3, 2, 0, 1, 4)
    out_bias_sum = jnp.sum(second_sums[:, :, 3], axis=0)
    down_bias_sum = jnp.sum(result_sums[:, :, 1], axis=0)
    column_sums = columns0 + columns1
    qv_bias_sum = jnp.zeros((2, 2 * D), F32)
    for part, column in ((0, 0), (1, 2 * own_width)):
        qv_bias_sum = lax.dynamic_update_slice_in_dim(
            qv_bias_sum, column_sums[:, column : column + own_width], part * D + first_feature, 1
        )
    up_bias_rows = lax.dynamic_update_slice_in_dim(
        jnp.zeros((2, B, S, hidden_columns), F32),
        up_bias_sum.reshape(2, B, 1, hidden_columns),
        seq_index,
        2,
    )
    bias_rows = jnp.concatenate(
        [
            qv_bias_sum.reshape(2, B, S, -1),
            out_bias_sum.reshape(2, B, S, -1),
            up_bias_rows,
            down_bias_sum.reshape(2, B, S, -1),
        ],
        axis=3,
    ).transpose(2, 1, 0, 3)
    packed = jnp.concatenate(
        [mod_rows.reshape(S, B, -1), bias_rows.reshape(S, B, -1)], axis=2
    )
    packed = jnp.sum(swap(packed, "seq"), axis=0)
    packed = swap(packed, "batch")
    mod_mine = (
        packed[:, : 2 * L * mod_width]
        .reshape(B, 2, L, mod_width)
        .transpose(1, 0, 2, 3)
        .reshape(2, B * L, mod_width)
        .astype(BF16)
    )
    bias_mine = jnp.sum(packed[:, 2 * L * mod_width :], axis=0).reshape(2, -1)
    qv_bias_grad, out_bias_grad, up_bias_grad, down_bias_grad = jnp.split(
        bias_mine, bias_ends[:3], axis=1
    )
    mod_weight_grad = jnp.einsum(
        "sd,tsf->tdf", smooth_all, mod_mine, preferred_element_type=F32
    )
    mod_bias_grad = jnp.sum(mod_mine.astype(F32), axis=1)
    smooth_part = jnp.einsum("tsf,tdf->sd", mod_mine, mod_weight, preferred_element_type=F32)
    smooth_grad = jnp.sum(swap(smooth_part.reshape(B, L, D), "batch"), axis=0)
    smooth_grad = after(smooth_grad, qkv_home)
    smooth_grad = smooth_grad + flip(smooth_grad, 1)
    smooth_grad = smooth_grad + flip(smooth_grad, 2)
    cond_grad = jax.vjp(jax.nn.silu, conditioning.astype(F32))[1](smooth_grad)[0]
    return (
        image_out,
        text_out[:, :live_text],
        image_grad,
        text_grad,
        cond_grad,
        mod_weight_grad,
        mod_bias_grad,
        qkv_weight_grad,
        qv_bias_grad,
        out_weight_grad,
        out_bias_grad,
        up_weight_grad,
        up_bias_grad,
        down_weight_grad,
        down_bias_grad,
    )


def choose_layer(mesh):
    if mesh.shape["seq"] == 4 and HEADS % 8 == 0:
        return swift_layer
    return general_layer


def solution(mesh):
    layer = choose_layer(mesh)
    return jax.shard_map(
        layer,
        mesh=mesh,
        in_specs=(
            P("batch", "seq", None),
            P("batch", "seq", None),
            P("batch", None),
            P("batch", None),
            P(None, None, ("batch", "seq")),
            P(None, ("batch", "seq")),
            P(None, None, ("batch", "seq")),
            P(None, ("batch", "seq")),
            P(None, None, ("batch", "seq")),
            P(None, ("batch", "seq")),
            P(None, None, ("batch", "seq")),
            P(None, ("batch", "seq")),
            P(None, None, ("batch", "seq")),
            P(None, ("batch", "seq")),
            P("batch", "seq", None),
            P("batch", "seq", None),
        ),
        out_specs=(
            P("batch", "seq", None),
            P("batch", "seq", None),
            P("batch", "seq", None),
            P("batch", "seq", None),
            P("batch", None),
            P(None, None, ("batch", "seq")),
            P(None, ("batch", "seq")),
            P(None, None, ("batch", "seq")),
            P(None, ("batch", "seq")),
            P(None, None, ("batch", "seq")),
            P(None, ("batch", "seq")),
            P(None, None, ("batch", "seq")),
            P(None, ("batch", "seq")),
            P(None, None, ("batch", "seq")),
            P(None, ("batch", "seq")),
        ),
        check_vma=False,
    )
```

```python
import functools
import math

import jax
import jax.numpy as jnp
import numpy as np
from jax import lax
from jax.experimental import pallas as pl
from jax.experimental.pallas import tpu as pltpu
from jax.sharding import PartitionSpec as P

HEADS = 24


NORM_EPSILON = 1e-06
FLOOR_SCORE = -10000.0


def modulate(tokens, shift_vec, scale_vec):
    row_mean = jnp.mean(tokens, axis=-1, keepdims=True)
    centered = tokens - row_mean
    row_var = jnp.mean(centered * centered, axis=-1, keepdims=True)
    return (
        centered * lax.rsqrt(row_var + NORM_EPSILON) * (1.0 + scale_vec[:, None, :])
        + shift_vec[:, None, :]
    )


def gelu_tanh(values):
    return jax.nn.gelu(values, approximate=True)


def unmix_columns(values, seq_devices, batch_devices):
    array_shape = values.shape
    piece_width = array_shape[-1] // (seq_devices * batch_devices)
    grid_view = values.reshape(array_shape[:-1] + (seq_devices, batch_devices, piece_width))
    return jnp.swapaxes(grid_view, -3, -2).reshape(array_shape)


def remix_columns(values, seq_devices, batch_devices):
    array_shape = values.shape
    piece_width = array_shape[-1] // (seq_devices * batch_devices)
    grid_view = values.reshape(array_shape[:-1] + (batch_devices, seq_devices, piece_width))
    return jnp.swapaxes(grid_view, -3, -2).reshape(array_shape)


def fetch_columns(
    up_weight,
    down_weight,
    mod_weight,
    qkv_weight,
    out_weight,
    up_bias,
    mod_bias,
    qv_bias,
    out_bias,
    down_bias,
):
    return (
        lax.all_gather(up_weight, "batch", axis=2, tiled=True),
        lax.all_gather(down_weight, "batch", axis=2, tiled=True),
        lax.all_gather(mod_weight, "batch", axis=2, tiled=True),
        lax.all_gather(qkv_weight, "batch", axis=2, tiled=True),
        lax.all_gather(out_weight, "batch", axis=2, tiled=True),
        lax.all_gather(up_bias, "batch", axis=1, tiled=True),
        lax.all_gather(mod_bias, "batch", axis=1, tiled=True),
        lax.all_gather(qv_bias, "batch", axis=1, tiled=True),
        lax.all_gather(out_bias, "batch", axis=1, tiled=True),
        lax.all_gather(down_bias, "batch", axis=1, tiled=True),
    )


def fetch_modulation(mod_part, mod_bias_part):
    return (
        lax.all_gather(mod_part, "seq", axis=2, tiled=True),
        lax.all_gather(mod_bias_part, "seq", axis=1, tiled=True),
    )


def gather_rows(first, second):
    return (
        lax.all_gather(first, "seq", axis=1, tiled=True),
        lax.all_gather(second, "seq", axis=1, tiled=True),
    )


def sum_rows(first, second, seq_devices):
    local_seqs, first_rows, width = first.shape
    first_local = first_rows // seq_devices
    second_local = second.shape[1] // seq_devices
    joined = jnp.concatenate(
        [
            first.reshape(local_seqs, seq_devices, first_local, width),
            second.reshape(local_seqs, seq_devices, second_local, width),
        ],
        axis=2,
    )
    joined = joined.reshape(local_seqs, seq_devices * (first_local + second_local), width)
    total = lax.psum_scatter(joined, "seq", scatter_dimension=1, tiled=True)
    return (total[:, :first_local], total[:, first_local:])


def to_rows(first, second):
    return (
        lax.all_to_all(first, "seq", split_axis=1, concat_axis=2, tiled=True),
        lax.all_to_all(second, "seq", split_axis=1, concat_axis=2, tiled=True),
    )


def to_columns(first, second):
    return (
        lax.all_to_all(first, "seq", split_axis=2, concat_axis=1, tiled=True),
        lax.all_to_all(second, "seq", split_axis=2, concat_axis=1, tiled=True),
    )


def own_block(values, seq_index, seq_devices):
    width = values.shape[1] // seq_devices
    return lax.dynamic_slice_in_dim(values, seq_index * width, width, 1)


def general_layer(
    image_tokens,
    text_tokens,
    conditioning,
    key_mask,
    mod_weight,
    mod_bias,
    qkv_weight,
    qv_bias,
    out_weight,
    out_bias,
    up_weight,
    up_bias,
    down_weight,
    down_bias,
    image_cotangent,
    text_cotangent,
):
    seq_devices = lax.axis_size("seq")
    batch_devices = lax.axis_size("batch")
    seq_index = lax.axis_index("seq")
    local_seqs, image_count, model_width = image_tokens.shape
    text_count = text_tokens.shape[1]
    block_rows = image_count + text_count
    key_count = block_rows * seq_devices
    head_size = model_width // HEADS
    factor = 1.0 / math.sqrt(head_size)
    inputs = (image_tokens.astype(jnp.float32), text_tokens.astype(jnp.float32))
    cotangents = (image_cotangent.astype(jnp.float32), text_cotangent.astype(jnp.float32))
    row_spans = ((0, image_count), (image_count, block_rows))
    image_keys = key_mask[:, : image_count * seq_devices].reshape(
        local_seqs, seq_devices, image_count
    )
    text_keys = key_mask[:, image_count * seq_devices :].reshape(
        local_seqs, seq_devices, text_count
    )
    key_live = (
        jnp.concatenate([image_keys, text_keys], axis=2).reshape(local_seqs, key_count) > 0
    )[:, None, None, :]
    cond_float = conditioning.astype(jnp.float32)
    smooth = jax.nn.silu(cond_float).astype(jnp.bfloat16)
    fetched = fetch_columns(
        up_weight,
        down_weight,
        mod_weight,
        qkv_weight,
        out_weight,
        up_bias,
        mod_bias,
        qv_bias,
        out_bias,
        down_bias,
    )
    (
        up_part,
        down_part,
        mod_part,
        qkv_part,
        out_part,
        up_bias_part,
        mod_bias_part,
        qv_part,
        out_bias_part,
        down_bias_part,
    ) = fetched
    mod_full, mod_bias_full = fetch_modulation(mod_part, mod_bias_part)
    mixed_mod = (
        jnp.einsum("sd,tdf->tsf", smooth, mod_full, preferred_element_type=jnp.float32)
        + mod_bias_full.astype(jnp.float32)[:, None, :]
    )
    modulation = unmix_columns(mixed_mod, seq_devices, batch_devices).reshape(
        2, local_seqs, 6, model_width
    )
    first_norms = []
    for modality in range(2):
        pieces = modulation[modality]
        first_norms.append(
            modulate(inputs[modality], pieces[:, 0], pieces[:, 1]).astype(jnp.bfloat16)
        )
    norm_image_all, norm_text_all, qv_seq, out_bias_seq, down_bias_seq = (
        lax.all_gather(first_norms[0], "seq", axis=1, tiled=True),
        lax.all_gather(first_norms[1], "seq", axis=1, tiled=True),
        lax.all_gather(qv_part, "seq", axis=1, tiled=True),
        lax.all_gather(out_bias_part, "seq", axis=1, tiled=True),
        lax.all_gather(down_bias_part, "seq", axis=1, tiled=True),
    )
    first_all = (norm_image_all, norm_text_all)
    qv_full = unmix_columns(qv_seq, seq_devices, batch_devices).astype(jnp.float32)
    out_bias_full = unmix_columns(out_bias_seq, seq_devices, batch_devices).astype(jnp.float32)
    down_bias_full = unmix_columns(down_bias_seq, seq_devices, batch_devices).astype(jnp.float32)
    qkv_cols = [
        jnp.einsum(
            "srd,df->srf",
            first_all[modality],
            qkv_part[modality],
            preferred_element_type=jnp.float32,
        )
        for modality in range(2)
    ]
    qkv_rows = to_rows(qkv_cols[0], qkv_cols[1])
    queries, keyvals = ([], [])
    for modality in range(2):
        projected = unmix_columns(qkv_rows[modality], seq_devices, batch_devices)
        qv_vector = qv_full[modality]
        queries.append(
            (projected[..., :model_width] + qv_vector[:model_width]).astype(jnp.bfloat16)
        )
        value_shift = jnp.concatenate(
            [jnp.zeros((model_width,), jnp.float32), qv_vector[model_width:]]
        )
        keyvals.append((projected[..., model_width:] + value_shift).astype(jnp.bfloat16))
    joined_query = jnp.concatenate(queries, axis=1)
    joined_keyval = jnp.concatenate(keyvals, axis=1)
    all_keyval = lax.all_gather(joined_keyval, "seq", axis=1, tiled=True)
    query_heads = joined_query.reshape(local_seqs, block_rows, HEADS, head_size)
    key_heads = all_keyval[..., :model_width].reshape(local_seqs, key_count, HEADS, head_size)
    value_heads = all_keyval[..., model_width:].reshape(local_seqs, key_count, HEADS, head_size)
    scores = (
        jnp.einsum("sqhe,skhe->shqk", query_heads, key_heads, preferred_element_type=jnp.float32)
        * factor
    )
    row_max = jnp.max(jnp.where(key_live, scores, FLOOR_SCORE), axis=-1, keepdims=True)
    exp_terms = jnp.exp(jnp.where(key_live, scores - row_max, FLOOR_SCORE))
    denominator = jnp.maximum(jnp.sum(exp_terms, axis=-1, keepdims=True), 1.0)
    prob_low = (exp_terms / denominator).astype(jnp.bfloat16)
    logsum = row_max + jnp.log(denominator)
    attended = jnp.einsum(
        "shqk,skhe->sqhe", prob_low, value_heads, preferred_element_type=jnp.float32
    )
    attended = attended.reshape(local_seqs, block_rows, model_width).astype(jnp.bfloat16)
    attended_all = gather_rows(attended[:, :image_count], attended[:, image_count:])
    out_cols = [
        jnp.einsum(
            "srd,df->srf",
            attended_all[modality],
            out_part[modality],
            preferred_element_type=jnp.float32,
        )
        for modality in range(2)
    ]
    out_rows = to_rows(out_cols[0], out_cols[1])
    projections, middles, second_norms = ([], [], [])
    for modality in range(2):
        pieces = modulation[modality]
        projection = (
            unmix_columns(out_rows[modality], seq_devices, batch_devices) + out_bias_full[modality]
        )
        middle = inputs[modality] + pieces[:, 2][:, None, :] * projection
        second_norms.append(modulate(middle, pieces[:, 3], pieces[:, 4]).astype(jnp.bfloat16))
        projections.append(projection)
        middles.append(middle)
    group_rows = gather_rows(second_norms[0], second_norms[1])
    hidden_pre, hidden_act, partials = ([], [], [])
    for modality in range(2):
        pre_values = jnp.einsum(
            "srd,df->srf",
            group_rows[modality],
            up_part[modality],
            preferred_element_type=jnp.float32,
        ) + up_bias_part[modality].astype(jnp.float32)
        act_values = gelu_tanh(pre_values).astype(jnp.bfloat16)
        partials.append(
            jnp.einsum(
                "srf,df->srd", act_values, down_part[modality], preferred_element_type=jnp.float32
            )
        )
        hidden_pre.append(pre_values)
        hidden_act.append(act_values)
    mlp_rows = sum_rows(partials[0], partials[1], seq_devices)
    mlp_outs, results = ([], [])
    for modality in range(2):
        pieces = modulation[modality]
        mlp_value = mlp_rows[modality] + down_bias_full[modality]
        results.append(
            (middles[modality] + pieces[:, 5][:, None, :] * mlp_value).astype(jnp.bfloat16)
        )
        mlp_outs.append(mlp_value)
    fetched_back = fetch_columns(
        up_weight,
        down_weight,
        mod_weight,
        qkv_weight,
        out_weight,
        up_bias,
        mod_bias,
        qv_bias,
        out_bias,
        down_bias,
    )
    up_back, down_back, mod_back, qkv_back, out_back = (
        fetched_back[0],
        fetched_back[1],
        fetched_back[2],
        fetched_back[3],
        fetched_back[4],
    )
    mod_bias_back = fetched_back[6]
    mlp_grads, gate_twos, down_bias_grads = ([], [], [])
    for modality in range(2):
        pieces = modulation[modality]
        mlp_grad = (pieces[:, 5][:, None, :] * cotangents[modality]).astype(jnp.bfloat16)
        gate_twos.append(jnp.sum(cotangents[modality] * mlp_outs[modality], axis=1))
        down_bias_grads.append(jnp.sum(mlp_grad.astype(jnp.float32), axis=(0, 1)))
        mlp_grads.append(mlp_grad)
    group_grads = gather_rows(mlp_grads[0], mlp_grads[1])
    down_grads, up_grads, up_bias_grads, norm_partials = ([], [], [], [])
    for modality in range(2):
        down_grads.append(
            jnp.einsum(
                "srd,srf->df",
                group_grads[modality],
                hidden_act[modality],
                preferred_element_type=jnp.float32,
            )
        )
        act_grad = jnp.einsum(
            "srd,df->srf",
            group_grads[modality],
            down_back[modality],
            preferred_element_type=jnp.float32,
        )
        pullback = jax.vjp(gelu_tanh, hidden_pre[modality])[1]
        pre_grad = pullback(act_grad)[0].astype(jnp.bfloat16)
        up_grads.append(
            jnp.einsum(
                "srd,srf->df", group_rows[modality], pre_grad, preferred_element_type=jnp.float32
            )
        )
        up_bias_grads.append(jnp.sum(pre_grad.astype(jnp.float32), axis=(0, 1)))
        norm_partials.append(
            jnp.einsum(
                "srf,df->srd", pre_grad, up_back[modality], preferred_element_type=jnp.float32
            )
        )
    norm_grads = sum_rows(norm_partials[0], norm_partials[1], seq_devices)
    middle_grads, shift_twos, scale_twos, gate_ones, out_bias_grads, proj_grads = (
        [],
        [],
        [],
        [],
        [],
        [],
    )
    for modality in range(2):
        pieces = modulation[modality]
        pullback = jax.vjp(modulate, middles[modality], pieces[:, 3], pieces[:, 4])[1]
        middle_part, shift_two, scale_two = pullback(norm_grads[modality])
        middle_grad = cotangents[modality] + middle_part
        proj_grad = (pieces[:, 2][:, None, :] * middle_grad).astype(jnp.bfloat16)
        gate_ones.append(jnp.sum(middle_grad * projections[modality], axis=1))
        out_bias_grads.append(jnp.sum(proj_grad.astype(jnp.float32), axis=(0, 1)))
        proj_grads.append(remix_columns(proj_grad, seq_devices, batch_devices))
        middle_grads.append(middle_grad)
        shift_twos.append(shift_two)
        scale_twos.append(scale_two)
    proj_cols = to_columns(proj_grads[0], proj_grads[1])
    out_grads, attended_partials = ([], [])
    for modality in range(2):
        out_grads.append(
            jnp.einsum(
                "srd,srf->df",
                attended_all[modality],
                proj_cols[modality],
                preferred_element_type=jnp.float32,
            )
        )
        attended_partials.append(
            jnp.einsum(
                "srf,df->srd",
                proj_cols[modality],
                out_back[modality],
                preferred_element_type=jnp.float32,
            )
        )
    attended_sums = sum_rows(attended_partials[0], attended_partials[1], seq_devices)
    attended_grad = jnp.concatenate([attended_sums[0], attended_sums[1]], axis=1).astype(
        jnp.bfloat16
    )
    grad_heads = attended_grad.reshape(local_seqs, block_rows, HEADS, head_size)
    scores_again = (
        jnp.einsum("sqhe,skhe->shqk", query_heads, key_heads, preferred_element_type=jnp.float32)
        * factor
    )
    probs_again = jnp.exp(jnp.where(key_live, scores_again - logsum, FLOOR_SCORE))
    probs_again_low = probs_again.astype(jnp.bfloat16)
    prob_grad = jnp.einsum(
        "sqhe,skhe->shqk", grad_heads, value_heads, preferred_element_type=jnp.float32
    )
    inner_sum = jnp.sum(probs_again * prob_grad, axis=-1, keepdims=True)
    score_grad = (probs_again * (prob_grad - inner_sum)).astype(jnp.bfloat16)
    query_grad = (
        jnp.einsum("shqk,skhe->sqhe", score_grad, key_heads, preferred_element_type=jnp.float32)
        * factor
    )
    query_grad = query_grad.reshape(local_seqs, block_rows, model_width).astype(jnp.bfloat16)
    key_grad = (
        jnp.einsum("shqk,sqhe->skhe", score_grad, query_heads, preferred_element_type=jnp.float32)
        * factor
    )
    value_grad = jnp.einsum(
        "shqk,sqhe->skhe", probs_again_low, grad_heads, preferred_element_type=jnp.float32
    )
    key_rows, value_rows = (
        lax.psum_scatter(
            key_grad.reshape(local_seqs, key_count, model_width),
            "seq",
            scatter_dimension=1,
            tiled=True,
        ),
        lax.psum_scatter(
            value_grad.reshape(local_seqs, key_count, model_width),
            "seq",
            scatter_dimension=1,
            tiled=True,
        ),
    )
    key_rows = key_rows.astype(jnp.bfloat16)
    value_rows = value_rows.astype(jnp.bfloat16)
    qv_bias_grads, joined_grads = ([], [])
    for modality in range(2):
        row_start, row_stop = row_spans[modality]
        query_part = query_grad[:, row_start:row_stop]
        value_part = value_rows[:, row_start:row_stop]
        joined_grad = jnp.concatenate(
            [query_part, key_rows[:, row_start:row_stop], value_part], axis=-1
        )
        qv_bias_grads.append(
            jnp.concatenate(
                [
                    jnp.sum(query_part.astype(jnp.float32), axis=(0, 1)),
                    jnp.sum(value_part.astype(jnp.float32), axis=(0, 1)),
                ]
            )
        )
        joined_grads.append(remix_columns(joined_grad, seq_devices, batch_devices))
    qkv_grad_cols = to_columns(joined_grads[0], joined_grads[1])
    qkv_grads, first_partials = ([], [])
    for modality in range(2):
        qkv_grads.append(
            jnp.einsum(
                "srd,srf->df",
                first_all[modality],
                qkv_grad_cols[modality],
                preferred_element_type=jnp.float32,
            )
        )
        first_partials.append(
            jnp.einsum(
                "srf,df->srd",
                qkv_grad_cols[modality],
                qkv_back[modality],
                preferred_element_type=jnp.float32,
            )
        )
    first_grads = sum_rows(first_partials[0], first_partials[1], seq_devices)
    input_grads, mod_partials = ([], [])
    for modality in range(2):
        pieces = modulation[modality]
        pullback = jax.vjp(modulate, inputs[modality], pieces[:, 0], pieces[:, 1])[1]
        input_part, shift_one, scale_one = pullback(first_grads[modality])
        input_grads.append(middle_grads[modality] + input_part)
        stacked = jnp.stack(
            [
                shift_one,
                scale_one,
                gate_ones[modality],
                shift_twos[modality],
                scale_twos[modality],
                gate_twos[modality],
            ],
            axis=1,
        )
        mod_partials.append(stacked.reshape(local_seqs, 6 * model_width))
    qv_mixed = remix_columns(jnp.stack(qv_bias_grads), seq_devices, batch_devices)
    out_bias_mixed = remix_columns(jnp.stack(out_bias_grads), seq_devices, batch_devices)
    down_bias_mixed = remix_columns(jnp.stack(down_bias_grads), seq_devices, batch_devices)
    mod_sum, qv_summed, out_bias_summed, down_bias_summed = lax.psum(
        (jnp.stack(mod_partials), qv_mixed, out_bias_mixed, down_bias_mixed), "seq"
    )
    mod_low = mod_sum.astype(jnp.bfloat16)
    mod_mixed = remix_columns(mod_low, seq_devices, batch_devices)
    columns = mod_part.shape[2]
    own_columns = lax.dynamic_slice_in_dim(mod_mixed, seq_index * columns, columns, 2)
    mod_grad = jnp.einsum("sd,tsf->tdf", smooth, own_columns, preferred_element_type=jnp.float32)
    mod_bias_grad = jnp.sum(own_columns.astype(jnp.float32), axis=1)
    mod_again = fetch_modulation(mod_back, mod_bias_back)[0]
    smooth_grad = jnp.einsum(
        "tsf,tdf->sd", mod_mixed, mod_again, preferred_element_type=jnp.float32
    )
    cond_pullback = jax.vjp(jax.nn.silu, cond_float)[1]
    cond_grad = cond_pullback(smooth_grad)[0]
    qv_own = own_block(qv_summed, seq_index, seq_devices)
    out_bias_own = own_block(out_bias_summed, seq_index, seq_devices)
    down_bias_own = own_block(down_bias_summed, seq_index, seq_devices)
    column_grads = (
        lax.psum_scatter(jnp.stack(up_grads), "batch", scatter_dimension=2, tiled=True),
        lax.psum_scatter(jnp.stack(down_grads), "batch", scatter_dimension=2, tiled=True),
        lax.psum_scatter(mod_grad, "batch", scatter_dimension=2, tiled=True),
        lax.psum_scatter(jnp.stack(qkv_grads), "batch", scatter_dimension=2, tiled=True),
        lax.psum_scatter(jnp.stack(out_grads), "batch", scatter_dimension=2, tiled=True),
        lax.psum_scatter(jnp.stack(up_bias_grads), "batch", scatter_dimension=1, tiled=True),
        lax.psum_scatter(mod_bias_grad, "batch", scatter_dimension=1, tiled=True),
        lax.psum_scatter(qv_own, "batch", scatter_dimension=1, tiled=True),
        lax.psum_scatter(out_bias_own, "batch", scatter_dimension=1, tiled=True),
        lax.psum_scatter(down_bias_own, "batch", scatter_dimension=1, tiled=True),
    )
    return (
        results[0],
        results[1],
        input_grads[0],
        input_grads[1],
        cond_grad,
        column_grads[2],
        column_grads[6],
        column_grads[3],
        column_grads[7],
        column_grads[4],
        column_grads[8],
        column_grads[0],
        column_grads[5],
        column_grads[1],
        column_grads[9],
    )


LOG2E = 1.4426950408889634
DEAD = -1e30
BF16 = jnp.bfloat16
F32 = jnp.float32


def dot_nt(a, b):
    return lax.dot_general(a, b, (((1,), (1,)), ((), ())), preferred_element_type=F32)


def dot_nn(a, b):
    return lax.dot_general(a, b, (((1,), (0,)), ((), ())), preferred_element_type=F32)


def dot_tn(a, b):
    return lax.dot_general(a, b, (((0,), (0,)), ((), ())), preferred_element_type=F32)


WEIGHT = {
    "attention": 6.8,
    "attention_back": 12.8,
    "project": 5.2,
    "partial_sums": 2,
    "middle": 2,
    "hidden": 7.2,
    "outer_sums": 7.2,
    "hidden_back": 8,
    "middle_back": 2.8,
    "attended_back": 2.4,
    "project_back": 4.8,
    "result": 2.8,
    "input_back": 3.6,
}


def lanes_of(columns, rows, width):
    lane = lax.broadcasted_iota(jnp.int32, (rows, width), 1)
    out = jnp.zeros((rows, width), F32)
    for k, column in enumerate(columns):
        out = jnp.where(lane == k, column, out)
    return out.astype(BF16)


def three_parts(column):
    high = column.astype(BF16).astype(F32)
    rest = column - high
    mid = rest.astype(BF16).astype(F32)
    return [high, mid, rest - mid]


def attention_kernel(
    query_rows, scale, head, bias_ref, floor_ref, qi, qt, ki, kt, vi, vt, oi, ot, li, lt, keys, values
):
    image_rows = qi.shape[0]
    rows = keys.shape[1]
    floor = floor_ref[0, 0]
    key_side = lanes_of([bias_ref[:, 0:1]], rows, head)
    value_side = lanes_of([1.0], rows, head)
    for side in range(2):
        lanes = slice(side * head, (side + 1) * head)
        for ref, extra, first, second in (
            (keys, key_side, ki, kt),
            (values, value_side, vi, vt),
        ):
            ref[side, :image_rows, :] = jnp.concatenate(
                [first[:, lanes], extra[:image_rows]], axis=1
            )
            ref[side, image_rows:, :] = jnp.concatenate(
                [second[:, lanes], extra[image_rows:]], axis=1
            )
    spans = [(qi, oi, li, start, query_rows) for start in range(0, image_rows, query_rows)]
    spans.append((qt, ot, lt, 0, qt.shape[0]))
    steps = [(*span, side) for span in spans for side in range(2)]

    def score(step):
        source, _, _, start, size, side = step
        query = source[start : start + size, side * head : (side + 1) * head]
        query = jnp.concatenate([query, lanes_of([1.0], size, head)], axis=1)
        return dot_nt(query, keys[side])

    ahead = score(steps[0])
    for at, (_, target, logs, start, size, side) in enumerate(steps):
        scores = ahead
        if at + 1 < len(steps):
            ahead = score(steps[at + 1])
        top = jnp.maximum(jnp.max(scores, axis=1, keepdims=True) * scale, floor)
        exps = jnp.exp2(scores * scale - top).astype(BF16)
        product = dot_nn(exps, values[side])
        total = jnp.maximum(product[:, head : head + 1], 1.0)
        span = slice(start, start + size)
        lanes = slice(side * head, (side + 1) * head)
        target[span, lanes] = (product[:, :head] * (1.0 / total)).astype(BF16)
        logs[span, lanes] = jnp.broadcast_to(top + jnp.log2(total), (size, head))


def pair_block(rows, lanes, pairs, part):
    return pl.BlockSpec((rows, lanes), lambda pair: (0, part * pairs + pair))


def attention(qkv_image, qkv_text, key_bias, floor, head):
    image_rows, width = qkv_image.shape
    text_rows = qkv_text.shape[0]
    rows = image_rows + text_rows
    lanes = 2 * head
    pairs = width // (3 * lanes)
    columns = [
        pair_block(count, lanes, pairs, part)
        for part in range(3)
        for count in (image_rows, text_rows)
    ]
    return pl.pallas_call(
        functools.partial(attention_kernel, 256, LOG2E / math.sqrt(head), head),
        grid=(pairs,),
        in_specs=[
            pl.BlockSpec((rows, 128), lambda pair: (0, 0)),
            pl.BlockSpec(memory_space=pltpu.SMEM),
            *columns,
        ],
        out_specs=[columns[0], columns[1], columns[0], columns[1]],
        out_shape=[
            jax.ShapeDtypeStruct((count, width // 3), dtype)
            for dtype in (BF16, F32)
            for count in (image_rows, text_rows)
        ],
        scratch_shapes=[pltpu.VMEM((2, rows, lanes), BF16)] * 2,
        compiler_params=pltpu.CompilerParams(vmem_limit_bytes=56 << 20),
        cost_estimate=pl.CostEstimate(
            flops=int(WEIGHT["attention"] * 1.15e9), bytes_accessed=1, transcendentals=0
        ),
        name="attention",
    )(key_bias, floor, qkv_image, qkv_text, qkv_image, qkv_text, qkv_image, qkv_text)


def attention_back_kernel(query_rows, scale, factor, head, pairs, *refs):
    (bias_ref, qi, qt, ki, kt, vi, vt, ai, at, li, lt, gi, gt) = refs[:13]
    oi, ot, keys, values, key_sum, value_sum = refs[13:]
    pair = pl.program_id(0)
    image_rows = qi.shape[0]
    rows = keys.shape[1]
    width = 2 * head
    key_side = lanes_of([bias_ref[:, 0:1], 1.0, 1.0, 1.0], rows, head)
    value_side = lanes_of([1.0, 1.0, 1.0], rows, head)
    for side in range(2):
        lanes = slice(side * head, (side + 1) * head)
        for ref, extra, first, second in (
            (keys, key_side, ki, kt),
            (values, value_side, vi, vt),
        ):
            ref[side, :image_rows, :] = jnp.concatenate(
                [first[:, lanes], extra[:image_rows]], axis=1
            )
            ref[side, image_rows:, :] = jnp.concatenate(
                [second[:, lanes], extra[image_rows:]], axis=1
            )
    key_sum[...] = jnp.zeros_like(key_sum)
    value_sum[...] = jnp.zeros_like(value_sum)
    spans = [(qi, ai, li, gi, oi, start, query_rows) for start in range(0, image_rows, query_rows)]
    spans.append((qt, at, lt, gt, ot, 0, qt.shape[0]))
    steps = [(*span, side) for span in spans for side in range(2)]
    query_lanes = pl.ds(pl.multiple_of(pair * width, width), width)
    key_lanes = pl.ds(pl.multiple_of((pairs + pair) * width, width), width)
    value_lanes = pl.ds(pl.multiple_of((2 * pairs + pair) * width, width), width)

    def products(step):
        source, outs, logs, grads, _, start, size, side = step
        span = slice(start, start + size)
        lanes = slice(side * head, (side + 1) * head)
        query, grad = (source[span, lanes], grads[span, lanes])
        log = logs[span, side * head : side * head + 1] * (-1.0 / scale)
        inner = -jnp.sum(
            grad.astype(F32) * outs[span, lanes].astype(F32), axis=1, keepdims=True
        )
        query_wide = jnp.concatenate(
            [query, lanes_of([1.0, *three_parts(log)], size, head)], axis=1
        )
        grad_wide = jnp.concatenate([grad, lanes_of(three_parts(inner), size, head)], axis=1)
        return (
            query,
            grad,
            dot_nt(keys[side], query_wide),
            dot_nt(values[side], grad_wide),
        )

    ahead = products(steps[0])
    dq = []
    for at_step, (_, _, _, _, target, start, size, side) in enumerate(steps):
        query, grad, scores, prob_grad = ahead
        if at_step + 1 < len(steps):
            ahead = products(steps[at_step + 1])
        probs = jnp.exp2(scores * scale)
        score_grad = (probs * prob_grad).astype(BF16)
        lanes = slice(side * head, (side + 1) * head)
        value_sum[:, lanes] += dot_nn(probs.astype(BF16), grad)
        key_sum[:, lanes] += dot_nn(score_grad, query)
        dq.append(dot_tn(score_grad, keys[side][:, :head]))
        if side == 1:
            target[start : start + size, query_lanes] = (
                jnp.concatenate(dq, axis=1) * factor
            ).astype(BF16)
            dq = []
    oi[:, key_lanes] = (key_sum[:image_rows] * factor).astype(BF16)
    ot[:, key_lanes] = (key_sum[image_rows:] * factor).astype(BF16)
    oi[:, value_lanes] = value_sum[:image_rows].astype(BF16)
    ot[:, value_lanes] = value_sum[image_rows:].astype(BF16)


def attention_back(
    qkv_image, qkv_text, out_image, out_text, log_image, log_text, grad_image, grad_text, key_bias, head
):
    image_rows, width = qkv_image.shape
    text_rows = qkv_text.shape[0]
    rows = image_rows + text_rows
    lanes = 2 * head
    pairs = width // (3 * lanes)
    columns = [
        pair_block(count, lanes, pairs, part)
        for part in range(3)
        for count in (image_rows, text_rows)
    ]
    return pl.pallas_call(
        functools.partial(
            attention_back_kernel, 512, LOG2E / math.sqrt(head), 1.0 / math.sqrt(head), head, pairs
        ),
        grid=(pairs,),
        in_specs=[
            pl.BlockSpec((rows, 128), lambda pair: (0, 0)),
            *columns,
            *(columns[:2] * 3),
        ],
        out_specs=[
            pl.BlockSpec((image_rows, width), lambda pair: (0, 0)),
            pl.BlockSpec((text_rows, width), lambda pair: (0, 0)),
        ],
        out_shape=[
            jax.ShapeDtypeStruct((image_rows, width), BF16),
            jax.ShapeDtypeStruct((text_rows, width), BF16),
        ],
        scratch_shapes=[pltpu.VMEM((2, rows, lanes), BF16)] * 2
        + [pltpu.VMEM((rows, lanes), F32)] * 2,
        compiler_params=pltpu.CompilerParams(vmem_limit_bytes=56 << 20),
        cost_estimate=pl.CostEstimate(
            flops=int(WEIGHT["attention_back"] * 1.15e9), bytes_accessed=1, transcendentals=0
        ),
        name="attention_back",
    )(
        key_bias,
        *(qkv_image, qkv_text) * 3,
        out_image, out_text, log_image, log_text, grad_image, grad_text,
    )


def flip(values, bit):
    return lax.ppermute(values, "seq", [(i, i ^ bit) for i in range(4)])


def gather_near(a, b):
    return (flip(a, 1), flip(b, 1), flip(a, 2), flip(b, 2))


def gather_far(a, b, near):
    return (a, b, *near, flip(near[0], 2), flip(near[3], 1))


def gather_halves(a, b):
    return gather_far(a, b, gather_near(a, b))


def add_low(a, b):
    return (a.astype(F32) + b.astype(F32)).astype(BF16)


def scatter_first(sent):
    return (flip(sent[1], 1), flip(sent[2], 2))


def scatter_added(sent, first):
    width = sent[3].shape[-1]
    return (
        add_low(sent[3], first[1][..., :width]),
        add_low(sent[4], first[0][..., :width]),
    )


def scatter_sent(sent, first, added):
    return (sent[0], *first, flip(added[0], 1), flip(added[1], 2))


def scatter_last(sent, first):
    return scatter_sent(sent, first, scatter_added(sent, first))


def scatter_halves(halves):
    return scatter_last(halves, scatter_first(halves))


ANYWHERE = pl.BlockSpec(memory_space=pl.ANY)
ON_CORE = pl.BlockSpec(memory_space=pltpu.VMEM)


class Copies:
    def __init__(self, semaphores):
        self.semaphores = semaphores
        self.count = 0
        self.open = []

    def start(self, source, target):
        copy = pltpu.make_async_copy(source, target, self.semaphores.at[self.count])
        self.count += 1
        copy.start()
        return copy

    def send(self, source, target):
        self.open.append(self.start(source, target))

    def finish(self):
        for copy in self.open:
            copy.wait()


def fetch_halves(copies, halves, rows, seq):
    width = rows.shape[2] // 2
    fetched = []
    for r in range(4):
        pair = []
        for side in range(2):
            half = halves[2 * r + side]
            half = half if seq is None else half.at[seq]
            pair.append(copies.start(half, rows.at[r, :, pl.ds(side * width, width)]))
        fetched.append(pair)
    return fetched


def send_block(copies, rows, sent, r):
    own, for_x, for_y, late_x, late_y = sent
    width = rows.shape[2] // 2
    low, high = pl.ds(0, width), pl.ds(width, width)
    if r == 0:
        copies.send(rows.at[0], own)
        return
    first, second = {
        1: (for_x.at[:, high], late_x),
        2: (late_y, for_y.at[:, high]),
        3: (for_x.at[:, low], for_y.at[:, low]),
    }[r]
    copies.send(rows.at[r, :, low], first)
    copies.send(rows.at[r, :, high], second)


def sent_shapes(block, D):
    return [((block, width), BF16) for width in (D, D, D, D // 2, D // 2)]


def normalize(values):
    mean = jnp.mean(values, axis=1, keepdims=True)
    centered = values - mean
    variance = jnp.mean(centered * centered, axis=1, keepdims=True)
    inverse = lax.rsqrt(variance + NORM_EPSILON)
    return centered * inverse, inverse


def normalize_back(norm, inverse, grad, scale):
    scaled = grad * (1.0 + scale)
    return inverse * (
        scaled
        - jnp.mean(scaled, axis=1, keepdims=True)
        - norm * jnp.mean(scaled * norm, axis=1, keepdims=True)
    )


def run(kernel, name, operands, specs, outs, out_specs, scratch, copies=0):
    if copies:
        scratch = [*scratch, pltpu.SemaphoreType.DMA((copies,))]
    return pl.pallas_call(
        kernel,
        in_specs=specs,
        out_specs=out_specs,
        out_shape=[jax.ShapeDtypeStruct(shape, dtype) for shape, dtype in outs],
        scratch_shapes=scratch,
        compiler_params=pltpu.CompilerParams(vmem_limit_bytes=56 << 20),
        cost_estimate=pl.CostEstimate(
            flops=int(WEIGHT[name] * 1.15e9), bytes_accessed=1, transcendentals=0
        ),
        name=name,
    )(*operands)


def project_kernel(seq, image_rows, *refs):
    halves, (weight, mods, bias) = (refs[:8], refs[8:11])
    qkv_i, qkv_t, norm_i, norm_t = refs[11:15]
    rows, held, image_norm, text_norm, image_out, text_out, semaphores = refs[15:]
    copies = Copies(semaphores)
    fetched = fetch_halves(copies, halves, rows, seq)
    weights = [copies.start(weight.at[t], held.at[t]) for t in range(2)]
    text_rows = rows.shape[1] - image_rows
    for r in range(4):
        for copy in fetched[r]:
            copy.wait()
        for t, norms, low, count in (
            (0, image_norm, 0, image_rows),
            (1, text_norm, image_rows, text_rows),
        ):
            norm, _ = normalize(rows[r, low : low + count, :].astype(F32))
            norm = norm * (1.0 + mods[t, seq, 1:2, :]) + mods[t, seq, 0:1, :]
            norms[r * count : (r + 1) * count, :] = norm.astype(BF16)
        if r == 0:
            weights[0].wait()
        span = pl.ds(r * image_rows, image_rows)
        product = dot_nt(image_norm[span, :], held[0]) + bias[0:1, :]
        image_out[span, :] = product.astype(BF16)
        copies.send(image_norm.at[span, :], norm_i.at[span, :])
        copies.send(image_out.at[span, :], qkv_i.at[span, :])
    weights[1].wait()
    text_out[...] = (dot_nt(text_norm[...], held[1]) + bias[1:2, :]).astype(BF16)
    copies.send(text_norm, norm_t)
    copies.send(text_out, qkv_t)
    copies.finish()


def project(halves, weight, mods, bias, seq, image_rows):
    block, width = halves[0].shape[-2:]
    D, W = 2 * width, weight.shape[1]
    image, text = 4 * image_rows, 4 * (block - image_rows)
    return run(
        functools.partial(project_kernel, seq, image_rows),
        "project",
        (*halves, weight, mods, bias),
        [ANYWHERE] * 9 + [ON_CORE] * 2,
        [((image, W), BF16), ((text, W), BF16), ((image, D), BF16), ((text, D), BF16)],
        [ANYWHERE] * 4,
        [
            pltpu.VMEM((4, block, D), BF16),
            pltpu.VMEM((2, W, D), BF16),
            pltpu.VMEM((image, D), BF16),
            pltpu.VMEM((text, D), BF16),
            pltpu.VMEM((image, W), BF16),
            pltpu.VMEM((text, W), BF16),
        ],
        20,
    )


def partial_kernel(seqs, dot, image_rows, *refs):
    inputs, weight, halves = (refs[: 2 * seqs], refs[2 * seqs], refs[2 * seqs + 1 : 7 * seqs + 1])
    lefts, held, rows, semaphores = (
        refs[7 * seqs + 1 : 9 * seqs + 1],
        refs[9 * seqs + 1],
        refs[9 * seqs + 2 : 10 * seqs + 2],
        refs[10 * seqs + 2],
    )
    copies = Copies(semaphores)
    weights = [copies.start(weight.at[t], held.at[t]) for t in (1, 0)]
    fetched = [
        [copies.start(inputs[2 * s + t], lefts[2 * s + t]) for t in (1, 0)] for s in range(seqs)
    ]
    text_rows = rows[0].shape[1] - image_rows
    for s in range(seqs):
        if s == 0:
            weights[0].wait()
        fetched[s][0].wait()
        text = dot(lefts[2 * s + 1][...], held[1]).astype(BF16)
        for r in range(4):
            rows[s][r, image_rows:, :] = text[r * text_rows : (r + 1) * text_rows]
        if s == 0:
            weights[1].wait()
        fetched[s][1].wait()
        for r in (3, 1, 2, 0):
            left = lefts[2 * s][r * image_rows : (r + 1) * image_rows, :]
            rows[s][r, :image_rows, :] = dot(left, held[0]).astype(BF16)
            send_block(copies, rows[s], halves[5 * s : 5 * s + 5], r)
    copies.finish()


def partial_sums(inputs, weight, dot, D, image_rows):
    seqs = len(inputs)
    image, K = inputs[0][0].shape
    text = inputs[0][1].shape[0]
    block = (image + text) // 4
    return run(
        functools.partial(partial_kernel, seqs, dot, image_rows),
        "partial_sums",
        (*[value for pair in inputs for value in pair], weight),
        [ANYWHERE] * (2 * seqs + 1),
        sent_shapes(block, D) * seqs,
        [ANYWHERE] * (5 * seqs),
        [pltpu.VMEM((count, K), BF16) for _ in range(seqs) for count in (image, text)]
        + [pltpu.VMEM(weight.shape, BF16)]
        + [pltpu.VMEM((4, block, D), BF16)] * seqs,
        2 + 2 * seqs + 7 * seqs,
    )


def piece_sum(pieces, low, count):
    own, from_x, from_y, late_x, late_y = pieces
    width = late_x.shape[-1]

    def add(*parts):
        return sum(part.astype(F32) for part in parts)

    span = pl.ds(low, count)
    return jnp.concatenate(
        [
            add(own[span, :width], from_x[span, width:], late_y[span, :]),
            add(own[span, width:], late_x[span, :], from_y[span, width:]),
        ],
        axis=1,
    )


def both_halves(halves, seq, low, count):
    return jnp.concatenate(
        [half[seq, low : low + count, :].astype(F32) for half in halves], axis=1
    )


def middle_kernel(seq, image_rows, *refs):
    pieces, tokens, (mods, bias) = (refs[:5], refs[5:7], refs[7:9])
    projection_ref, middle_ref, second_a, second_b = refs[9:]
    block, width = second_a.shape
    for t, low, count in ((0, 0, image_rows), (1, image_rows, block - image_rows)):
        span = slice(low, low + count)
        projection = piece_sum(pieces, low, count) + bias[t : t + 1, :]
        middle = both_halves(tokens, seq, low, count) + mods[t, seq, 2:3, :] * projection
        norm, _ = normalize(middle)
        second = (norm * (1.0 + mods[t, seq, 4:5, :]) + mods[t, seq, 3:4, :]).astype(BF16)
        projection_ref[span, :] = projection
        middle_ref[span, :] = middle
        second_a[span, :] = second[:, :width]
        second_b[span, :] = second[:, width:]


def middle_step(pieces, tokens, mods, bias, seq, image_rows):
    block, width = pieces[3].shape
    return run(
        functools.partial(middle_kernel, seq, image_rows),
        "middle",
        (*pieces, *tokens, mods, bias),
        [ON_CORE] * 9,
        [((block, 2 * width), F32)] * 2 + [((block, width), BF16)] * 2,
        [ON_CORE] * 4,
        [],
    )


GELU_SCALE = math.sqrt(2.0 / math.pi)
GELU_CUBE = 0.044715


def hidden_kernel(seq, image_rows, *refs):
    halves, cotangents, (weight, bias, mods) = (refs[:8], refs[8:16], refs[16:19])
    outs = refs[19:27]
    act_i, act_t, slope_i, slope_t, grad_i, grad_t, second_i, second_t = outs
    rows, given, held, acts, slopes, grads, texts, semaphores = refs[27:]
    copies = Copies(semaphores)
    fetched = fetch_halves(copies, halves, rows, None)
    weights = [copies.start(weight.at[t], held.at[t]) for t in range(2)]
    other = fetch_halves(copies, cotangents, given, seq)
    text_rows = rows.shape[1] - image_rows
    second_text, grad_text, act_text, slope_text = texts

    def activate(pre):
        squared = pre * pre
        bent = jnp.tanh(pre * (GELU_SCALE + (GELU_SCALE * GELU_CUBE) * squared))
        rise = 0.5 + 0.5 * bent
        act = pre * rise
        slope = rise + (act * (1.0 - rise)) * (
            2.0 * GELU_SCALE + (6.0 * GELU_SCALE * GELU_CUBE) * squared
        )
        return act.astype(BF16), slope.astype(BF16)

    for r in range(4):
        for copy in fetched[r]:
            copy.wait()
        if r == 0:
            weights[0].wait()
        span = pl.ds(r * image_rows, image_rows)
        text_span = slice(r * text_rows, (r + 1) * text_rows)
        pre = dot_nt(rows[r, :image_rows, :], held[0]) + bias[0:1, :]
        act, slope = activate(pre)
        acts[span, :] = act
        slopes[span, :] = slope
        second_text[text_span, :] = rows[r, image_rows:, :]
        for copy in other[r]:
            copy.wait()
        for t, target, place, low, count in (
            (0, grads, span, 0, image_rows),
            (1, grad_text, text_span, image_rows, text_rows),
        ):
            value = given[r, low : low + count, :].astype(F32) * mods[t, seq, 5:6, :]
            target[place, :] = value.astype(BF16)
        copies.send(acts.at[span, :], act_i.at[span, :])
        copies.send(slopes.at[span, :], slope_i.at[span, :])
        copies.send(grads.at[span, :], grad_i.at[span, :])
        copies.send(rows.at[r, pl.ds(0, image_rows), :], second_i.at[span, :])
    weights[1].wait()
    act_text[...], slope_text[...] = activate(
        dot_nt(second_text[...], held[1]) + bias[1:2, :]
    )
    for source, target in (
        (act_text, act_t),
        (slope_text, slope_t),
        (grad_text, grad_t),
        (second_text, second_t),
    ):
        copies.send(source, target)
    copies.finish()


def hidden_step(halves, cotangents, weight, bias, mods, seq, image_rows):
    block, width = halves[0].shape
    D, F = 2 * width, weight.shape[1]
    image, text = 4 * image_rows, 4 * (block - image_rows)

    def kernel(*refs):
        texts, semaphores = (refs[-5:-1], refs[-1])
        hidden_kernel(seq, image_rows, *refs[:-5], texts, semaphores)

    return run(
        kernel,
        "hidden",
        (*halves, *cotangents, weight, bias, mods),
        [ANYWHERE] * 17 + [ON_CORE] * 2,
        [((count, wide), BF16) for wide in (F, F, D, D) for count in (image, text)],
        [ANYWHERE] * 8,
        [
            pltpu.VMEM((4, block, D), BF16),
            pltpu.VMEM((4, block, D), BF16),
            pltpu.VMEM((2, F, D), BF16),
            pltpu.VMEM((image, F), BF16),
            pltpu.VMEM((image, F), BF16),
            pltpu.VMEM((image, D), BF16),
        ]
        + [pltpu.VMEM((text, wide), BF16) for wide in (D, D, F, F)],
        38,
    )


def outer_kernel(seqs, chunk, *refs):
    inputs, out = (refs[: 4 * seqs], refs[4 * seqs])
    held, result, semaphores = (refs[4 * seqs + 1 : -2], refs[-2], refs[-1])
    copies = Copies(semaphores)
    order = [4 * s + 2 * t + side for t in (1, 0) for s in range(seqs) for side in range(2)]
    fetched = {k: copies.start(inputs[k], held[k]) for k in order}
    columns = result.shape[1]
    for t in (1, 0):
        for s in range(seqs):
            fetched[4 * s + 2 * t].wait()
            fetched[4 * s + 2 * t + 1].wait()
        for low in range(0, columns, chunk):
            span = pl.ds(low, chunk)
            total = dot_tn(held[2 * t][:, span], held[2 * t + 1][...])
            for s in range(1, seqs):
                total = total + dot_tn(held[4 * s + 2 * t][:, span], held[4 * s + 2 * t + 1][...])
            result[t, span, :] = total.astype(BF16)
            copies.send(result.at[t, span, :], out.at[t, span, :])
    copies.finish()


def outer_sums(lefts, rights, chunk):
    seqs = len(lefts)
    columns, width = lefts[0][0].shape[1], rights[0][0].shape[1]
    operands = [side[s][t] for s in range(seqs) for t in range(2) for side in (lefts, rights)]
    return run(
        functools.partial(outer_kernel, seqs, chunk),
        "outer_sums",
        operands,
        [ANYWHERE] * (4 * seqs),
        [((2, columns, width), BF16)],
        [ANYWHERE],
        [pltpu.VMEM(value.shape, BF16) for value in operands]
        + [pltpu.VMEM((2, columns, width), BF16)],
        4 * seqs + 2 * (columns // chunk),
    )[0]


def hidden_back_kernel(image_rows, *refs):
    (grad_i, grad_t, slope_i, slope_t, down, up) = refs[:6]
    pre_i, pre_t, sums, sent = (refs[6], refs[7], refs[8], refs[9:14])
    grads, slopes, pres, grad_text, slope_text, pre_text, held_down, held_up, rows, semaphores = (
        refs[14:]
    )
    copies = Copies(semaphores)
    order = (3, 1, 2, 0)
    spans = {r: pl.ds(r * image_rows, image_rows) for r in order}
    images = {}
    downs, ups = ([None, None], [None, None])
    for k, r in enumerate(order):
        images[r] = [copies.start(grad_i.at[spans[r], :], grads.at[spans[r], :])]
        if k == 0:
            downs[0] = copies.start(down.at[0], held_down.at[0])
        images[r].append(copies.start(slope_i.at[spans[r], :], slopes.at[spans[r], :]))
        if k == 0:
            ups[0] = copies.start(up.at[0], held_up.at[0])
    texts = [copies.start(grad_t, grad_text), copies.start(slope_t, slope_text)]
    downs[1] = copies.start(down.at[1], held_down.at[1])
    ups[1] = copies.start(up.at[1], held_up.at[1])
    text_rows = rows.shape[1] - image_rows
    total = jnp.zeros((1, pres.shape[1]), F32)
    for k, r in enumerate(order):
        for copy in images[r]:
            copy.wait()
        if k == 0:
            downs[0].wait()
        product = dot_nt(grads[spans[r], :], held_down[0]) * slopes[spans[r], :].astype(F32)
        low = product.astype(BF16)
        pres[spans[r], :] = low
        copies.send(pres.at[spans[r], :], pre_i.at[spans[r], :])
        total = total + jnp.sum(low.astype(F32), axis=0, keepdims=True)
        if k == 0:
            ups[0].wait()
        rows[r, :image_rows, :] = dot_nn(pres[spans[r], :], held_up[0]).astype(BF16)
        if k == 1:
            for copy in texts:
                copy.wait()
            downs[1].wait()
            product = dot_nt(grad_text[...], held_down[1]) * slope_text[...].astype(F32)
            pre_text[...] = product.astype(BF16)
            copies.send(pre_text, pre_t)
            sums[1:2, :] = jnp.sum(pre_text[...].astype(F32), axis=0, keepdims=True)
            ups[1].wait()
            back = dot_nn(pre_text[...], held_up[1]).astype(BF16)
            for q in range(4):
                rows[q, image_rows:, :] = back[q * text_rows : (q + 1) * text_rows]
            send_block(copies, rows, sent, order[0])
        if k >= 1:
            send_block(copies, rows, sent, r)
    sums[0:1, :] = total
    copies.finish()


def hidden_back(grads, slopes, down, up, image_rows):
    image, D = grads[0].shape
    text = grads[1].shape[0]
    F = up.shape[1]
    block = (image + text) // 4
    outs = run(
        functools.partial(hidden_back_kernel, image_rows),
        "hidden_back",
        (*grads, *slopes, down, up),
        [ANYWHERE] * 6,
        [((image, F), BF16), ((text, F), BF16), ((2, F), F32)] + sent_shapes(block, D),
        [ANYWHERE] * 2 + [ON_CORE] + [ANYWHERE] * 5,
        [
            pltpu.VMEM((image, D), BF16),
            pltpu.VMEM((image, F), BF16),
            pltpu.VMEM((image, F), BF16),
            pltpu.VMEM((text, D), BF16),
            pltpu.VMEM((text, F), BF16),
            pltpu.VMEM((text, F), BF16),
            pltpu.VMEM((2, F, D), BF16),
            pltpu.VMEM((2, F, D), BF16),
            pltpu.VMEM((4, block, D), BF16),
        ],
        8 + 2 + 4 + 1 + 4 + 7,
    )
    return outs[0:2], outs[2], outs[3:]


def middle_back_kernel(seq, image_rows, *refs):
    pieces, cotangents, (middle_ref, projection_ref, mods) = (refs[:5], refs[5:7], refs[7:10])
    grad_ref, low_a, low_b, sums = refs[10:]
    block, width = low_a.shape
    for t, low, count in ((0, 0, image_rows), (1, image_rows, block - image_rows)):
        span = slice(low, low + count)
        norm_grad = piece_sum(pieces, low, count)
        norm, inverse = normalize(middle_ref[span, :])
        grad = both_halves(cotangents, seq, low, count) + normalize_back(
            norm, inverse, norm_grad, mods[t, seq, 4:5, :]
        )
        rounded = (mods[t, seq, 2:3, :] * grad).astype(BF16)
        grad_ref[span, :] = grad
        low_a[span, :] = rounded[:, :width]
        low_b[span, :] = rounded[:, width:]
        for k, value in enumerate(
            (norm_grad, norm_grad * norm, grad * projection_ref[span, :], rounded.astype(F32))
        ):
            sums[4 * t + k : 4 * t + k + 1, :] = jnp.sum(value, axis=0, keepdims=True)


def middle_back(pieces, cotangents, middle, projection, mods, seq, image_rows):
    block, width = pieces[3].shape
    return run(
        functools.partial(middle_back_kernel, seq, image_rows),
        "middle_back",
        (*pieces, *cotangents, middle, projection, mods),
        [ON_CORE] * 10,
        [((block, 2 * width), F32)] + [((block, width), BF16)] * 2 + [((8, 2 * width), F32)],
        [ON_CORE] * 4,
        [],
    )


def attended_back_kernel(image_rows, *refs):
    halves, weight = (refs[:8], refs[8])
    grad_i, grad_t, proj_i, proj_t = refs[9:13]
    rows, held, image_out, text_in, text_out, semaphores = refs[13:]
    copies = Copies(semaphores)
    fetched = fetch_halves(copies, halves, rows, None)
    weights = [copies.start(weight.at[t], held.at[t]) for t in range(2)]
    text_rows = rows.shape[1] - image_rows
    for r in range(4):
        for copy in fetched[r]:
            copy.wait()
        if r == 0:
            weights[0].wait()
        span = pl.ds(r * image_rows, image_rows)
        text_in[r * text_rows : (r + 1) * text_rows, :] = rows[r, image_rows:, :]
        copies.send(rows.at[r, pl.ds(0, image_rows), :], proj_i.at[span, :])
        image_out[span, :] = dot_nn(rows[r, :image_rows, :], held[0]).astype(BF16)
    copies.send(image_out, grad_i)
    copies.send(text_in, proj_t)
    weights[1].wait()
    text_out[...] = dot_nn(text_in[...], held[1]).astype(BF16)
    copies.send(text_out, grad_t)
    copies.finish()


def attended_back(halves, weight, image_rows):
    block, width = halves[0].shape
    D, E = 2 * width, weight.shape[2]
    image, text = 4 * image_rows, 4 * (block - image_rows)
    outs = run(
        functools.partial(attended_back_kernel, image_rows),
        "attended_back",
        (*halves, weight),
        [ANYWHERE] * 9,
        [((image, E), BF16), ((text, E), BF16), ((image, D), BF16), ((text, D), BF16)],
        [ANYWHERE] * 4,
        [
            pltpu.VMEM((4, block, D), BF16),
            pltpu.VMEM(weight.shape, BF16),
            pltpu.VMEM((image, E), BF16),
            pltpu.VMEM((text, D), BF16),
            pltpu.VMEM((text, E), BF16),
        ],
        10 + 7,
    )
    return outs[:2], outs[2:]


def project_back_kernel(seq, image_rows, *refs):
    (grad_i, grad_t, weight), tokens = (refs[:3], refs[3:11])
    sums, column_sums, sent = (refs[11], refs[12], refs[13:18])
    grads, grad_text, held, given, rows, semaphores = refs[18:]
    copies = Copies(semaphores)
    weights = [copies.start(weight.at[t], held.at[t]) for t in (1, 0)]
    text_in = copies.start(grad_t, grad_text)
    image_in = copies.start(grad_i, grads)
    fetched = fetch_halves(copies, tokens, given, seq)
    text_rows = rows.shape[1] - image_rows
    weights[0].wait()
    text_in.wait()
    text = dot_nn(grad_text[...], held[1])
    column_sums[1:2, :] = jnp.sum(grad_text[...].astype(F32), axis=0, keepdims=True)
    weights[1].wait()
    image_in.wait()
    totals = [jnp.zeros((1, rows.shape[2]), F32) for _ in range(4)]
    columns = jnp.zeros((1, grads.shape[1]), F32)
    for r in (3, 1, 2, 0):
        for copy in fetched[r]:
            copy.wait()
        span = pl.ds(r * image_rows, image_rows)
        for t, low, count in ((0, 0, image_rows), (1, image_rows, text_rows)):
            if t == 0:
                back = dot_nn(grads[span, :], held[0])
                columns = columns + jnp.sum(grads[span, :].astype(F32), axis=0, keepdims=True)
            else:
                back = text[r * text_rows : (r + 1) * text_rows, :]
            norm, _ = normalize(given[r, low : low + count, :].astype(F32))
            totals[2 * t] = totals[2 * t] + jnp.sum(back, axis=0, keepdims=True)
            totals[2 * t + 1] = totals[2 * t + 1] + jnp.sum(back * norm, axis=0, keepdims=True)
            rows[r, low : low + count, :] = back.astype(BF16)
        send_block(copies, rows, sent, r)
    column_sums[0:1, :] = columns
    for k in range(4):
        sums[k : k + 1, :] = totals[k]
    copies.finish()


def project_back(grads, weight, tokens, seq, image_rows):
    image, W = grads[0].shape
    text = grads[1].shape[0]
    D = weight.shape[2]
    block = (image + text) // 4
    outs = run(
        functools.partial(project_back_kernel, seq, image_rows),
        "project_back",
        (*grads, weight, *tokens),
        [ANYWHERE] * 11,
        [((4, D), F32), ((2, W), F32)] + sent_shapes(block, D),
        [ON_CORE] * 2 + [ANYWHERE] * 5,
        [
            pltpu.VMEM((image, W), BF16),
            pltpu.VMEM((text, W), BF16),
            pltpu.VMEM(weight.shape, BF16),
            pltpu.VMEM((4, block, D), BF16),
            pltpu.VMEM((4, block, D), BF16),
        ],
        4 + 8 + 7,
    )
    return outs[0], outs[1], outs[2:]


def result_kernel(image_rows, *refs):
    pieces, cotangents, middles = (refs[:10], refs[10:12], refs[12:14])
    mods, bias, image_out, text_out, sums = refs[14:]
    block = middles[0].shape[0]
    for seq in range(2):
        for t, low, count in ((0, 0, image_rows), (1, image_rows, block - image_rows)):
            span = slice(low, low + count)
            value = piece_sum(pieces[5 * seq : 5 * seq + 5], low, count) + bias[t : t + 1, :]
            gate = mods[t, seq, 5:6, :]
            out = (middles[seq][span, :] + gate * value).astype(BF16)
            if t == 0:
                image_out[seq] = out
            else:
                text_out[seq] = out
            grad = both_halves(cotangents, seq, low, count)
            low_grad = (gate * grad).astype(BF16).astype(F32)
            at = 4 * seq + 2 * t
            sums[at : at + 1, :] = jnp.sum(grad * value, axis=0, keepdims=True)
            sums[at + 1 : at + 2, :] = jnp.sum(low_grad, axis=0, keepdims=True)


def result_step(pieces, cotangents, middles, mods, bias, image_rows):
    seqs, (block, width) = (len(middles), pieces[3].shape)
    return run(
        functools.partial(result_kernel, image_rows),
        "result",
        (*pieces, *cotangents, *middles, mods, bias),
        [ON_CORE] * 16,
        [
            ((seqs, image_rows, 2 * width), BF16),
            ((seqs, block - image_rows, 2 * width), BF16),
            ((8, 2 * width), F32),
        ],
        [ON_CORE] * 3,
        [],
    )


def input_back_kernel(image_rows, live_text, *refs):
    pieces, tokens, grads, mods = (refs[:10], refs[10:12], refs[12:14], refs[14])
    image_out, text_out = refs[15:]
    block = grads[0].shape[0]
    for seq in range(2):
        for t, low, count in ((0, 0, image_rows), (1, image_rows, block - image_rows)):
            norm_grad = piece_sum(pieces[5 * seq : 5 * seq + 5], low, count)
            norm, inverse = normalize(both_halves(tokens, seq, low, count))
            out = grads[seq][low : low + count, :] + normalize_back(
                norm, inverse, norm_grad, mods[t, seq, 1:2, :]
            )
            if t == 0:
                image_out[seq] = out
            else:
                text_out[seq] = out[:live_text]


def input_back(pieces, tokens, grads, mods, image_rows, live_text):
    block, width = pieces[0][3].shape
    return run(
        functools.partial(input_back_kernel, image_rows, live_text),
        "input_back",
        (*pieces[0], *pieces[1], *tokens, *grads, mods),
        [ON_CORE] * 15,
        [((2, image_rows, 2 * width), F32), ((2, live_text, 2 * width), F32)],
        [ON_CORE] * 2,
        [],
    )


def match_units(batch_devices, seq_devices, per_device, group_units):
    devices = batch_devices * seq_devices
    total = devices * per_device
    part_units = total // 3
    sources, targets = ([], [])
    for seq_at in range(seq_devices):
        listed = [
            part * part_units + seq_at * group_units + k
            for part in range(3)
            for k in range(group_units)
        ]
        for place, unit in enumerate(listed):
            sources.append((unit // per_device, unit % per_device))
            targets.append(
                ((place // per_device) * seq_devices + seq_at, place % per_device)
            )
    edges = list(zip(sources, targets))
    rounds = []
    left = list(range(total))
    for _ in range(per_device):
        by_source = {}
        for e in left:
            by_source.setdefault(edges[e][0][0], []).append(e)
        taken = {}

        def place_edge(device, seen):
            for e in by_source[device]:
                target = edges[e][1][0]
                if target in seen:
                    continue
                seen.add(target)
                if target not in taken or place_edge(edges[taken[target]][0][0], seen):
                    taken[target] = e
                    return True
            return False

        for device in range(devices):
            place_edge(device, set())
        chosen = sorted(taken.values())
        rounds.append(chosen)
        left = [e for e in left if e not in chosen]
    send = np.zeros((per_device, devices), np.int32)
    land = np.zeros((per_device, devices), np.int32)
    perms = []
    for k, chosen in enumerate(rounds):
        pairs = []
        for e in chosen:
            (source, source_slot), (target, target_slot) = edges[e]
            pairs.append((source, target))
            send[k, source] = source_slot
            land[k, target] = target_slot
        perms.append(sorted(pairs))
    return perms, send, land


def move_units(units, perms, take, put, place):
    arrived = jnp.zeros_like(units)
    for k, pairs in enumerate(perms):
        slot = jnp.asarray(take[k])[place]
        moved = lax.ppermute(
            lax.dynamic_index_in_dim(units, slot, 0, keepdims=True), ("batch", "seq"), pairs
        )
        arrived = lax.dynamic_update_slice_in_dim(arrived, moved, jnp.asarray(put[k])[place], 0)
    return arrived


def gather_rows_over_batch(values):
    return lax.all_gather(values, "batch", axis=1, tiled=True)


def after(values, *others):
    return lax.optimization_barrier((values, others))[0]


def gather_small(values, axis, last=()):
    count = lax.axis_size(axis)
    held = values[None]
    bit = 1
    while bit < count:
        pairs = [(i, i ^ bit) for i in range(count)]
        if 2 * bit == count:
            held = after(held, last)
        held = jnp.concatenate([held, lax.ppermute(held, axis, pairs)])
        bit *= 2
    return jnp.take(held, jnp.bitwise_xor(lax.axis_index(axis), jnp.arange(count)), axis=0)


def scatter_rows_over_batch(values):
    dimension = values.ndim - 2
    return lax.psum_scatter(values, "batch", scatter_dimension=dimension, tiled=True)


def swap(values, axis):
    return lax.all_to_all(values, axis, 0, 0, tiled=True)


def swift_layer(
    image_tokens,
    text_tokens,
    conditioning,
    key_mask,
    mod_weight,
    mod_bias,
    qkv_weight,
    qv_bias,
    out_weight,
    out_bias,
    up_weight,
    up_bias,
    down_weight,
    down_bias,
    image_cotangent,
    text_cotangent,
):
    S = lax.axis_size("seq")
    B = lax.axis_size("batch")
    seq_index = lax.axis_index("seq")
    place = lax.axis_index(("batch", "seq"))
    L, image_count, D = image_tokens.shape
    live_text = text_tokens.shape[1]
    text_count = -(-live_text // 16) * 16
    pad = ((0, 0), (0, text_count - live_text), (0, 0))
    head = D // HEADS
    own_width = D // S
    half = D // 2

    unit = math.gcd(qkv_weight.shape[2], own_width)
    per_device = qkv_weight.shape[2] // unit
    perms, send, land = match_units(B, S, per_device, own_width // unit)
    back_perms = [[(target, source) for source, target in pairs] for pairs in perms]
    qkv_units = jnp.swapaxes(qkv_weight, 1, 2).reshape(2, per_device, unit, D).swapaxes(0, 1)
    qkv_mine = move_units(qkv_units, perms, send, land, place).swapaxes(0, 1)
    qkv_width = per_device * unit
    qkv_part = gather_rows_over_batch(qkv_mine.reshape(2, qkv_width, D))
    padded = jnp.concatenate([image_tokens, jnp.pad(text_tokens, pad)], axis=1)
    tokens = after((padded[..., :half], padded[..., half:]), qkv_mine)
    tokens_near = gather_near(*tokens)

    bias_widths = [array.shape[1] for array in (qv_bias, out_bias, up_bias, down_bias)]
    bias_ends = np.cumsum(bias_widths)
    own_biases = jnp.concatenate([qv_bias, out_bias, up_bias, down_bias], axis=1)
    near = gather_small(
        jnp.concatenate([conditioning, own_biases], axis=1),
        "batch",
        (tokens_near[0], tokens_near[3]),
    )
    cond_all = near[:, :, :D].reshape(B * L, D)
    column_biases = near[:, :, D:].astype(F32)
    smooth_all = jax.nn.silu(cond_all.astype(F32)).astype(BF16)
    mod_own = (
        jnp.einsum("sd,tdf->tsf", smooth_all, mod_weight, preferred_element_type=F32)
        + mod_bias.astype(F32)[:, None, :]
    )
    mod_width = mod_own.shape[2]
    mod_all = gather_small(mod_own, "batch", (tokens_near[1], tokens_near[2]))
    mod_came = lax.dynamic_slice_in_dim(mod_all, lax.axis_index("batch") * L, L, 2)
    small = jnp.concatenate(
        [mod_came.reshape(B, 2 * L * mod_width), column_biases.reshape(B, -1)], axis=1
    )
    tokens_all = gather_far(*tokens, tokens_near)
    small_all = gather_small(small, "seq", tokens_all[6:])
    modulation = (
        small_all[:, :, : 2 * L * mod_width]
        .reshape(S, B, 2, L, mod_width)
        .transpose(2, 3, 1, 0, 4)
        .reshape(2, L, 6, D)
    )
    bias_all = (
        small_all[:, :, 2 * L * mod_width :].reshape(S, B, 2, -1).transpose(2, 1, 0, 3)
    )
    qv_full = bias_all[..., : bias_ends[0]].reshape(2, 2 * D)
    out_bias_full = bias_all[..., bias_ends[0] : bias_ends[1]].reshape(2, D)
    down_bias_full = bias_all[..., bias_ends[2] :].reshape(2, D)
    up_bias_part = (
        column_biases[:, :, bias_ends[1] : bias_ends[2]].transpose(1, 0, 2).reshape(2, -1)
    )
    first_feature = seq_index * own_width
    qkv_bias = jnp.concatenate(
        [
            lax.dynamic_slice_in_dim(qv_full, first_feature, own_width, 1),
            jnp.zeros((2, own_width), F32),
            lax.dynamic_slice_in_dim(qv_full, D + first_feature, own_width, 1),
        ],
        axis=1,
    )

    out_units = jnp.swapaxes(out_weight, 1, 2).reshape(2, -1, S, own_width).transpose(2, 0, 1, 3)
    order = jnp.bitwise_xor(seq_index, jnp.arange(S))
    out_units = jnp.take(after(out_units, mod_own), order, axis=0)
    out_mine = jnp.stack([out_units[0], *(flip(out_units[r], r) for r in range(1, S))])
    out_mine = jnp.take(out_mine, order, axis=0)
    out_columns = out_mine.shape[2]
    out_rows = out_mine.transpose(1, 0, 2, 3).reshape(2, S * out_columns, own_width)
    out_part = gather_rows_over_batch(out_rows)
    hidden_columns = up_weight.shape[2]
    padded = jnp.concatenate([image_cotangent, jnp.pad(text_cotangent, pad)], axis=1)
    cotangents = (padded[..., :half], padded[..., half:])
    near_grads = gather_near(*after(cotangents, tokens_all, small_all))
    up_part = gather_rows_over_batch(after(jnp.swapaxes(up_weight, 1, 2), out_mine, mod_own))
    down_part = gather_rows_over_batch(after(jnp.swapaxes(down_weight, 1, 2), out_mine, mod_own))

    image_keys = jnp.take(
        key_mask[:, : S * image_count].reshape(L, S, image_count), order, axis=1
    )
    text_keys = jnp.take(
        key_mask[:, S * image_count :].reshape(L, S, live_text), order, axis=1
    )
    text_keys = jnp.pad(text_keys, ((0, 0), (0, 0), (0, text_count - live_text)))
    live = jnp.concatenate([image_keys.reshape(L, -1), text_keys.reshape(L, -1)], axis=1) > 0
    key_bias = jnp.where(live, 0.0, DEAD).astype(F32)
    floors = jnp.where(jnp.all(key_mask > 0, axis=1), -3e38, FLOOR_SCORE * LOG2E).astype(F32)
    floors = floors.reshape(L, 1, 1)
    key_bias = jnp.broadcast_to(key_bias[:, :, None], (*key_bias.shape, 128))

    kept = []
    first = project(tokens_all, qkv_part, modulation, qkv_bias, 0, image_count)
    attended = attention(first[0], first[1], key_bias[0], floors[0], head)
    attended, logs = (attended[:2], attended[2:])
    attended = after(attended, near_grads)
    parts = partial_sums([attended], out_part, dot_nt, D, image_count)
    kept.append((first, attended, logs, parts))
    again = after(tokens_all, parts)
    first = project(again, qkv_part, modulation, qkv_bias, 1, image_count)
    attended = attention(first[0], first[1], key_bias[1], floors[1], head)
    attended, logs = (attended[:2], attended[2:])
    cotangents_all = gather_far(*cotangents, after(near_grads, kept[0][1]))
    out_first = scatter_first(kept[0][3])
    out_added = scatter_added(kept[0][3], after(out_first, attended))
    attended = after(attended, cotangents_all, out_added)
    parts = partial_sums([attended], out_part, dot_nt, D, image_count)
    kept.append((first, attended, logs, parts))
    firsts, attendeds, logs, out_halves = zip(*kept)
    out_pieces = [scatter_sent(out_halves[0], out_first, out_added)]
    out_pieces.append(scatter_halves(after(out_halves[1], out_pieces[0])))
    steps = []
    for s in range(L):
        steps.append(
            middle_step(
                out_pieces[s],
                tokens,
                modulation,
                out_bias_full,
                s,
                image_count,
            )
        )
    second_near = [gather_near(*step[2:]) for step in steps]
    hidden = []
    for s in range(L):
        near = after(second_near[s], hidden[-1]) if s else second_near[s]
        halves = gather_far(*steps[s][2:], near)
        hidden.append(
            hidden_step(
                halves, cotangents_all, up_part, up_bias_part, modulation, s, image_count
            )
        )
    acts, slopes, grads, norms = [[step[i : i + 2] for step in hidden] for i in (0, 2, 4, 6)]

    down_sum = outer_sums(acts, grads, 256)
    down_came = scatter_rows_over_batch(down_sum)
    pres, bias_sums, norm2_halves = ([], [], [])
    gate = down_sum
    for s in range(L):
        pre, sums, halves = hidden_back(
            after(grads[s], gate), slopes[s], down_part, up_part, image_count
        )
        gate = halves
        pres.append(pre)
        bias_sums.append(sums)
        norm2_halves.append(halves)
    up_bias_sum = sum(bias_sums)
    norm2_first = scatter_first(norm2_halves[0])
    norm2_added = scatter_added(norm2_halves[0], after(norm2_first, gate))
    norm2_pieces = scatter_sent(norm2_halves[0], norm2_first, norm2_added)
    norm2_first1 = scatter_first(after(norm2_halves[1], norm2_pieces[3:]))
    backs = [
        middle_back(
            after(norm2_pieces, gate),
            cotangents,
            *steps[0][1::-1],
            modulation,
            0,
            image_count,
        )
    ]
    proj_near0 = gather_near(*backs[0][1:3])
    mlp_halves = partial_sums(after(acts, backs[0]), down_part, dot_nn, D, image_count)
    up_sum = outer_sums(after(pres, mlp_halves), norms, 256)
    norm2_added = scatter_added(norm2_halves[1], after(norm2_first1, mlp_halves))
    norm2_pieces = scatter_sent(norm2_halves[1], norm2_first1, norm2_added)
    projs = [gather_far(*backs[0][1:3], after(proj_near0, up_sum))]
    backs.append(
        middle_back(
            after(norm2_pieces, up_sum, proj_near0),
            cotangents,
            *steps[1][1::-1],
            modulation,
            1,
            image_count,
        )
    )
    proj_near1 = gather_near(*backs[1][1:3])
    grad0, proj0 = attended_back(
        after(projs[0], backs[1], down_came), out_part, image_count
    )
    up_came = scatter_rows_over_batch(after(up_sum, backs[1]))
    qkv_grad0 = attention_back(
        *firsts[0][:2], *attendeds[0], *logs[0], *grad0, key_bias[0], head
    )
    projs.append(gather_far(*backs[1][1:3], after(proj_near1, qkv_grad0)))
    mlp_halves = (mlp_halves[:5], mlp_halves[5:])
    mlp_first = [scatter_first(after(mlp_halves[0], grad0))]
    sums0, columns0, halves0 = project_back(
        after(qkv_grad0, mlp_first), qkv_part, tokens_all, 0, image_count
    )
    grad1, proj1 = attended_back(after(projs[1], halves0), out_part, image_count)
    mlp_first.append(scatter_first(after(mlp_halves[1], projs[1])))
    out_sum = outer_sums([proj0, proj1], attendeds, 256)
    out_came = scatter_rows_over_batch(out_sum)
    grad1 = after(grad1, out_sum)
    qkv_grad1 = attention_back(
        *firsts[1][:2], *attendeds[1], *logs[1], *grad1, key_bias[1], head
    )
    mlp_added = [
        scatter_added(halves, after(first, qkv_grad1))
        for halves, first in zip(mlp_halves, mlp_first)
    ]
    mlp_pieces = [
        piece
        for halves, first, added in zip(mlp_halves, mlp_first, mlp_added)
        for piece in scatter_sent(halves, first, added)
    ]
    qkv_sum = outer_sums(
        [qkv_grad0, after(qkv_grad1, mlp_added, up_came)],
        [first[2:] for first in firsts],
        128 if qkv_width % 256 else 256,
    )
    qkv_came = scatter_rows_over_batch(after(qkv_sum, out_came))
    sums1, columns1, halves1 = project_back(
        after(qkv_grad1, qkv_sum), qkv_part, tokens_all, 1, image_count
    )
    norm1_pieces = [
        scatter_halves(after(halves0, qkv_sum)),
        scatter_halves(after(halves1, mlp_pieces)),
    ]
    image_out, text_out, result_sums = result_step(
        after(mlp_pieces, halves1),
        cotangents,
        [step[1] for step in steps],
        modulation,
        down_bias_full,
        image_count,
    )
    image_grad, text_grad = input_back(
        after(norm1_pieces, qkv_came),
        tokens,
        [back[0] for back in backs],
        modulation,
        image_count,
        live_text,
    )
    out_home = swap(
        after(out_came, image_grad).reshape(2, S, out_columns, own_width).swapaxes(0, 1), "seq"
    )
    qkv_home = move_units(
        qkv_came.reshape(2, per_device, unit, D).swapaxes(0, 1),
        back_perms, land, send, place
    )
    qkv_weight_grad = qkv_home.swapaxes(0, 1).reshape(2, -1, D).swapaxes(1, 2).astype(F32)
    out_weight_grad = (
        out_home.transpose(1, 2, 0, 3).reshape(2, out_columns, D).swapaxes(1, 2).astype(F32)
    )
    up_weight_grad = up_came.swapaxes(1, 2).astype(F32)
    down_weight_grad = down_came.swapaxes(1, 2).astype(F32)


    first_sums = jnp.stack([sums0, sums1]).reshape(L, 2, 2, D)
    second_sums = jnp.stack([back[3] for back in backs]).reshape(L, 2, 4, D)
    result_sums = result_sums.reshape(L, 2, 2, D)
    mod_rows = jnp.concatenate(
        [
            first_sums,
            second_sums[:, :, 2:3],
            second_sums[:, :, :2],
            result_sums[:, :, :1],
        ],
        axis=2,
    ).swapaxes(0, 1)
    mod_rows = mod_rows.reshape(2, L, B, S, mod_width).transpose(3, 2, 0, 1, 4)
    out_bias_sum = jnp.sum(second_sums[:, :, 3], axis=0)
    down_bias_sum = jnp.sum(result_sums[:, :, 1], axis=0)
    column_sums = columns0 + columns1
    qv_bias_sum = jnp.zeros((2, 2 * D), F32)
    for part, column in ((0, 0), (1, 2 * own_width)):
        qv_bias_sum = lax.dynamic_update_slice_in_dim(
            qv_bias_sum, column_sums[:, column : column + own_width], part * D + first_feature, 1
        )
    up_bias_rows = lax.dynamic_update_slice_in_dim(
        jnp.zeros((2, B, S, hidden_columns), F32),
        up_bias_sum.reshape(2, B, 1, hidden_columns),
        seq_index,
        2,
    )
    bias_rows = jnp.concatenate(
        [
            qv_bias_sum.reshape(2, B, S, -1),
            out_bias_sum.reshape(2, B, S, -1),
            up_bias_rows,
            down_bias_sum.reshape(2, B, S, -1),
        ],
        axis=3,
    ).transpose(2, 1, 0, 3)
    packed = jnp.concatenate(
        [mod_rows.reshape(S, B, -1), bias_rows.reshape(S, B, -1)], axis=2
    )
    packed = jnp.sum(swap(packed, "seq"), axis=0)
    packed = swap(packed, "batch")
    mod_mine = (
        packed[:, : 2 * L * mod_width]
        .reshape(B, 2, L, mod_width)
        .transpose(1, 0, 2, 3)
        .reshape(2, B * L, mod_width)
        .astype(BF16)
    )
    bias_mine = jnp.sum(packed[:, 2 * L * mod_width :], axis=0).reshape(2, -1)
    qv_bias_grad, out_bias_grad, up_bias_grad, down_bias_grad = jnp.split(
        bias_mine, bias_ends[:3], axis=1
    )
    mod_weight_grad = jnp.einsum(
        "sd,tsf->tdf", smooth_all, mod_mine, preferred_element_type=F32
    )
    mod_bias_grad = jnp.sum(mod_mine.astype(F32), axis=1)
    smooth_part = jnp.einsum("tsf,tdf->sd", mod_mine, mod_weight, preferred_element_type=F32)
    smooth_grad = jnp.sum(swap(smooth_part.reshape(B, L, D), "batch"), axis=0)
    smooth_grad = after(smooth_grad, qkv_home)
    smooth_grad = smooth_grad + flip(smooth_grad, 1)
    smooth_grad = smooth_grad + flip(smooth_grad, 2)
    cond_grad = jax.vjp(jax.nn.silu, conditioning.astype(F32))[1](smooth_grad)[0]
    return (
        image_out,
        text_out[:, :live_text],
        image_grad,
        text_grad,
        cond_grad,
        mod_weight_grad,
        mod_bias_grad,
        qkv_weight_grad,
        qv_bias_grad,
        out_weight_grad,
        out_bias_grad,
        up_weight_grad,
        up_bias_grad,
        down_weight_grad,
        down_bias_grad,
    )


def choose_layer(mesh):
    if mesh.shape["seq"] == 4 and HEADS % 8 == 0:
        return swift_layer
    return general_layer


def solution(mesh):
    layer = choose_layer(mesh)
    return jax.shard_map(
        layer,
        mesh=mesh,
        in_specs=(
            P("batch", "seq", None),
            P("batch", "seq", None),
            P("batch", None),
            P("batch", None),
            P(None, None, ("batch", "seq")),
            P(None, ("batch", "seq")),
            P(None, None, ("batch", "seq")),
            P(None, ("batch", "seq")),
            P(None, None, ("batch", "seq")),
            P(None, ("batch", "seq")),
            P(None, None, ("batch", "seq")),
            P(None, ("batch", "seq")),
            P(None, None, ("batch", "seq")),
            P(None, ("batch", "seq")),
            P("batch", "seq", None),
            P("batch", "seq", None),
        ),
        out_specs=(
            P("batch", "seq", None),
            P("batch", "seq", None),
            P("batch", "seq", None),
            P("batch", "seq", None),
            P("batch", None),
            P(None, None, ("batch", "seq")),
            P(None, ("batch", "seq")),
            P(None, None, ("batch", "seq")),
            P(None, ("batch", "seq")),
            P(None, None, ("batch", "seq")),
            P(None, ("batch", "seq")),
            P(None, None, ("batch", "seq")),
            P(None, ("batch", "seq")),
            P(None, None, ("batch", "seq")),
            P(None, ("batch", "seq")),
        ),
        check_vma=False,
    )
```
